32 devices in a mesh: seq: 4 (over y, x), grp: 8 (over z, core).
Axes of the slice: x: 2, y: 2, z: 4, core: 2. Of those that a mesh axis runs over, the one named last changes fastest.
Arguments:
- tokens: bfloat16 [8, 4608, 512], P('grp', 'seq'), may hold values from -6 to 6
- cotangent: bfloat16 [8, 4608, 512], P('grp', 'seq'), may hold values from -6 to 6
- lengths: int32 [8], P('grp'), may hold values from 3457 to 4608, as said below
- weight_query: float32 [512, 512], P(('seq', 'grp')), may hold values from -0.25 to 0.25
- weight_memory: float32 [3, 512, 1024], P(None, ('seq', 'grp')), may hold values from -0.15625 to 0.15625
- weight_out: float32 [512, 512], P(('seq', 'grp')), may hold values from -1.5 to 1.5
- weight_up: float32 [512, 2048], P(('seq', 'grp')), may hold values from -0.25 to 0.25
- weight_down: float32 [2048, 512], P(('seq', 'grp')), may hold values from -0.125 to 0.125
- vectors: float32 [9, 512], P(None, ('seq', 'grp')), may hold values from -0.5 to 1.5, as said below
- first_query: float32 [512, 512], P(('seq', 'grp')), may hold values from -64 to 64
- first_memory: float32 [3, 512, 1024], P(None, ('seq', 'grp')), may hold values from -40 to 40
- first_out: float32 [512, 512], P(('seq', 'grp')), may hold values from -24 to 24
- first_up: float32 [512, 2048], P(('seq', 'grp')), may hold values from -40 to 40
- first_down: float32 [2048, 512], P(('seq', 'grp')), may hold values from -80 to 80
- first_vectors: float32 [9, 512], P(None, ('seq', 'grp')), may hold values from -128 to 128
- second_query: float32 [512, 512], P(('seq', 'grp')), may hold values from 484.7616 to 1939.0464
- second_memory: float32 [3, 512, 1024], P(None, ('seq', 'grp')), may hold values from 174.36671 to 696.7296
- second_out: float32 [512, 512], P(('seq', 'grp')), may hold values from 77.4144 to 309.6576
- second_up: float32 [512, 2048], P(('seq', 'grp')), may hold values from 174.36671 to 696.7296
- second_down: float32 [2048, 512], P(('seq', 'grp')), may hold values from 696.7296 to 2790.6047
- second_vectors: float32 [9, 512], P(None, ('seq', 'grp')), may hold values from 1939.0464 to 7741.44
Outputs:
- out_tokens: bfloat16 [8, 4608, 512], P('grp', 'seq')
- grad_tokens: bfloat16 [8, 4608, 512], P('grp', 'seq')
- moment_query: float32 [512, 512], P(('seq', 'grp'))
- moment_memory: float32 [3, 512, 1024], P(None, ('seq', 'grp'))
- moment_out: float32 [512, 512], P(('seq', 'grp'))
- moment_up: float32 [512, 2048], P(('seq', 'grp'))
- moment_down: float32 [2048, 512], P(('seq', 'grp'))
- moment_vectors: float32 [9, 512], P(None, ('seq', 'grp'))
- square_query: float32 [512, 512], P(('seq', 'grp'))
- square_memory: float32 [3, 512, 1024], P(None, ('seq', 'grp'))
- square_out: float32 [512, 512], P(('seq', 'grp'))
- square_up: float32 [512, 2048], P(('seq', 'grp'))
- square_down: float32 [2048, 512], P(('seq', 'grp'))
- square_vectors: float32 [9, 512], P(None, ('seq', 'grp'))
- master_query: float32 [512, 512], P(('seq', 'grp'))
- master_memory: float32 [3, 512, 1024], P(None, ('seq', 'grp'))
- master_out: float32 [512, 512], P(('seq', 'grp'))
- master_up: float32 [512, 2048], P(('seq', 'grp'))
- master_down: float32 [2048, 512], P(('seq', 'grp'))
- master_vectors: float32 [9, 512], P(None, ('seq', 'grp'))
- copy_query: bfloat16 [512, 512], P(('seq', 'grp'))
- copy_memory: bfloat16 [3, 512, 1024], P(None, ('seq', 'grp'))
- copy_out: bfloat16 [512, 512], P(('seq', 'grp'))
- copy_up: bfloat16 [512, 2048], P(('seq', 'grp'))
- copy_down: bfloat16 [2048, 512], P(('seq', 'grp'))
- copy_vectors: bfloat16 [9, 512], P(None, ('seq', 'grp'))
The draws below stay inside these ranges and needn't reach their ends.
Inputs may be any that keep to these rules, and one draw needn't show every extreme that they name: `lengths`: every sequence has more than 3456 live positions; some sequence fills all 4608. `vectors`: rows 0 and 2 lie between 0.5 and 1.5, the other rows between -0.5 and 0.5.
All inputs are finite; a program needn't handle non-finite values.
Results may differ from the reference program's by a relative error of at most 0.012.
The reference program's roundings to bfloat16 on the way count: a program that leaves them out, or rounds other values in their place, can miss the bound.
Values may be sent and summed in bfloat16 or wider, within the bound.
A program may use at most 128 MiB of HBM per device.

```python
import math
import jax
import jax.numpy as jnp
from jax import lax

D = 512
FF = 2048
H = 8
HEAD_WIDTH = 64
TOK_DEV = 1152
STEP = 10
SEQ_CAP = 4608
GROUPS = 8
TOKENS = 36864


def draw_lengths(key, part):
    key_short, key_full = jax.random.split(key)
    shortened = SEQ_CAP - jax.random.randint(key_short, (GROUPS,), 0, TOK_DEV)
    chosen = jax.random.randint(key_full, (), 0, GROUPS)
    return jnp.where(jnp.arange(GROUPS) == chosen, SEQ_CAP, shortened).astype(jnp.int32)


def draw_vectors(key, part):
    key_gain, key_shift = jax.random.split(key)
    gain_rows = 1.0 + 0.2 * jnp.clip(jax.random.normal(key_gain, (9, D), jnp.float32), -2.5, 2.5)
    shifts = 0.2 * jnp.clip(jax.random.normal(key_shift, (9, D), jnp.float32), -2.5, 2.5)
    row_index = jnp.arange(9)[:, None]
    return jnp.where((row_index == 0) | (row_index == 2), gain_rows, shifts)


def steps_of(rng, shape, pieces, low, largest):
    factor_of, own = 1.0, jax.random.fold_in(rng, 6)
    for position, shards_of in pieces:
        heights = jnp.exp(jax.random.uniform(jax.random.fold_in(own, position), (shards_of,), jnp.float32, low / len(pieces), largest / len(pieces)))
        factor_of = factor_of * jnp.repeat(heights, shape[position] // shards_of).reshape([-1 if axis == position else 1 for axis in range(len(shape))])
    return factor_of


def noise(stream_key, extent, width, reach, shards=(), kind=jnp.bfloat16):
    factor_of = steps_of(stream_key, extent, shards, -0.22, 0.18) if shards else 1.0
    values = jax.random.normal(stream_key, extent, jnp.float32) * width * factor_of
    return jnp.minimum(jnp.maximum(values, -reach), reach).astype(kind)


def setup_inputs(seed: int = 0) -> dict:
    key_of = jax.random.split(jax.random.key(seed), 22)
    tokens = noise(key_of[0], (GROUPS, SEQ_CAP, D), 1.0, 6.0, ((0, 8), (1, 4)))
    cotangent = noise(key_of[1], (GROUPS, SEQ_CAP, D), 1.0, 6.0, ((0, 8), (1, 4)))
    lengths = draw_lengths(jax.random.fold_in(key_of[21], 71), 0)
    weight_query = noise(key_of[3], (D, D), D ** -0.5, 0.25, ((0, 32),), jnp.float32)
    weight_memory = noise(key_of[4], (3, D, 2 * D), (3 * D) ** -0.5, 0.15625, ((1, 32),), jnp.float32)
    weight_out = noise(key_of[5], (D, D), (D // 32) ** -0.5, 1.5, ((0, 32),), jnp.float32)
    weight_up = noise(key_of[6], (D, FF), D ** -0.5, 0.25, ((0, 32),), jnp.float32)
    weight_down = noise(key_of[7], (FF, D), FF ** -0.5, 0.125, ((0, 32),), jnp.float32)
    vectors = draw_vectors(jax.random.fold_in(key_of[21], 71), 0)
    first_query = noise(key_of[9], (D, D), (0.0555 * TOKENS ** 0.5), 64.0, ((0, 32),), jnp.float32)
    first_memory = noise(key_of[10], (3, D, 2 * D), (0.0333 * TOKENS ** 0.5), 40.0, ((1, 32),), jnp.float32)
    first_out = noise(key_of[11], (D, D), (0.0222 * TOKENS ** 0.5), 24.0, ((0, 32),), jnp.float32)
    first_up = noise(key_of[12], (D, FF), (0.0333 * TOKENS ** 0.5), 40.0, ((0, 32),), jnp.float32)
    first_down = noise(key_of[13], (FF, D), (0.0666 * TOKENS ** 0.5), 80.0, ((0, 32),), jnp.float32)
    first_vectors = noise(key_of[14], (9, D), (0.111 * TOKENS ** 0.5), 128.0, ((1, 32),), jnp.float32)
    second_query = jnp.clip(jnp.exp(math.log(1939.0464) - 1.3862944 * jax.random.uniform(key_of[15], (D, D), jnp.float32) ** steps_of(key_of[15], (D, D), ((0, 32),), -0.2, 0.2)), 484.7616, 1939.0464)
    second_memory = jnp.clip(jnp.exp(math.log(696.7296) - 1.38523677 * jax.random.uniform(key_of[16], (3, D, 2 * D), jnp.float32) ** steps_of(key_of[16], (3, D, 2 * D), ((1, 32),), -0.2, 0.2)), 174.36671, 696.7296)
    second_out = jnp.clip(jnp.exp(math.log(309.6576) - 1.3862944 * jax.random.uniform(key_of[17], (D, D), jnp.float32) ** steps_of(key_of[17], (D, D), ((0, 32),), -0.2, 0.2)), 77.4144, 309.6576)
    second_up = jnp.clip(jnp.exp(math.log(696.7296) - 1.38523677 * jax.random.uniform(key_of[18], (D, FF), jnp.float32) ** steps_of(key_of[18], (D, FF), ((0, 32),), -0.2, 0.2)), 174.36671, 696.7296)
    second_down = jnp.clip(jnp.exp(math.log(2790.6047) - 1.3876162 * jax.random.uniform(key_of[19], (FF, D), jnp.float32) ** steps_of(key_of[19], (FF, D), ((0, 32),), -0.2, 0.2)), 696.7296, 2790.6047)
    second_vectors = jnp.clip(jnp.exp(math.log(7741.44) - 1.3843914 * jax.random.uniform(key_of[20], (9, D), jnp.float32) ** steps_of(key_of[20], (9, D), ((1, 32),), -0.2, 0.2)), 1939.0464, 7741.44)
    return dict(tokens=tokens, cotangent=cotangent, lengths=lengths, weight_query=weight_query, weight_memory=weight_memory, weight_out=weight_out, weight_up=weight_up, weight_down=weight_down, vectors=vectors, first_query=first_query, first_memory=first_memory, first_out=first_out, first_up=first_up, first_down=first_down, first_vectors=first_vectors, second_query=second_query, second_memory=second_memory, second_out=second_out, second_up=second_up, second_down=second_down, second_vectors=second_vectors)


@jax.custom_vjp
def low(v):
    return lax.optimization_barrier(v.astype(jnp.bfloat16)).astype(jnp.float32)

@jax.custom_vjp
def reduced_backward(v):
    return v

def low_keep(v):
    return (low(v), None)

def low_pass(kept, grad):
    return (grad,)

def back_keep(v):
    return (v, None)

def back_low(kept, grad):
    return (low(grad),)
low.defvjp(low_keep, low_pass)
reduced_backward.defvjp(back_keep, back_low)
NORM_EPSILON = 1e-05
BETA_FIRST = 0.9
BETA_SECOND = 0.95
ADAM_EPSILON = 1e-08
WEIGHT_DECAY = 0.1
LEARNING_RATES = (0.05, 0.04, 0.3, 0.05, 0.03, 0.5)
MASKED_SCORE = -1e+30

def product(left, right):
    return jnp.dot(left, right, precision=lax.Precision.HIGHEST, preferred_element_type=jnp.float32)

def layer_norm(values, gain, shift):
    centred = values - lax.optimization_barrier(jnp.mean(values, axis=-1, keepdims=True))
    spread = lax.optimization_barrier(jnp.mean(centred * centred, axis=-1, keepdims=True))
    return centred * lax.rsqrt(spread + NORM_EPSILON) * gain + shift

def forward(weight_query, weight_memory, weight_out, weight_up, weight_down, vectors, tokens):
    length_rows = tokens.shape[0]
    slot_count = length_rows // 3
    normed = low(layer_norm(tokens, vectors[0], vectors[1]))
    queries = reduced_backward(low(product(normed, weight_query)))
    padded = jnp.concatenate([jnp.zeros((2, D), jnp.float32), normed], axis=0)
    windows = padded[:length_rows].reshape(slot_count, 3 * D)
    memory = reduced_backward(low(product(windows, weight_memory.reshape(3 * D, 2 * D))))
    key_row_block = memory[:, :D].reshape(slot_count, H, HEAD_WIDTH)
    value_row_block = memory[:, D:].reshape(slot_count, H, HEAD_WIDTH)
    block_rows = min(512, length_rows)
    block_count = length_rows // block_rows
    slot_starts = 3 * jnp.arange(slot_count, dtype=jnp.int32)

    def attend(inputs):
        query_tile_rows, offset_rows = inputs
        positions = offset_rows + jnp.arange(block_rows, dtype=jnp.int32)
        score_matrix = reduced_backward(jnp.einsum('azv,lzv->zal', query_tile_rows, key_row_block, precision=lax.Precision.HIGHEST) * HEAD_WIDTH ** (-0.5))
        visible = slot_starts[None, :] <= positions[:, None]
        score_matrix = jnp.where(visible[None], score_matrix, MASKED_SCORE)
        highest = lax.optimization_barrier(jnp.max(score_matrix, axis=-1, keepdims=True))
        exponent = jnp.exp(score_matrix - highest)
        attention_layer = low(exponent / lax.optimization_barrier(jnp.sum(exponent, axis=-1, keepdims=True)))
        return jnp.einsum('yup,pyb->uyb', attention_layer, value_row_block, precision=lax.Precision.HIGHEST)
    block_queries = queries.reshape(block_count, block_rows, H, HEAD_WIDTH)
    block_offsets = block_rows * jnp.arange(block_count, dtype=jnp.int32)
    mixed = lax.map(jax.checkpoint(attend), (block_queries, block_offsets))
    attended = reduced_backward(low(mixed.reshape(length_rows, D)))
    residual = tokens + reduced_backward(product(attended, weight_out))
    normed_two = low(layer_norm(residual, vectors[2], vectors[3]))
    pre_act = reduced_backward(product(normed_two, weight_up) + vectors[5:].reshape(FF))
    activated = low(jax.nn.gelu(pre_act))
    return residual + product(activated, weight_down) + vectors[4]

def adamw(weight, gradient, moment, square, step_rate):
    moment_new = BETA_FIRST * moment + (1.0 - BETA_FIRST) * gradient
    square_new = BETA_SECOND * square + (1.0 - BETA_SECOND) * gradient * gradient
    fixed_first = 1.0 - BETA_FIRST ** STEP
    fixed_second = 1.0 - BETA_SECOND ** STEP
    update = moment_new / fixed_first / (jnp.sqrt(square_new / fixed_second) + ADAM_EPSILON) + WEIGHT_DECAY * weight
    master = weight - step_rate * update
    return (moment_new, square_new, master, master.astype(jnp.bfloat16))

def reference(tokens, cotangent, lengths, weight_query, weight_memory, weight_out, weight_up, weight_down, vectors, first_query, first_memory, first_out, first_up, first_down, first_vectors, second_query, second_memory, second_out, second_up, second_down, second_vectors):
    masters = (weight_query, weight_memory, weight_out, weight_up, weight_down, vectors)
    rounded = tuple((member.astype(jnp.bfloat16).astype(jnp.float32) for member in masters))

    def one_group(totals, inputs):
        group_tokens, group_cot, group_length = inputs
        live_mask = (jnp.arange(SEQ_CAP, dtype=jnp.int32) < group_length).astype(jnp.float32)
        result, pullback = jax.vjp(forward, rounded[0], rounded[1], rounded[2], rounded[3], rounded[4], rounded[5], group_tokens.astype(jnp.float32))
        gradients = pullback(group_cot.astype(jnp.float32) * live_mask[:, None])
        totals = tuple((summed + extra for summed, extra in zip(totals, gradients[:6])))
        return (totals, (result.astype(jnp.bfloat16), gradients[6].astype(jnp.bfloat16)))
    zeros_init = tuple((jnp.zeros(member.shape, jnp.float32) for member in masters))
    totals, (out_tokens, grad_tokens) = lax.scan(one_group, zeros_init, (tokens, cotangent, lengths))
    new_query = adamw(weight_query, totals[0], first_query, second_query, LEARNING_RATES[0])
    new_memory = adamw(weight_memory, totals[1], first_memory, second_memory, LEARNING_RATES[1])
    new_out = adamw(weight_out, totals[2], first_out, second_out, LEARNING_RATES[2])
    new_up = adamw(weight_up, totals[3], first_up, second_up, LEARNING_RATES[3])
    new_down = adamw(weight_down, totals[4], first_down, second_down, LEARNING_RATES[4])
    new_vectors = adamw(vectors, totals[5], first_vectors, second_vectors, LEARNING_RATES[5])
    return (out_tokens, grad_tokens, new_query[0], new_memory[0], new_out[0], new_up[0], new_down[0], new_vectors[0], new_query[1], new_memory[1], new_out[1], new_up[1], new_down[1], new_vectors[1], new_query[2], new_memory[2], new_out[2], new_up[2], new_down[2], new_vectors[2], new_query[3], new_memory[3], new_out[3], new_up[3], new_down[3], new_vectors[3])
```

```python
import functools

import jax
import jax.numpy as jnp
from jax import lax
from jax.experimental import pallas as pl
from jax.experimental.pallas import tpu as pltpu
from jax.sharding import PartitionSpec as P

H = 8
STEP = 10


NORM_EPSILON = 1e-05
BETA_FIRST = 0.9
BETA_SECOND = 0.95
ADAM_EPSILON = 1e-08
WEIGHT_DECAY = 0.1
LEARNING_RATES = (0.05, 0.04, 0.3, 0.05, 0.03, 0.5)
MASKED_SCORE = -1e30


def from_behind(x, axis, by):
    peers = lax.axis_size(axis)
    pairs = [(i, i + by) for i in range(peers) if 0 <= i + by < peers]
    return lax.ppermute(x, axis, pairs)


def matmul(left, right):
    return jnp.dot(left, right, preferred_element_type=jnp.float32)


def over_rows(left, right):
    return lax.dot_general(
        left, right, (((0,), (0,)), ((), ())), preferred_element_type=jnp.float32
    )


def against(left, right):
    return lax.dot_general(
        left, right, (((1,), (1,)), ((), ())), preferred_element_type=jnp.float32
    )


def norm_forward(values, gain, shift):
    centred = values - jnp.mean(values, axis=-1, keepdims=True)
    factor = lax.rsqrt(jnp.mean(centred * centred, axis=-1, keepdims=True) + NORM_EPSILON)
    unit_rows = centred * factor
    return (unit_rows * gain + shift, unit_rows, factor)


def norm_backward(upstream, unit_rows, factor, gain):
    scaled = upstream * gain
    inward = factor * (
        scaled
        - jnp.mean(scaled, axis=-1, keepdims=True)
        - unit_rows * jnp.mean(scaled * unit_rows, axis=-1, keepdims=True)
    )
    return (inward, jnp.sum(upstream * unit_rows, axis=0), jnp.sum(upstream, axis=0))


MESH = pl.DeviceIdType.MESH
ROWS = 16
VMEM_LIMIT = 60 * 1024 * 1024


def in_vmem(count):
    return [pl.BlockSpec(memory_space=pltpu.VMEM)] * count


class Place:
    def __init__(self, depth):
        seq, grp = lax.axis_index("seq"), lax.axis_index("grp")
        self.depth = depth
        self.y, self.x = lax.div(seq, 2), lax.rem(seq, 2)
        self.z, self.c = lax.div(grp, 2), lax.rem(grp, 2)
        self.seq, self.grp = seq, grp

    def over_x(self):
        return {"seq": 2 * self.y + 1 - self.x}

    def over_y(self):
        return {"seq": 2 * (1 - self.y) + self.x}

    def over_core(self):
        return {"grp": 2 * self.z + 1 - self.c}

    def z_of(self, step):
        return lax.rem(self.z + step, self.depth)

    def over_z(self, step):
        return {"grp": 2 * self.z_of(step) + self.c}

    def peers(self):
        return [self.over_x(), self.over_y(), self.over_core()] + [
            self.over_z(step) for step in range(1, self.depth)
        ]

    def greet(self, peers):
        barrier = pltpu.get_barrier_semaphore()
        for peer in peers:
            pl.semaphore_signal(barrier, inc=1, device_id=peer, device_id_type=MESH)
        pl.semaphore_wait(barrier, len(peers))


def copy_to(source, target, sems, index, peer):
    send, recv = sems
    return pltpu.make_async_remote_copy(
        src_ref=source,
        dst_ref=target,
        send_sem=send.at[index],
        recv_sem=recv.at[index],
        device_id=peer,
        device_id_type=MESH,
    )


class Gather:
    def __init__(self, place, view, sems, base, x_first):
        self.at, self.view, self.sems, self.base, self.x_first = place, view, sems, base, x_first

    def copy(self, region, slot, peer):
        made = copy_to(region, region, self.sems, self.base + slot, peer)
        made.start()
        return made

    def stage0(self):
        p = self.at
        own = self.view(p.y, p.x, p.z, p.c)
        self.open = [self.copy(own, step - 1, p.over_z(step)) for step in range(1, p.depth)]

    def stage1(self):
        p = self.at
        for made in self.open:
            made.wait()
        region = self.view(p.y, p.x, slice(None), p.c)
        self.open = [self.copy(region, p.depth - 1, p.over_x() if self.x_first else p.over_y())]

    def stage2(self):
        p = self.at
        self.open[0].wait()
        if self.x_first:
            region, peer = self.view(p.y, slice(None), slice(None), p.c), p.over_y()
        else:
            region, peer = self.view(slice(None), p.x, slice(None), p.c), p.over_x()
        self.open = [self.copy(region, p.depth, peer), self.copy(region, p.depth + 1, p.over_core())]

    def stage3(self):
        p = self.at
        self.open[0].wait()
        if self.x_first:
            region = self.view(1 - p.y, slice(None), slice(None), p.c)
        else:
            region = self.view(slice(None), 1 - p.x, slice(None), p.c)
        self.open = [self.open[1], self.copy(region, p.depth + 2, p.over_core())]

    def stage4(self):
        for made in self.open:
            made.wait()


def gather_slots(depth):
    return depth + 3


def gather_kernel(depth, wq, wm, wo, wu, wd, vec, stack, down, vectors, tiles, send, recv):
    p = Place(depth)
    own = (p.y, p.x, p.z, p.c)
    low = jnp.bfloat16
    width = stack.shape[-1]
    stack[(0,) + own] = wq[...].astype(low)
    for tap in range(3):
        for half in range(2):
            stack[(1 + 2 * tap + half,) + own] = wm[tap, :, half * width : (half + 1) * width].astype(low)
    stack[(7,) + own] = wo[...].astype(low)
    for part in range(4):
        stack[(8 + part,) + own] = wu[:, part * width : (part + 1) * width].astype(low)
    down[own] = wd[...].astype(low)
    tiles[own] = vec[...].astype(low)
    p.greet(p.peers())
    views = [lambda *i: tiles.at[i]]
    views += [functools.partial(lambda j, *i: stack.at[(j,) + i], j) for j in range(12)]
    views += [
        functools.partial(lambda k, *i: down.at[i + (pl.ds(k * ROWS, ROWS),)], k)
        for k in range(down.shape[4] // ROWS)
    ]
    views = [
        functools.partial(lambda v, *i: v(*[pl.ds(0, n) if isinstance(k, slice) else k for k, n in zip(i, (2, 2, depth, 2))]), v)
        for v in views
    ]
    slots = gather_slots(depth)
    pieces = [
        Gather(p, view, (send, recv), slots * k, k % 2 == 0) for k, view in enumerate(views)
    ]
    for stage in ("stage0", "stage1", "stage2", "stage3", "stage4"):
        for piece in pieces:
            getattr(piece, stage)()
    lanes = tiles.shape[-1]
    for y in range(2):
        for x in range(2):
            total = jnp.zeros(tiles.shape[-2:], jnp.float32)
            for z in range(depth):
                for c in range(2):
                    total += tiles[y, x, z, c].astype(jnp.float32)
            s = 2 * y + x
            vectors[:, s * lanes : (s + 1) * lanes] = total


def gather_plain(params):
    wq, wm, wo, wu, wd, vec = [member.astype(jnp.bfloat16) for member in params]
    axes = ("seq", "grp")
    return (
        lax.all_gather(wq, axes, axis=0, tiled=True),
        lax.all_gather(wm, axes, axis=1, tiled=True),
        lax.all_gather(wo, axes, axis=0, tiled=True),
        lax.all_gather(wu, axes, axis=0, tiled=True),
        lax.all_gather(wd, axes, axis=0, tiled=True),
        lax.all_gather(vec, axes, axis=1, tiled=True).astype(jnp.float32),
    )


def gather_parameters(params):
    wq, wm, wo, wu, wd, vec = params
    groups = lax.axis_size("grp")
    depth = groups // 2
    rows, width = wq.shape
    lanes = vec.shape[1] * groups
    tile = lax.dynamic_update_slice(
        jnp.zeros((ROWS, lanes), jnp.float32), vec, (0, vec.shape[1] * lax.axis_index("grp"))
    )
    low = jnp.bfloat16
    pieces = 13 + wd.shape[0] // ROWS
    sems = pltpu.SemaphoreType.DMA((pieces * gather_slots(depth),))
    stack, down, vectors = pl.pallas_call(
        functools.partial(gather_kernel, depth),
        out_shape=(
            jax.ShapeDtypeStruct((12, 2, 2, depth, 2, rows, width), low),
            jax.ShapeDtypeStruct((2, 2, depth, 2) + wd.shape, low),
            jax.ShapeDtypeStruct((ROWS, 4 * lanes), jnp.float32),
        ),
        in_specs=in_vmem(6),
        out_specs=in_vmem(3),
        scratch_shapes=[pltpu.VMEM((2, 2, depth, 2, ROWS, lanes), low), sems, sems],
        compiler_params=pltpu.CompilerParams(
            collective_id=0, has_side_effects=True, vmem_limit_bytes=VMEM_LIMIT
        ),
    )(wq, wm, wo, wu, wd, tile)
    full = stack.reshape(12, width, width)
    memory = jnp.stack([jnp.concatenate([full[1 + 2 * k], full[2 + 2 * k]], axis=1) for k in range(3)])
    up = jnp.concatenate([full[8 + k] for k in range(4)], axis=1)
    return (full[0], memory, full[7], up, down.reshape(-1, width), vectors[:9])


class Scatter:
    def __init__(self, place, view, out, scratch, sems, base, number, x_first):
        self.at, self.view, self.out, self.sems, self.base = place, view, out, sems, base
        self.bufs = [ref.at[number] for ref in scratch]
        self.x_first = x_first

    def copy(self, source, target, slot, peer):
        made = copy_to(source, target, self.sems, self.base + slot, peer)
        made.start()
        return made

    def stage0(self):
        p = self.at
        give, get = self.bufs[0], self.bufs[1]
        for y in range(2):
            for x in range(2):
                give[y, x] = self.view(y, x, pl.ds(0, p.depth), 1 - p.c)[...].astype(jnp.bfloat16)
        self.open = [self.copy(give, get, 0, p.over_core())]

    def part(self, other, kept):
        p = self.at
        y, x = (other, kept) if self.x_first else (kept, other)
        return self.view(y, x, pl.ds(0, p.depth), p.c)[...] + self.bufs[1][y, x].astype(jnp.float32)

    def stage1(self):
        p = self.at
        _, _, give, get, keep = self.bufs[:5]
        self.open[0].wait()
        mine, peer = (p.x, p.over_x()) if self.x_first else (p.y, p.over_y())
        for other in range(2):
            give[other] = self.part(other, 1 - mine).astype(jnp.bfloat16)
        self.open = [self.copy(give, get, 1, peer)]
        for other in range(2):
            keep[other] = self.part(other, mine)

    def stage2(self):
        p = self.at
        _, _, _, get, keep, give_two, get_two, _, _ = self.bufs
        self.open[0].wait()
        mine, peer = (p.y, p.over_y()) if self.x_first else (p.x, p.over_x())
        give_two[...] = (keep[1 - mine] + get[1 - mine].astype(jnp.float32)).astype(jnp.bfloat16)
        self.open = [self.copy(give_two, get_two, 2, peer)]
        keep[mine] = keep[mine] + get[mine].astype(jnp.float32)

    def stage3(self):
        p = self.at
        keep, _, get_two, give_z, get_z = self.bufs[4:]
        self.open[0].wait()
        mine = p.y if self.x_first else p.x
        total = keep[mine] + get_two[...].astype(jnp.float32)
        keep[mine] = total
        give_z[...] = total.astype(jnp.bfloat16)
        self.open = [
            self.copy(give_z.at[p.z_of(step)], get_z.at[step - 1], 2 + step, p.over_z(step))
            for step in range(1, p.depth)
        ]

    def stage4(self):
        p = self.at
        keep, _, _, _, get_z = self.bufs[4:]
        mine = p.y if self.x_first else p.x
        for made in self.open:
            made.wait()
        total = keep[mine, p.z]
        for step in range(1, p.depth):
            total = total + get_z[step - 1].astype(jnp.float32)
        self.out(total)


def scatter_slots(depth):
    return depth + 2


def scatter_scratch(count, depth, width):
    low, wide = jnp.bfloat16, jnp.float32
    return [
        pltpu.VMEM((count, 2, 2, depth, ROWS, width), low),
        pltpu.VMEM((count, 2, 2, depth, ROWS, width), low),
        pltpu.VMEM((count, 2, depth, ROWS, width), low),
        pltpu.VMEM((count, 2, depth, ROWS, width), low),
        pltpu.VMEM((count, 2, depth, ROWS, width), wide),
        pltpu.VMEM((count, depth, ROWS, width), low),
        pltpu.VMEM((count, depth, ROWS, width), low),
        pltpu.VMEM((count, depth, ROWS, width), low),
        pltpu.VMEM((count, depth - 1, ROWS, width), low),
    ]


class SumAll:
    def __init__(self, place, out, give, get, sems, base):
        self.at, self.out, self.give, self.get, self.sems, self.base = place, out, give, get, sems, base

    def send(self, slot, peer):
        made = copy_to(self.give.at[min(slot, 3)], self.get.at[slot], self.sems, self.base + slot, peer)
        made.start()
        return made

    def stage(self, number):
        p = self.at
        if number:
            self.open[0].wait()
            self.give[number] = self.give[number - 1] + self.get[number - 1]
        if number < 3:
            self.open = [self.send(number, (p.over_core(), p.over_x(), p.over_y())[number])]
        else:
            self.open = [self.send(2 + step, p.over_z(step)) for step in range(1, p.depth)]

    def finish(self):
        total = self.give[3]
        for made in self.open:
            made.wait()
        for step in range(1, self.at.depth):
            total = total + self.get[2 + step]
        self.out[...] = total


def scatter_kernel(depth, stack, down, vec, out_stack, out_down, out_vec, *scratch):
    p = Place(depth)
    bufs, (give, get, send, recv) = scratch[:-4], scratch[-4:]
    count = 12 + down.shape[4] // ROWS
    slots = scatter_slots(depth)
    p.greet(p.peers())

    def to_stack(j, value):
        out_stack[j] = value

    def to_down(k, value):
        out_down[k * ROWS : (k + 1) * ROWS] = value

    pieces = []
    for j in range(count):
        if j < 12:
            view = functools.partial(lambda j, *i: stack.at[(j,) + i], j)
            out = functools.partial(to_stack, j)
        else:
            view = functools.partial(lambda k, *i: down.at[i + (pl.ds(k * ROWS, ROWS),)], j - 12)
            out = functools.partial(to_down, j - 12)
        pieces.append(Scatter(p, view, out, bufs, (send, recv), slots * j, j, j % 2 == 0))
    small = SumAll(p, out_vec, give, get, (send, recv), slots * count)
    give[0] = vec[...]
    for number in range(4):
        small.stage(number)
        for piece in pieces:
            getattr(piece, f"stage{number}")()
    for piece in pieces:
        piece.stage4()
    small.finish()


def scatter_plain(grads):
    axes = ("seq", "grp")
    return tuple(
        lax.psum_scatter(member, axes, scatter_dimension=dim, tiled=True)
        for member, dim in zip(grads, (0, 1, 0, 0, 0, 1))
    )


def scatter_gradients(grads):
    gq, gm, go, gu, gd, gv = grads
    groups = lax.axis_size("grp")
    depth = groups // 2
    width = gq.shape[1]
    devices = 4 * groups
    shape = (2, 2, depth, 2)
    own_down = gd.shape[0] // devices
    stack = jnp.stack(
        [gq]
        + [gm[k, :, h * width : (h + 1) * width] for k in range(3) for h in range(2)]
        + [go]
        + [gu[:, k * width : (k + 1) * width] for k in range(4)]
    ).reshape((12,) + shape + (ROWS, width))
    count = 12 + own_down // ROWS
    sems = pltpu.SemaphoreType.DMA((count * scatter_slots(depth) + depth + 2,))
    vec = jnp.pad(gv, ((0, ROWS - gv.shape[0]), (0, 0)))
    wide = jnp.float32
    out_stack, out_down, out_vec = pl.pallas_call(
        functools.partial(scatter_kernel, depth),
        out_shape=(
            jax.ShapeDtypeStruct((12, ROWS, width), wide),
            jax.ShapeDtypeStruct((own_down, width), wide),
            jax.ShapeDtypeStruct(vec.shape, wide),
        ),
        in_specs=in_vmem(3),
        out_specs=in_vmem(3),
        scratch_shapes=scatter_scratch(count, depth, width)
        + [
            pltpu.VMEM((4,) + vec.shape, wide),
            pltpu.VMEM((depth + 2,) + vec.shape, wide),
            sems,
            sems,
        ],
        compiler_params=pltpu.CompilerParams(
            collective_id=1, has_side_effects=True, vmem_limit_bytes=VMEM_LIMIT
        ),
    )(stack, gd.reshape(shape + (own_down, width)), vec)
    share = gv.shape[1] // devices
    index = lax.axis_index("seq") * groups + lax.axis_index("grp")
    return (
        out_stack[0],
        jnp.stack([jnp.concatenate([out_stack[1 + 2 * k], out_stack[2 + 2 * k]], axis=1) for k in range(3)]),
        out_stack[7],
        jnp.concatenate([out_stack[8 + k] for k in range(4)], axis=1),
        out_down,
        lax.dynamic_slice(out_vec, (0, index * share), (gv.shape[0], share)),
    )


STRIP = 256
NT = (((1,), (1,)), ((), ()))


def head_only(values, head, size):
    lane = lax.broadcasted_iota(jnp.int32, values.shape, 1)
    keep = jnp.logical_and(lane >= head * size, lane < (head + 1) * size)
    return jnp.where(keep, values, jnp.zeros_like(values))


def hide_future(scores, first_slot, first_row):
    slot = lax.broadcasted_iota(jnp.int32, scores.shape, 0) + first_slot
    row = lax.broadcasted_iota(jnp.int32, scores.shape, 1) + first_row
    return jnp.where(3 * slot <= row, scores, MASKED_SCORE)


def strip_scores(keys, queries, seen, first_row):
    if seen == STRIP:
        return hide_future(lax.dot_general(keys[0:seen, :], queries, NT, preferred_element_type=jnp.float32), 0, first_row)
    whole = seen - STRIP
    past = lax.dot_general(keys[0:whole, :], queries, NT, preferred_element_type=jnp.float32)
    last = lax.dot_general(keys[whole:seen, :], queries, NT, preferred_element_type=jnp.float32)
    return jnp.concatenate([past, hide_future(last, whole, first_row)], axis=0)


def forward_kernel(heads, q_ref, k_ref, v_ref, o_ref, lse_ref, vt_ref):
    lanes = q_ref.shape[1]
    size = lanes // heads
    vt_ref[...] = v_ref[...].T
    for block in range(q_ref.shape[0] // (3 * STRIP)):
        seen = STRIP * (block + 1)

        @pl.loop(0, 3)
        def _(part):
            first = pl.multiple_of((3 * block + part) * STRIP, STRIP)
            rows = pl.ds(first, STRIP)
            queries = q_ref[rows, :] * jnp.bfloat16(size ** (-0.5))
            mixed = []
            for head in range(heads):
                scores = strip_scores(k_ref, head_only(queries, head, size), seen, first)
                highest = jnp.max(scores, axis=0, keepdims=True)
                exponent = jnp.exp(scores - highest)
                summed = jnp.sum(exponent, axis=0, keepdims=True)
                out = jnp.dot(
                    vt_ref[head * size : (head + 1) * size, 0:seen],
                    exponent.astype(jnp.bfloat16),
                    preferred_element_type=jnp.float32,
                )
                mixed.append(out / summed)
                lse_ref[head : head + 1, rows] = highest + jnp.log(summed)
            o_ref[rows, :] = jnp.concatenate(mixed, axis=0).T.astype(jnp.bfloat16)


def backward_kernel(heads, q_ref, k_ref, v_ref, do_ref, o_ref, lse_ref, dq_ref, dk_ref, dv_ref, kt_ref):
    lanes = q_ref.shape[1]
    size = lanes // heads
    scale = size ** (-0.5)
    low = jnp.bfloat16
    kt_ref[...] = k_ref[...].T
    dk_ref[...] = jnp.zeros_like(dk_ref)
    dv_ref[...] = jnp.zeros_like(dv_ref)
    for block in range(q_ref.shape[0] // (3 * STRIP)):
        seen = STRIP * (block + 1)

        @pl.loop(0, 3)
        def _(part):
            first = pl.multiple_of((3 * block + part) * STRIP, STRIP)
            rows = pl.ds(first, STRIP)
            queries = q_ref[rows, :] * low(scale)
            incoming = do_ref[rows, :]
            centre = (incoming.astype(jnp.float32) * o_ref[rows, :].astype(jnp.float32)).T
            grads = []
            for head in range(heads):
                own_q = head_only(queries, head, size)
                own_do = head_only(incoming, head, size)
                scores = strip_scores(k_ref, own_q, seen, first)
                weights = jnp.exp(scores - lse_ref[head : head + 1, rows])
                back = lax.dot_general(v_ref[0:seen, :], own_do, NT, preferred_element_type=jnp.float32)
                middle = jnp.sum(centre[head * size : (head + 1) * size], axis=0, keepdims=True)
                slope = (weights * (back - middle)).astype(low)
                dv_ref[0:seen, :] += jnp.dot(weights.astype(low), own_do, preferred_element_type=jnp.float32)
                dk_ref[0:seen, :] += jnp.dot(slope, own_q, preferred_element_type=jnp.float32)
                grads.append(
                    jnp.dot(kt_ref[head * size : (head + 1) * size, 0:seen], slope, preferred_element_type=jnp.float32)
                )
            dq_ref[rows, :] = (jnp.concatenate(grads, axis=0) * scale).T.astype(low)


def attend_forward(queries, keys, values):
    rows, lanes = queries.shape
    heads = H * lanes // (lax.axis_size("seq") * lanes)
    return pl.pallas_call(
        functools.partial(forward_kernel, heads),
        out_shape=(
            jax.ShapeDtypeStruct((rows, lanes), jnp.bfloat16),
            jax.ShapeDtypeStruct((heads, rows), jnp.float32),
        ),
        in_specs=in_vmem(3),
        out_specs=in_vmem(2),
        scratch_shapes=[pltpu.VMEM((lanes, keys.shape[0]), jnp.bfloat16)],
        compiler_params=pltpu.CompilerParams(vmem_limit_bytes=VMEM_LIMIT),
    )(queries, keys, values)


def attend_backward(queries, keys, values, upstream, mixed, logsum):
    rows, lanes = queries.shape
    heads = logsum.shape[0]
    return pl.pallas_call(
        functools.partial(backward_kernel, heads),
        out_shape=(
            jax.ShapeDtypeStruct((rows, lanes), jnp.bfloat16),
            jax.ShapeDtypeStruct(keys.shape, jnp.float32),
            jax.ShapeDtypeStruct(keys.shape, jnp.float32),
        ),
        in_specs=in_vmem(6),
        out_specs=in_vmem(3),
        scratch_shapes=[pltpu.VMEM((lanes, keys.shape[0]), jnp.bfloat16)],
        compiler_params=pltpu.CompilerParams(vmem_limit_bytes=VMEM_LIMIT),
    )(queries, keys, values, upstream, mixed, logsum)


def adamw(weight, gradient, moment, square, step_rate):
    moment_new = BETA_FIRST * moment + (1.0 - BETA_FIRST) * gradient
    square_new = BETA_SECOND * square + (1.0 - BETA_SECOND) * gradient * gradient
    fixed_first = 1.0 - BETA_FIRST**STEP
    fixed_second = 1.0 - BETA_SECOND**STEP
    update = (
        moment_new / fixed_first / (jnp.sqrt(square_new / fixed_second) + ADAM_EPSILON)
        + WEIGHT_DECAY * weight
    )
    master = weight - step_rate * update
    return (moment_new, square_new, master, master.astype(jnp.bfloat16))


def body(
    tokens,
    cotangent,
    lengths,
    weight_query,
    weight_memory,
    weight_out,
    weight_up,
    weight_down,
    vectors,
    first_query,
    first_memory,
    first_out,
    first_up,
    first_down,
    first_vectors,
    second_query,
    second_memory,
    second_out,
    second_up,
    second_down,
    second_vectors,
):
    fast = weight_query.shape[0] % 16 == 0 and lax.axis_size("seq") == 4
    params = (weight_query, weight_memory, weight_out, weight_up, weight_down, vectors)
    gathered = gather_parameters(params) if fast else gather_plain(params)
    query_w, memory_w, out_w, up_w, down_w, vector_rows = gathered
    model_width = query_w.shape[0]
    hidden_units = up_w.shape[1]
    head_size = model_width // H
    seq_count = lax.axis_size("seq")
    seq_index = lax.axis_index("seq")
    local_rows = tokens.shape[1]
    local_slots = local_rows // 3
    inputs = tokens[0].astype(jnp.float32)
    normed, unit_one, factor_one = norm_forward(inputs, vector_rows[0], vector_rows[1])
    normed_low = normed.astype(jnp.bfloat16)
    queries = matmul(normed_low, query_w).astype(jnp.bfloat16)
    borrowed = from_behind(normed_low[local_rows - 2 :], "seq", 1)
    extended = jnp.concatenate([borrowed, normed_low], axis=0)
    windows = extended[:local_rows].reshape(local_slots, 3 * model_width)
    memory_flat = memory_w.reshape(3 * model_width, 2 * model_width)
    memory = matmul(windows, memory_flat).astype(jnp.bfloat16)
    share_width = model_width // seq_count
    local_heads = H // seq_count
    head_queries, head_memory = (
        lax.all_to_all(
            queries.reshape(local_rows, 1, seq_count, share_width),
            "seq",
            split_axis=2,
            concat_axis=0,
            tiled=True,
        ),
        lax.all_to_all(
            memory.reshape(local_slots, 2, seq_count, share_width),
            "seq",
            split_axis=2,
            concat_axis=0,
            tiled=True,
        ),
    )
    total_rows = head_queries.shape[0]
    total_slots = head_memory.shape[0]
    query_heads = head_queries.reshape(total_rows, share_width)
    key_heads = head_memory[:, 0].reshape(total_slots, share_width)
    value_heads = head_memory[:, 1].reshape(total_slots, share_width)
    mixed, logsum = attend_forward(query_heads, key_heads, value_heads)
    mixed_low = mixed.reshape(total_rows, 1, share_width)
    attended = lax.all_to_all(mixed_low, "seq", split_axis=0, concat_axis=1, tiled=True).reshape(
        local_rows, model_width
    )
    residual = inputs + matmul(attended, out_w)
    normed_two, unit_two, factor_two = norm_forward(residual, vector_rows[2], vector_rows[3])
    normed_two_low = normed_two.astype(jnp.bfloat16)
    pre_act = matmul(normed_two_low, up_w) + vector_rows[5:].reshape(hidden_units)
    activated, gelu_pull = jax.vjp(jax.nn.gelu, pre_act)
    activated_low = activated.astype(jnp.bfloat16)
    result = residual + matmul(activated_low, down_w) + vector_rows[4]
    positions = seq_index * local_rows + jnp.arange(local_rows, dtype=jnp.int32)
    live_mask = (positions < lengths[0]).astype(jnp.float32)
    grad_out = cotangent[0].astype(jnp.float32) * live_mask[:, None]
    grad_out_low = grad_out.astype(jnp.bfloat16)
    grad_down = over_rows(activated_low, grad_out_low)
    grad_activated = against(grad_out_low, down_w)
    grad_pre_low = gelu_pull(grad_activated)[0].astype(jnp.bfloat16)
    grad_up = over_rows(normed_two_low, grad_pre_low)
    grad_up_bias = jnp.sum(grad_pre_low.astype(jnp.float32), axis=0)
    grad_normed_two = against(grad_pre_low, up_w)
    grad_norm_two, grad_gain_two, grad_shift_two = norm_backward(
        grad_normed_two, unit_two, factor_two, vector_rows[2]
    )
    grad_residual = grad_out + grad_norm_two
    grad_branch_low = grad_residual.astype(jnp.bfloat16)
    grad_outw = over_rows(attended, grad_branch_low)
    grad_attended_low = against(grad_branch_low, out_w).astype(jnp.bfloat16)
    grad_heads = lax.all_to_all(
        grad_attended_low.reshape(local_rows, 1, seq_count, share_width),
        "seq",
        split_axis=2,
        concat_axis=0,
        tiled=True,
    ).reshape(total_rows, share_width)
    grad_q, grad_k, grad_v = attend_backward(
        query_heads, key_heads, value_heads, grad_heads, mixed, logsum
    )
    packed = (
        jnp.stack([grad_k, grad_v], axis=1)
        .astype(jnp.bfloat16)
        .reshape(total_slots, 2, 1, share_width)
    )
    token_queries, token_memory = (
        lax.all_to_all(
            grad_q.astype(jnp.bfloat16).reshape(total_rows, 1, 1, share_width),
            "seq",
            split_axis=0,
            concat_axis=2,
            tiled=True,
        ),
        lax.all_to_all(packed, "seq", split_axis=0, concat_axis=2, tiled=True),
    )
    grad_queries_low = token_queries.reshape(local_rows, model_width)
    grad_memory_low = token_memory.reshape(local_slots, 2 * model_width)
    grad_queryw = over_rows(normed_low, grad_queries_low)
    grad_normed = against(grad_queries_low, query_w)
    grad_memoryw = over_rows(windows, grad_memory_low).reshape(3, model_width, 2 * model_width)
    grad_windows = against(grad_memory_low, memory_flat).reshape(local_rows, model_width)
    returned = from_behind(grad_windows[:2], "seq", -1)
    grad_normed = grad_normed + jnp.concatenate([grad_windows[2:], returned], axis=0)
    grad_norm_one, grad_gain_one, grad_shift_one = norm_backward(
        grad_normed, unit_one, factor_one, vector_rows[0]
    )
    grad_inputs = (grad_residual + grad_norm_one).astype(jnp.bfloat16)
    grad_vector_rows = jnp.concatenate(
        [
            jnp.stack(
                [
                    grad_gain_one,
                    grad_shift_one,
                    grad_gain_two,
                    grad_shift_two,
                    jnp.sum(grad_out, axis=0),
                ]
            ),
            grad_up_bias.reshape(4, model_width),
        ],
        axis=0,
    )
    grads = (grad_queryw, grad_memoryw, grad_outw, grad_up, grad_down, grad_vector_rows)
    reduced = scatter_gradients(grads) if fast else scatter_plain(grads)
    new_query = adamw(weight_query, reduced[0], first_query, second_query, LEARNING_RATES[0])
    new_memory = adamw(weight_memory, reduced[1], first_memory, second_memory, LEARNING_RATES[1])
    new_out = adamw(weight_out, reduced[2], first_out, second_out, LEARNING_RATES[2])
    new_up = adamw(weight_up, reduced[3], first_up, second_up, LEARNING_RATES[3])
    new_down = adamw(weight_down, reduced[4], first_down, second_down, LEARNING_RATES[4])
    new_vectors = adamw(vectors, reduced[5], first_vectors, second_vectors, LEARNING_RATES[5])
    return (
        result.astype(jnp.bfloat16)[None],
        grad_inputs[None],
        new_query[0],
        new_memory[0],
        new_out[0],
        new_up[0],
        new_down[0],
        new_vectors[0],
        new_query[1],
        new_memory[1],
        new_out[1],
        new_up[1],
        new_down[1],
        new_vectors[1],
        new_query[2],
        new_memory[2],
        new_out[2],
        new_up[2],
        new_down[2],
        new_vectors[2],
        new_query[3],
        new_memory[3],
        new_out[3],
        new_up[3],
        new_down[3],
        new_vectors[3],
    )


def solution(mesh):
    in_specs = (
        P("grp", "seq", None),
        P("grp", "seq", None),
        P("grp"),
        P(("seq", "grp"), None),
        P(None, ("seq", "grp"), None),
        P(("seq", "grp"), None),
        P(("seq", "grp"), None),
        P(("seq", "grp"), None),
        P(None, ("seq", "grp")),
        P(("seq", "grp"), None),
        P(None, ("seq", "grp"), None),
        P(("seq", "grp"), None),
        P(("seq", "grp"), None),
        P(("seq", "grp"), None),
        P(None, ("seq", "grp")),
        P(("seq", "grp"), None),
        P(None, ("seq", "grp"), None),
        P(("seq", "grp"), None),
        P(("seq", "grp"), None),
        P(("seq", "grp"), None),
        P(None, ("seq", "grp")),
    )
    out_specs = (
        P("grp", "seq", None),
        P("grp", "seq", None),
        P(("seq", "grp"), None),
        P(None, ("seq", "grp"), None),
        P(("seq", "grp"), None),
        P(("seq", "grp"), None),
        P(("seq", "grp"), None),
        P(None, ("seq", "grp")),
        P(("seq", "grp"), None),
        P(None, ("seq", "grp"), None),
        P(("seq", "grp"), None),
        P(("seq", "grp"), None),
        P(("seq", "grp"), None),
        P(None, ("seq", "grp")),
        P(("seq", "grp"), None),
        P(None, ("seq", "grp"), None),
        P(("seq", "grp"), None),
        P(("seq", "grp"), None),
        P(("seq", "grp"), None),
        P(None, ("seq", "grp")),
        P(("seq", "grp"), None),
        P(None, ("seq", "grp"), None),
        P(("seq", "grp"), None),
        P(("seq", "grp"), None),
        P(("seq", "grp"), None),
        P(None, ("seq", "grp")),
    )
    return jax.shard_map(body, mesh=mesh, in_specs=in_specs, out_specs=out_specs, check_vma=False)
```

```python
import functools

import jax
import jax.numpy as jnp
from jax import lax
from jax.experimental import pallas as pl
from jax.experimental.pallas import tpu as pltpu
from jax.sharding import PartitionSpec as P

H = 8
STEP = 10


NORM_EPSILON = 1e-05
BETA_FIRST = 0.9
BETA_SECOND = 0.95
ADAM_EPSILON = 1e-08
WEIGHT_DECAY = 0.1
LEARNING_RATES = (0.05, 0.04, 0.3, 0.05, 0.03, 0.5)
MASKED_SCORE = -1e30
NT = (((1,), (1,)), ((), ()))


def from_behind(x, axis, by):
    peers = lax.axis_size(axis)
    pairs = [(i, i + by) for i in range(peers) if 0 <= i + by < peers]
    return lax.ppermute(x, axis, pairs)


def matmul(left, right):
    return jnp.dot(left, right, preferred_element_type=jnp.float32)


def over_rows(left, right):
    return lax.dot_general(
        left, right, (((0,), (0,)), ((), ())), preferred_element_type=jnp.float32
    )


def against(left, right):
    return lax.dot_general(
        left, right, (((1,), (1,)), ((), ())), preferred_element_type=jnp.float32
    )


def norm_forward(values, gain, shift):
    centred = values - jnp.mean(values, axis=-1, keepdims=True)
    factor = lax.rsqrt(jnp.mean(centred * centred, axis=-1, keepdims=True) + NORM_EPSILON)
    unit_rows = centred * factor
    return (unit_rows * gain + shift, unit_rows, factor)


def norm_backward(upstream, unit_rows, factor, gain):
    scaled = upstream * gain
    inward = factor * (
        scaled
        - jnp.mean(scaled, axis=-1, keepdims=True)
        - unit_rows * jnp.mean(scaled * unit_rows, axis=-1, keepdims=True)
    )
    return (inward, jnp.sum(upstream * unit_rows, axis=0), jnp.sum(upstream, axis=0))


def masked_scores(query_tile_rows, key_row_block, positions):
    slot_starts = 3 * jnp.arange(key_row_block.shape[0], dtype=jnp.int32)
    score_matrix = jnp.einsum(
        "azv,lzv->zal", query_tile_rows, key_row_block, preferred_element_type=jnp.float32
    ) * query_tile_rows.shape[2] ** (-0.5)
    visible = slot_starts[None, :] <= positions[:, None]
    return jnp.where(visible[None], score_matrix, MASKED_SCORE)


def attend_forward(queries, key_row_block, value_row_block, anchor, block_rows):
    block_count = queries.shape[0] // block_rows
    offsets = block_rows * jnp.arange(block_count, dtype=jnp.int32)

    def attend_block(inputs):
        query_tile_rows, offset_rows = inputs
        score_matrix = masked_scores(
            query_tile_rows,
            key_row_block,
            anchor + offset_rows + jnp.arange(block_rows, dtype=jnp.int32),
        )
        highest = jnp.max(score_matrix, axis=-1, keepdims=True)
        exponent = jnp.exp(score_matrix - highest)
        summed = jnp.sum(exponent, axis=-1, keepdims=True)
        reduced_weights = (exponent / summed).astype(jnp.bfloat16)
        mixed = jnp.einsum(
            "yup,pyb->uyb", reduced_weights, value_row_block, preferred_element_type=jnp.float32
        )
        return (mixed, (highest + jnp.log(summed))[..., 0])

    blocks_in = queries.reshape(block_count, block_rows, queries.shape[1], queries.shape[2])
    mixed, logsum = lax.map(attend_block, (blocks_in, offsets))
    return (mixed.reshape(queries.shape), logsum)


def attend_backward(queries, key_row_block, value_row_block, upstream, logsum, anchor, block_rows):
    block_count = queries.shape[0] // block_rows
    offsets = block_rows * jnp.arange(block_count, dtype=jnp.int32)
    scale_factor = queries.shape[2] ** (-0.5)

    def attend_back(carry, inputs):
        grad_keys, grad_values = carry
        query_tile_rows, incoming_gradient_rows, logsum_block, offset_rows = inputs
        score_matrix = masked_scores(
            query_tile_rows,
            key_row_block,
            anchor + offset_rows + jnp.arange(block_rows, dtype=jnp.int32),
        )
        weights_soft = jnp.exp(score_matrix - logsum_block[..., None])
        grad_weights = jnp.einsum(
            "azv,lzv->zal",
            incoming_gradient_rows,
            value_row_block,
            preferred_element_type=jnp.float32,
        )
        centre = jnp.sum(weights_soft * grad_weights, axis=-1, keepdims=True)
        score_gradient = (weights_soft * (grad_weights - centre)).astype(jnp.bfloat16)
        grad_query = (
            jnp.einsum(
                "yup,pyb->uyb", score_gradient, key_row_block, preferred_element_type=jnp.float32
            )
            * scale_factor
        )
        grad_keys = (
            grad_keys
            + jnp.einsum(
                "xof,oxa->fxa", score_gradient, query_tile_rows, preferred_element_type=jnp.float32
            )
            * scale_factor
        )
        grad_values = grad_values + jnp.einsum(
            "xof,oxa->fxa",
            weights_soft.astype(jnp.bfloat16),
            incoming_gradient_rows,
            preferred_element_type=jnp.float32,
        )
        return ((grad_keys, grad_values), grad_query)

    shape_blocks = (block_count, block_rows, queries.shape[1], queries.shape[2])
    zeros_init = jnp.zeros(key_row_block.shape, jnp.float32)
    (grad_keys, grad_values), grad_query = lax.scan(
        attend_back,
        (zeros_init, zeros_init),
        (queries.reshape(shape_blocks), upstream.reshape(shape_blocks), logsum, offsets),
    )
    return (grad_query.reshape(queries.shape), grad_keys, grad_values)


def adamw(weight, gradient, moment, square, step_rate):
    moment_new = BETA_FIRST * moment + (1.0 - BETA_FIRST) * gradient
    square_new = BETA_SECOND * square + (1.0 - BETA_SECOND) * gradient * gradient
    fixed_first = 1.0 - BETA_FIRST**STEP
    fixed_second = 1.0 - BETA_SECOND**STEP
    update = (
        moment_new / fixed_first / (jnp.sqrt(square_new / fixed_second) + ADAM_EPSILON)
        + WEIGHT_DECAY * weight
    )
    master = weight - step_rate * update
    return (moment_new, square_new, master, master.astype(jnp.bfloat16))


def plain(
    tokens,
    cotangent,
    lengths,
    weight_query,
    weight_memory,
    weight_out,
    weight_up,
    weight_down,
    vectors,
    first_query,
    first_memory,
    first_out,
    first_up,
    first_down,
    first_vectors,
    second_query,
    second_memory,
    second_out,
    second_up,
    second_down,
    second_vectors,
):
    gathered = (
        lax.all_gather(weight_query.astype(jnp.bfloat16), ("seq", "grp"), axis=0, tiled=True),
        lax.all_gather(weight_memory.astype(jnp.bfloat16), ("seq", "grp"), axis=1, tiled=True),
        lax.all_gather(weight_out.astype(jnp.bfloat16), ("seq", "grp"), axis=0, tiled=True),
        lax.all_gather(weight_up.astype(jnp.bfloat16), ("seq", "grp"), axis=0, tiled=True),
        lax.all_gather(weight_down.astype(jnp.bfloat16), ("seq", "grp"), axis=0, tiled=True),
        lax.all_gather(vectors.astype(jnp.bfloat16), ("seq", "grp"), axis=1, tiled=True),
    )
    query_w, memory_w, out_w, up_w, down_w, vector_low = gathered
    vector_rows = vector_low.astype(jnp.float32)
    model_width = query_w.shape[0]
    hidden_units = up_w.shape[1]
    head_size = model_width // H
    seq_count = lax.axis_size("seq")
    seq_index = lax.axis_index("seq")
    local_rows = tokens.shape[1]
    local_slots = local_rows // 3
    inputs = tokens[0].astype(jnp.float32)
    normed, unit_one, factor_one = norm_forward(inputs, vector_rows[0], vector_rows[1])
    normed_low = normed.astype(jnp.bfloat16)
    queries = matmul(normed_low, query_w).astype(jnp.bfloat16)
    borrowed = from_behind(normed_low[local_rows - 2 :], "seq", 1)
    extended = jnp.concatenate([borrowed, normed_low], axis=0)
    windows = extended[:local_rows].reshape(local_slots, 3 * model_width)
    memory_flat = memory_w.reshape(3 * model_width, 2 * model_width)
    memory = matmul(windows, memory_flat).astype(jnp.bfloat16)
    share_width = model_width // seq_count
    local_heads = H // seq_count
    head_queries, head_memory = (
        lax.all_to_all(
            queries.reshape(local_rows, 1, seq_count, share_width),
            "seq",
            split_axis=2,
            concat_axis=0,
            tiled=True,
        ),
        lax.all_to_all(
            memory.reshape(local_slots, 2, seq_count, share_width),
            "seq",
            split_axis=2,
            concat_axis=0,
            tiled=True,
        ),
    )
    total_rows = head_queries.shape[0]
    total_slots = head_memory.shape[0]
    query_heads = head_queries.reshape(total_rows, local_heads, head_size)
    key_heads = head_memory[:, 0].reshape(total_slots, local_heads, head_size)
    value_heads = head_memory[:, 1].reshape(total_slots, local_heads, head_size)
    block_rows = min(512, total_rows)
    mixed, logsum = attend_forward(query_heads, key_heads, value_heads, 0, block_rows)
    mixed_low = mixed.astype(jnp.bfloat16).reshape(total_rows, 1, share_width)
    attended = lax.all_to_all(mixed_low, "seq", split_axis=0, concat_axis=1, tiled=True).reshape(
        local_rows, model_width
    )
    residual = inputs + matmul(attended, out_w)
    normed_two, unit_two, factor_two = norm_forward(residual, vector_rows[2], vector_rows[3])
    normed_two_low = normed_two.astype(jnp.bfloat16)
    pre_act = matmul(normed_two_low, up_w) + vector_rows[5:].reshape(hidden_units)
    activated, gelu_pull = jax.vjp(jax.nn.gelu, pre_act)
    activated_low = activated.astype(jnp.bfloat16)
    result = residual + matmul(activated_low, down_w) + vector_rows[4]
    positions = seq_index * local_rows + jnp.arange(local_rows, dtype=jnp.int32)
    live_mask = (positions < lengths[0]).astype(jnp.float32)
    grad_out = cotangent[0].astype(jnp.float32) * live_mask[:, None]
    grad_out_low = grad_out.astype(jnp.bfloat16)
    grad_down = over_rows(activated_low, grad_out_low)
    grad_activated = against(grad_out_low, down_w)
    grad_pre_low = gelu_pull(grad_activated)[0].astype(jnp.bfloat16)
    grad_up = over_rows(normed_two_low, grad_pre_low)
    grad_up_bias = jnp.sum(grad_pre_low.astype(jnp.float32), axis=0)
    grad_normed_two = against(grad_pre_low, up_w)
    grad_norm_two, grad_gain_two, grad_shift_two = norm_backward(
        grad_normed_two, unit_two, factor_two, vector_rows[2]
    )
    grad_residual = grad_out + grad_norm_two
    grad_branch_low = grad_residual.astype(jnp.bfloat16)
    grad_outw = over_rows(attended, grad_branch_low)
    grad_attended_low = against(grad_branch_low, out_w).astype(jnp.bfloat16)
    grad_heads = lax.all_to_all(
        grad_attended_low.reshape(local_rows, 1, seq_count, share_width),
        "seq",
        split_axis=2,
        concat_axis=0,
        tiled=True,
    ).reshape(total_rows, local_heads, head_size)
    grad_q, grad_k, grad_v = attend_backward(
        query_heads, key_heads, value_heads, grad_heads, logsum, 0, block_rows
    )
    packed = (
        jnp.stack([grad_k, grad_v], axis=1)
        .astype(jnp.bfloat16)
        .reshape(total_slots, 2, 1, share_width)
    )
    token_queries, token_memory = (
        lax.all_to_all(
            grad_q.astype(jnp.bfloat16).reshape(total_rows, 1, 1, share_width),
            "seq",
            split_axis=0,
            concat_axis=2,
            tiled=True,
        ),
        lax.all_to_all(packed, "seq", split_axis=0, concat_axis=2, tiled=True),
    )
    grad_queries_low = token_queries.reshape(local_rows, model_width)
    grad_memory_low = token_memory.reshape(local_slots, 2 * model_width)
    grad_queryw = over_rows(normed_low, grad_queries_low)
    grad_normed = against(grad_queries_low, query_w)
    grad_memoryw = over_rows(windows, grad_memory_low).reshape(3, model_width, 2 * model_width)
    grad_windows = against(grad_memory_low, memory_flat).reshape(local_rows, model_width)
    returned = from_behind(grad_windows[:2], "seq", -1)
    grad_normed = grad_normed + jnp.concatenate([grad_windows[2:], returned], axis=0)
    grad_norm_one, grad_gain_one, grad_shift_one = norm_backward(
        grad_normed, unit_one, factor_one, vector_rows[0]
    )
    grad_inputs = (grad_residual + grad_norm_one).astype(jnp.bfloat16)
    grad_vector_rows = jnp.concatenate(
        [
            jnp.stack(
                [
                    grad_gain_one,
                    grad_shift_one,
                    grad_gain_two,
                    grad_shift_two,
                    jnp.sum(grad_out, axis=0),
                ]
            ),
            grad_up_bias.reshape(4, model_width),
        ],
        axis=0,
    )
    reduced = (
        lax.psum_scatter(grad_queryw, ("seq", "grp"), scatter_dimension=0, tiled=True),
        lax.psum_scatter(grad_memoryw, ("seq", "grp"), scatter_dimension=1, tiled=True),
        lax.psum_scatter(grad_outw, ("seq", "grp"), scatter_dimension=0, tiled=True),
        lax.psum_scatter(grad_up, ("seq", "grp"), scatter_dimension=0, tiled=True),
        lax.psum_scatter(grad_down, ("seq", "grp"), scatter_dimension=0, tiled=True),
        lax.psum_scatter(grad_vector_rows, ("seq", "grp"), scatter_dimension=1, tiled=True),
    )
    new_query = adamw(weight_query, reduced[0], first_query, second_query, LEARNING_RATES[0])
    new_memory = adamw(weight_memory, reduced[1], first_memory, second_memory, LEARNING_RATES[1])
    new_out = adamw(weight_out, reduced[2], first_out, second_out, LEARNING_RATES[2])
    new_up = adamw(weight_up, reduced[3], first_up, second_up, LEARNING_RATES[3])
    new_down = adamw(weight_down, reduced[4], first_down, second_down, LEARNING_RATES[4])
    new_vectors = adamw(vectors, reduced[5], first_vectors, second_vectors, LEARNING_RATES[5])
    return (
        result.astype(jnp.bfloat16)[None],
        grad_inputs[None],
        new_query[0],
        new_memory[0],
        new_out[0],
        new_up[0],
        new_down[0],
        new_vectors[0],
        new_query[1],
        new_memory[1],
        new_out[1],
        new_up[1],
        new_down[1],
        new_vectors[1],
        new_query[2],
        new_memory[2],
        new_out[2],
        new_up[2],
        new_down[2],
        new_vectors[2],
        new_query[3],
        new_memory[3],
        new_out[3],
        new_up[3],
        new_down[3],
        new_vectors[3],
    )


MESH = pl.DeviceIdType.MESH
LOW, WIDE = jnp.bfloat16, jnp.float32
ROWS = 16
STRIP = 384
SLOTS = STRIP // 3
EARLY = 7
LATE = 5
MEGA = 1024 * 1024


def in_vmem(count):
    return [pl.BlockSpec(memory_space=pltpu.VMEM)] * count


def shaped(*shape, kind=jnp.bfloat16):
    return jax.ShapeDtypeStruct(shape, kind)


def dot(left, right):
    return jnp.dot(left, right, preferred_element_type=jnp.float32)


def differ(bit, other):
    return bit + other - 2 * bit * other


class Place:
    def __init__(self, depth):
        self.seq, self.grp = lax.axis_index("seq"), lax.axis_index("grp")
        self.depth = depth
        self.y, self.x = lax.div(self.seq, 2), lax.rem(self.seq, 2)
        self.z, self.c = lax.div(self.grp, 2), lax.rem(self.grp, 2)

    def shard(self, turn):
        return 2 * differ(self.y, lax.div(turn, 2)) + differ(self.x, lax.rem(turn, 2))

    def over_seq(self, turn):
        return {"seq": self.shard(turn)}

    def over_core(self):
        return {"grp": 2 * self.z + 1 - self.c}

    def z_of(self, step):
        return lax.rem(self.z + step, self.depth)

    def over_z(self, step):
        return {"grp": 2 * self.z_of(step) + self.c}

    def greet(self, beyond=True):
        peers = [self.over_seq(turn) for turn in (1, 2, 3)]
        if beyond:
            peers += [self.over_core()] + [self.over_z(step) for step in range(1, self.depth)]
        barrier = pltpu.get_barrier_semaphore()
        for peer in peers:
            pl.semaphore_signal(barrier, inc=1, device_id=peer, device_id_type=MESH)
        pl.semaphore_wait(barrier, len(peers))


def copy_to(source, target, sems, index, peer):
    send, recv = sems
    return pltpu.make_async_remote_copy(
        src_ref=source,
        dst_ref=target,
        send_sem=send.at[index],
        recv_sem=recv.at[index],
        device_id=peer,
        device_id_type=MESH,
    )


class Gather:
    def __init__(self, place, view, sems, base, x_first):
        self.at, self.view, self.sems, self.base, self.x_first = place, view, sems, base, x_first

    def moves(self, stage):
        p = self.at
        two, deep = pl.ds(0, 2), pl.ds(0, p.depth)
        if stage == 0:
            own = self.view(p.y, p.x, p.z, p.c)
            return [(own, step - 1, p.over_z(step)) for step in range(1, p.depth)]
        first, second = (1, 2) if self.x_first else (2, 1)
        if stage == 1:
            return [(self.view(p.y, p.x, deep, p.c), p.depth - 1, p.over_seq(first))]
        near = self.view(p.y, two, deep, p.c) if self.x_first else self.view(two, p.x, deep, p.c)
        if stage == 2:
            return [(near, p.depth, p.over_seq(second)), (near, p.depth + 1, p.over_core())]
        far = self.view(1 - p.y, two, deep, p.c) if self.x_first else self.view(two, 1 - p.x, deep, p.c)
        return [(far, p.depth + 2, p.over_core())]

    def copies(self, stage, pick=slice(None)):
        return [copy_to(r, r, self.sems, self.base + slot, peer) for r, slot, peer in self.moves(stage)[pick]]

    def step(self, stage):
        if stage in (1, 2):
            for made in self.copies(stage - 1):
                made.wait()
        elif stage == 3:
            self.copies(2, slice(0, 1))[0].wait()
        elif stage == 4:
            for made in self.copies(2, slice(1, 2)) + self.copies(3):
                made.wait()
        if stage < 4:
            for made in self.copies(stage):
                made.start()


def gather_slots(depth):
    return depth + 3


def bind(ref, *lead):
    return lambda *i: ref.at[lead + i]


def bind_rows(ref, part):
    return lambda *i: ref.at[i + (pl.ds(part * ROWS, ROWS),)]


class Scatter:
    def __init__(self, place, view, out, scratch, sems, base, number, x_first):
        self.at, self.view, self.out, self.sems, self.base = place, view, out, sems, base
        self.bufs = [ref.at[number] for ref in scratch]
        self.x_first = x_first

    def copies(self, stage):
        p = self.at
        get, give_one, get_one, keep, give_two, get_two, give_z, get_z = self.bufs
        first, second = (1, 2) if self.x_first else (2, 1)
        if stage == 0:
            two = pl.ds(0, 2)
            source = self.view(two, two, pl.ds(0, p.depth), 1 - p.c)
            moves = [(source, get, 0, p.over_core())]
        elif stage == 1:
            moves = [(give_one, get_one, 1, p.over_seq(first))]
        elif stage == 2:
            moves = [(give_two, get_two, 2, p.over_seq(second))]
        else:
            moves = [
                (give_z.at[p.z_of(step)], get_z.at[step - 1], 2 + step, p.over_z(step))
                for step in range(1, p.depth)
            ]
        return [copy_to(a, b, self.sems, self.base + slot, peer) for a, b, slot, peer in moves]

    def part(self, other, kept):
        p = self.at
        y, x = (other, kept) if self.x_first else (kept, other)
        own = self.view(y, x, pl.ds(0, p.depth), p.c)[...]
        return own.astype(WIDE) + self.bufs[0][y, x].astype(WIDE)

    def step(self, stage):
        p = self.at
        get, give_one, get_one, keep, give_two, get_two, give_z, get_z = self.bufs
        outer, inner = (p.y, p.x) if self.x_first else (p.x, p.y)
        if stage:
            for made in self.copies(stage - 1):
                made.wait()
        if stage == 1:
            for other in range(2):
                give_one[other] = self.part(other, 1 - inner).astype(LOW)
        elif stage == 2:
            give_two[...] = (keep[1 - outer] + get_one[1 - outer].astype(WIDE)).astype(LOW)
        elif stage == 3:
            total = keep[outer] + get_one[outer].astype(WIDE) + get_two[...].astype(WIDE)
            keep[outer] = total
            give_z[...] = total.astype(LOW)
        if stage < 4:
            for made in self.copies(stage):
                made.start()
        if stage == 1:
            for other in range(2):
                keep[other] = self.part(other, inner)
        elif stage == 4:
            total = keep[outer, p.z]
            for step in range(1, p.depth):
                total = total + get_z[step - 1].astype(WIDE)
            self.out(total)


def scatter_slots(depth):
    return depth + 2


def scatter_scratch(count, depth, width):
    return [
        pltpu.VMEM((count, 2, 2, depth, ROWS, width), LOW),
        pltpu.VMEM((count, 2, depth, ROWS, width), LOW),
        pltpu.VMEM((count, 2, depth, ROWS, width), LOW),
        pltpu.VMEM((count, 2, depth, ROWS, width), WIDE),
        pltpu.VMEM((count, depth, ROWS, width), LOW),
        pltpu.VMEM((count, depth, ROWS, width), LOW),
        pltpu.VMEM((count, depth, ROWS, width), LOW),
        pltpu.VMEM((count, depth - 1, ROWS, width), LOW),
    ]


class SumAll:
    def __init__(self, place, out, give, get, sems, base):
        self.at, self.out, self.give, self.get, self.sems, self.base = place, out, give, get, sems, base

    def copies(self, stage):
        p = self.at
        if stage < 3:
            peer = (p.over_core, lambda: p.over_seq(1), lambda: p.over_seq(2))[stage]()
            moves = [(stage, stage, peer)]
        else:
            moves = [(3, 2 + step, p.over_z(step)) for step in range(1, p.depth)]
        return [
            copy_to(self.give.at[a], self.get.at[b], self.sems, self.base + b, peer)
            for a, b, peer in moves
        ]

    def step(self, stage):
        if stage:
            for made in self.copies(stage - 1):
                made.wait()
        if stage == 4:
            total = self.give[3]
            for step in range(1, self.at.depth):
                total = total + self.get[2 + step]
            self.out[...] = total
            return
        if stage:
            self.give[stage] = self.give[stage - 1] + self.get[stage - 1]
        for made in self.copies(stage):
            made.start()


def unit_rows_of(values):
    centred = values - jnp.mean(values, axis=-1, keepdims=True)
    factor = lax.rsqrt(jnp.mean(centred * centred, axis=-1, keepdims=True) + NORM_EPSILON)
    return centred * factor, factor


def put_tiles(ref, here, value):
    for k in range(ref.shape[0]):
        ref[k, here, :] = value[:, 128 * k : 128 * (k + 1)]


def get_tiles(ref, here):
    return jnp.concatenate([ref[k, here, :] for k in range(ref.shape[0])], axis=1)


def heads_apart(values, heads):
    size = values.shape[1] // heads
    lane = lax.broadcasted_iota(jnp.int32, values.shape, 1)
    parts = []
    for head in range(heads):
        own = jnp.logical_and(lane >= head * size, lane < (head + 1) * size)
        parts.append(jnp.where(own, values, jnp.zeros_like(values)))
    return jnp.concatenate(parts, axis=0)


def heads_together(turned, heads):
    size, rows = turned.shape[0] // heads, turned.shape[1] // heads
    return jnp.concatenate(
        [turned[h * size : (h + 1) * size, h * rows : (h + 1) * rows] for h in range(heads)], axis=0
    )


def hide_future(scores, first_slot, first_row, heads):
    rows = scores.shape[1] // heads
    slot = lax.broadcasted_iota(jnp.int32, scores.shape, 0) + first_slot
    column = lax.broadcasted_iota(jnp.int32, scores.shape, 1)
    for head in range(1, heads):
        column = jnp.where(column >= rows, column - rows, column)
    return jnp.where(3 * slot <= column + first_row, scores, MASKED_SCORE)


def front_kernel(depth, heads, tok, wq, wm, wo, wu, wd, tile, *refs):
    early, late, down, vectors, edge, qh, kh, vh, mixed, lse, attended = refs[:11]
    tiles, wide_a, low_a, qs, ms, vt, gsend, grecv, xsend, xrecv = refs[11:]
    p = Place(depth)
    own = (p.y, p.x, p.z, p.c)
    rows, width = tok.shape
    slots = rows // 3
    lanes = qh.shape[1]
    size = lanes // heads
    tiles[own] = tile[...].astype(LOW)
    early[(0,) + own] = wq[...].astype(LOW)
    for tap in range(3):
        for half in range(2):
            early[(1 + 2 * tap + half,) + own] = wm[tap, :, half * width : (half + 1) * width].astype(LOW)
    late[(0,) + own] = wo[...].astype(LOW)
    for part in range(4):
        late[(1 + part,) + own] = wu[:, part * width : (part + 1) * width].astype(LOW)
    down[own] = wd[...].astype(LOW)
    p.greet()
    views = [bind(tiles)] + [bind(early, 1 + j) for j in range(EARLY - 1)] + [bind(early, 0)]
    views += [bind(late, j) for j in range(LATE)]
    views += [bind_rows(down, k) for k in range(down.shape[4] // ROWS)]
    step = gather_slots(depth)
    pieces = [Gather(p, view, (gsend, grecv), step * k, k % 2 == 0) for k, view in enumerate(views)]
    soon, later = pieces[1 : 1 + EARLY], pieces[1 + EARLY :]
    vector_piece = pieces[0]
    for piece in pieces:
        piece.step(0)

    block = 128

    @pl.loop(0, rows // block)
    def _(number):
        at = pl.multiple_of(number * block, block)
        unit, _ = unit_rows_of(tok[pl.ds(at, block), :].astype(WIDE))
        put_tiles(wide_a, pl.ds(at + 8, block), unit)

    for stage in range(1, 3):
        for piece in [vector_piece] + soon:
            piece.step(stage)
    vector_piece.step(3)
    vector_piece.step(4)
    tile_lanes = tiles.shape[-1]
    for y in range(2):
        for x in range(2):
            total = jnp.zeros(tiles.shape[-2:], WIDE)
            for z in range(depth):
                for c in range(2):
                    total += tiles[y, x, z, c].astype(WIDE)
            s = 2 * y + x
            vectors[:, s * tile_lanes : (s + 1) * tile_lanes] = total
    gain, shift = vectors[0:1, :], vectors[1:2, :]

    @pl.loop(0, rows // block)
    def _(number):
        at = pl.multiple_of(number * block, block)
        normed = (get_tiles(wide_a, pl.ds(at + 8, block)) * gain + shift).astype(LOW)
        low_a[pl.ds(at, block), :] = normed
        put_tiles(wide_a, pl.ds(at + 8, block), normed.astype(WIDE))

    last = p.seq == 3

    def edge_copy():
        return copy_to(
            wide_a.at[:, pl.ds(rows, 8)], wide_a.at[:, pl.ds(0, 8)], (xsend, xrecv), 0, {"seq": lax.rem(p.seq + 1, 4)}
        )

    @pl.when(jnp.logical_not(last))
    def _():
        edge_copy().start()

    for piece in soon:
        piece.step(3)
    for piece in soon:
        piece.step(4)

    @pl.when(p.seq > 0)
    def _():
        edge_copy().wait_recv()

    @pl.when(jnp.logical_not(last))
    def _():
        edge_copy().wait_send()

    @pl.when(p.seq == 0)
    def _():
        wide_a[:, 0:8, :] = jnp.zeros((width // 128, 8, 128), WIDE)

    edge[...] = wide_a[:, 0:8, :]

    def weight(j):
        return early[j].reshape(width, width)

    windows = [get_tiles(wide_a, pl.ds(6 + tap, slots, stride=3)).astype(LOW) for tap in range(3)]
    for half in range(2):
        total = dot(windows[0], weight(1 + half))
        for tap in range(1, 3):
            total += dot(windows[tap], weight(1 + 2 * tap + half))
        ms[:, half * width : (half + 1) * width] = total.astype(LOW)

    def columns(shard, base=0):
        return pl.ds(pl.multiple_of(base + shard * lanes, lanes), lanes)

    def rows_of(shard, count):
        return pl.ds(pl.multiple_of(shard * count, count), count)

    mine = rows_of(p.seq, slots)

    def memory_copies(turn):
        shard = p.shard(turn)
        return [
            copy_to(ms.at[:, columns(shard)], kh.at[mine], (xsend, xrecv), 2 * turn - 1, p.over_seq(turn)),
            copy_to(ms.at[:, columns(shard, width)], vh.at[mine], (xsend, xrecv), 2 * turn, p.over_seq(turn)),
        ]

    for turn in (3, 1, 2):
        for made in memory_copies(turn):
            made.start()
    kh[mine, :] = ms[:, columns(p.seq)]
    vh[mine, :] = ms[:, columns(p.seq, width)]
    qs[...] = dot(low_a[...], weight(0)).astype(LOW)

    def query_copy(turn):
        return copy_to(
            qs.at[:, columns(p.shard(turn))], qh.at[rows_of(p.seq, rows)], (xsend, xrecv), 6 + turn, p.over_seq(turn)
        )

    for turn in (1, 2, 3):
        query_copy(turn).start()
    qh[rows_of(p.seq, rows), :] = qs[:, columns(p.seq)]
    for turn in (1, 2, 3):
        for made in memory_copies(turn):
            made.wait()
    vt[...] = vh[...].T
    parts = rows // STRIP
    groups = qh.shape[0] // (2 * STRIP)

    def mixed_copy(turn, part):
        shard = p.shard(turn)
        return copy_to(
            mixed.at[pl.ds(pl.multiple_of((shard * parts + part) * STRIP, STRIP), STRIP)],
            attended.at[pl.ds(pl.multiple_of(part * STRIP, STRIP), STRIP), columns(p.seq)],
            (xsend, xrecv),
            10 + (turn - 1) * parts + part,
            p.over_seq(turn),
        )

    def attend(seen, strip):
        first = pl.multiple_of(strip * STRIP, STRIP)
        queries = heads_apart(qh[pl.ds(first, STRIP), :] * jnp.bfloat16(size ** (-0.5)), heads)
        whole = seen - 2 * SLOTS
        recent = lax.dot_general(kh[whole:seen, :], queries, NT, preferred_element_type=WIDE)
        scores = hide_future(recent, whole, first, heads)
        if whole:
            past = lax.dot_general(kh[0:whole, :], queries, NT, preferred_element_type=WIDE)
            scores = jnp.concatenate([past, scores], axis=0)
        highest = jnp.max(scores, axis=0, keepdims=True)
        exponent = jnp.exp(scores - highest)
        summed = jnp.sum(exponent, axis=0, keepdims=True)
        out = dot(vt[:, 0:seen], exponent.astype(LOW)) * (1.0 / summed)
        lse[strip] = highest + jnp.log(summed)
        mixed[pl.ds(first, STRIP), :] = heads_together(out, heads).T.astype(LOW)

    @pl.loop(0, 4 * parts)
    def _(it):
        turn, part = lax.div(it, parts), lax.rem(it, parts)
        for k in (1, 2, 3):

            @pl.when(it == k * parts)
            def _():
                query_copy(k).wait()

        strip = p.shard(turn) * parts + part
        for group in range(groups):

            @pl.when(lax.div(strip, 2) == group)
            def _():
                attend(2 * SLOTS * (group + 1), strip)

        @pl.when(turn > 0)
        def _():
            mixed_copy(turn, part).start()

        @pl.when(turn == 0)
        def _():
            attended[pl.ds(pl.multiple_of(part * STRIP, STRIP), STRIP), columns(p.seq)] = mixed[
                pl.ds(pl.multiple_of(strip * STRIP, STRIP), STRIP), :
            ]

        for stage, when in ((1, 2), (2, 5), (3, 8)):

            @pl.when(it == when)
            def _():
                for piece in later:
                    piece.step(stage)

    for piece in later:
        piece.step(4)
    for turn in (1, 2, 3):
        for part in range(parts):
            mixed_copy(turn, part).wait()


def front(tok, params, heads, lanes):
    wq, wm, wo, wu, wd, vec = params
    groups = lax.axis_size("grp")
    depth = groups // 2
    rows, width = tok.shape
    own, slots = wq.shape[0], rows // 3
    tile_lanes = vec.shape[1] * groups
    tile = lax.dynamic_update_slice(
        jnp.zeros((ROWS, tile_lanes), WIDE), vec, (0, vec.shape[1] * lax.axis_index("grp"))
    )
    whole = (2, 2, depth, 2)
    pieces = 1 + EARLY + LATE + wd.shape[0] // ROWS
    sems = pltpu.SemaphoreType.DMA((pieces * gather_slots(depth),))
    parts = rows // STRIP
    swaps = pltpu.SemaphoreType.DMA((10 + 3 * parts,))
    return pl.pallas_call(
        functools.partial(front_kernel, depth, heads),
        out_shape=(
            shaped(EARLY, *whole, own, width),
            shaped(LATE, *whole, own, width),
            shaped(*whole, *wd.shape),
            shaped(ROWS, 4 * tile_lanes, kind=WIDE),
            shaped(width // 128, 8, 128, kind=WIDE),
            shaped(4 * rows, lanes),
            shaped(4 * slots, lanes),
            shaped(4 * slots, lanes),
            shaped(4 * rows, lanes),
            shaped(4 * parts, 1, heads * STRIP, kind=WIDE),
            shaped(rows, width),
        ),
        in_specs=in_vmem(7),
        out_specs=in_vmem(11),
        scratch_shapes=[
            pltpu.VMEM((*whole, ROWS, tile_lanes), LOW),
            pltpu.VMEM((width // 128, rows + 8, 128), WIDE),
            pltpu.VMEM((rows, width), LOW),
            pltpu.VMEM((rows, width), LOW),
            pltpu.VMEM((slots, 2 * width), LOW),
            pltpu.VMEM((lanes, 4 * slots), LOW),
            sems,
            sems,
            swaps,
            swaps,
        ],
        compiler_params=pltpu.CompilerParams(
            collective_id=0, has_side_effects=True, vmem_limit_bytes=58 * MEGA
        ),
    )(tok, wq, wm, wo, wu, wd, tile)


def middle_kernel(depth, tok, cot, att, late, down, vec, length, *refs):
    out, dres, doh, g_stack, g_down, g_vec = refs[:6]
    zs, dus, cs, es, ys, dos, xsend, xrecv = refs[6:]
    p = Place(depth)
    p.greet(beyond=False)
    rows, width = tok.shape
    hidden = zs.shape[1]
    lanes = doh.shape[1]
    gain, shift, bias = vec[2:3, :], vec[3:4, :], vec[4:5, :]
    inner = 0.7978845608028654
    cubic = inner * 0.044715
    g_vec[...] = jnp.zeros_like(g_vec)

    def columns(shard):
        return pl.ds(pl.multiple_of(shard * lanes, lanes), lanes)

    def do_copy(number, turn):
        at = pl.multiple_of(number * STRIP, STRIP)
        return copy_to(
            dos.at[pl.ds(at, STRIP), columns(p.shard(turn))],
            doh.at[pl.ds(pl.multiple_of(p.seq * rows + at, STRIP), STRIP)],
            (xsend, xrecv),
            3 * number + turn - 1,
            p.over_seq(turn),
        )

    @pl.loop(0, rows // STRIP)
    def _(number):
        at = pl.multiple_of(number * STRIP, STRIP)
        here = pl.ds(at, STRIP)
        residual = tok[here, :].astype(WIDE) + dot(att[here, :], late[0])
        unit, factor = unit_rows_of(residual)
        normed = (unit * gain + shift).astype(LOW)
        cs[here, :] = normed
        place = lax.broadcasted_iota(jnp.int32, (STRIP, 1), 0) + (p.seq * rows + at)
        live = (place < length[0, 0]).astype(WIDE)
        upstream = cot[here, :].astype(WIDE) * live
        upstream_low = upstream.astype(LOW)
        es[here, :] = upstream_low
        result = residual + bias
        back = jnp.zeros((STRIP, width), WIDE)
        for part in range(hidden // width):
            here_hidden = pl.ds(part * width, width)
            u = dot(normed, late[1 + part]) + vec[5 + part : 6 + part, :]
            square = u * u
            half = 0.5 + 0.5 * jnp.tanh(u * (inner + cubic * square))
            active = u * half
            slope = half + active * (1.0 - half) * (2.0 * inner + 6.0 * cubic * square)
            active_low = active.astype(LOW)
            zs[here, here_hidden] = active_low
            result += dot(active_low, down[here_hidden, :])
            pulled = lax.dot_general(upstream_low, down[here_hidden, :], NT, preferred_element_type=WIDE)
            grad = (pulled * slope).astype(LOW)
            dus[here, here_hidden] = grad
            g_vec[5 + part : 6 + part, :] += jnp.sum(grad.astype(WIDE), axis=0, keepdims=True)
            back += lax.dot_general(grad, late[1 + part], NT, preferred_element_type=WIDE)
        out[here, :] = result.astype(LOW)
        scaled = back * gain
        total = upstream + factor * (
            scaled
            - jnp.mean(scaled, axis=-1, keepdims=True)
            - unit * jnp.mean(scaled * unit, axis=-1, keepdims=True)
        )
        dres[here, :] = total
        branch = total.astype(LOW)
        ys[here, :] = branch
        dos[here, :] = lax.dot_general(branch, late[0], NT, preferred_element_type=WIDE).astype(LOW)
        for turn in (3, 1, 2):
            do_copy(number, turn).start()
        doh[pl.ds(pl.multiple_of(p.seq * rows + at, STRIP), STRIP), :] = dos[here, columns(p.seq)]
        g_vec[2:3, :] += jnp.sum(back * unit, axis=0, keepdims=True)
        g_vec[3:4, :] += jnp.sum(back, axis=0, keepdims=True)
        g_vec[4:5, :] += jnp.sum(upstream, axis=0, keepdims=True)

    g_stack[0] = over_rows(att[...], ys[...]).astype(LOW)
    for part in range(hidden // width):
        piece = pl.ds(part * width, width)
        g_stack[1 + part] = over_rows(cs[...], dus[:, piece]).astype(LOW)
        g_down[piece, :] = over_rows(zs[:, piece], es[...]).astype(LOW)
    for number in range(rows // STRIP):
        for turn in (1, 2, 3):
            do_copy(number, turn).wait()


def middle(tok, cot, att, late, down, vec, length, lanes):
    rows, width = tok.shape
    hidden = down.shape[0]
    sems = pltpu.SemaphoreType.DMA((3 * (rows // STRIP),))
    return pl.pallas_call(
        functools.partial(middle_kernel, lax.axis_size("grp") // 2),
        out_shape=(
            shaped(rows, width),
            shaped(rows, width, kind=WIDE),
            shaped(4 * rows, lanes),
            shaped(LATE, width, width),
            shaped(hidden, width),
            shaped(*vec.shape, kind=WIDE),
        ),
        in_specs=in_vmem(6) + [pl.BlockSpec(memory_space=pltpu.SMEM)],
        out_specs=in_vmem(6),
        scratch_shapes=[
            pltpu.VMEM((rows, hidden), LOW),
            pltpu.VMEM((rows, hidden), LOW),
            pltpu.VMEM((rows, width), LOW),
            pltpu.VMEM((rows, width), LOW),
            pltpu.VMEM((rows, width), LOW),
            pltpu.VMEM((rows, width), LOW),
            sems,
            sems,
        ],
        compiler_params=pltpu.CompilerParams(
            collective_id=1, has_side_effects=True, vmem_limit_bytes=58 * MEGA
        ),
    )(tok, cot, att, late, down, vec, length)


def back_kernel(depth, heads, *refs):
    qh, kh, vh, mixed, lse, doh, tok, dres, early, vec, edge, g_late, g_down, g_vec = refs[:14]
    grad, out_early, out_late, out_down, out_vec = refs[14:19]
    scatter = refs[19:27]
    g_early, dk, dv, kt, dqs, dq, dms, dm, wide_a, low_a, wide_da, da, after, give, get = refs[27:42]
    rsend, rrecv, xsend, xrecv = refs[42:]
    p = Place(depth)
    rows, width = tok.shape
    slots = rows // 3
    lanes = qh.shape[1]
    size = lanes // heads
    scale = size ** (-0.5)
    parts = rows // STRIP
    groups = qh.shape[0] // (2 * STRIP)
    downs = g_down.shape[4] // ROWS
    step = scatter_slots(depth)
    p.greet()

    def out_to(ref, *lead):
        def put(value):
            ref[lead] = value

        return put

    def rows_to(k):
        def put(value):
            out_down[k * ROWS : (k + 1) * ROWS] = value

        return put

    todo = [(bind(g_late, j), out_to(out_late, j)) for j in range(LATE)]
    todo += [(bind_rows(g_down, k), rows_to(k)) for k in range(downs)]
    todo += [(bind(g_early, j), out_to(out_early, j)) for j in range(EARLY)]
    pieces = [
        Scatter(p, view, out, scatter, (rsend, rrecv), step * k, k, k % 2 == 0)
        for k, (view, out) in enumerate(todo)
    ]
    soon, later = pieces[: LATE + downs], pieces[LATE + downs :]
    small = SumAll(p, out_vec, give, get, (rsend, rrecv), step * len(pieces))
    for piece in soon:
        piece.step(0)
    kt[...] = kh[...].T
    dk[...] = jnp.zeros_like(dk)
    dv[...] = jnp.zeros_like(dv)

    def columns(shard, base=0):
        return pl.ds(pl.multiple_of(base + shard * lanes, lanes), lanes)

    def strip_rows(number):
        return pl.ds(pl.multiple_of(number * STRIP, STRIP), STRIP)

    def dq_copy(turn, part):
        return copy_to(
            dqs.at[strip_rows(p.shard(turn) * parts + part)],
            dq.at[strip_rows(part), columns(p.seq)],
            (xsend, xrecv),
            (turn - 1) * parts + part,
            p.over_seq(turn),
        )

    def attend(seen, strip):
        here = strip_rows(strip)
        first = strip * STRIP
        incoming = doh[here, :]
        centre = (incoming.astype(WIDE) * mixed[here, :].astype(WIDE)).T
        middle = jnp.concatenate(
            [jnp.sum(centre[h * size : (h + 1) * size], axis=0, keepdims=True) for h in range(heads)], axis=1
        )
        queries = heads_apart(qh[here, :] * jnp.bfloat16(scale), heads)
        incoming = heads_apart(incoming, heads)
        total = lse[strip]
        turned = jnp.zeros((lanes, heads * STRIP), WIDE)
        for start in range(0, seen, 4 * SLOTS):
            stop = min(start + 4 * SLOTS, seen)
            if stop == seen:
                start_masked = max(seen - 2 * SLOTS, start)
            else:
                start_masked = stop
            scores = lax.dot_general(kh[start:stop, :], queries, NT, preferred_element_type=WIDE)
            if start_masked < stop:
                masked = hide_future(scores[start_masked - start :], start_masked, first, heads)
                if start_masked > start:
                    scores = jnp.concatenate([scores[: start_masked - start], masked], axis=0)
                else:
                    scores = masked
            weights = jnp.exp(scores - total)
            pulled = lax.dot_general(vh[start:stop, :], incoming, NT, preferred_element_type=WIDE)
            slope = (weights * (pulled - middle)).astype(LOW)
            dv[start:stop, :] += dot(weights.astype(LOW), incoming)
            dk[start:stop, :] += dot(slope, queries)
            turned += dot(kt[:, start:stop], slope)
        dqs[here, :] = (heads_together(turned, heads) * scale).T.astype(LOW)

    @pl.loop(0, 4 * parts)
    def _(it):
        turn, part = lax.rem(lax.div(it, parts) + 1, 4), lax.rem(it, parts)
        strip = p.shard(turn) * parts + part
        for group in range(groups):

            @pl.when(lax.div(strip, 2) == group)
            def _():
                attend(2 * SLOTS * (group + 1), strip)

        @pl.when(turn > 0)
        def _():
            dq_copy(turn, part).start()

        @pl.when(turn == 0)
        def _():
            dq[strip_rows(part), columns(p.seq)] = dqs[strip_rows(strip), :]

        for stage, when in ((1, 1), (2, 4), (3, 7), (4, 10)):

            @pl.when(it == when)
            def _():
                for piece in soon:
                    piece.step(stage)

    dms[:, 0:lanes] = dk[...].astype(LOW)
    dms[:, lanes : 2 * lanes] = dv[...].astype(LOW)

    def rows_of(shard):
        return pl.ds(pl.multiple_of(shard * slots, slots), slots)

    def memory_copies(turn):
        theirs = rows_of(p.shard(turn))
        base = 3 * parts + 2 * (turn - 1)
        return [
            copy_to(
                dms.at[theirs, half * lanes : (half + 1) * lanes],
                dm.at[:, columns(p.seq, half * width)],
                (xsend, xrecv),
                base + half,
                p.over_seq(turn),
            )
            for half in range(2)
        ]

    for turn in (3, 1, 2):
        for made in memory_copies(turn):
            made.start()
    for half in range(2):
        dm[:, columns(p.seq, half * width)] = dms[rows_of(p.seq), half * lanes : (half + 1) * lanes]

    gain, shift = vec[0:1, :], vec[1:2, :]
    block = 128
    wide_a[:, 0:8, :] = edge[...]

    @pl.loop(0, rows // block)
    def _(number):
        at = pl.multiple_of(number * block, block)
        unit, _ = unit_rows_of(tok[pl.ds(at, block), :].astype(WIDE))
        normed = (unit * gain + shift).astype(LOW)
        low_a[pl.ds(at, block), :] = normed
        put_tiles(wide_a, pl.ds(at + 8, block), normed.astype(WIDE))

    for turn in (1, 2, 3):
        for part in range(parts):
            dq_copy(turn, part).wait()

    def to_early(j, value):
        g_early[j] = value.astype(LOW).reshape(g_early.shape[1:])
        later[j].step(0)

    to_early(0, over_rows(low_a[...], dq[...]))
    da[...] = lax.dot_general(dq[...], early[0], NT, preferred_element_type=WIDE)
    for turn in (1, 2, 3):
        for made in memory_copies(turn):
            made.wait()
    halves = [dm[:, half * width : (half + 1) * width] for half in range(2)]
    for tap in range(3):
        window = get_tiles(wide_a, pl.ds(6 + tap, slots, stride=3)).astype(LOW)
        for half in range(2):
            to_early(1 + 2 * tap + half, over_rows(window, halves[half]))
    for piece in later:
        piece.step(1)
    wide_da[:, 0:8, :] = jnp.zeros((width // 128, 8, 128), WIDE)
    for tap in range(3):
        pulled = lax.dot_general(halves[0], early[1 + 2 * tap], NT, preferred_element_type=WIDE)
        pulled += lax.dot_general(halves[1], early[2 + 2 * tap], NT, preferred_element_type=WIDE)
        put_tiles(wide_da, pl.ds(6 + tap, slots, stride=3), pulled)

    def edge_copy():
        return copy_to(
            wide_da.at[:, pl.ds(0, 8)], after, (xsend, xrecv), 3 * parts + 6, {"seq": lax.rem(p.seq + 3, 4)}
        )

    @pl.when(p.seq > 0)
    def _():
        edge_copy().start()

    for piece in later:
        piece.step(2)

    @pl.when(p.seq < 3)
    def _():
        edge_copy().wait_recv()

    @pl.when(p.seq > 0)
    def _():
        edge_copy().wait_send()

    @pl.when(p.seq == 3)
    def _():
        after[...] = jnp.zeros_like(after)

    wide_da[:, rows + 6 : rows + 8, :] = after[:, 6:8, :]
    give[0] = g_vec[...]

    @pl.loop(0, rows // block)
    def _(number):
        at = pl.multiple_of(number * block, block)
        here = pl.ds(at, block)
        unit, factor = unit_rows_of(tok[here, :].astype(WIDE))
        upstream = da[here, :] + get_tiles(wide_da, pl.ds(at + 8, block))
        scaled = upstream * gain
        inward = factor * (
            scaled
            - jnp.mean(scaled, axis=-1, keepdims=True)
            - unit * jnp.mean(scaled * unit, axis=-1, keepdims=True)
        )
        grad[here, :] = (dres[here, :] + inward).astype(LOW)
        give[0, 0:1, :] += jnp.sum(upstream * unit, axis=0, keepdims=True)
        give[0, 1:2, :] += jnp.sum(upstream, axis=0, keepdims=True)

    small.step(0)
    for stage in (1, 2):
        small.step(stage)
    for piece in later:
        piece.step(3)
    for stage in (3, 4):
        small.step(stage)
    for piece in later:
        piece.step(4)


def back(saved, tok, dres, early, vec, edge, grads, heads):
    qh, kh, vh, mixed, lse, doh = saved
    g_late, g_down, g_vec = grads
    depth = lax.axis_size("grp") // 2
    rows, width = tok.shape
    lanes, slots = qh.shape[1], rows // 3
    whole = (2, 2, depth, 2)
    own_down = g_down.shape[0] // (8 * depth)
    parts = rows // STRIP
    pieces = EARLY + LATE + own_down // ROWS
    ring = pltpu.SemaphoreType.DMA((pieces * scatter_slots(depth) + depth + 2,))
    swaps = pltpu.SemaphoreType.DMA((3 * parts + 7,))
    return pl.pallas_call(
        functools.partial(back_kernel, depth, heads),
        out_shape=(
            shaped(rows, width),
            shaped(EARLY, ROWS, width, kind=WIDE),
            shaped(LATE, ROWS, width, kind=WIDE),
            shaped(own_down, width, kind=WIDE),
            shaped(*vec.shape, kind=WIDE),
        ),
        in_specs=in_vmem(14),
        out_specs=in_vmem(5),
        scratch_shapes=scatter_scratch(pieces, depth, width)
        + [
            pltpu.VMEM((EARLY, *whole, ROWS, width), LOW),
            pltpu.VMEM(kh.shape, WIDE),
            pltpu.VMEM(kh.shape, WIDE),
            pltpu.VMEM((lanes, kh.shape[0]), LOW),
            pltpu.VMEM(qh.shape, LOW),
            pltpu.VMEM((rows, width), LOW),
            pltpu.VMEM((4 * slots, 2 * lanes), LOW),
            pltpu.VMEM((slots, 2 * width), LOW),
            pltpu.VMEM((width // 128, rows + 8, 128), WIDE),
            pltpu.VMEM((rows, width), LOW),
            pltpu.VMEM((width // 128, rows + 8, 128), WIDE),
            pltpu.VMEM((rows, width), WIDE),
            pltpu.VMEM((width // 128, 8, 128), WIDE),
            pltpu.VMEM((4,) + vec.shape, WIDE),
            pltpu.VMEM((depth + 2,) + vec.shape, WIDE),
            ring,
            ring,
            swaps,
            swaps,
        ],
        compiler_params=pltpu.CompilerParams(
            collective_id=2, has_side_effects=True, vmem_limit_bytes=62 * MEGA
        ),
    )(
        qh,
        kh,
        vh,
        mixed,
        lse,
        doh,
        tok,
        dres,
        early,
        vec,
        edge,
        g_late.reshape(LATE, *whole, ROWS, width),
        g_down.reshape(*whole, own_down, width),
        g_vec,
    )


def update_kernel(*refs):
    weights, firsts, seconds = refs[0:6], refs[6:12], refs[12:18]
    early, late, down, vec = refs[18:22]
    outs = refs[22:]
    width = early.shape[-1]

    def put(which, at, gradient):
        results = adamw(
            weights[which][at], gradient, firsts[which][at], seconds[which][at], LEARNING_RATES[which]
        )
        for group, value in enumerate(results):
            outs[6 * group + which][at] = value

    every = slice(None)
    put(0, (every, every), early[0])
    for tap in range(3):
        for half in range(2):
            put(1, (tap, every, slice(half * width, (half + 1) * width)), early[1 + 2 * tap + half])
    put(2, (every, every), late[0])
    for part in range(4):
        put(3, (every, slice(part * width, (part + 1) * width)), late[1 + part])
    put(4, (every, every), down[...])
    put(5, (every, every), vec[...])


def update(params, firsts, seconds, grads):
    outs = [jax.ShapeDtypeStruct(member.shape, WIDE) for member in params] * 3
    outs += [jax.ShapeDtypeStruct(member.shape, LOW) for member in params]
    return pl.pallas_call(
        update_kernel,
        out_shape=tuple(outs),
        in_specs=in_vmem(22),
        out_specs=in_vmem(24),
    )(*params, *firsts, *seconds, *grads)


def fused(tokens, cotangent, lengths, *state):
    params, firsts, seconds = state[0:6], state[6:12], state[12:18]
    width = tokens.shape[2]
    lanes = width // lax.axis_size("seq")
    heads = H // lax.axis_size("seq")
    tok, cot = tokens[0], cotangent[0]
    early, late, down, vec, edge, qh, kh, vh, mixed, lse, attended = front(tok, params, heads, lanes)
    early = early.reshape(EARLY, width, width)
    late = late.reshape(LATE, width, width)
    down = down.reshape(-1, width)
    out, dres, doh, g_late, g_down, g_vec = middle(
        tok, cot, attended, late, down, vec, lengths.reshape(1, 1), lanes
    )
    grad, r_early, r_late, r_down, r_vec = back(
        (qh, kh, vh, mixed, lse, doh), tok, dres, early, vec, edge, (g_late, g_down, g_vec), heads
    )
    share = params[5].shape[1]
    index = lax.axis_index("seq") * lax.axis_size("grp") + lax.axis_index("grp")
    own_vec = lax.dynamic_slice(r_vec, (0, index * share), (params[5].shape[0], share))
    new = update(params, firsts, seconds, (r_early, r_late, r_down, own_vec))
    return (out[None], grad[None], *new)


def body(*arguments):
    tokens, shard = arguments[0], arguments[3]
    whole_tiles = shard.shape[0] % ROWS == 0 and tokens.shape[1] % STRIP == 0
    four = lax.axis_size("seq") == 4 and lax.axis_size("grp") % 2 == 0
    return (fused if whole_tiles and four else plain)(*arguments)


def solution(mesh):
    in_specs = (
        P("grp", "seq", None),
        P("grp", "seq", None),
        P("grp"),
        P(("seq", "grp"), None),
        P(None, ("seq", "grp"), None),
        P(("seq", "grp"), None),
        P(("seq", "grp"), None),
        P(("seq", "grp"), None),
        P(None, ("seq", "grp")),
        P(("seq", "grp"), None),
        P(None, ("seq", "grp"), None),
        P(("seq", "grp"), None),
        P(("seq", "grp"), None),
        P(("seq", "grp"), None),
        P(None, ("seq", "grp")),
        P(("seq", "grp"), None),
        P(None, ("seq", "grp"), None),
        P(("seq", "grp"), None),
        P(("seq", "grp"), None),
        P(("seq", "grp"), None),
        P(None, ("seq", "grp")),
    )
    out_specs = (
        P("grp", "seq", None),
        P("grp", "seq", None),
        P(("seq", "grp"), None),
        P(None, ("seq", "grp"), None),
        P(("seq", "grp"), None),
        P(("seq", "grp"), None),
        P(("seq", "grp"), None),
        P(None, ("seq", "grp")),
        P(("seq", "grp"), None),
        P(None, ("seq", "grp"), None),
        P(("seq", "grp"), None),
        P(("seq", "grp"), None),
        P(("seq", "grp"), None),
        P(None, ("seq", "grp")),
        P(("seq", "grp"), None),
        P(None, ("seq", "grp"), None),
        P(("seq", "grp"), None),
        P(("seq", "grp"), None),
        P(("seq", "grp"), None),
        P(None, ("seq", "grp")),
        P(("seq", "grp"), None),
        P(None, ("seq", "grp"), None),
        P(("seq", "grp"), None),
        P(("seq", "grp"), None),
        P(("seq", "grp"), None),
        P(None, ("seq", "grp")),
    )
    return jax.shard_map(body, mesh=mesh, in_specs=in_specs, out_specs=out_specs, check_vma=False)
```

```python
import functools

import jax
import jax.numpy as jnp
from jax import lax
from jax.experimental import pallas as pl
from jax.experimental.pallas import tpu as pltpu
from jax.sharding import PartitionSpec as P

H = 8
STEP = 10


NORM_EPSILON = 1e-05
BETA_FIRST = 0.9
BETA_SECOND = 0.95
ADAM_EPSILON = 1e-08
WEIGHT_DECAY = 0.1
LEARNING_RATES = (0.05, 0.04, 0.3, 0.05, 0.03, 0.5)
MASKED_SCORE = -1e30
NT = (((1,), (1,)), ((), ()))


def from_behind(x, axis, by):
    peers = lax.axis_size(axis)
    pairs = [(i, i + by) for i in range(peers) if 0 <= i + by < peers]
    return lax.ppermute(x, axis, pairs)


def matmul(left, right):
    return jnp.dot(left, right, preferred_element_type=jnp.float32)


def over_rows(left, right):
    return lax.dot_general(
        left, right, (((0,), (0,)), ((), ())), preferred_element_type=jnp.float32
    )


def against(left, right):
    return lax.dot_general(
        left, right, (((1,), (1,)), ((), ())), preferred_element_type=jnp.float32
    )


def norm_forward(values, gain, shift):
    centred = values - jnp.mean(values, axis=-1, keepdims=True)
    factor = lax.rsqrt(jnp.mean(centred * centred, axis=-1, keepdims=True) + NORM_EPSILON)
    unit_rows = centred * factor
    return (unit_rows * gain + shift, unit_rows, factor)


def norm_backward(upstream, unit_rows, factor, gain):
    scaled = upstream * gain
    inward = factor * (
        scaled
        - jnp.mean(scaled, axis=-1, keepdims=True)
        - unit_rows * jnp.mean(scaled * unit_rows, axis=-1, keepdims=True)
    )
    return (inward, jnp.sum(upstream * unit_rows, axis=0), jnp.sum(upstream, axis=0))


def masked_scores(query_tile_rows, key_row_block, positions):
    slot_starts = 3 * jnp.arange(key_row_block.shape[0], dtype=jnp.int32)
    score_matrix = jnp.einsum(
        "azv,lzv->zal", query_tile_rows, key_row_block, preferred_element_type=jnp.float32
    ) * query_tile_rows.shape[2] ** (-0.5)
    visible = slot_starts[None, :] <= positions[:, None]
    return jnp.where(visible[None], score_matrix, MASKED_SCORE)


def attend_forward(queries, key_row_block, value_row_block, anchor, block_rows):
    block_count = queries.shape[0] // block_rows
    offsets = block_rows * jnp.arange(block_count, dtype=jnp.int32)

    def attend_block(inputs):
        query_tile_rows, offset_rows = inputs
        score_matrix = masked_scores(
            query_tile_rows,
            key_row_block,
            anchor + offset_rows + jnp.arange(block_rows, dtype=jnp.int32),
        )
        highest = jnp.max(score_matrix, axis=-1, keepdims=True)
        exponent = jnp.exp(score_matrix - highest)
        summed = jnp.sum(exponent, axis=-1, keepdims=True)
        reduced_weights = (exponent / summed).astype(jnp.bfloat16)
        mixed = jnp.einsum(
            "yup,pyb->uyb", reduced_weights, value_row_block, preferred_element_type=jnp.float32
        )
        return (mixed, (highest + jnp.log(summed))[..., 0])

    blocks_in = queries.reshape(block_count, block_rows, queries.shape[1], queries.shape[2])
    mixed, logsum = lax.map(attend_block, (blocks_in, offsets))
    return (mixed.reshape(queries.shape), logsum)


def attend_backward(queries, key_row_block, value_row_block, upstream, logsum, anchor, block_rows):
    block_count = queries.shape[0] // block_rows
    offsets = block_rows * jnp.arange(block_count, dtype=jnp.int32)
    scale_factor = queries.shape[2] ** (-0.5)

    def attend_back(carry, inputs):
        grad_keys, grad_values = carry
        query_tile_rows, incoming_gradient_rows, logsum_block, offset_rows = inputs
        score_matrix = masked_scores(
            query_tile_rows,
            key_row_block,
            anchor + offset_rows + jnp.arange(block_rows, dtype=jnp.int32),
        )
        weights_soft = jnp.exp(score_matrix - logsum_block[..., None])
        grad_weights = jnp.einsum(
            "azv,lzv->zal",
            incoming_gradient_rows,
            value_row_block,
            preferred_element_type=jnp.float32,
        )
        centre = jnp.sum(weights_soft * grad_weights, axis=-1, keepdims=True)
        score_gradient = (weights_soft * (grad_weights - centre)).astype(jnp.bfloat16)
        grad_query = (
            jnp.einsum(
                "yup,pyb->uyb", score_gradient, key_row_block, preferred_element_type=jnp.float32
            )
            * scale_factor
        )
        grad_keys = (
            grad_keys
            + jnp.einsum(
                "xof,oxa->fxa", score_gradient, query_tile_rows, preferred_element_type=jnp.float32
            )
            * scale_factor
        )
        grad_values = grad_values + jnp.einsum(
            "xof,oxa->fxa",
            weights_soft.astype(jnp.bfloat16),
            incoming_gradient_rows,
            preferred_element_type=jnp.float32,
        )
        return ((grad_keys, grad_values), grad_query)

    shape_blocks = (block_count, block_rows, queries.shape[1], queries.shape[2])
    zeros_init = jnp.zeros(key_row_block.shape, jnp.float32)
    (grad_keys, grad_values), grad_query = lax.scan(
        attend_back,
        (zeros_init, zeros_init),
        (queries.reshape(shape_blocks), upstream.reshape(shape_blocks), logsum, offsets),
    )
    return (grad_query.reshape(queries.shape), grad_keys, grad_values)


def adamw(weight, gradient, moment, square, step_rate):
    moment_new = BETA_FIRST * moment + (1.0 - BETA_FIRST) * gradient
    square_new = BETA_SECOND * square + (1.0 - BETA_SECOND) * gradient * gradient
    fixed_first = 1.0 - BETA_FIRST**STEP
    fixed_second = 1.0 - BETA_SECOND**STEP
    update = (
        moment_new / fixed_first / (jnp.sqrt(square_new / fixed_second) + ADAM_EPSILON)
        + WEIGHT_DECAY * weight
    )
    master = weight - step_rate * update
    return (moment_new, square_new, master, master.astype(jnp.bfloat16))


def plain(
    tokens,
    cotangent,
    lengths,
    weight_query,
    weight_memory,
    weight_out,
    weight_up,
    weight_down,
    vectors,
    first_query,
    first_memory,
    first_out,
    first_up,
    first_down,
    first_vectors,
    second_query,
    second_memory,
    second_out,
    second_up,
    second_down,
    second_vectors,
):
    gathered = (
        lax.all_gather(weight_query.astype(jnp.bfloat16), ("seq", "grp"), axis=0, tiled=True),
        lax.all_gather(weight_memory.astype(jnp.bfloat16), ("seq", "grp"), axis=1, tiled=True),
        lax.all_gather(weight_out.astype(jnp.bfloat16), ("seq", "grp"), axis=0, tiled=True),
        lax.all_gather(weight_up.astype(jnp.bfloat16), ("seq", "grp"), axis=0, tiled=True),
        lax.all_gather(weight_down.astype(jnp.bfloat16), ("seq", "grp"), axis=0, tiled=True),
        lax.all_gather(vectors.astype(jnp.bfloat16), ("seq", "grp"), axis=1, tiled=True),
    )
    query_w, memory_w, out_w, up_w, down_w, vector_low = gathered
    vector_rows = vector_low.astype(jnp.float32)
    model_width = query_w.shape[0]
    hidden_units = up_w.shape[1]
    head_size = model_width // H
    seq_count = lax.axis_size("seq")
    seq_index = lax.axis_index("seq")
    local_rows = tokens.shape[1]
    local_slots = local_rows // 3
    inputs = tokens[0].astype(jnp.float32)
    normed, unit_one, factor_one = norm_forward(inputs, vector_rows[0], vector_rows[1])
    normed_low = normed.astype(jnp.bfloat16)
    queries = matmul(normed_low, query_w).astype(jnp.bfloat16)
    borrowed = from_behind(normed_low[local_rows - 2 :], "seq", 1)
    extended = jnp.concatenate([borrowed, normed_low], axis=0)
    windows = extended[:local_rows].reshape(local_slots, 3 * model_width)
    memory_flat = memory_w.reshape(3 * model_width, 2 * model_width)
    memory = matmul(windows, memory_flat).astype(jnp.bfloat16)
    share_width = model_width // seq_count
    local_heads = H // seq_count
    head_queries, head_memory = (
        lax.all_to_all(
            queries.reshape(local_rows, 1, seq_count, share_width),
            "seq",
            split_axis=2,
            concat_axis=0,
            tiled=True,
        ),
        lax.all_to_all(
            memory.reshape(local_slots, 2, seq_count, share_width),
            "seq",
            split_axis=2,
            concat_axis=0,
            tiled=True,
        ),
    )
    total_rows = head_queries.shape[0]
    total_slots = head_memory.shape[0]
    query_heads = head_queries.reshape(total_rows, local_heads, head_size)
    key_heads = head_memory[:, 0].reshape(total_slots, local_heads, head_size)
    value_heads = head_memory[:, 1].reshape(total_slots, local_heads, head_size)
    block_rows = min(512, total_rows)
    mixed, logsum = attend_forward(query_heads, key_heads, value_heads, 0, block_rows)
    mixed_low = mixed.astype(jnp.bfloat16).reshape(total_rows, 1, share_width)
    attended = lax.all_to_all(mixed_low, "seq", split_axis=0, concat_axis=1, tiled=True).reshape(
        local_rows, model_width
    )
    residual = inputs + matmul(attended, out_w)
    normed_two, unit_two, factor_two = norm_forward(residual, vector_rows[2], vector_rows[3])
    normed_two_low = normed_two.astype(jnp.bfloat16)
    pre_act = matmul(normed_two_low, up_w) + vector_rows[5:].reshape(hidden_units)
    activated, gelu_pull = jax.vjp(jax.nn.gelu, pre_act)
    activated_low = activated.astype(jnp.bfloat16)
    result = residual + matmul(activated_low, down_w) + vector_rows[4]
    positions = seq_index * local_rows + jnp.arange(local_rows, dtype=jnp.int32)
    live_mask = (positions < lengths[0]).astype(jnp.float32)
    grad_out = cotangent[0].astype(jnp.float32) * live_mask[:, None]
    grad_out_low = grad_out.astype(jnp.bfloat16)
    grad_down = over_rows(activated_low, grad_out_low)
    grad_activated = against(grad_out_low, down_w)
    grad_pre_low = gelu_pull(grad_activated)[0].astype(jnp.bfloat16)
    grad_up = over_rows(normed_two_low, grad_pre_low)
    grad_up_bias = jnp.sum(grad_pre_low.astype(jnp.float32), axis=0)
    grad_normed_two = against(grad_pre_low, up_w)
    grad_norm_two, grad_gain_two, grad_shift_two = norm_backward(
        grad_normed_two, unit_two, factor_two, vector_rows[2]
    )
    grad_residual = grad_out + grad_norm_two
    grad_branch_low = grad_residual.astype(jnp.bfloat16)
    grad_outw = over_rows(attended, grad_branch_low)
    grad_attended_low = against(grad_branch_low, out_w).astype(jnp.bfloat16)
    grad_heads = lax.all_to_all(
        grad_attended_low.reshape(local_rows, 1, seq_count, share_width),
        "seq",
        split_axis=2,
        concat_axis=0,
        tiled=True,
    ).reshape(total_rows, local_heads, head_size)
    grad_q, grad_k, grad_v = attend_backward(
        query_heads, key_heads, value_heads, grad_heads, logsum, 0, block_rows
    )
    packed = (
        jnp.stack([grad_k, grad_v], axis=1)
        .astype(jnp.bfloat16)
        .reshape(total_slots, 2, 1, share_width)
    )
    token_queries, token_memory = (
        lax.all_to_all(
            grad_q.astype(jnp.bfloat16).reshape(total_rows, 1, 1, share_width),
            "seq",
            split_axis=0,
            concat_axis=2,
            tiled=True,
        ),
        lax.all_to_all(packed, "seq", split_axis=0, concat_axis=2, tiled=True),
    )
    grad_queries_low = token_queries.reshape(local_rows, model_width)
    grad_memory_low = token_memory.reshape(local_slots, 2 * model_width)
    grad_queryw = over_rows(normed_low, grad_queries_low)
    grad_normed = against(grad_queries_low, query_w)
    grad_memoryw = over_rows(windows, grad_memory_low).reshape(3, model_width, 2 * model_width)
    grad_windows = against(grad_memory_low, memory_flat).reshape(local_rows, model_width)
    returned = from_behind(grad_windows[:2], "seq", -1)
    grad_normed = grad_normed + jnp.concatenate([grad_windows[2:], returned], axis=0)
    grad_norm_one, grad_gain_one, grad_shift_one = norm_backward(
        grad_normed, unit_one, factor_one, vector_rows[0]
    )
    grad_inputs = (grad_residual + grad_norm_one).astype(jnp.bfloat16)
    grad_vector_rows = jnp.concatenate(
        [
            jnp.stack(
                [
                    grad_gain_one,
                    grad_shift_one,
                    grad_gain_two,
                    grad_shift_two,
                    jnp.sum(grad_out, axis=0),
                ]
            ),
            grad_up_bias.reshape(4, model_width),
        ],
        axis=0,
    )
    reduced = (
        lax.psum_scatter(grad_queryw, ("seq", "grp"), scatter_dimension=0, tiled=True),
        lax.psum_scatter(grad_memoryw, ("seq", "grp"), scatter_dimension=1, tiled=True),
        lax.psum_scatter(grad_outw, ("seq", "grp"), scatter_dimension=0, tiled=True),
        lax.psum_scatter(grad_up, ("seq", "grp"), scatter_dimension=0, tiled=True),
        lax.psum_scatter(grad_down, ("seq", "grp"), scatter_dimension=0, tiled=True),
        lax.psum_scatter(grad_vector_rows, ("seq", "grp"), scatter_dimension=1, tiled=True),
    )
    new_query = adamw(weight_query, reduced[0], first_query, second_query, LEARNING_RATES[0])
    new_memory = adamw(weight_memory, reduced[1], first_memory, second_memory, LEARNING_RATES[1])
    new_out = adamw(weight_out, reduced[2], first_out, second_out, LEARNING_RATES[2])
    new_up = adamw(weight_up, reduced[3], first_up, second_up, LEARNING_RATES[3])
    new_down = adamw(weight_down, reduced[4], first_down, second_down, LEARNING_RATES[4])
    new_vectors = adamw(vectors, reduced[5], first_vectors, second_vectors, LEARNING_RATES[5])
    return (
        result.astype(jnp.bfloat16)[None],
        grad_inputs[None],
        new_query[0],
        new_memory[0],
        new_out[0],
        new_up[0],
        new_down[0],
        new_vectors[0],
        new_query[1],
        new_memory[1],
        new_out[1],
        new_up[1],
        new_down[1],
        new_vectors[1],
        new_query[2],
        new_memory[2],
        new_out[2],
        new_up[2],
        new_down[2],
        new_vectors[2],
        new_query[3],
        new_memory[3],
        new_out[3],
        new_up[3],
        new_down[3],
        new_vectors[3],
    )


MESH = pl.DeviceIdType.MESH
LOW, WIDE = jnp.bfloat16, jnp.float32
ROWS = 16
PART = 384
STRIP = 2 * PART
SLOTS = STRIP // 3
EARLY = 7
LATE = 5
MEGA = 1024 * 1024
SCATTER_ORDERS = ("yzx", "xzy", "xzy", "yzx", "yxz", "xyz", "yzx", "yxz", "xzy")


def in_vmem(count):
    return [pl.BlockSpec(memory_space=pltpu.VMEM)] * count


def shaped(*shape, kind=jnp.bfloat16):
    return jax.ShapeDtypeStruct(shape, kind)


def dot(left, right):
    return jnp.dot(left, right, preferred_element_type=jnp.float32)


def differ(bit, other):
    return bit + other - 2 * bit * other


class Place:
    def __init__(self, depth):
        self.seq, self.grp = lax.axis_index("seq"), lax.axis_index("grp")
        self.depth = depth
        self.y, self.x = lax.div(self.seq, 2), lax.rem(self.seq, 2)
        self.z, self.c = lax.div(self.grp, 2), lax.rem(self.grp, 2)
        self.own = {"y": self.y, "x": self.x, "z": self.z}
        self.size = {"y": 2, "x": 2, "z": depth}

    def turn_to(self, shard):
        return 2 * differ(self.y, lax.div(shard, 2)) + differ(self.x, lax.rem(shard, 2))

    def strip(self, it):
        half, pos = differ(lax.div(it, 3), self.y), lax.rem(it, 3)
        return 3 * half + pos + self.x * (2 - 2 * pos)

    def shard(self, turn):
        return 2 * differ(self.y, lax.div(turn, 2)) + differ(self.x, lax.rem(turn, 2))

    def over_seq(self, turn):
        return {"seq": self.shard(turn)}

    def over_core(self):
        return {"grp": 2 * self.z + 1 - self.c}

    def z_of(self, step):
        return lax.rem(self.z + step, self.depth)

    def over_z(self, step):
        return {"grp": 2 * self.z_of(step) + self.c}

    def step_of(self, axis, step):
        return self.z_of(step) if axis == "z" else 1 - self.own[axis]

    def others(self, axis):
        if axis == "z":
            return [self.over_z(step) for step in range(1, self.depth)]
        return [self.over_seq({"x": 1, "y": 2}[axis])]

    def greet(self, beyond=True):
        peers = [self.over_seq(turn) for turn in (1, 2, 3)]
        if beyond:
            peers += [self.over_core()] + [self.over_z(step) for step in range(1, self.depth)]
        barrier = pltpu.get_barrier_semaphore()
        for peer in peers:
            pl.semaphore_signal(barrier, inc=1, device_id=peer, device_id_type=MESH)
        pl.semaphore_wait(barrier, len(peers))


def copy_to(source, target, sems, index, peer):
    send, recv = sems
    return pltpu.make_async_remote_copy(
        src_ref=source,
        dst_ref=target,
        send_sem=send.at[index],
        recv_sem=recv.at[index],
        device_id=peer,
        device_id_type=MESH,
    )


class Gather:
    def __init__(self, place, view, sems, base, order, own=None):
        self.at, self.view, self.sems, self.base, self.order = place, view, sems, base, order
        self.own = own

    def moves(self, stage):
        p = self.at
        done = self.order[:stage]
        where = [pl.ds(0, p.size[axis]) if axis in done else p.own[axis] for axis in "yxz"]
        region = self.view(*where, p.c)
        if stage == 3:
            return [(region, p.depth + 1, p.over_core())]
        base = sum(p.size[axis] - 1 for axis in done)
        return [(region, base + i, peer) for i, peer in enumerate(p.others(self.order[stage]))]

    def copies(self, stage):
        source = self.own if stage == 0 else None
        return [
            copy_to(r if source is None else source, r, self.sems, self.base + slot, peer)
            for r, slot, peer in self.moves(stage)
        ]

    def place_own(self, sem):
        p = self.at
        return pltpu.make_async_copy(self.own, self.view(p.y, p.x, p.z, p.c), sem)

    def step(self, stage):
        if stage:
            for made in self.copies(stage - 1):
                made.wait()
        if stage < 4:
            for made in self.copies(stage):
                made.start()


def gather_slots(depth):
    return depth + 2


def bind(ref, first, count):
    return lambda *i: ref.at[(pl.ds(first, count),) + i]


def bind_rows(ref, first, count):
    return lambda *i: ref.at[i + (pl.ds(first, count),)]


class Scatter:
    def __init__(self, place, view, out, bufs, sems, base, order):
        self.at, self.view, self.out, self.sems, self.base, self.order = place, view, out, sems, base, order
        self.get_core, self.give, self.get, self.keep = bufs

    def plan(self, number):
        p = self.at
        axis = self.order[number]
        rest = [other for other in "yxz" if other not in self.order[: number + 1]]
        combos = [{}]
        for other in rest:
            combos = [{**c, other: i} for c in combos for i in range(p.size[other])]
        first = 0
        for k in range(number):
            left = 1
            for other in self.order[k + 1 :]:
                left *= p.size[other]
            first += left * (p.size[self.order[k]] - 1)
        return axis, combos, first

    def kept(self, index):
        p = self.at
        linear = 0
        for axis in "yxz":
            if axis != self.order[0]:
                linear = linear * p.size[axis] + index.get(axis, p.own[axis])
        return linear

    def now(self, number, index):
        p = self.at
        if number:
            return self.keep[self.kept(index)]
        where = [index.get(axis, p.own[axis]) for axis in "yxz"]
        lead = (slice(None),) * (len(self.get_core.shape) - 5)
        return self.view(*where, p.c)[...].astype(WIDE) + self.get_core[lead + tuple(where)].astype(WIDE)

    def copies(self, stage):
        p = self.at
        if stage == 0:
            source = self.view(pl.ds(0, 2), pl.ds(0, 2), pl.ds(0, p.depth), 1 - p.c)
            return [copy_to(source, self.get_core, self.sems, self.base, p.over_core())]
        axis, combos, first = self.plan(stage - 1)
        slot = 1 + sum(p.size[other] - 1 for other in self.order[: stage - 1])
        made = []
        for i, peer in enumerate(p.others(axis)):
            here = pl.ds(first + i * len(combos), len(combos))
            made.append(copy_to(self.give.at[here], self.get.at[here], self.sems, self.base + slot + i, peer))
        return made

    def step(self, stage):
        p = self.at
        if stage:
            for made in self.copies(stage - 1):
                made.wait()
        if stage >= 2:
            axis, combos, first = self.plan(stage - 2)
            for k, index in enumerate(combos):
                total = self.keep[self.kept(index)]
                for i in range(p.size[axis] - 1):
                    total = total + self.get[first + i * len(combos) + k].astype(WIDE)
                if stage == 4:
                    self.out(total)
                else:
                    self.keep[self.kept(index)] = total
        if 1 <= stage < 4:
            axis, combos, first = self.plan(stage - 1)
            for i in range(p.size[axis] - 1):
                for k, index in enumerate(combos):
                    target = {**index, axis: p.step_of(axis, i + 1)}
                    self.give[first + i * len(combos) + k] = self.now(stage - 1, target).astype(LOW)
        if stage < 4:
            for made in self.copies(stage):
                made.start()
        if stage == 1:
            axis, combos, first = self.plan(0)
            for index in combos:
                self.keep[self.kept(index)] = self.now(0, index)


def scatter_slots(depth):
    return depth + 2


def scatter_scratch(depth, order, shape):
    kept = 4 if order[0] == "z" else 2 * depth
    return [
        pltpu.VMEM(shape[:-2] + (2, 2, depth) + shape[-2:], LOW),
        pltpu.VMEM((4 * depth - 1,) + shape, LOW),
        pltpu.VMEM((4 * depth - 1,) + shape, LOW),
        pltpu.VMEM((kept,) + shape, WIDE),
    ]


class SumAll:
    def __init__(self, place, out, give, get, sems, base):
        self.at, self.out, self.give, self.get, self.sems, self.base = place, out, give, get, sems, base

    def copies(self, stage):
        p = self.at
        if stage == 0:
            moves = [(0, p.over_core())]
        elif stage == 1:
            moves = [(turn, p.over_seq(turn)) for turn in (1, 2, 3)]
        else:
            moves = [(3 + step, p.over_z(step)) for step in range(1, p.depth)]
        return [
            copy_to(self.give.at[stage], self.get.at[slot], self.sems, self.base + slot, peer)
            for slot, peer in moves
        ]

    def step(self, stage):
        if stage:
            for made in self.copies(stage - 1):
                made.wait()
            total = self.give[stage - 1]
            for slot in ((), (0,), (1, 2, 3), range(4, 3 + self.at.depth))[stage]:
                total = total + self.get[slot]
            if stage == 3:
                self.out[...] = total
                return
            self.give[stage] = total
        for made in self.copies(stage):
            made.start()


def run(steps):
    for piece, stage in steps:
        piece.step(stage)


def skewed(pieces, stages):
    stages = list(stages)
    return [
        (piece, stages[slot - k])
        for slot in range(len(pieces) + len(stages) - 1)
        for k, piece in enumerate(pieces)
        if 0 <= slot - k < len(stages)
    ]


def unit_rows_of(values):
    centred = values - jnp.mean(values, axis=-1, keepdims=True)
    factor = lax.rsqrt(jnp.mean(centred * centred, axis=-1, keepdims=True) + NORM_EPSILON)
    return centred * factor, factor


def put_tiles(ref, here, value):
    for k in range(ref.shape[0]):
        ref[k, here, :] = value[:, 128 * k : 128 * (k + 1)]


def get_tiles(ref, here):
    return jnp.concatenate([ref[k, here, :] for k in range(ref.shape[0])], axis=1)


def hide_future(scores, first_slot, first_row):
    slot = lax.broadcasted_iota(jnp.int32, scores.shape, 0) + first_slot
    row = lax.broadcasted_iota(jnp.int32, scores.shape, 1) + first_row
    return jnp.where(3 * slot <= row, scores, MASKED_SCORE)


def span(number, size):
    return pl.ds(pl.multiple_of(number * size, size), size)


def front_kernel(depth, tok, wq, wm, wo, wu, wd, tile, *refs):
    early, late, down, vectors, edge, qh, kv, mixed, lse, attended = refs[:10]
    tiles, wide_a, low_a, qs, ms, kvt, own_late, own_down, gsend, grecv, xsend, xrecv, lsem = refs[10:]
    p = Place(depth)
    own = (p.y, p.x, p.z, p.c)
    rows, width = tok.shape
    slots = rows // 3
    size = qh.shape[1]
    lanes = 2 * size
    tiles[own] = tile[...].astype(LOW)
    early[(0,) + own] = wq[...].astype(LOW)
    for tap in range(3):
        for half in range(2):
            columns = []
            for head in range(4 * half, 4 * half + 4):
                columns.append(wm[tap, :, head * size : (head + 1) * size])
                columns.append(wm[tap, :, width + head * size : width + (head + 1) * size])
            early[(1 + 3 * half + tap,) + own] = jnp.concatenate(columns, axis=1).astype(LOW)
    own_late[0] = wo[...].astype(LOW)
    for part in range(4):
        own_late[1 + part] = wu[:, part * width : (part + 1) * width].astype(LOW)
    own_down[...] = wd[...].astype(LOW)
    p.greet()
    half_down = down.shape[4] // 2
    views = [
        (lambda *i: tiles.at[i], "zxy", None),
        (bind(early, 1, 1), "zxy", None),
        (bind(early, 2, 1), "zyx", None),
        (bind(early, 3, 1), "xzy", None),
        (bind(early, 0, 1), "yzx", None),
        (bind(early, 4, 1), "zyx", None),
        (bind(early, 5, 1), "zxy", None),
        (bind(early, 6, 1), "yzx", None),
        (bind(late, 0, 3), "xyz", own_late.at[pl.ds(0, 3)]),
        (bind(late, 3, 2), "yzx", own_late.at[pl.ds(3, 2)]),
        (bind_rows(down, 0, half_down), "yxz", own_down.at[pl.ds(0, half_down)]),
        (bind_rows(down, half_down, half_down), "xyz", own_down.at[pl.ds(half_down, half_down)]),
    ]
    step = gather_slots(depth)
    pieces = [
        Gather(p, view, (gsend, grecv), step * k, order, first) for k, (view, order, first) in enumerate(views)
    ]
    vector_piece, soon, next_up, later = pieces[0], pieces[1:5], pieces[5:8], pieces[8:]
    for piece in pieces[:5]:
        piece.step(0)
    for k, piece in enumerate(later):
        piece.place_own(lsem.at[k]).start()
        piece.step(0)

    block = 128

    @pl.loop(0, rows // block)
    def _(number):
        at = pl.multiple_of(number * block, block)
        unit, _ = unit_rows_of(tok[pl.ds(at, block), :].astype(WIDE))
        put_tiles(wide_a, pl.ds(at + 8, block), unit)

    vector_piece.step(1)
    for piece in soon[2:] + soon[:2]:
        piece.step(1)
    for piece in next_up:
        piece.step(0)
    vector_piece.step(2)
    vector_piece.step(3)
    vector_piece.step(4)
    tile_lanes = tiles.shape[-1]
    for y in range(2):
        for x in range(2):
            total = jnp.zeros(tiles.shape[-2:], WIDE)
            for z in range(depth):
                for c in range(2):
                    total += tiles[y, x, z, c].astype(WIDE)
            s = 2 * y + x
            vectors[:, s * tile_lanes : (s + 1) * tile_lanes] = total
    gain, shift = vectors[0:1, :], vectors[1:2, :]

    @pl.loop(0, rows // block)
    def _(number):
        at = pl.multiple_of(number * block, block)
        normed = (get_tiles(wide_a, pl.ds(at + 8, block)) * gain + shift).astype(LOW)
        low_a[pl.ds(at, block), :] = normed
        put_tiles(wide_a, pl.ds(at + 8, block), normed.astype(WIDE))

    last = p.seq == 3

    def edge_copy():
        return copy_to(
            wide_a.at[:, pl.ds(rows, 8)], wide_a.at[:, pl.ds(0, 8)], (xsend, xrecv), 0, {"seq": lax.rem(p.seq + 1, 4)}
        )

    @pl.when(jnp.logical_not(last))
    def _():
        edge_copy().start()

    for stage in (2, 3):
        for piece in soon:
            piece.step(stage)
    for k, piece in enumerate(later):
        piece.place_own(lsem.at[k]).wait()
        piece.step(1)
    for piece in soon:
        piece.step(4)

    @pl.when(p.seq > 0)
    def _():
        edge_copy().wait_recv()

    @pl.when(jnp.logical_not(last))
    def _():
        edge_copy().wait_send()

    @pl.when(p.seq == 0)
    def _():
        wide_a[:, 0:8, :] = jnp.zeros((width // 128, 8, 128), WIDE)

    edge[...] = wide_a[:, 0:8, :]

    def weight(j):
        return early[j].reshape(width, width)

    mine = span(p.seq, slots)

    def memory_copy(half, turn):
        return copy_to(
            ms.at[half, :, span(p.shard(turn), lanes)],
            kv.at[half, mine],
            (xsend, xrecv),
            1 + 3 * half + turn - 1,
            p.over_seq(turn),
        )

    def project(half):
        for tap in range(3):
            window = get_tiles(wide_a, pl.ds(6 + tap, slots, stride=3)).astype(LOW)
            part = dot(window, weight(1 + 3 * half + tap))
            total = part if tap == 0 else total + part
        ms[half] = total.astype(LOW)
        for turn in (3, 1, 2):
            memory_copy(half, turn).start()
        kv[half, mine, :] = ms[half, :, span(p.seq, lanes)]

    def query_copy(half, turn):
        return copy_to(
            qs.at[half, p.shard(turn)],
            qh.at[half, :, span(p.seq, rows)],
            (xsend, xrecv),
            7 + 3 * half + turn - 1,
            p.over_seq(turn),
        )

    def send_queries(half):
        for turn in (1, 2, 3):
            query_copy(half, turn).start()
        qh[half, :, span(p.seq, rows)] = qs[half, p.seq]

    project(0)
    turned = lax.dot_general(weight(0).T, low_a[...], NT, preferred_element_type=WIDE)
    qs[...] = turned.astype(LOW).reshape(qs.shape)
    send_queries(0)
    for piece in next_up:
        piece.step(1)
    for piece in later:
        piece.step(2)
    for turn in (1, 2, 3):
        memory_copy(0, turn).wait()
    kvt[0] = kv[0].T
    parts = rows // PART
    strips = qh.shape[2] // STRIP

    def mixed_copy(half, turn, part):
        shard = p.shard(turn)
        return copy_to(
            mixed.at[half, :, span(shard * parts + part, PART)],
            attended.at[half, p.seq, :, span(part, PART)],
            (xsend, xrecv),
            13 + (3 * half + turn - 1) * parts + part,
            p.over_seq(turn),
        )

    def attend(half, seen, strip):
        here = span(strip, STRIP)
        queries = qh[half, :, here] * jnp.bfloat16(size ** (-0.5))
        queries = jnp.concatenate([queries, jnp.zeros_like(queries)], axis=0)
        whole = seen - SLOTS
        scores = hide_future(dot(kv[half, whole:seen, :], queries), whole, strip * STRIP)
        if whole:
            scores = jnp.concatenate([dot(kv[half, 0:whole, :], queries), scores], axis=0)
        highest = jnp.max(scores, axis=0, keepdims=True)
        exponent = jnp.exp(scores - highest)
        summed = jnp.sum(exponent, axis=0, keepdims=True)
        out = dot(kvt[half, size:lanes, 0:seen], exponent.astype(LOW)) * (1.0 / summed)
        lse[half, strip] = highest + jnp.log(summed)
        mixed[half, :, here] = out.astype(LOW)

    @pl.loop(0, 2 * strips)
    def _(turn_number):
        half, it = lax.div(turn_number, strips), lax.rem(turn_number, strips)
        for number, turn in ((1, 1), (3, 2), (4, 3)):

            @pl.when(it == number)
            def _():
                query_copy(half, turn).wait()

        @pl.when(turn_number == 1)
        def _():
            for piece in next_up:
                piece.step(2)

        @pl.when(turn_number == 2)
        def _():
            for piece in next_up:
                piece.step(3)
            for piece in next_up:
                piece.step(4)
            project(1)
            send_queries(1)

        @pl.when(turn_number == strips)
        def _():
            for turn in (1, 2, 3):
                memory_copy(1, turn).wait()
            kvt[1] = kv[1].T

        strip = p.strip(it)
        for group in range(strips):

            @pl.when(strip == group)
            def _():
                attend(half, SLOTS * (group + 1), strip)

        for k in range(2):
            granule = 2 * strip + k
            shard, part = lax.div(granule, parts), lax.rem(granule, parts)
            turn = p.turn_to(shard)

            @pl.when(turn > 0)
            def _():
                mixed_copy(half, turn, part).start()

            @pl.when(turn == 0)
            def _():
                attended[half, p.seq, :, span(part, PART)] = mixed[half, :, span(granule, PART)]

        @pl.when(turn_number == 9)
        def _():
            later[1].step(3)

    for piece in later[:1] + later[2:]:
        piece.step(3)
    for piece in later:
        piece.step(4)
    for half in range(2):
        for turn in (1, 2, 3):
            for part in range(parts):
                mixed_copy(half, turn, part).wait()


def front(tok, params):
    wq, wm, wo, wu, wd, vec = params
    groups = lax.axis_size("grp")
    depth = groups // 2
    rows, width = tok.shape
    own, slots, size = wq.shape[0], rows // 3, width // H
    lanes = 2 * size
    tile_lanes = vec.shape[1] * groups
    tile = lax.dynamic_update_slice(
        jnp.zeros((ROWS, tile_lanes), WIDE), vec, (0, vec.shape[1] * lax.axis_index("grp"))
    )
    whole = (2, 2, depth, 2)
    sems = pltpu.SemaphoreType.DMA((12 * gather_slots(depth),))
    parts = rows // PART
    swaps = pltpu.SemaphoreType.DMA((13 + 6 * parts,))
    anywhere = pl.BlockSpec(memory_space=pl.ANY)
    vmem = pl.BlockSpec(memory_space=pltpu.VMEM)
    return pl.pallas_call(
        functools.partial(front_kernel, depth),
        out_shape=(
            shaped(EARLY, *whole, own, width),
            shaped(LATE, *whole, own, width),
            shaped(*whole, *wd.shape),
            shaped(ROWS, 4 * tile_lanes, kind=WIDE),
            shaped(width // 128, 8, 128, kind=WIDE),
            shaped(2, size, 4 * rows),
            shaped(2, 4 * slots, lanes),
            shaped(2, size, 4 * rows),
            shaped(2, 4 * rows // STRIP, 1, STRIP, kind=WIDE),
            shaped(2, 4, size, rows),
        ),
        in_specs=in_vmem(7),
        out_specs=[vmem, anywhere, anywhere] + [vmem] * 7,
        scratch_shapes=[
            pltpu.VMEM((*whole, ROWS, tile_lanes), LOW),
            pltpu.VMEM((width // 128, rows + 8, 128), WIDE),
            pltpu.VMEM((rows, width), LOW),
            pltpu.VMEM((2, 4, size, rows), LOW),
            pltpu.VMEM((2, slots, width), LOW),
            pltpu.VMEM((2, lanes, 4 * slots), LOW),
            pltpu.VMEM((LATE, own, width), LOW),
            pltpu.VMEM(wd.shape, LOW),
            sems,
            sems,
            swaps,
            swaps,
            pltpu.SemaphoreType.DMA((4,)),
        ],
        compiler_params=pltpu.CompilerParams(
            collective_id=0, has_side_effects=True, vmem_limit_bytes=58 * MEGA
        ),
    )(tok, wq, wm, wo, wu, wd, tile)


def middle_kernel(depth, tok, cot, att, late, down, vec, length, *refs):
    out, dres, doh, g_stack, g_down, g_vec = refs[:6]
    zs, dus, cs, es, ys, dos, xsend, xrecv = refs[6:]
    p = Place(depth)
    p.greet(beyond=False)
    rows, width = tok.shape
    hidden = zs.shape[1]
    gain, shift, bias = vec[2:3, :], vec[3:4, :], vec[4:5, :]
    inner = 0.7978845608028654
    cubic = inner * 0.044715
    g_vec[...] = jnp.zeros_like(g_vec)

    parts = rows // PART

    def do_copy(number, turn):
        return copy_to(
            dos.at[:, p.shard(turn), :, span(number, PART)],
            doh.at[:, :, span(p.seq * parts + number, PART)],
            (xsend, xrecv),
            3 * number + turn - 1,
            p.over_seq(turn),
        )

    @pl.loop(0, parts)
    def _(number):
        at = pl.multiple_of(number * PART, PART)
        here = pl.ds(at, PART)
        attended = att[:, :, :, here].reshape(width, PART).T
        residual = tok[here, :].astype(WIDE) + dot(attended, late[0])
        unit, factor = unit_rows_of(residual)
        normed = (unit * gain + shift).astype(LOW)
        cs[here, :] = normed
        place = lax.broadcasted_iota(jnp.int32, (PART, 1), 0) + (p.seq * rows + at)
        live = (place < length[0, 0]).astype(WIDE)
        upstream = cot[here, :].astype(WIDE) * live
        upstream_low = upstream.astype(LOW)
        es[here, :] = upstream_low
        result = residual + bias
        back = jnp.zeros((PART, width), WIDE)
        for part in range(hidden // width):
            here_hidden = pl.ds(part * width, width)
            u = dot(normed, late[1 + part]) + vec[5 + part : 6 + part, :]
            square = u * u
            half = 0.5 + 0.5 * jnp.tanh(u * (inner + cubic * square))
            active = u * half
            slope = half + active * (1.0 - half) * (2.0 * inner + 6.0 * cubic * square)
            active_low = active.astype(LOW)
            zs[here, here_hidden] = active_low
            result += dot(active_low, down[here_hidden, :])
            pulled = lax.dot_general(upstream_low, down[here_hidden, :], NT, preferred_element_type=WIDE)
            grad = (pulled * slope).astype(LOW)
            dus[here, here_hidden] = grad
            g_vec[5 + part : 6 + part, :] += jnp.sum(grad.astype(WIDE), axis=0, keepdims=True)
            back += lax.dot_general(grad, late[1 + part], NT, preferred_element_type=WIDE)
        out[here, :] = result.astype(LOW)
        scaled = back * gain
        total = upstream + factor * (
            scaled
            - jnp.mean(scaled, axis=-1, keepdims=True)
            - unit * jnp.mean(scaled * unit, axis=-1, keepdims=True)
        )
        dres[here, :] = total
        branch = total.astype(LOW)
        ys[here, :] = branch
        turned = lax.dot_general(late[0], branch, NT, preferred_element_type=WIDE)
        dos[:, :, :, here] = turned.astype(LOW).reshape(dos.shape[:3] + (PART,))
        for turn in (3, 1, 2):
            do_copy(number, turn).start()
        doh[:, :, span(p.seq * parts + number, PART)] = dos[:, p.seq, :, here]
        g_vec[2:3, :] += jnp.sum(back * unit, axis=0, keepdims=True)
        g_vec[3:4, :] += jnp.sum(back, axis=0, keepdims=True)
        g_vec[4:5, :] += jnp.sum(upstream, axis=0, keepdims=True)

    g_stack[0] = dot(att[...].reshape(width, rows), ys[...]).astype(LOW)
    for part in range(hidden // width):
        piece = pl.ds(part * width, width)
        g_stack[1 + part] = over_rows(cs[...], dus[:, piece]).astype(LOW)
        g_down[piece, :] = over_rows(zs[:, piece], es[...]).astype(LOW)
    for number in range(parts):
        for turn in (1, 2, 3):
            do_copy(number, turn).wait()


def middle(tok, cot, att, late, down, vec, length):
    rows, width = tok.shape
    hidden = down.shape[0]
    sems = pltpu.SemaphoreType.DMA((3 * (rows // PART),))
    return pl.pallas_call(
        functools.partial(middle_kernel, lax.axis_size("grp") // 2),
        out_shape=(
            shaped(rows, width),
            shaped(rows, width, kind=WIDE),
            shaped(2, width // H, 4 * rows),
            shaped(LATE, width, width),
            shaped(hidden, width),
            shaped(*vec.shape, kind=WIDE),
        ),
        in_specs=in_vmem(6) + [pl.BlockSpec(memory_space=pltpu.SMEM)],
        out_specs=in_vmem(6),
        scratch_shapes=[
            pltpu.VMEM((rows, hidden), LOW),
            pltpu.VMEM((rows, hidden), LOW),
            pltpu.VMEM((rows, width), LOW),
            pltpu.VMEM((rows, width), LOW),
            pltpu.VMEM((rows, width), LOW),
            pltpu.VMEM(att.shape, LOW),
            sems,
            sems,
        ],
        compiler_params=pltpu.CompilerParams(
            collective_id=1, has_side_effects=True, vmem_limit_bytes=58 * MEGA
        ),
    )(tok, cot, att, late, down, vec, length)


def back_kernel(depth, *refs):
    qh, kv, mixed, lse, doh, tok, dres, early, vec, edge, g_late, g_down, g_vec = refs[:13]
    grad, out_early, out_late, out_down, out_vec = refs[13:18]
    scatter, refs = refs[18:54], refs[54:]
    g_early, dkv, kvt, dqs, dq, dms, dm, wide_a, low_a, wide_da, da, after, give, get = refs[:14]
    rsend, rrecv, xsend, xrecv = refs[14:]
    p = Place(depth)
    rows, width = tok.shape
    slots = rows // 3
    size = qh.shape[1]
    lanes = 2 * size
    scale = size ** (-0.5)
    parts = rows // PART
    strips = qh.shape[2] // STRIP
    step = scatter_slots(depth)
    p.greet()

    def out_to(ref, first, count):
        def put(value):
            ref[first : first + count] = value

        return put

    half_down = g_down.shape[4] // 2
    todo = [
        (bind(g_late, 0, 3), out_to(out_late, 0, 3)),
        (bind(g_late, 3, 2), out_to(out_late, 3, 2)),
        (bind_rows(g_down, 0, half_down), out_to(out_down, 0, half_down)),
        (bind_rows(g_down, half_down, half_down), out_to(out_down, half_down, half_down)),
        (bind(g_early, 0, 1), out_to(out_early, 0, 1)),
        (bind(g_early, 1, 2), out_to(out_early, 1, 2)),
        (bind(g_early, 3, 1), out_to(out_early, 3, 1)),
        (bind(g_early, 4, 2), out_to(out_early, 4, 2)),
        (bind(g_early, 6, 1), out_to(out_early, 6, 1)),
    ]
    pieces = [
        Scatter(p, view, out, scatter[4 * k : 4 * k + 4], (rsend, rrecv), step * k, SCATTER_ORDERS[k])
        for k, (view, out) in enumerate(todo)
    ]
    soon, query, first, second = pieces[:4], pieces[4:5], pieces[5:7], pieces[7:]
    small = SumAll(p, out_vec, give, get, (rsend, rrecv), step * len(pieces))
    for piece in soon:
        piece.step(0)
    gain, shift = vec[0:1, :], vec[1:2, :]
    block = 128
    wide_a[:, 0:8, :] = edge[...]

    @pl.loop(0, rows // block)
    def _(number):
        at = pl.multiple_of(number * block, block)
        unit, _ = unit_rows_of(tok[pl.ds(at, block), :].astype(WIDE))
        normed = (unit * gain + shift).astype(LOW)
        low_a[pl.ds(at, block), :] = normed
        put_tiles(wide_a, pl.ds(at + 8, block), normed.astype(WIDE))

    for half in range(2):
        kvt[half] = kv[half].T
    dkv[...] = jnp.zeros_like(dkv)

    def dq_copy(half, turn, part):
        return copy_to(
            dqs.at[half, :, span(p.shard(turn) * parts + part, PART)],
            dq.at[half, p.seq, :, span(part, PART)],
            (xsend, xrecv),
            (3 * half + turn - 1) * parts + part,
            p.over_seq(turn),
        )

    def attend(half, seen, strip):
        here = span(strip, STRIP)
        queries = qh[half, :, here] * jnp.bfloat16(scale)
        incoming = doh[half, :, here]
        middle = jnp.sum(incoming.astype(WIDE) * mixed[half, :, here].astype(WIDE), axis=0, keepdims=True)
        blank = jnp.zeros_like(queries)
        queries = jnp.concatenate([queries, blank], axis=0)
        incoming = jnp.concatenate([blank, incoming], axis=0)
        total = lse[half, strip]
        turned = jnp.zeros((size, STRIP), WIDE)
        for start in range(0, seen, 2 * SLOTS):
            stop = min(start + 2 * SLOTS, seen)
            keys = kv[half, start:stop, :]
            scores = dot(keys, queries)
            if stop == seen:
                clear = stop - SLOTS - start
                masked = hide_future(scores[clear:], stop - SLOTS, strip * STRIP)
                scores = jnp.concatenate([scores[:clear], masked], axis=0) if clear else masked
            weights = jnp.exp(scores - total)
            slope = (weights * (dot(keys, incoming) - middle)).astype(LOW)
            dkv[half, start:stop, :] += lax.dot_general(
                slope, queries, NT, preferred_element_type=WIDE
            ) + lax.dot_general(weights.astype(LOW), incoming, NT, preferred_element_type=WIDE)
            turned += dot(kvt[half, 0:size, start:stop], slope)
        dqs[half, :, here] = (turned * scale).astype(LOW)

    def memory_copy(half, turn):
        return copy_to(
            dms.at[half, span(p.shard(turn), slots)],
            dm.at[half, :, span(p.seq, lanes)],
            (xsend, xrecv),
            6 * parts + 3 * half + turn - 1,
            p.over_seq(turn),
        )

    def send_memory(half):
        dms[half] = dkv[half].astype(LOW)
        for turn in (3, 1, 2):
            memory_copy(half, turn).start()
        dm[half, :, span(p.seq, lanes)] = dms[half, span(p.seq, slots), :]

    def put_early(j, value):
        g_early[j] = value.astype(LOW).reshape(g_early.shape[1:])

    def memory_gradient(half, tap):
        window = get_tiles(wide_a, pl.ds(6 + tap, slots, stride=3)).astype(LOW)
        put_early(1 + 3 * half + tap, over_rows(window, dm[half]))

    @pl.loop(0, 2 * strips)
    def _(turn_number):
        half, it = lax.div(turn_number, strips), lax.rem(turn_number, strips)

        @pl.when(turn_number == strips)
        def _():
            send_memory(0)

        @pl.when(turn_number == strips + 2)
        def _():
            for turn in (1, 2, 3):
                memory_copy(0, turn).wait()
            for tap in range(3):
                memory_gradient(0, tap)
            for piece in first:
                piece.step(0)

        strip = p.strip(strips - 1 - it)
        for group in range(strips):

            @pl.when(strip == group)
            def _():
                attend(half, SLOTS * (group + 1), strip)

        for k in range(2):
            granule = 2 * strip + k
            shard, part = lax.div(granule, parts), lax.rem(granule, parts)
            turn = p.turn_to(shard)

            @pl.when(turn > 0)
            def _():
                dq_copy(half, turn, part).start()

            @pl.when(turn == 0)
            def _():
                dq[half, p.seq, :, span(part, PART)] = dqs[half, :, span(granule, PART)]

        for when, steps in (
            (1, [(piece, 1) for piece in soon]),
            (7, [(piece, 2) for piece in soon]),
            (9, [(piece, 1) for piece in first]),
            (10, [(piece, 3) for piece in soon]),
        ):

            @pl.when(turn_number == when)
            def _():
                run(steps)

    send_memory(1)
    for half in range(2):
        for turn in (1, 2, 3):
            for part in range(parts):
                dq_copy(half, turn, part).wait()
    turned = dq[...].reshape(width, rows)
    put_early(0, dot(turned, low_a[...]).T)
    query[0].step(0)
    da[...] = lax.dot_general(turned.T, early[0], NT, preferred_element_type=WIDE)
    query[0].step(1)
    run([(piece, 2) for piece in first])
    for turn in (1, 2, 3):
        memory_copy(1, turn).wait()
    for tap in range(3):
        memory_gradient(1, tap)
        if tap:
            second[tap - 1].step(0)
    wide_da[:, 0:8, :] = jnp.zeros((width // 128, 8, 128), WIDE)
    for tap in range(3):
        pulled = lax.dot_general(dm[0], early[1 + tap], NT, preferred_element_type=WIDE)
        pulled += lax.dot_general(dm[1], early[4 + tap], NT, preferred_element_type=WIDE)
        put_tiles(wide_da, pl.ds(6 + tap, slots, stride=3), pulled)

    def edge_copy():
        return copy_to(
            wide_da.at[:, pl.ds(0, 8)], after, (xsend, xrecv), 6 * parts + 6, {"seq": lax.rem(p.seq + 3, 4)}
        )

    @pl.when(p.seq > 0)
    def _():
        edge_copy().start()

    run([(piece, 1) for piece in second])
    run([(piece, 4) for piece in soon])
    run([(query[0], 2), (first[0], 3), (first[1], 3)])

    @pl.when(p.seq < 3)
    def _():
        edge_copy().wait_recv()

    @pl.when(p.seq > 0)
    def _():
        edge_copy().wait_send()

    @pl.when(p.seq == 3)
    def _():
        after[...] = jnp.zeros_like(after)

    wide_da[:, rows + 6 : rows + 8, :] = after[:, 6:8, :]
    give[0] = g_vec[...]

    @pl.loop(0, rows // block)
    def _(number):
        at = pl.multiple_of(number * block, block)
        here = pl.ds(at, block)
        unit, factor = unit_rows_of(tok[here, :].astype(WIDE))
        upstream = da[here, :] + get_tiles(wide_da, pl.ds(at + 8, block))
        scaled = upstream * gain
        inward = factor * (
            scaled
            - jnp.mean(scaled, axis=-1, keepdims=True)
            - unit * jnp.mean(scaled * unit, axis=-1, keepdims=True)
        )
        grad[here, :] = (dres[here, :] + inward).astype(LOW)
        give[0, 0:1, :] += jnp.sum(upstream * unit, axis=0, keepdims=True)
        give[0, 1:2, :] += jnp.sum(upstream, axis=0, keepdims=True)

    small.step(0)
    run([(piece, 2) for piece in second])
    small.step(1)
    run([(query[0], 3), (second[0], 3), (second[1], 3)])
    run([(first[0], 4), (first[1], 4)])
    small.step(2)
    run([(query[0], 4), (second[0], 4), (second[1], 4)])
    small.step(3)


def back(saved, tok, dres, early, vec, edge, grads):
    qh, kv, mixed, lse, doh = saved
    g_late, g_down, g_vec = grads
    depth = lax.axis_size("grp") // 2
    rows, width = tok.shape
    size, slots = qh.shape[1], rows // 3
    lanes = 2 * size
    whole = (2, 2, depth, 2)
    own_down = g_down.shape[0] // (8 * depth)
    parts = rows // PART
    shapes = [(3, ROWS, width), (2, ROWS, width)] + [(own_down // 2, width)] * 2
    shapes += [(1, ROWS, width)] + [(2, ROWS, width), (1, ROWS, width)] * 2
    ring = pltpu.SemaphoreType.DMA((9 * scatter_slots(depth) + depth + 3,))
    swaps = pltpu.SemaphoreType.DMA((6 * parts + 7,))
    return pl.pallas_call(
        functools.partial(back_kernel, depth),
        out_shape=(
            shaped(rows, width),
            shaped(EARLY, ROWS, width, kind=WIDE),
            shaped(LATE, ROWS, width, kind=WIDE),
            shaped(own_down, width, kind=WIDE),
            shaped(*vec.shape, kind=WIDE),
        ),
        in_specs=in_vmem(13),
        out_specs=in_vmem(5),
        scratch_shapes=[
            buf for order, shape in zip(SCATTER_ORDERS, shapes) for buf in scatter_scratch(depth, order, shape)
        ]
        + [
            pltpu.VMEM((EARLY, *whole, ROWS, width), LOW),
            pltpu.VMEM(kv.shape, WIDE),
            pltpu.VMEM((2, lanes, 4 * slots), LOW),
            pltpu.VMEM(qh.shape, LOW),
            pltpu.VMEM((2, 4, size, rows), LOW),
            pltpu.VMEM(kv.shape, LOW),
            pltpu.VMEM((2, slots, width), LOW),
            pltpu.VMEM((width // 128, rows + 8, 128), WIDE),
            pltpu.VMEM((rows, width), LOW),
            pltpu.VMEM((width // 128, rows + 8, 128), WIDE),
            pltpu.VMEM((rows, width), WIDE),
            pltpu.VMEM((width // 128, 8, 128), WIDE),
            pltpu.VMEM((3,) + vec.shape, WIDE),
            pltpu.VMEM((depth + 3,) + vec.shape, WIDE),
            ring,
            ring,
            swaps,
            swaps,
        ],
        compiler_params=pltpu.CompilerParams(
            collective_id=2, has_side_effects=True, vmem_limit_bytes=62 * MEGA
        ),
    )(
        qh,
        kv,
        mixed,
        lse,
        doh,
        tok,
        dres,
        early,
        vec,
        edge,
        g_late.reshape(LATE, *whole, ROWS, width),
        g_down.reshape(*whole, own_down, width),
        g_vec,
    )


def update_kernel(*refs):
    weights, firsts, seconds = refs[0:6], refs[6:12], refs[12:18]
    early, late, down, vec = refs[18:22]
    outs = refs[22:]
    width = early.shape[-1]

    def put(which, at, gradient):
        results = adamw(
            weights[which][at], gradient, firsts[which][at], seconds[which][at], LEARNING_RATES[which]
        )
        for group, value in enumerate(results):
            outs[6 * group + which][at] = value

    every = slice(None)
    put(0, (every, every), early[0])
    size = width // H
    for tap in range(3):
        for kind in range(2):
            columns = [
                early[1 + 3 * half + tap, :, (2 * s + kind) * size : (2 * s + kind + 1) * size]
                for half in range(2)
                for s in range(4)
            ]
            put(1, (tap, every, slice(kind * width, (kind + 1) * width)), jnp.concatenate(columns, axis=1))
    put(2, (every, every), late[0])
    for part in range(4):
        put(3, (every, slice(part * width, (part + 1) * width)), late[1 + part])
    put(4, (every, every), down[...])
    put(5, (every, every), vec[...])


def update(params, firsts, seconds, grads):
    outs = [jax.ShapeDtypeStruct(member.shape, WIDE) for member in params] * 3
    outs += [jax.ShapeDtypeStruct(member.shape, LOW) for member in params]
    return pl.pallas_call(
        update_kernel,
        out_shape=tuple(outs),
        in_specs=in_vmem(22),
        out_specs=in_vmem(24),
    )(*params, *firsts, *seconds, *grads)


def fused(tokens, cotangent, lengths, *state):
    params, firsts, seconds = state[0:6], state[6:12], state[12:18]
    width = tokens.shape[2]
    tok, cot = tokens[0], cotangent[0]
    early, late, down, vec, edge, qh, kv, mixed, lse, attended = front(tok, params)
    early = early.reshape(EARLY, width, width)
    late = late.reshape(LATE, width, width)
    down = down.reshape(-1, width)
    out, dres, doh, g_late, g_down, g_vec = middle(
        tok, cot, attended, late, down, vec, lengths.reshape(1, 1)
    )
    grad, r_early, r_late, r_down, r_vec = back(
        (qh, kv, mixed, lse, doh), tok, dres, early, vec, edge, (g_late, g_down, g_vec)
    )
    share = params[5].shape[1]
    index = lax.axis_index("seq") * lax.axis_size("grp") + lax.axis_index("grp")
    own_vec = lax.dynamic_slice(r_vec, (0, index * share), (params[5].shape[0], share))
    new = update(params, firsts, seconds, (r_early, r_late, r_down, own_vec))
    return (out[None], grad[None], *new)


def body(*arguments):
    tokens, shard = arguments[0], arguments[3]
    whole_tiles = shard.shape[0] % ROWS == 0 and tokens.shape[1] % PART == 0
    four = lax.axis_size("seq") == 4 and lax.axis_size("grp") % 2 == 0
    return (fused if whole_tiles and four else plain)(*arguments)


def solution(mesh):
    in_specs = (
        P("grp", "seq", None),
        P("grp", "seq", None),
        P("grp"),
        P(("seq", "grp"), None),
        P(None, ("seq", "grp"), None),
        P(("seq", "grp"), None),
        P(("seq", "grp"), None),
        P(("seq", "grp"), None),
        P(None, ("seq", "grp")),
        P(("seq", "grp"), None),
        P(None, ("seq", "grp"), None),
        P(("seq", "grp"), None),
        P(("seq", "grp"), None),
        P(("seq", "grp"), None),
        P(None, ("seq", "grp")),
        P(("seq", "grp"), None),
        P(None, ("seq", "grp"), None),
        P(("seq", "grp"), None),
        P(("seq", "grp"), None),
        P(("seq", "grp"), None),
        P(None, ("seq", "grp")),
    )
    out_specs = (
        P("grp", "seq", None),
        P("grp", "seq", None),
        P(("seq", "grp"), None),
        P(None, ("seq", "grp"), None),
        P(("seq", "grp"), None),
        P(("seq", "grp"), None),
        P(("seq", "grp"), None),
        P(None, ("seq", "grp")),
        P(("seq", "grp"), None),
        P(None, ("seq", "grp"), None),
        P(("seq", "grp"), None),
        P(("seq", "grp"), None),
        P(("seq", "grp"), None),
        P(None, ("seq", "grp")),
        P(("seq", "grp"), None),
        P(None, ("seq", "grp"), None),
        P(("seq", "grp"), None),
        P(("seq", "grp"), None),
        P(("seq", "grp"), None),
        P(None, ("seq", "grp")),
        P(("seq", "grp"), None),
        P(None, ("seq", "grp"), None),
        P(("seq", "grp"), None),
        P(("seq", "grp"), None),
        P(("seq", "grp"), None),
        P(None, ("seq", "grp")),
    )
    return jax.shard_map(body, mesh=mesh, in_specs=in_specs, out_specs=out_specs, check_vma=False)
```

```python
import functools

import jax
import jax.numpy as jnp
from jax import lax
from jax.experimental import pallas as pl
from jax.experimental.pallas import tpu as pltpu
from jax.sharding import PartitionSpec as P

H = 8
STEP = 10


NORM_EPSILON = 1e-05
BETA_FIRST = 0.9
BETA_SECOND = 0.95
ADAM_EPSILON = 1e-08
WEIGHT_DECAY = 0.1
LEARNING_RATES = (0.05, 0.04, 0.3, 0.05, 0.03, 0.5)
MASKED_SCORE = -1e30
NT = (((1,), (1,)), ((), ()))


def from_behind(x, axis, by):
    peers = lax.axis_size(axis)
    pairs = [(i, i + by) for i in range(peers) if 0 <= i + by < peers]
    return lax.ppermute(x, axis, pairs)


def matmul(left, right):
    return jnp.dot(left, right, preferred_element_type=jnp.float32)


def over_rows(left, right):
    return lax.dot_general(
        left, right, (((0,), (0,)), ((), ())), preferred_element_type=jnp.float32
    )


def against(left, right):
    return lax.dot_general(
        left, right, (((1,), (1,)), ((), ())), preferred_element_type=jnp.float32
    )


def norm_forward(values, gain, shift):
    centred = values - jnp.mean(values, axis=-1, keepdims=True)
    factor = lax.rsqrt(jnp.mean(centred * centred, axis=-1, keepdims=True) + NORM_EPSILON)
    unit_rows = centred * factor
    return (unit_rows * gain + shift, unit_rows, factor)


def norm_backward(upstream, unit_rows, factor, gain):
    scaled = upstream * gain
    inward = factor * (
        scaled
        - jnp.mean(scaled, axis=-1, keepdims=True)
        - unit_rows * jnp.mean(scaled * unit_rows, axis=-1, keepdims=True)
    )
    return (inward, jnp.sum(upstream * unit_rows, axis=0), jnp.sum(upstream, axis=0))


def masked_scores(query_tile_rows, key_row_block, positions):
    slot_starts = 3 * jnp.arange(key_row_block.shape[0], dtype=jnp.int32)
    score_matrix = jnp.einsum(
        "azv,lzv->zal", query_tile_rows, key_row_block, preferred_element_type=jnp.float32
    ) * query_tile_rows.shape[2] ** (-0.5)
    visible = slot_starts[None, :] <= positions[:, None]
    return jnp.where(visible[None], score_matrix, MASKED_SCORE)


def attend_forward(queries, key_row_block, value_row_block, anchor, block_rows):
    block_count = queries.shape[0] // block_rows
    offsets = block_rows * jnp.arange(block_count, dtype=jnp.int32)

    def attend_block(inputs):
        query_tile_rows, offset_rows = inputs
        score_matrix = masked_scores(
            query_tile_rows,
            key_row_block,
            anchor + offset_rows + jnp.arange(block_rows, dtype=jnp.int32),
        )
        highest = jnp.max(score_matrix, axis=-1, keepdims=True)
        exponent = jnp.exp(score_matrix - highest)
        summed = jnp.sum(exponent, axis=-1, keepdims=True)
        reduced_weights = (exponent / summed).astype(jnp.bfloat16)
        mixed = jnp.einsum(
            "yup,pyb->uyb", reduced_weights, value_row_block, preferred_element_type=jnp.float32
        )
        return (mixed, (highest + jnp.log(summed))[..., 0])

    blocks_in = queries.reshape(block_count, block_rows, queries.shape[1], queries.shape[2])
    mixed, logsum = lax.map(attend_block, (blocks_in, offsets))
    return (mixed.reshape(queries.shape), logsum)


def attend_backward(queries, key_row_block, value_row_block, upstream, logsum, anchor, block_rows):
    block_count = queries.shape[0] // block_rows
    offsets = block_rows * jnp.arange(block_count, dtype=jnp.int32)
    scale_factor = queries.shape[2] ** (-0.5)

    def attend_back(carry, inputs):
        grad_keys, grad_values = carry
        query_tile_rows, incoming_gradient_rows, logsum_block, offset_rows = inputs
        score_matrix = masked_scores(
            query_tile_rows,
            key_row_block,
            anchor + offset_rows + jnp.arange(block_rows, dtype=jnp.int32),
        )
        weights_soft = jnp.exp(score_matrix - logsum_block[..., None])
        grad_weights = jnp.einsum(
            "azv,lzv->zal",
            incoming_gradient_rows,
            value_row_block,
            preferred_element_type=jnp.float32,
        )
        centre = jnp.sum(weights_soft * grad_weights, axis=-1, keepdims=True)
        score_gradient = (weights_soft * (grad_weights - centre)).astype(jnp.bfloat16)
        grad_query = (
            jnp.einsum(
                "yup,pyb->uyb", score_gradient, key_row_block, preferred_element_type=jnp.float32
            )
            * scale_factor
        )
        grad_keys = (
            grad_keys
            + jnp.einsum(
                "xof,oxa->fxa", score_gradient, query_tile_rows, preferred_element_type=jnp.float32
            )
            * scale_factor
        )
        grad_values = grad_values + jnp.einsum(
            "xof,oxa->fxa",
            weights_soft.astype(jnp.bfloat16),
            incoming_gradient_rows,
            preferred_element_type=jnp.float32,
        )
        return ((grad_keys, grad_values), grad_query)

    shape_blocks = (block_count, block_rows, queries.shape[1], queries.shape[2])
    zeros_init = jnp.zeros(key_row_block.shape, jnp.float32)
    (grad_keys, grad_values), grad_query = lax.scan(
        attend_back,
        (zeros_init, zeros_init),
        (queries.reshape(shape_blocks), upstream.reshape(shape_blocks), logsum, offsets),
    )
    return (grad_query.reshape(queries.shape), grad_keys, grad_values)


def adamw(weight, gradient, moment, square, step_rate):
    moment_new = BETA_FIRST * moment + (1.0 - BETA_FIRST) * gradient
    square_new = BETA_SECOND * square + (1.0 - BETA_SECOND) * gradient * gradient
    fixed_first = 1.0 - BETA_FIRST**STEP
    fixed_second = 1.0 - BETA_SECOND**STEP
    update = (
        moment_new / fixed_first / (jnp.sqrt(square_new / fixed_second) + ADAM_EPSILON)
        + WEIGHT_DECAY * weight
    )
    master = weight - step_rate * update
    return (moment_new, square_new, master, master.astype(jnp.bfloat16))


def plain(
    tokens,
    cotangent,
    lengths,
    weight_query,
    weight_memory,
    weight_out,
    weight_up,
    weight_down,
    vectors,
    first_query,
    first_memory,
    first_out,
    first_up,
    first_down,
    first_vectors,
    second_query,
    second_memory,
    second_out,
    second_up,
    second_down,
    second_vectors,
):
    gathered = (
        lax.all_gather(weight_query.astype(jnp.bfloat16), ("seq", "grp"), axis=0, tiled=True),
        lax.all_gather(weight_memory.astype(jnp.bfloat16), ("seq", "grp"), axis=1, tiled=True),
        lax.all_gather(weight_out.astype(jnp.bfloat16), ("seq", "grp"), axis=0, tiled=True),
        lax.all_gather(weight_up.astype(jnp.bfloat16), ("seq", "grp"), axis=0, tiled=True),
        lax.all_gather(weight_down.astype(jnp.bfloat16), ("seq", "grp"), axis=0, tiled=True),
        lax.all_gather(vectors.astype(jnp.bfloat16), ("seq", "grp"), axis=1, tiled=True),
    )
    query_w, memory_w, out_w, up_w, down_w, vector_low = gathered
    vector_rows = vector_low.astype(jnp.float32)
    model_width = query_w.shape[0]
    hidden_units = up_w.shape[1]
    head_size = model_width // H
    seq_count = lax.axis_size("seq")
    seq_index = lax.axis_index("seq")
    local_rows = tokens.shape[1]
    local_slots = local_rows // 3
    inputs = tokens[0].astype(jnp.float32)
    normed, unit_one, factor_one = norm_forward(inputs, vector_rows[0], vector_rows[1])
    normed_low = normed.astype(jnp.bfloat16)
    queries = matmul(normed_low, query_w).astype(jnp.bfloat16)
    borrowed = from_behind(normed_low[local_rows - 2 :], "seq", 1)
    extended = jnp.concatenate([borrowed, normed_low], axis=0)
    windows = extended[:local_rows].reshape(local_slots, 3 * model_width)
    memory_flat = memory_w.reshape(3 * model_width, 2 * model_width)
    memory = matmul(windows, memory_flat).astype(jnp.bfloat16)
    share_width = model_width // seq_count
    local_heads = H // seq_count
    head_queries, head_memory = (
        lax.all_to_all(
            queries.reshape(local_rows, 1, seq_count, share_width),
            "seq",
            split_axis=2,
            concat_axis=0,
            tiled=True,
        ),
        lax.all_to_all(
            memory.reshape(local_slots, 2, seq_count, share_width),
            "seq",
            split_axis=2,
            concat_axis=0,
            tiled=True,
        ),
    )
    total_rows = head_queries.shape[0]
    total_slots = head_memory.shape[0]
    query_heads = head_queries.reshape(total_rows, local_heads, head_size)
    key_heads = head_memory[:, 0].reshape(total_slots, local_heads, head_size)
    value_heads = head_memory[:, 1].reshape(total_slots, local_heads, head_size)
    block_rows = min(512, total_rows)
    mixed, logsum = attend_forward(query_heads, key_heads, value_heads, 0, block_rows)
    mixed_low = mixed.astype(jnp.bfloat16).reshape(total_rows, 1, share_width)
    attended = lax.all_to_all(mixed_low, "seq", split_axis=0, concat_axis=1, tiled=True).reshape(
        local_rows, model_width
    )
    residual = inputs + matmul(attended, out_w)
    normed_two, unit_two, factor_two = norm_forward(residual, vector_rows[2], vector_rows[3])
    normed_two_low = normed_two.astype(jnp.bfloat16)
    pre_act = matmul(normed_two_low, up_w) + vector_rows[5:].reshape(hidden_units)
    activated, gelu_pull = jax.vjp(jax.nn.gelu, pre_act)
    activated_low = activated.astype(jnp.bfloat16)
    result = residual + matmul(activated_low, down_w) + vector_rows[4]
    positions = seq_index * local_rows + jnp.arange(local_rows, dtype=jnp.int32)
    live_mask = (positions < lengths[0]).astype(jnp.float32)
    grad_out = cotangent[0].astype(jnp.float32) * live_mask[:, None]
    grad_out_low = grad_out.astype(jnp.bfloat16)
    grad_down = over_rows(activated_low, grad_out_low)
    grad_activated = against(grad_out_low, down_w)
    grad_pre_low = gelu_pull(grad_activated)[0].astype(jnp.bfloat16)
    grad_up = over_rows(normed_two_low, grad_pre_low)
    grad_up_bias = jnp.sum(grad_pre_low.astype(jnp.float32), axis=0)
    grad_normed_two = against(grad_pre_low, up_w)
    grad_norm_two, grad_gain_two, grad_shift_two = norm_backward(
        grad_normed_two, unit_two, factor_two, vector_rows[2]
    )
    grad_residual = grad_out + grad_norm_two
    grad_branch_low = grad_residual.astype(jnp.bfloat16)
    grad_outw = over_rows(attended, grad_branch_low)
    grad_attended_low = against(grad_branch_low, out_w).astype(jnp.bfloat16)
    grad_heads = lax.all_to_all(
        grad_attended_low.reshape(local_rows, 1, seq_count, share_width),
        "seq",
        split_axis=2,
        concat_axis=0,
        tiled=True,
    ).reshape(total_rows, local_heads, head_size)
    grad_q, grad_k, grad_v = attend_backward(
        query_heads, key_heads, value_heads, grad_heads, logsum, 0, block_rows
    )
    packed = (
        jnp.stack([grad_k, grad_v], axis=1)
        .astype(jnp.bfloat16)
        .reshape(total_slots, 2, 1, share_width)
    )
    token_queries, token_memory = (
        lax.all_to_all(
            grad_q.astype(jnp.bfloat16).reshape(total_rows, 1, 1, share_width),
            "seq",
            split_axis=0,
            concat_axis=2,
            tiled=True,
        ),
        lax.all_to_all(packed, "seq", split_axis=0, concat_axis=2, tiled=True),
    )
    grad_queries_low = token_queries.reshape(local_rows, model_width)
    grad_memory_low = token_memory.reshape(local_slots, 2 * model_width)
    grad_queryw = over_rows(normed_low, grad_queries_low)
    grad_normed = against(grad_queries_low, query_w)
    grad_memoryw = over_rows(windows, grad_memory_low).reshape(3, model_width, 2 * model_width)
    grad_windows = against(grad_memory_low, memory_flat).reshape(local_rows, model_width)
    returned = from_behind(grad_windows[:2], "seq", -1)
    grad_normed = grad_normed + jnp.concatenate([grad_windows[2:], returned], axis=0)
    grad_norm_one, grad_gain_one, grad_shift_one = norm_backward(
        grad_normed, unit_one, factor_one, vector_rows[0]
    )
    grad_inputs = (grad_residual + grad_norm_one).astype(jnp.bfloat16)
    grad_vector_rows = jnp.concatenate(
        [
            jnp.stack(
                [
                    grad_gain_one,
                    grad_shift_one,
                    grad_gain_two,
                    grad_shift_two,
                    jnp.sum(grad_out, axis=0),
                ]
            ),
            grad_up_bias.reshape(4, model_width),
        ],
        axis=0,
    )
    reduced = (
        lax.psum_scatter(grad_queryw, ("seq", "grp"), scatter_dimension=0, tiled=True),
        lax.psum_scatter(grad_memoryw, ("seq", "grp"), scatter_dimension=1, tiled=True),
        lax.psum_scatter(grad_outw, ("seq", "grp"), scatter_dimension=0, tiled=True),
        lax.psum_scatter(grad_up, ("seq", "grp"), scatter_dimension=0, tiled=True),
        lax.psum_scatter(grad_down, ("seq", "grp"), scatter_dimension=0, tiled=True),
        lax.psum_scatter(grad_vector_rows, ("seq", "grp"), scatter_dimension=1, tiled=True),
    )
    new_query = adamw(weight_query, reduced[0], first_query, second_query, LEARNING_RATES[0])
    new_memory = adamw(weight_memory, reduced[1], first_memory, second_memory, LEARNING_RATES[1])
    new_out = adamw(weight_out, reduced[2], first_out, second_out, LEARNING_RATES[2])
    new_up = adamw(weight_up, reduced[3], first_up, second_up, LEARNING_RATES[3])
    new_down = adamw(weight_down, reduced[4], first_down, second_down, LEARNING_RATES[4])
    new_vectors = adamw(vectors, reduced[5], first_vectors, second_vectors, LEARNING_RATES[5])
    return (
        result.astype(jnp.bfloat16)[None],
        grad_inputs[None],
        new_query[0],
        new_memory[0],
        new_out[0],
        new_up[0],
        new_down[0],
        new_vectors[0],
        new_query[1],
        new_memory[1],
        new_out[1],
        new_up[1],
        new_down[1],
        new_vectors[1],
        new_query[2],
        new_memory[2],
        new_out[2],
        new_up[2],
        new_down[2],
        new_vectors[2],
        new_query[3],
        new_memory[3],
        new_out[3],
        new_up[3],
        new_down[3],
        new_vectors[3],
    )


MESH = pl.DeviceIdType.MESH
LOW, WIDE = jnp.bfloat16, jnp.float32
ROWS = 16
PART = 384
STRIP = 2 * PART
SLOTS = STRIP // 3
EARLY = 7
LATE = 5
MEGA = 1024 * 1024
SCATTER_ORDERS = ("yzx", "xyz", "zxy", "xyz", "yxz", "xyz", "yzx", "yxz", "xzy")


def in_vmem(count):
    return [pl.BlockSpec(memory_space=pltpu.VMEM)] * count


def shaped(*shape, kind=jnp.bfloat16):
    return jax.ShapeDtypeStruct(shape, kind)


def dot(left, right):
    return jnp.dot(left, right, preferred_element_type=jnp.float32)


def differ(bit, other):
    return bit + other - 2 * bit * other


class Place:
    def __init__(self, depth):
        self.seq, self.grp = lax.axis_index("seq"), lax.axis_index("grp")
        self.depth = depth
        self.y, self.x = lax.div(self.seq, 2), lax.rem(self.seq, 2)
        self.z, self.c = lax.div(self.grp, 2), lax.rem(self.grp, 2)
        self.own = {"y": self.y, "x": self.x, "z": self.z}
        self.size = {"y": 2, "x": 2, "z": depth}

    def turn_to(self, shard):
        return 2 * differ(self.y, lax.div(shard, 2)) + differ(self.x, lax.rem(shard, 2))

    def strip(self, it):
        half, pos = differ(lax.div(it, 3), self.y), lax.rem(it, 3)
        return 3 * half + pos + self.x * (2 - 2 * pos)

    def shard(self, turn):
        return 2 * differ(self.y, lax.div(turn, 2)) + differ(self.x, lax.rem(turn, 2))

    def over_seq(self, turn):
        return {"seq": self.shard(turn)}

    def over_core(self):
        return {"grp": 2 * self.z + 1 - self.c}

    def z_of(self, step):
        return lax.rem(self.z + step, self.depth)

    def over_z(self, step):
        return {"grp": 2 * self.z_of(step) + self.c}

    def step_of(self, axis, step):
        return self.z_of(step) if axis == "z" else 1 - self.own[axis]

    def others(self, axis):
        if axis == "z":
            return [self.over_z(step) for step in range(1, self.depth)]
        return [self.over_seq({"x": 1, "y": 2}[axis])]

    def greet(self, beyond=True):
        peers = [self.over_seq(turn) for turn in (1, 2, 3)]
        if beyond:
            peers += [self.over_core()] + [self.over_z(step) for step in range(1, self.depth)]
        barrier = pltpu.get_barrier_semaphore()
        for peer in peers:
            pl.semaphore_signal(barrier, inc=1, device_id=peer, device_id_type=MESH)
        pl.semaphore_wait(barrier, len(peers))


def copy_to(source, target, sems, index, peer):
    send, recv = sems
    return pltpu.make_async_remote_copy(
        src_ref=source,
        dst_ref=target,
        send_sem=send.at[index],
        recv_sem=recv.at[index],
        device_id=peer,
        device_id_type=MESH,
    )


class Gather:
    def __init__(self, place, view, sems, base, order, own=None):
        self.at, self.view, self.sems, self.base, self.order = place, view, sems, base, order
        self.own = own

    def moves(self, stage):
        p = self.at
        done = self.order[:stage]
        where = [pl.ds(0, p.size[axis]) if axis in done else p.own[axis] for axis in "yxz"]
        region = self.view(*where, p.c)
        if stage == 3:
            return [(region, p.depth + 1, p.over_core())]
        base = sum(p.size[axis] - 1 for axis in done)
        return [(region, base + i, peer) for i, peer in enumerate(p.others(self.order[stage]))]

    def copies(self, stage):
        source = self.own if stage == 0 else None
        return [
            copy_to(r if source is None else source, r, self.sems, self.base + slot, peer)
            for r, slot, peer in self.moves(stage)
        ]

    def place_own(self, sem):
        p = self.at
        return pltpu.make_async_copy(self.own, self.view(p.y, p.x, p.z, p.c), sem)

    def step(self, stage):
        if stage:
            for made in self.copies(stage - 1):
                made.wait()
        if stage < 4:
            for made in self.copies(stage):
                made.start()


def gather_slots(depth):
    return depth + 2


def bind(ref, first, count):
    return lambda *i: ref.at[(pl.ds(first, count),) + i]


def bind_rows(ref, first, count):
    return lambda *i: ref.at[i + (pl.ds(first, count),)]


class Scatter:
    def __init__(self, place, view, out, bufs, sems, base, order, far=None):
        self.far = far or view
        self.at, self.view, self.out, self.sems, self.base, self.order = place, view, out, sems, base, order
        self.get_core, self.give, self.get, self.keep = bufs

    def plan(self, number):
        p = self.at
        axis = self.order[number]
        rest = [other for other in "yxz" if other not in self.order[: number + 1]]
        combos = [{}]
        for other in rest:
            combos = [{**c, other: i} for c in combos for i in range(p.size[other])]
        first = 0
        for k in range(number):
            left = 1
            for other in self.order[k + 1 :]:
                left *= p.size[other]
            first += left * (p.size[self.order[k]] - 1)
        return axis, combos, first

    def kept(self, index):
        p = self.at
        linear = 0
        for axis in "yxz":
            if axis != self.order[0]:
                linear = linear * p.size[axis] + index.get(axis, p.own[axis])
        return linear

    def now(self, number, index):
        p = self.at
        if number:
            return self.keep[self.kept(index)]
        where = [index.get(axis, p.own[axis]) for axis in "yxz"]
        lead = (slice(None),) * (len(self.get_core.shape) - 5)
        return self.view(*where, p.c)[...].astype(WIDE) + self.get_core[lead + tuple(where)].astype(WIDE)

    def copies(self, stage):
        p = self.at
        if stage == 0:
            source = self.far(pl.ds(0, 2), pl.ds(0, 2), pl.ds(0, p.depth), 1 - p.c)
            return [copy_to(source, self.get_core, self.sems, self.base, p.over_core())]
        axis, combos, first = self.plan(stage - 1)
        slot = 1 + sum(p.size[other] - 1 for other in self.order[: stage - 1])
        made = []
        for i, peer in enumerate(p.others(axis)):
            here = pl.ds(first + i * len(combos), len(combos))
            made.append(copy_to(self.give.at[here], self.get.at[here], self.sems, self.base + slot + i, peer))
        return made

    def step(self, stage):
        p = self.at
        if stage:
            for made in self.copies(stage - 1):
                made.wait()
        if stage >= 2:
            axis, combos, first = self.plan(stage - 2)
            for k, index in enumerate(combos):
                total = self.keep[self.kept(index)]
                for i in range(p.size[axis] - 1):
                    total = total + self.get[first + i * len(combos) + k].astype(WIDE)
                if stage == 4:
                    self.out(total)
                else:
                    self.keep[self.kept(index)] = total
        if 1 <= stage < 4:
            axis, combos, first = self.plan(stage - 1)
            for i in range(p.size[axis] - 1):
                for k, index in enumerate(combos):
                    target = {**index, axis: p.step_of(axis, i + 1)}
                    self.give[first + i * len(combos) + k] = self.now(stage - 1, target).astype(LOW)
        if stage < 4:
            for made in self.copies(stage):
                made.start()
        if stage == 1:
            axis, combos, first = self.plan(0)
            for index in combos:
                self.keep[self.kept(index)] = self.now(0, index)


def scatter_slots(depth):
    return depth + 2


def scatter_scratch(depth, order, shape):
    kept = 4 if order[0] == "z" else 2 * depth
    return [
        pltpu.VMEM(shape[:-2] + (2, 2, depth) + shape[-2:], LOW),
        pltpu.VMEM((4 * depth - 1,) + shape, LOW),
        pltpu.VMEM((4 * depth - 1,) + shape, LOW),
        pltpu.VMEM((kept,) + shape, WIDE),
    ]


class SumAll:
    def __init__(self, place, out, give, get, sems, base):
        self.at, self.out, self.give, self.get, self.sems, self.base = place, out, give, get, sems, base

    def copies(self, stage):
        p = self.at
        if stage == 0:
            moves = [(0, p.over_core())]
        elif stage == 1:
            moves = [(turn, p.over_seq(turn)) for turn in (1, 2, 3)]
        else:
            moves = [(3 + step, p.over_z(step)) for step in range(1, p.depth)]
        return [
            copy_to(self.give.at[stage], self.get.at[slot], self.sems, self.base + slot, peer)
            for slot, peer in moves
        ]

    def step(self, stage):
        if stage:
            for made in self.copies(stage - 1):
                made.wait()
            total = self.give[stage - 1]
            for slot in ((), (0,), (1, 2, 3), range(4, 3 + self.at.depth))[stage]:
                total = total + self.get[slot]
            if stage == 3:
                self.out[...] = total
                return
            self.give[stage] = total
        for made in self.copies(stage):
            made.start()


def run(steps):
    for piece, stage in steps:
        piece.step(stage)


def skewed(pieces, stages):
    stages = list(stages)
    return [
        (piece, stages[slot - k])
        for slot in range(len(pieces) + len(stages) - 1)
        for k, piece in enumerate(pieces)
        if 0 <= slot - k < len(stages)
    ]


def unit_rows_of(values):
    centred = values - jnp.mean(values, axis=-1, keepdims=True)
    factor = lax.rsqrt(jnp.mean(centred * centred, axis=-1, keepdims=True) + NORM_EPSILON)
    return centred * factor, factor


def put_tiles(ref, here, value):
    for k in range(ref.shape[0]):
        ref[k, here, :] = value[:, 128 * k : 128 * (k + 1)]


def get_tiles(ref, here):
    return jnp.concatenate([ref[k, here, :] for k in range(ref.shape[0])], axis=1)


def hide_future(scores, first_slot, first_row):
    slot = lax.broadcasted_iota(jnp.int32, scores.shape, 0) + first_slot
    row = lax.broadcasted_iota(jnp.int32, scores.shape, 1) + first_row
    return jnp.where(3 * slot <= row, scores, MASKED_SCORE)


def span(number, size):
    return pl.ds(pl.multiple_of(number * size, size), size)


def front_kernel(depth, tok, wq, wm, wo, wu, wd, vec, *refs):
    early_out, late, down, vectors, edge, qh_out, kv_out, mixed_out, lse, attended = refs[:10]
    tiles, wide_a, low_a, qs, ms, kvt, own_late, own_down, tile, early, qh, kv, mixed = refs[10:23]
    gsend, grecv, xsend, xrecv, lsem, osem = refs[23:]
    p = Place(depth)
    own = (p.y, p.x, p.z, p.c)
    rows, width = tok.shape
    slots = rows // 3
    size = qh.shape[1]
    lanes = 2 * size
    shard_lanes = vec.shape[1]
    tile[...] = jnp.zeros_like(tile)
    tile[0 : vec.shape[0], 0:shard_lanes] = vec[...]
    tiles[own] = pltpu.roll(tile[...], p.grp * shard_lanes, 1).astype(LOW)
    early[(0,) + own] = wq[...].astype(LOW)
    for tap in range(3):
        for half in range(2):
            columns = []
            for head in range(4 * half, 4 * half + 4):
                columns.append(wm[tap, :, head * size : (head + 1) * size])
                columns.append(wm[tap, :, width + head * size : width + (head + 1) * size])
            early[(1 + 3 * half + tap,) + own] = jnp.concatenate(columns, axis=1).astype(LOW)
    own_late[0] = wo[...].astype(LOW)
    for part in range(4):
        own_late[1 + part] = wu[:, part * width : (part + 1) * width].astype(LOW)
    own_down[...] = wd[...].astype(LOW)
    p.greet()
    half_down = down.shape[4] // 2
    views = [
        (lambda *i: tiles.at[i], "zxy", None),
        (bind(early, 1, 1), "zxy", None),
        (bind(early, 2, 1), "zyx", None),
        (bind(early, 3, 1), "xzy", None),
        (bind(early, 0, 1), "yzx", None),
        (bind(early, 4, 1), "zyx", None),
        (bind(early, 5, 1), "zxy", None),
        (bind(early, 6, 1), "xyz", None),
        (bind(late, 0, 3), "xyz", own_late.at[pl.ds(0, 3)]),
        (bind(late, 3, 2), "yzx", own_late.at[pl.ds(3, 2)]),
        (bind_rows(down, 0, half_down), "yxz", own_down.at[pl.ds(0, half_down)]),
        (bind_rows(down, half_down, half_down), "xyz", own_down.at[pl.ds(half_down, half_down)]),
    ]
    step = gather_slots(depth)
    pieces = [
        Gather(p, view, (gsend, grecv), step * k, order, first) for k, (view, order, first) in enumerate(views)
    ]
    vector_piece, soon, later = pieces[0], pieces[1:8], pieces[8:]
    for piece in pieces[:8]:
        piece.step(0)
    for k, piece in enumerate(later):
        piece.place_own(lsem.at[k]).start()
        piece.step(0)

    block = 128

    @pl.loop(0, rows // block)
    def _(number):
        at = pl.multiple_of(number * block, block)
        unit, _ = unit_rows_of(tok[pl.ds(at, block), :].astype(WIDE))
        put_tiles(wide_a, pl.ds(at + 8, block), unit)

    vector_piece.step(1)
    for piece in soon[2:4] + soon[6:] + soon[:2] + soon[4:6]:
        piece.step(1)
    vector_piece.step(2)
    vector_piece.step(3)
    vector_piece.step(4)
    tile_lanes = tiles.shape[-1]
    for y in range(2):
        for x in range(2):
            total = jnp.zeros(tiles.shape[-2:], WIDE)
            for z in range(depth):
                for c in range(2):
                    total += tiles[y, x, z, c].astype(WIDE)
            s = 2 * y + x
            vectors[:, s * tile_lanes : (s + 1) * tile_lanes] = total
    gain, shift = vectors[0:1, :], vectors[1:2, :]

    @pl.loop(0, rows // block)
    def _(number):
        at = pl.multiple_of(number * block, block)
        normed = (get_tiles(wide_a, pl.ds(at + 8, block)) * gain + shift).astype(LOW)
        low_a[pl.ds(at, block), :] = normed
        put_tiles(wide_a, pl.ds(at + 8, block), normed.astype(WIDE))

    last = p.seq == 3

    def edge_copy():
        return copy_to(
            wide_a.at[:, pl.ds(rows, 8)], wide_a.at[:, pl.ds(0, 8)], (xsend, xrecv), 0, {"seq": lax.rem(p.seq + 1, 4)}
        )

    @pl.when(jnp.logical_not(last))
    def _():
        edge_copy().start()

    for piece in soon[:2] + soon[4:7] + soon[2:4]:
        piece.step(2)
    for k, piece in enumerate(later):
        piece.place_own(lsem.at[k]).wait()
        piece.step(1)
    for piece in soon:
        piece.step(3)
    for piece in soon:
        piece.step(4)

    @pl.when(p.seq > 0)
    def _():
        edge_copy().wait_recv()

    @pl.when(jnp.logical_not(last))
    def _():
        edge_copy().wait_send()

    @pl.when(p.seq == 0)
    def _():
        wide_a[:, 0:8, :] = jnp.zeros((width // 128, 8, 128), WIDE)

    edge[...] = wide_a[:, 0:8, :]
    parts = rows // PART
    strips = qh.shape[2] // STRIP

    def early_leaves():
        return pltpu.make_async_copy(early, early_out, osem.at[0])

    def kv_leaves(half):
        return pltpu.make_async_copy(kv.at[half], kv_out.at[half], osem.at[1 + half])

    def qh_leaves(half):
        return pltpu.make_async_copy(qh.at[half], qh_out.at[half], osem.at[3 + half])

    def mixed_leaves(half, strip, index):
        here = span(strip, STRIP)
        return pltpu.make_async_copy(mixed.at[half, :, here], mixed_out.at[half, :, here], osem.at[index])

    def mixed_stays(half, part):
        return pltpu.make_async_copy(
            mixed.at[half, :, span(p.seq * parts + part, PART)],
            attended.at[half, p.seq, :, span(part, PART)],
            osem.at[5 + 2 * strips + half * parts + part],
        )

    early_leaves().start()

    def weight(j):
        return early[j].reshape(width, width)

    mine = span(p.seq, slots)

    def memory_copy(half, turn):
        return copy_to(
            ms.at[half, :, span(p.shard(turn), lanes)],
            kv.at[half, mine],
            (xsend, xrecv),
            1 + 3 * half + turn - 1,
            p.over_seq(turn),
        )

    def project(half):
        for tap in range(3):
            window = get_tiles(wide_a, pl.ds(6 + tap, slots, stride=3)).astype(LOW)
            part = dot(window, weight(1 + 3 * half + tap))
            total = part if tap == 0 else total + part
        ms[half] = total.astype(LOW)
        for turn in (3, 1, 2):
            memory_copy(half, turn).start()
        kv[half, mine, :] = ms[half, :, span(p.seq, lanes)]

    def query_copy(half, turn):
        return copy_to(
            qs.at[half, p.shard(turn)],
            qh.at[half, :, span(p.seq, rows)],
            (xsend, xrecv),
            7 + 3 * half + turn - 1,
            p.over_seq(turn),
        )

    def send_queries(half):
        for turn in (1, 2, 3):
            query_copy(half, turn).start()
        qh[half, :, span(p.seq, rows)] = qs[half, p.seq]

    project(0)
    turned = lax.dot_general(weight(0).T, low_a[...], NT, preferred_element_type=WIDE)
    qs[...] = turned.astype(LOW).reshape(qs.shape)
    send_queries(0)
    project(1)
    send_queries(1)
    for piece in later:
        piece.step(2)
    for turn in (1, 2, 3):
        memory_copy(0, turn).wait()
    kvt[0] = kv[0].T
    kv_leaves(0).start()

    def mixed_copy(half, turn, part):
        shard = p.shard(turn)
        return copy_to(
            mixed.at[half, :, span(shard * parts + part, PART)],
            attended.at[half, p.seq, :, span(part, PART)],
            (xsend, xrecv),
            13 + (3 * half + turn - 1) * parts + part,
            p.over_seq(turn),
        )

    def attend(half, seen, strip):
        here = span(strip, STRIP)
        queries = qh[half, :, here] * jnp.bfloat16(size ** (-0.5))
        queries = jnp.concatenate([queries, jnp.zeros_like(queries)], axis=0)
        whole = seen - SLOTS
        scores = hide_future(dot(kv[half, whole:seen, :], queries), whole, strip * STRIP)
        if whole:
            scores = jnp.concatenate([dot(kv[half, 0:whole, :], queries), scores], axis=0)
        highest = jnp.max(scores, axis=0, keepdims=True)
        exponent = jnp.exp(scores - highest)
        summed = jnp.sum(exponent, axis=0, keepdims=True)
        out = dot(kvt[half, size:lanes, 0:seen], exponent.astype(LOW)) * (1.0 / summed)
        lse[half, strip] = highest + jnp.log(summed)
        mixed[half, :, here] = out.astype(LOW)

    @pl.loop(0, 2 * strips)
    def _(turn_number):
        half, it = lax.div(turn_number, strips), lax.rem(turn_number, strips)
        for number, turn in ((1, 1), (3, 2), (4, 3)):

            @pl.when(it == number)
            def _():
                query_copy(half, turn).wait()

        @pl.when(turn_number == strips)
        def _():
            for turn in (1, 2, 3):
                memory_copy(1, turn).wait()
            kvt[1] = kv[1].T
            kv_leaves(1).start()
            qh_leaves(0).start()

        strip = p.strip(it)
        for group in range(strips):

            @pl.when(strip == group)
            def _():
                attend(half, SLOTS * (group + 1), strip)

        mixed_leaves(half, strip, 5 + turn_number).start()
        for k in range(2):
            granule = 2 * strip + k
            shard, part = lax.div(granule, parts), lax.rem(granule, parts)
            turn = p.turn_to(shard)

            @pl.when(turn > 0)
            def _():
                mixed_copy(half, turn, part).start()

            @pl.when(turn == 0)
            def _():
                mixed_stays(half, part).start()

        @pl.when(turn_number == 9)
        def _():
            later[1].step(3)

    qh_leaves(1).start()
    for piece in later[:1] + later[2:]:
        piece.step(3)
    for piece in later:
        piece.step(4)
    early_leaves().wait()
    for half in range(2):
        kv_leaves(half).wait()
        qh_leaves(half).wait()
        for it in range(strips):
            mixed_leaves(half, p.strip(it), 5 + half * strips + it).wait()
        for part in range(parts):
            mixed_stays(half, part).wait()
            for turn in (1, 2, 3):
                mixed_copy(half, turn, part).wait()


def front(tok, params):
    wq, wm, wo, wu, wd, vec = params
    groups = lax.axis_size("grp")
    depth = groups // 2
    rows, width = tok.shape
    own, slots, size = wq.shape[0], rows // 3, width // H
    lanes = 2 * size
    tile_lanes = vec.shape[1] * groups
    whole = (2, 2, depth, 2)
    sems = pltpu.SemaphoreType.DMA((12 * gather_slots(depth),))
    parts = rows // PART
    swaps = pltpu.SemaphoreType.DMA((13 + 6 * parts,))
    anywhere = pl.BlockSpec(memory_space=pl.ANY)
    vmem = pl.BlockSpec(memory_space=pltpu.VMEM)
    return pl.pallas_call(
        functools.partial(front_kernel, depth),
        out_shape=(
            shaped(EARLY, *whole, own, width),
            shaped(LATE, *whole, own, width),
            shaped(*whole, *wd.shape),
            shaped(ROWS, 4 * tile_lanes, kind=WIDE),
            shaped(width // 128, 8, 128, kind=WIDE),
            shaped(2, size, 4 * rows),
            shaped(2, 4 * slots, lanes),
            shaped(2, size, 4 * rows),
            shaped(2, 4 * rows // STRIP, 1, STRIP, kind=WIDE),
            shaped(2, 4, size, rows),
        ),
        in_specs=in_vmem(7),
        out_specs=[anywhere] * 3 + [vmem] * 2 + [anywhere] * 3 + [vmem, anywhere],
        scratch_shapes=[
            pltpu.VMEM((*whole, ROWS, tile_lanes), LOW),
            pltpu.VMEM((width // 128, rows + 8, 128), WIDE),
            pltpu.VMEM((rows, width), LOW),
            pltpu.VMEM((2, 4, size, rows), LOW),
            pltpu.VMEM((2, slots, width), LOW),
            pltpu.VMEM((2, lanes, 4 * slots), LOW),
            pltpu.VMEM((LATE, own, width), LOW),
            pltpu.VMEM(wd.shape, LOW),
            pltpu.VMEM((ROWS, tile_lanes), WIDE),
            pltpu.VMEM((EARLY, *whole, own, width), LOW),
            pltpu.VMEM((2, size, 4 * rows), LOW),
            pltpu.VMEM((2, 4 * slots, lanes), LOW),
            pltpu.VMEM((2, size, 4 * rows), LOW),
            sems,
            sems,
            swaps,
            swaps,
            pltpu.SemaphoreType.DMA((4,)),
            pltpu.SemaphoreType.DMA((5 + 2 * (4 * rows // STRIP) + 2 * parts,)),
        ],
        compiler_params=pltpu.CompilerParams(
            collective_id=0, has_side_effects=True, vmem_limit_bytes=58 * MEGA
        ),
    )(tok, wq, wm, wo, wu, wd, vec)


def middle_kernel(depth, tok_in, cot_in, att_in, late_in, down_in, vec, length, *refs):
    out_to, dres_to, doh, g_stack_to, g_down_to, g_vec = refs[:6]
    tok, cot, att, late, down, out, dres, g_stack, g_down = refs[6:15]
    zs, dus, cs, es, ys, dos, xsend, xrecv, isem, osem, gsem = refs[15:]
    p = Place(depth)
    arriving = [
        pltpu.make_async_copy(source, target, isem.at[k])
        for k, (source, target) in enumerate(
            ((att_in, att), (tok_in, tok), (late_in, late), (down_in, down), (cot_in, cot))
        )
    ]
    for made in arriving:
        made.start()
    p.greet(beyond=False)
    rows, width = tok.shape
    hidden = zs.shape[1]
    gain, shift, bias = vec[2:3, :], vec[3:4, :], vec[4:5, :]
    inner = 0.7978845608028654
    cubic = inner * 0.044715
    g_vec[...] = jnp.zeros_like(g_vec)

    parts = rows // PART

    def do_copy(number, turn):
        return copy_to(
            dos.at[:, p.shard(turn), :, span(number, PART)],
            doh.at[:, :, span(p.seq * parts + number, PART)],
            (xsend, xrecv),
            3 * number + turn - 1,
            p.over_seq(turn),
        )

    def leave(number):
        here = span(number, PART)
        pairs = (
            (out.at[here], out_to.at[here]),
            (dres.at[here], dres_to.at[here]),
            (dos.at[:, p.seq, :, here], doh.at[:, :, span(p.seq * parts + number, PART)]),
        )
        return [pltpu.make_async_copy(a, b, osem.at[3 * number + k]) for k, (a, b) in enumerate(pairs)]

    for made in arriving:
        made.wait()

    @pl.loop(0, parts)
    def _(number):
        at = pl.multiple_of(number * PART, PART)
        here = pl.ds(at, PART)
        attended = att[:, :, :, here].reshape(width, PART).T
        residual = tok[here, :].astype(WIDE) + dot(attended, late[0])
        unit, factor = unit_rows_of(residual)
        normed = (unit * gain + shift).astype(LOW)
        cs[here, :] = normed
        place = lax.broadcasted_iota(jnp.int32, (PART, 1), 0) + (p.seq * rows + at)
        live = (place < length[0, 0]).astype(WIDE)
        upstream = cot[here, :].astype(WIDE) * live
        upstream_low = upstream.astype(LOW)
        es[here, :] = upstream_low
        result = residual + bias
        back = jnp.zeros((PART, width), WIDE)
        for part in range(hidden // width):
            here_hidden = pl.ds(part * width, width)
            u = dot(normed, late[1 + part]) + vec[5 + part : 6 + part, :]
            square = u * u
            half = 0.5 + 0.5 * jnp.tanh(u * (inner + cubic * square))
            active = u * half
            slope = half + active * (1.0 - half) * (2.0 * inner + 6.0 * cubic * square)
            active_low = active.astype(LOW)
            zs[here, here_hidden] = active_low
            result += dot(active_low, down[here_hidden, :])
            pulled = lax.dot_general(upstream_low, down[here_hidden, :], NT, preferred_element_type=WIDE)
            grad = (pulled * slope).astype(LOW)
            dus[here, here_hidden] = grad
            g_vec[5 + part : 6 + part, :] += jnp.sum(grad.astype(WIDE), axis=0, keepdims=True)
            back += lax.dot_general(grad, late[1 + part], NT, preferred_element_type=WIDE)
        out[here, :] = result.astype(LOW)
        scaled = back * gain
        total = upstream + factor * (
            scaled
            - jnp.mean(scaled, axis=-1, keepdims=True)
            - unit * jnp.mean(scaled * unit, axis=-1, keepdims=True)
        )
        dres[here, :] = total
        branch = total.astype(LOW)
        ys[here, :] = branch
        turned = lax.dot_general(late[0], branch, NT, preferred_element_type=WIDE)
        dos[:, :, :, here] = turned.astype(LOW).reshape(dos.shape[:3] + (PART,))
        for turn in (3, 1, 2):
            do_copy(number, turn).start()
        for made in leave(number):
            made.start()
        g_vec[2:3, :] += jnp.sum(back * unit, axis=0, keepdims=True)
        g_vec[3:4, :] += jnp.sum(back, axis=0, keepdims=True)
        g_vec[4:5, :] += jnp.sum(upstream, axis=0, keepdims=True)

    def finished(ref, target, index):
        made = pltpu.make_async_copy(ref, target, gsem.at[index])
        made.start()
        return made

    left = []
    for part in range(hidden // width):
        piece = pl.ds(part * width, width)
        g_down[piece, :] = over_rows(zs[:, piece], es[...]).astype(LOW)
        left.append(finished(g_down.at[piece], g_down_to.at[piece], 5 + part))
    g_stack[0] = dot(att[...].reshape(width, rows), ys[...]).astype(LOW)
    left.append(finished(g_stack.at[0], g_stack_to.at[0], 0))
    for part in range(hidden // width):
        piece = pl.ds(part * width, width)
        g_stack[1 + part] = over_rows(cs[...], dus[:, piece]).astype(LOW)
        left.append(finished(g_stack.at[1 + part], g_stack_to.at[1 + part], 1 + part))
    for number in range(parts):
        for turn in (1, 2, 3):
            do_copy(number, turn).wait()
        for made in leave(number):
            made.wait()
    for made in left:
        made.wait()


def middle(tok, cot, att, late, down, vec, length):
    rows, width = tok.shape
    hidden = down.shape[0]
    sems = pltpu.SemaphoreType.DMA((3 * (rows // PART),))
    return pl.pallas_call(
        functools.partial(middle_kernel, lax.axis_size("grp") // 2),
        out_shape=(
            shaped(rows, width),
            shaped(rows, width, kind=WIDE),
            shaped(2, width // H, 4 * rows),
            shaped(LATE, width, width),
            shaped(hidden, width),
            shaped(*vec.shape, kind=WIDE),
        ),
        in_specs=[pl.BlockSpec(memory_space=pl.ANY)] * 5
        + [pl.BlockSpec(memory_space=pltpu.VMEM), pl.BlockSpec(memory_space=pltpu.SMEM)],
        out_specs=[pl.BlockSpec(memory_space=pl.ANY)] * 5 + [pl.BlockSpec(memory_space=pltpu.VMEM)],
        scratch_shapes=[pltpu.VMEM(x.shape, x.dtype) for x in (tok, cot, att, late, down)]
        + [
            pltpu.VMEM((rows, width), LOW),
            pltpu.VMEM((rows, width), WIDE),
            pltpu.VMEM((LATE, width, width), LOW),
            pltpu.VMEM((hidden, width), LOW),
            pltpu.VMEM((rows, hidden), LOW),
            pltpu.VMEM((rows, hidden), LOW),
            pltpu.VMEM((rows, width), LOW),
            pltpu.VMEM((rows, width), LOW),
            pltpu.VMEM((rows, width), LOW),
            pltpu.VMEM(att.shape, LOW),
            sems,
            sems,
            pltpu.SemaphoreType.DMA((5,)),
            sems,
            pltpu.SemaphoreType.DMA((LATE + hidden // width,)),
        ],
        compiler_params=pltpu.CompilerParams(
            collective_id=1, has_side_effects=True, vmem_limit_bytes=58 * MEGA
        ),
    )(tok, cot, att, late, down, vec, length)


def back_kernel(depth, *refs):
    far_inputs, (lse, vec, edge, g_vec) = refs[:9], refs[9:13]
    grad, out_early, out_late, out_down, out_vec = refs[13:18]
    scatter, refs = refs[18:54], refs[54:]
    near_inputs, refs = refs[:9], refs[9:]
    tok, kv, doh, qh, mixed, g_late, g_down, early, dres = near_inputs
    g_early, dkv, kvt, dqs, dq, dms, dm, wide_a, low_a, wide_da, da, after, give, get = refs[:14]
    rsend, rrecv, xsend, xrecv, isem = refs[14:]
    p = Place(depth)
    arriving = [
        pltpu.make_async_copy(a, b, isem.at[k]) for k, (a, b) in enumerate(zip(far_inputs, near_inputs))
    ]
    for made in arriving:
        made.start()
    rows, width = tok.shape
    slots = rows // 3
    size = qh.shape[1]
    lanes = 2 * size
    scale = size ** (-0.5)
    parts = rows // PART
    strips = qh.shape[2] // STRIP
    step = scatter_slots(depth)
    p.greet()

    def out_to(ref, first, count):
        def put(value):
            ref[first : first + count] = value

        return put

    half_down = g_down.shape[4] // 2
    todo = [
        (bind(g_late, 0, 3), out_to(out_late, 0, 3), bind(far_inputs[5], 0, 3)),
        (bind(g_late, 3, 2), out_to(out_late, 3, 2), bind(far_inputs[5], 3, 2)),
        (bind_rows(g_down, 0, half_down), out_to(out_down, 0, half_down), bind_rows(far_inputs[6], 0, half_down)),
        (
            bind_rows(g_down, half_down, half_down),
            out_to(out_down, half_down, half_down),
            bind_rows(far_inputs[6], half_down, half_down),
        ),
        (bind(g_early, 0, 1), out_to(out_early, 0, 1), None),
        (bind(g_early, 1, 2), out_to(out_early, 1, 2), None),
        (bind(g_early, 3, 1), out_to(out_early, 3, 1), None),
        (bind(g_early, 4, 2), out_to(out_early, 4, 2), None),
        (bind(g_early, 6, 1), out_to(out_early, 6, 1), None),
    ]
    pieces = [
        Scatter(p, view, out, scatter[4 * k : 4 * k + 4], (rsend, rrecv), step * k, SCATTER_ORDERS[k], far)
        for k, (view, out, far) in enumerate(todo)
    ]
    soon, query, first, second = pieces[:4], pieces[4:5], pieces[5:7], pieces[7:]
    small = SumAll(p, out_vec, give, get, (rsend, rrecv), step * len(pieces))
    for piece in soon:
        piece.step(0)
    gain, shift = vec[0:1, :], vec[1:2, :]
    block = 128
    wide_a[:, 0:8, :] = edge[...]
    arriving[0].wait()

    @pl.loop(0, rows // block)
    def _(number):
        at = pl.multiple_of(number * block, block)
        unit, _ = unit_rows_of(tok[pl.ds(at, block), :].astype(WIDE))
        normed = (unit * gain + shift).astype(LOW)
        low_a[pl.ds(at, block), :] = normed
        put_tiles(wide_a, pl.ds(at + 8, block), normed.astype(WIDE))

    for made in arriving[1:5]:
        made.wait()
    for half in range(2):
        kvt[half] = kv[half].T
    dkv[...] = jnp.zeros_like(dkv)

    def dq_copy(half, turn, part):
        return copy_to(
            dqs.at[half, :, span(p.shard(turn) * parts + part, PART)],
            dq.at[half, p.seq, :, span(part, PART)],
            (xsend, xrecv),
            (3 * half + turn - 1) * parts + part,
            p.over_seq(turn),
        )

    def attend(half, seen, strip):
        here = span(strip, STRIP)
        queries = qh[half, :, here] * jnp.bfloat16(scale)
        incoming = doh[half, :, here]
        middle = jnp.sum(incoming.astype(WIDE) * mixed[half, :, here].astype(WIDE), axis=0, keepdims=True)
        blank = jnp.zeros_like(queries)
        queries = jnp.concatenate([queries, blank], axis=0)
        incoming = jnp.concatenate([blank, incoming], axis=0)
        total = lse[half, strip]
        turned = jnp.zeros((size, STRIP), WIDE)
        for start in range(0, seen, 2 * SLOTS):
            stop = min(start + 2 * SLOTS, seen)
            keys = kv[half, start:stop, :]
            scores = dot(keys, queries)
            if stop == seen:
                clear = stop - SLOTS - start
                masked = hide_future(scores[clear:], stop - SLOTS, strip * STRIP)
                scores = jnp.concatenate([scores[:clear], masked], axis=0) if clear else masked
            weights = jnp.exp(scores - total)
            slope = (weights * (dot(keys, incoming) - middle)).astype(LOW)
            dkv[half, start:stop, :] += lax.dot_general(
                slope, queries, NT, preferred_element_type=WIDE
            ) + lax.dot_general(weights.astype(LOW), incoming, NT, preferred_element_type=WIDE)
            turned += dot(kvt[half, 0:size, start:stop], slope)
        dqs[half, :, here] = (turned * scale).astype(LOW)

    def memory_copy(half, turn):
        return copy_to(
            dms.at[half, span(p.shard(turn), slots)],
            dm.at[half, :, span(p.seq, lanes)],
            (xsend, xrecv),
            6 * parts + 3 * half + turn - 1,
            p.over_seq(turn),
        )

    def send_memory(half):
        dms[half] = dkv[half].astype(LOW)
        for turn in (3, 1, 2):
            memory_copy(half, turn).start()
        dm[half, :, span(p.seq, lanes)] = dms[half, span(p.seq, slots), :]

    def put_early(j, value):
        g_early[j] = value.astype(LOW).reshape(g_early.shape[1:])

    def memory_gradient(half, tap):
        window = get_tiles(wide_a, pl.ds(6 + tap, slots, stride=3)).astype(LOW)
        put_early(1 + 3 * half + tap, over_rows(window, dm[half]))

    @pl.loop(0, 2 * strips)
    def _(turn_number):
        half, it = lax.div(turn_number, strips), lax.rem(turn_number, strips)

        @pl.when(turn_number == strips)
        def _():
            send_memory(0)

        @pl.when(turn_number == strips + 2)
        def _():
            for turn in (1, 2, 3):
                memory_copy(0, turn).wait()
            for tap in range(3):
                memory_gradient(0, tap)
            for piece in first:
                piece.step(0)

        strip = p.strip(strips - 1 - it)
        for group in range(strips):

            @pl.when(strip == group)
            def _():
                attend(half, SLOTS * (group + 1), strip)

        for k in range(2):
            granule = 2 * strip + k
            shard, part = lax.div(granule, parts), lax.rem(granule, parts)
            turn = p.turn_to(shard)

            @pl.when(turn > 0)
            def _():
                dq_copy(half, turn, part).start()

            @pl.when(turn == 0)
            def _():
                dq[half, p.seq, :, span(part, PART)] = dqs[half, :, span(granule, PART)]

        @pl.when(turn_number == 1)
        def _():
            for k in (5, 6):
                pltpu.make_async_copy(far_inputs[k], near_inputs[k], isem.at[k]).wait()

        for when, steps in (
            (1, [(piece, 1) for piece in soon]),
            (7, [(piece, 2) for piece in soon]),
            (9, [(piece, 1) for piece in first]),
            (10, [(piece, 3) for piece in soon]),
        ):

            @pl.when(turn_number == when)
            def _():
                run(steps)

    send_memory(1)
    for half in range(2):
        for turn in (1, 2, 3):
            for part in range(parts):
                dq_copy(half, turn, part).wait()
    for made in arriving[7:]:
        made.wait()
    turned = dq[...].reshape(width, rows)
    put_early(0, dot(turned, low_a[...]).T)
    query[0].step(0)
    da[...] = lax.dot_general(turned.T, early[0], NT, preferred_element_type=WIDE)
    query[0].step(1)
    run([(piece, 2) for piece in first])
    for turn in (1, 2, 3):
        memory_copy(1, turn).wait()
    for tap in range(3):
        memory_gradient(1, tap)
        if tap:
            second[tap - 1].step(0)
    wide_da[:, 0:8, :] = jnp.zeros((width // 128, 8, 128), WIDE)
    for tap in range(3):
        pulled = lax.dot_general(dm[0], early[1 + tap], NT, preferred_element_type=WIDE)
        pulled += lax.dot_general(dm[1], early[4 + tap], NT, preferred_element_type=WIDE)
        put_tiles(wide_da, pl.ds(6 + tap, slots, stride=3), pulled)

    def edge_copy():
        return copy_to(
            wide_da.at[:, pl.ds(0, 8)], after, (xsend, xrecv), 6 * parts + 6, {"seq": lax.rem(p.seq + 3, 4)}
        )

    @pl.when(p.seq > 0)
    def _():
        edge_copy().start()

    run([(piece, 1) for piece in second])
    run([(piece, 4) for piece in soon])
    run([(query[0], 2), (first[0], 3), (first[1], 3)])

    @pl.when(p.seq < 3)
    def _():
        edge_copy().wait_recv()

    @pl.when(p.seq > 0)
    def _():
        edge_copy().wait_send()

    @pl.when(p.seq == 3)
    def _():
        after[...] = jnp.zeros_like(after)

    wide_da[:, rows + 6 : rows + 8, :] = after[:, 6:8, :]
    give[0] = g_vec[...]

    @pl.loop(0, rows // block)
    def _(number):
        at = pl.multiple_of(number * block, block)
        here = pl.ds(at, block)
        unit, factor = unit_rows_of(tok[here, :].astype(WIDE))
        upstream = da[here, :] + get_tiles(wide_da, pl.ds(at + 8, block))
        scaled = upstream * gain
        inward = factor * (
            scaled
            - jnp.mean(scaled, axis=-1, keepdims=True)
            - unit * jnp.mean(scaled * unit, axis=-1, keepdims=True)
        )
        grad[here, :] = (dres[here, :] + inward).astype(LOW)
        give[0, 0:1, :] += jnp.sum(upstream * unit, axis=0, keepdims=True)
        give[0, 1:2, :] += jnp.sum(upstream, axis=0, keepdims=True)

    small.step(0)
    run([(piece, 2) for piece in second])
    small.step(1)
    run([(query[0], 3), (second[0], 3), (second[1], 3)])
    run([(first[0], 4), (first[1], 4)])
    small.step(2)
    run([(query[0], 4), (second[0], 4), (second[1], 4)])
    small.step(3)


def back(saved, tok, dres, early, vec, edge, grads):
    qh, kv, mixed, lse, doh = saved
    g_late, g_down, g_vec = grads
    depth = lax.axis_size("grp") // 2
    rows, width = tok.shape
    size, slots = qh.shape[1], rows // 3
    lanes = 2 * size
    whole = (2, 2, depth, 2)
    own_down = g_down.shape[0] // (8 * depth)
    parts = rows // PART
    shapes = [(3, ROWS, width), (2, ROWS, width)] + [(own_down // 2, width)] * 2
    shapes += [(1, ROWS, width)] + [(2, ROWS, width), (1, ROWS, width)] * 2
    ring = pltpu.SemaphoreType.DMA((9 * scatter_slots(depth) + depth + 3,))
    swaps = pltpu.SemaphoreType.DMA((6 * parts + 7,))
    g_late = g_late.reshape(LATE, *whole, ROWS, width)
    g_down = g_down.reshape(*whole, own_down, width)
    inputs = (tok, kv, doh, qh, mixed, g_late, g_down, early, dres)
    return pl.pallas_call(
        functools.partial(back_kernel, depth),
        out_shape=(
            shaped(rows, width),
            shaped(EARLY, ROWS, width, kind=WIDE),
            shaped(LATE, ROWS, width, kind=WIDE),
            shaped(own_down, width, kind=WIDE),
            shaped(*vec.shape, kind=WIDE),
        ),
        in_specs=[pl.BlockSpec(memory_space=pl.ANY)] * 9 + in_vmem(4),
        out_specs=in_vmem(5),
        scratch_shapes=[
            buf for order, shape in zip(SCATTER_ORDERS, shapes) for buf in scatter_scratch(depth, order, shape)
        ]
        + [pltpu.VMEM(x.shape, x.dtype) for x in inputs]
        + [
            pltpu.VMEM((EARLY, *whole, ROWS, width), LOW),
            pltpu.VMEM(kv.shape, WIDE),
            pltpu.VMEM((2, lanes, 4 * slots), LOW),
            pltpu.VMEM(qh.shape, LOW),
            pltpu.VMEM((2, 4, size, rows), LOW),
            pltpu.VMEM(kv.shape, LOW),
            pltpu.VMEM((2, slots, width), LOW),
            pltpu.VMEM((width // 128, rows + 8, 128), WIDE),
            pltpu.VMEM((rows, width), LOW),
            pltpu.VMEM((width // 128, rows + 8, 128), WIDE),
            pltpu.VMEM((rows, width), WIDE),
            pltpu.VMEM((width // 128, 8, 128), WIDE),
            pltpu.VMEM((3,) + vec.shape, WIDE),
            pltpu.VMEM((depth + 3,) + vec.shape, WIDE),
            ring,
            ring,
            swaps,
            swaps,
            pltpu.SemaphoreType.DMA((9,)),
        ],
        compiler_params=pltpu.CompilerParams(
            collective_id=2, has_side_effects=True, vmem_limit_bytes=62 * MEGA
        ),
    )(*inputs, lse, vec, edge, g_vec)


def update_kernel(*refs):
    weights, firsts, seconds = refs[0:6], refs[6:12], refs[12:18]
    early, late, down, vec = refs[18:22]
    held, outs, passed, kept, sems = refs[22:24], refs[24:48], refs[48:50], refs[50:52], refs[52]
    arriving = [pltpu.make_async_copy(held[k], kept[k], sems.at[k]) for k in range(2)]
    leaving = [pltpu.make_async_copy(kept[k], passed[k], sems.at[2 + k]) for k in range(2)]
    for made in arriving:
        made.start()
    width = early.shape[-1]

    def put(which, at, gradient):
        results = adamw(
            weights[which][at], gradient, firsts[which][at], seconds[which][at], LEARNING_RATES[which]
        )
        for group, value in enumerate(results):
            outs[6 * group + which][at] = value

    every = slice(None)
    put(0, (every, every), early[0])
    for k in range(2):
        arriving[k].wait()
        leaving[k].start()
    size = width // H
    for tap in range(3):
        for kind in range(2):
            columns = [
                early[1 + 3 * half + tap, :, (2 * s + kind) * size : (2 * s + kind + 1) * size]
                for half in range(2)
                for s in range(4)
            ]
            put(1, (tap, every, slice(kind * width, (kind + 1) * width)), jnp.concatenate(columns, axis=1))
    put(2, (every, every), late[0])
    for part in range(4):
        put(3, (every, slice(part * width, (part + 1) * width)), late[1 + part])
    put(4, (every, every), down[...])
    share = weights[5].shape[1]
    tile_lanes = vec.shape[1] // 4
    seq, grp = lax.axis_index("seq"), lax.axis_index("grp")
    tile = vec[:, pl.ds(pl.multiple_of(seq * tile_lanes, tile_lanes), tile_lanes)]
    tile = pltpu.roll(tile, lax.rem(tile_lanes - grp * share, tile_lanes), 1)
    put(5, (every, every), tile[0 : weights[5].shape[0], 0:share])
    for made in leaving:
        made.wait()


def update(params, firsts, seconds, grads, held):
    outs = [jax.ShapeDtypeStruct(member.shape, WIDE) for member in params] * 3
    outs += [jax.ShapeDtypeStruct(member.shape, LOW) for member in params]
    return pl.pallas_call(
        update_kernel,
        out_shape=tuple(outs) + tuple(jax.ShapeDtypeStruct(x.shape, x.dtype) for x in held),
        in_specs=in_vmem(22) + [pl.BlockSpec(memory_space=pl.ANY)] * 2,
        out_specs=in_vmem(24) + [pl.BlockSpec(memory_space=pl.ANY)] * 2,
        scratch_shapes=[pltpu.VMEM(x.shape, x.dtype) for x in held] + [pltpu.SemaphoreType.DMA((4,))],
    )(*params, *firsts, *seconds, *grads, *held)


def fused(tokens, cotangent, lengths, *state):
    params, firsts, seconds = state[0:6], state[6:12], state[12:18]
    width = tokens.shape[2]
    tok, cot = tokens[0], cotangent[0]
    early, late, down, vec, edge, qh, kv, mixed, lse, attended = front(tok, params)
    early = early.reshape(EARLY, width, width)
    late = late.reshape(LATE, width, width)
    down = down.reshape(-1, width)
    out, dres, doh, g_late, g_down, g_vec = middle(
        tok, cot, attended, late, down, vec, lengths.reshape(1, 1)
    )
    grad, r_early, r_late, r_down, r_vec = back(
        (qh, kv, mixed, lse, doh), tok, dres, early, vec, edge, (g_late, g_down, g_vec)
    )
    *new, out, grad = update(params, firsts, seconds, (r_early, r_late, r_down, r_vec), (out, grad))
    return (out[None], grad[None], *new)


def body(*arguments):
    tokens, shard = arguments[0], arguments[3]
    whole_tiles = shard.shape[0] % ROWS == 0 and tokens.shape[1] % PART == 0
    four = lax.axis_size("seq") == 4 and lax.axis_size("grp") % 2 == 0
    return (fused if whole_tiles and four else plain)(*arguments)


def solution(mesh):
    in_specs = (
        P("grp", "seq", None),
        P("grp", "seq", None),
        P("grp"),
        P(("seq", "grp"), None),
        P(None, ("seq", "grp"), None),
        P(("seq", "grp"), None),
        P(("seq", "grp"), None),
        P(("seq", "grp"), None),
        P(None, ("seq", "grp")),
        P(("seq", "grp"), None),
        P(None, ("seq", "grp"), None),
        P(("seq", "grp"), None),
        P(("seq", "grp"), None),
        P(("seq", "grp"), None),
        P(None, ("seq", "grp")),
        P(("seq", "grp"), None),
        P(None, ("seq", "grp"), None),
        P(("seq", "grp"), None),
        P(("seq", "grp"), None),
        P(("seq", "grp"), None),
        P(None, ("seq", "grp")),
    )
    out_specs = (
        P("grp", "seq", None),
        P("grp", "seq", None),
        P(("seq", "grp"), None),
        P(None, ("seq", "grp"), None),
        P(("seq", "grp"), None),
        P(("seq", "grp"), None),
        P(("seq", "grp"), None),
        P(None, ("seq", "grp")),
        P(("seq", "grp"), None),
        P(None, ("seq", "grp"), None),
        P(("seq", "grp"), None),
        P(("seq", "grp"), None),
        P(("seq", "grp"), None),
        P(None, ("seq", "grp")),
        P(("seq", "grp"), None),
        P(None, ("seq", "grp"), None),
        P(("seq", "grp"), None),
        P(("seq", "grp"), None),
        P(("seq", "grp"), None),
        P(None, ("seq", "grp")),
        P(("seq", "grp"), None),
        P(None, ("seq", "grp"), None),
        P(("seq", "grp"), None),
        P(("seq", "grp"), None),
        P(("seq", "grp"), None),
        P(None, ("seq", "grp")),
    )
    return jax.shard_map(body, mesh=mesh, in_specs=in_specs, out_specs=out_specs, check_vma=False)
```

```python
import functools

import jax
import jax.numpy as jnp
from jax import lax
from jax.experimental import pallas as pl
from jax.experimental.pallas import tpu as pltpu
from jax.sharding import PartitionSpec as P

H = 8
STEP = 10


NORM_EPSILON = 1e-05
BETA_FIRST = 0.9
BETA_SECOND = 0.95
ADAM_EPSILON = 1e-08
WEIGHT_DECAY = 0.1
LEARNING_RATES = (0.05, 0.04, 0.3, 0.05, 0.03, 0.5)
MASKED_SCORE = -1e30
NT = (((1,), (1,)), ((), ()))


def from_behind(x, axis, by):
    peers = lax.axis_size(axis)
    pairs = [(i, i + by) for i in range(peers) if 0 <= i + by < peers]
    return lax.ppermute(x, axis, pairs)


def matmul(left, right):
    return jnp.dot(left, right, preferred_element_type=jnp.float32)


def over_rows(left, right):
    return lax.dot_general(
        left, right, (((0,), (0,)), ((), ())), preferred_element_type=jnp.float32
    )


def against(left, right):
    return lax.dot_general(
        left, right, (((1,), (1,)), ((), ())), preferred_element_type=jnp.float32
    )


def norm_forward(values, gain, shift):
    centred = values - jnp.mean(values, axis=-1, keepdims=True)
    factor = lax.rsqrt(jnp.mean(centred * centred, axis=-1, keepdims=True) + NORM_EPSILON)
    unit_rows = centred * factor
    return (unit_rows * gain + shift, unit_rows, factor)


def norm_backward(upstream, unit_rows, factor, gain):
    scaled = upstream * gain
    inward = factor * (
        scaled
        - jnp.mean(scaled, axis=-1, keepdims=True)
        - unit_rows * jnp.mean(scaled * unit_rows, axis=-1, keepdims=True)
    )
    return (inward, jnp.sum(upstream * unit_rows, axis=0), jnp.sum(upstream, axis=0))


def masked_scores(query_tile_rows, key_row_block, positions):
    slot_starts = 3 * jnp.arange(key_row_block.shape[0], dtype=jnp.int32)
    score_matrix = jnp.einsum(
        "azv,lzv->zal", query_tile_rows, key_row_block, preferred_element_type=jnp.float32
    ) * query_tile_rows.shape[2] ** (-0.5)
    visible = slot_starts[None, :] <= positions[:, None]
    return jnp.where(visible[None], score_matrix, MASKED_SCORE)


def attend_forward(queries, key_row_block, value_row_block, anchor, block_rows):
    block_count = queries.shape[0] // block_rows
    offsets = block_rows * jnp.arange(block_count, dtype=jnp.int32)

    def attend_block(inputs):
        query_tile_rows, offset_rows = inputs
        score_matrix = masked_scores(
            query_tile_rows,
            key_row_block,
            anchor + offset_rows + jnp.arange(block_rows, dtype=jnp.int32),
        )
        highest = jnp.max(score_matrix, axis=-1, keepdims=True)
        exponent = jnp.exp(score_matrix - highest)
        summed = jnp.sum(exponent, axis=-1, keepdims=True)
        reduced_weights = (exponent / summed).astype(jnp.bfloat16)
        mixed = jnp.einsum(
            "yup,pyb->uyb", reduced_weights, value_row_block, preferred_element_type=jnp.float32
        )
        return (mixed, (highest + jnp.log(summed))[..., 0])

    blocks_in = queries.reshape(block_count, block_rows, queries.shape[1], queries.shape[2])
    mixed, logsum = lax.map(attend_block, (blocks_in, offsets))
    return (mixed.reshape(queries.shape), logsum)


def attend_backward(queries, key_row_block, value_row_block, upstream, logsum, anchor, block_rows):
    block_count = queries.shape[0] // block_rows
    offsets = block_rows * jnp.arange(block_count, dtype=jnp.int32)
    scale_factor = queries.shape[2] ** (-0.5)

    def attend_back(carry, inputs):
        grad_keys, grad_values = carry
        query_tile_rows, incoming_gradient_rows, logsum_block, offset_rows = inputs
        score_matrix = masked_scores(
            query_tile_rows,
            key_row_block,
            anchor + offset_rows + jnp.arange(block_rows, dtype=jnp.int32),
        )
        weights_soft = jnp.exp(score_matrix - logsum_block[..., None])
        grad_weights = jnp.einsum(
            "azv,lzv->zal",
            incoming_gradient_rows,
            value_row_block,
            preferred_element_type=jnp.float32,
        )
        centre = jnp.sum(weights_soft * grad_weights, axis=-1, keepdims=True)
        score_gradient = (weights_soft * (grad_weights - centre)).astype(jnp.bfloat16)
        grad_query = (
            jnp.einsum(
                "yup,pyb->uyb", score_gradient, key_row_block, preferred_element_type=jnp.float32
            )
            * scale_factor
        )
        grad_keys = (
            grad_keys
            + jnp.einsum(
                "xof,oxa->fxa", score_gradient, query_tile_rows, preferred_element_type=jnp.float32
            )
            * scale_factor
        )
        grad_values = grad_values + jnp.einsum(
            "xof,oxa->fxa",
            weights_soft.astype(jnp.bfloat16),
            incoming_gradient_rows,
            preferred_element_type=jnp.float32,
        )
        return ((grad_keys, grad_values), grad_query)

    shape_blocks = (block_count, block_rows, queries.shape[1], queries.shape[2])
    zeros_init = jnp.zeros(key_row_block.shape, jnp.float32)
    (grad_keys, grad_values), grad_query = lax.scan(
        attend_back,
        (zeros_init, zeros_init),
        (queries.reshape(shape_blocks), upstream.reshape(shape_blocks), logsum, offsets),
    )
    return (grad_query.reshape(queries.shape), grad_keys, grad_values)


def adamw(weight, gradient, moment, square, step_rate):
    moment_new = BETA_FIRST * moment + (1.0 - BETA_FIRST) * gradient
    square_new = BETA_SECOND * square + (1.0 - BETA_SECOND) * gradient * gradient
    fixed_first = 1.0 - BETA_FIRST**STEP
    fixed_second = 1.0 - BETA_SECOND**STEP
    update = (
        moment_new / fixed_first / (jnp.sqrt(square_new / fixed_second) + ADAM_EPSILON)
        + WEIGHT_DECAY * weight
    )
    master = weight - step_rate * update
    return (moment_new, square_new, master, master.astype(jnp.bfloat16))


def plain(
    tokens,
    cotangent,
    lengths,
    weight_query,
    weight_memory,
    weight_out,
    weight_up,
    weight_down,
    vectors,
    first_query,
    first_memory,
    first_out,
    first_up,
    first_down,
    first_vectors,
    second_query,
    second_memory,
    second_out,
    second_up,
    second_down,
    second_vectors,
):
    gathered = (
        lax.all_gather(weight_query.astype(jnp.bfloat16), ("seq", "grp"), axis=0, tiled=True),
        lax.all_gather(weight_memory.astype(jnp.bfloat16), ("seq", "grp"), axis=1, tiled=True),
        lax.all_gather(weight_out.astype(jnp.bfloat16), ("seq", "grp"), axis=0, tiled=True),
        lax.all_gather(weight_up.astype(jnp.bfloat16), ("seq", "grp"), axis=0, tiled=True),
        lax.all_gather(weight_down.astype(jnp.bfloat16), ("seq", "grp"), axis=0, tiled=True),
        lax.all_gather(vectors.astype(jnp.bfloat16), ("seq", "grp"), axis=1, tiled=True),
    )
    query_w, memory_w, out_w, up_w, down_w, vector_low = gathered
    vector_rows = vector_low.astype(jnp.float32)
    model_width = query_w.shape[0]
    hidden_units = up_w.shape[1]
    head_size = model_width // H
    seq_count = lax.axis_size("seq")
    seq_index = lax.axis_index("seq")
    local_rows = tokens.shape[1]
    local_slots = local_rows // 3
    inputs = tokens[0].astype(jnp.float32)
    normed, unit_one, factor_one = norm_forward(inputs, vector_rows[0], vector_rows[1])
    normed_low = normed.astype(jnp.bfloat16)
    queries = matmul(normed_low, query_w).astype(jnp.bfloat16)
    borrowed = from_behind(normed_low[local_rows - 2 :], "seq", 1)
    extended = jnp.concatenate([borrowed, normed_low], axis=0)
    windows = extended[:local_rows].reshape(local_slots, 3 * model_width)
    memory_flat = memory_w.reshape(3 * model_width, 2 * model_width)
    memory = matmul(windows, memory_flat).astype(jnp.bfloat16)
    share_width = model_width // seq_count
    local_heads = H // seq_count
    head_queries, head_memory = (
        lax.all_to_all(
            queries.reshape(local_rows, 1, seq_count, share_width),
            "seq",
            split_axis=2,
            concat_axis=0,
            tiled=True,
        ),
        lax.all_to_all(
            memory.reshape(local_slots, 2, seq_count, share_width),
            "seq",
            split_axis=2,
            concat_axis=0,
            tiled=True,
        ),
    )
    total_rows = head_queries.shape[0]
    total_slots = head_memory.shape[0]
    query_heads = head_queries.reshape(total_rows, local_heads, head_size)
    key_heads = head_memory[:, 0].reshape(total_slots, local_heads, head_size)
    value_heads = head_memory[:, 1].reshape(total_slots, local_heads, head_size)
    block_rows = min(512, total_rows)
    mixed, logsum = attend_forward(query_heads, key_heads, value_heads, 0, block_rows)
    mixed_low = mixed.astype(jnp.bfloat16).reshape(total_rows, 1, share_width)
    attended = lax.all_to_all(mixed_low, "seq", split_axis=0, concat_axis=1, tiled=True).reshape(
        local_rows, model_width
    )
    residual = inputs + matmul(attended, out_w)
    normed_two, unit_two, factor_two = norm_forward(residual, vector_rows[2], vector_rows[3])
    normed_two_low = normed_two.astype(jnp.bfloat16)
    pre_act = matmul(normed_two_low, up_w) + vector_rows[5:].reshape(hidden_units)
    activated, gelu_pull = jax.vjp(jax.nn.gelu, pre_act)
    activated_low = activated.astype(jnp.bfloat16)
    result = residual + matmul(activated_low, down_w) + vector_rows[4]
    positions = seq_index * local_rows + jnp.arange(local_rows, dtype=jnp.int32)
    live_mask = (positions < lengths[0]).astype(jnp.float32)
    grad_out = cotangent[0].astype(jnp.float32) * live_mask[:, None]
    grad_out_low = grad_out.astype(jnp.bfloat16)
    grad_down = over_rows(activated_low, grad_out_low)
    grad_activated = against(grad_out_low, down_w)
    grad_pre_low = gelu_pull(grad_activated)[0].astype(jnp.bfloat16)
    grad_up = over_rows(normed_two_low, grad_pre_low)
    grad_up_bias = jnp.sum(grad_pre_low.astype(jnp.float32), axis=0)
    grad_normed_two = against(grad_pre_low, up_w)
    grad_norm_two, grad_gain_two, grad_shift_two = norm_backward(
        grad_normed_two, unit_two, factor_two, vector_rows[2]
    )
    grad_residual = grad_out + grad_norm_two
    grad_branch_low = grad_residual.astype(jnp.bfloat16)
    grad_outw = over_rows(attended, grad_branch_low)
    grad_attended_low = against(grad_branch_low, out_w).astype(jnp.bfloat16)
    grad_heads = lax.all_to_all(
        grad_attended_low.reshape(local_rows, 1, seq_count, share_width),
        "seq",
        split_axis=2,
        concat_axis=0,
        tiled=True,
    ).reshape(total_rows, local_heads, head_size)
    grad_q, grad_k, grad_v = attend_backward(
        query_heads, key_heads, value_heads, grad_heads, logsum, 0, block_rows
    )
    packed = (
        jnp.stack([grad_k, grad_v], axis=1)
        .astype(jnp.bfloat16)
        .reshape(total_slots, 2, 1, share_width)
    )
    token_queries, token_memory = (
        lax.all_to_all(
            grad_q.astype(jnp.bfloat16).reshape(total_rows, 1, 1, share_width),
            "seq",
            split_axis=0,
            concat_axis=2,
            tiled=True,
        ),
        lax.all_to_all(packed, "seq", split_axis=0, concat_axis=2, tiled=True),
    )
    grad_queries_low = token_queries.reshape(local_rows, model_width)
    grad_memory_low = token_memory.reshape(local_slots, 2 * model_width)
    grad_queryw = over_rows(normed_low, grad_queries_low)
    grad_normed = against(grad_queries_low, query_w)
    grad_memoryw = over_rows(windows, grad_memory_low).reshape(3, model_width, 2 * model_width)
    grad_windows = against(grad_memory_low, memory_flat).reshape(local_rows, model_width)
    returned = from_behind(grad_windows[:2], "seq", -1)
    grad_normed = grad_normed + jnp.concatenate([grad_windows[2:], returned], axis=0)
    grad_norm_one, grad_gain_one, grad_shift_one = norm_backward(
        grad_normed, unit_one, factor_one, vector_rows[0]
    )
    grad_inputs = (grad_residual + grad_norm_one).astype(jnp.bfloat16)
    grad_vector_rows = jnp.concatenate(
        [
            jnp.stack(
                [
                    grad_gain_one,
                    grad_shift_one,
                    grad_gain_two,
                    grad_shift_two,
                    jnp.sum(grad_out, axis=0),
                ]
            ),
            grad_up_bias.reshape(4, model_width),
        ],
        axis=0,
    )
    reduced = (
        lax.psum_scatter(grad_queryw, ("seq", "grp"), scatter_dimension=0, tiled=True),
        lax.psum_scatter(grad_memoryw, ("seq", "grp"), scatter_dimension=1, tiled=True),
        lax.psum_scatter(grad_outw, ("seq", "grp"), scatter_dimension=0, tiled=True),
        lax.psum_scatter(grad_up, ("seq", "grp"), scatter_dimension=0, tiled=True),
        lax.psum_scatter(grad_down, ("seq", "grp"), scatter_dimension=0, tiled=True),
        lax.psum_scatter(grad_vector_rows, ("seq", "grp"), scatter_dimension=1, tiled=True),
    )
    new_query = adamw(weight_query, reduced[0], first_query, second_query, LEARNING_RATES[0])
    new_memory = adamw(weight_memory, reduced[1], first_memory, second_memory, LEARNING_RATES[1])
    new_out = adamw(weight_out, reduced[2], first_out, second_out, LEARNING_RATES[2])
    new_up = adamw(weight_up, reduced[3], first_up, second_up, LEARNING_RATES[3])
    new_down = adamw(weight_down, reduced[4], first_down, second_down, LEARNING_RATES[4])
    new_vectors = adamw(vectors, reduced[5], first_vectors, second_vectors, LEARNING_RATES[5])
    return (
        result.astype(jnp.bfloat16)[None],
        grad_inputs[None],
        new_query[0],
        new_memory[0],
        new_out[0],
        new_up[0],
        new_down[0],
        new_vectors[0],
        new_query[1],
        new_memory[1],
        new_out[1],
        new_up[1],
        new_down[1],
        new_vectors[1],
        new_query[2],
        new_memory[2],
        new_out[2],
        new_up[2],
        new_down[2],
        new_vectors[2],
        new_query[3],
        new_memory[3],
        new_out[3],
        new_up[3],
        new_down[3],
        new_vectors[3],
    )


MESH = pl.DeviceIdType.MESH
LOW, WIDE = jnp.bfloat16, jnp.float32
ROWS = 16
PART = 384
STRIP = 2 * PART
SLOTS = STRIP // 3
EARLY = 7
LATE = 5
MEGA = 1024 * 1024
SCATTER_ORDERS = ("yzx", "xyz", "zxy", "xyz", "sz", "xyz", "yzx", "sz", "sz")


def in_vmem(count):
    return [pl.BlockSpec(memory_space=pltpu.VMEM)] * count


def shaped(*shape, kind=jnp.bfloat16):
    return jax.ShapeDtypeStruct(shape, kind)


def dot(left, right):
    return jnp.dot(left, right, preferred_element_type=jnp.float32)


def differ(bit, other):
    return bit + other - 2 * bit * other


class Place:
    def __init__(self, depth):
        self.seq, self.grp = lax.axis_index("seq"), lax.axis_index("grp")
        self.depth = depth
        self.y, self.x = lax.div(self.seq, 2), lax.rem(self.seq, 2)
        self.z, self.c = lax.div(self.grp, 2), lax.rem(self.grp, 2)
        self.own = {"y": self.y, "x": self.x, "z": self.z, "s": self.seq}
        self.size = {"y": 2, "x": 2, "z": depth, "s": 4}

    def turn_to(self, shard):
        return 2 * differ(self.y, lax.div(shard, 2)) + differ(self.x, lax.rem(shard, 2))

    def strip(self, it):
        half, pos = differ(lax.div(it, 3), self.y), lax.rem(it, 3)
        return 3 * half + pos + self.x * (2 - 2 * pos)

    def shard(self, turn):
        return 2 * differ(self.y, lax.div(turn, 2)) + differ(self.x, lax.rem(turn, 2))

    def over_seq(self, turn):
        return {"seq": self.shard(turn)}

    def over_core(self):
        return {"grp": 2 * self.z + 1 - self.c}

    def z_of(self, step):
        return lax.rem(self.z + step, self.depth)

    def over_grp(self, step):
        return {"grp": lax.rem(self.grp + step, 2 * self.depth)}

    def over_z(self, step):
        return {"grp": 2 * self.z_of(step) + self.c}

    def step_of(self, axis, step):
        if axis == "s":
            return self.shard(step)
        return self.z_of(step) if axis == "z" else 1 - self.own[axis]

    def others(self, axis):
        if axis == "z":
            return [self.over_z(step) for step in range(1, self.depth)]
        if axis == "s":
            return [self.over_seq(turn) for turn in (1, 2, 3)]
        return [self.over_seq({"x": 1, "y": 2}[axis])]

    def greet(self, beyond=True):
        peers = [self.over_seq(turn) for turn in (1, 2, 3)]
        if beyond:
            peers += [self.over_grp(step) for step in range(1, 2 * self.depth)]
        barrier = pltpu.get_barrier_semaphore()
        for peer in peers:
            pl.semaphore_signal(barrier, inc=1, device_id=peer, device_id_type=MESH)
        pl.semaphore_wait(barrier, len(peers))


def copy_to(source, target, sems, index, peer):
    send, recv = sems
    return pltpu.make_async_remote_copy(
        src_ref=source,
        dst_ref=target,
        send_sem=send.at[index],
        recv_sem=recv.at[index],
        device_id=peer,
        device_id_type=MESH,
    )


class Gather:
    def __init__(self, place, view, sems, base, order, own=None):
        self.at, self.view, self.sems, self.base, self.order = place, view, sems, base, order
        self.own = own

    def moves(self, stage):
        p = self.at
        done = self.order[:stage]
        where = [pl.ds(0, p.size[axis]) if axis in done else p.own[axis] for axis in "yxz"]
        region = self.view(*where, p.c)
        if stage == 3:
            return [(region, p.depth + 1, p.over_core())]
        base = sum(p.size[axis] - 1 for axis in done)
        return [(region, base + i, peer) for i, peer in enumerate(p.others(self.order[stage]))]

    def copies(self, stage):
        source = self.own if stage == 0 else None
        return [
            copy_to(r if source is None else source, r, self.sems, self.base + slot, peer)
            for r, slot, peer in self.moves(stage)
        ]

    def place_own(self, sem):
        p = self.at
        return pltpu.make_async_copy(self.own, self.view(p.y, p.x, p.z, p.c), sem)

    def step(self, stage):
        if stage:
            for made in self.copies(stage - 1):
                made.wait()
        if stage < 4:
            for made in self.copies(stage):
                made.start()


def gather_slots(depth):
    return depth + 2


def bind(ref, first, count):
    return lambda *i: ref.at[(pl.ds(first, count),) + i]


def bind_rows(ref, first, count):
    return lambda *i: ref.at[i + (pl.ds(first, count),)]


class Scatter:
    def __init__(self, place, view, out, bufs, sems, base, order, far=None):
        self.far = far or view
        self.at, self.view, self.out, self.sems, self.base, self.order = place, view, out, sems, base, order
        self.get_core, self.give, self.get, self.keep = bufs

    def plan(self, number):
        p = self.at
        axis = self.order[number]
        rest = [other for other in sorted(self.order) if other not in self.order[: number + 1]]
        combos = [{}]
        for other in rest:
            combos = [{**c, other: i} for c in combos for i in range(p.size[other])]
        first = 0
        for k in range(number):
            left = 1
            for other in self.order[k + 1 :]:
                left *= p.size[other]
            first += left * (p.size[self.order[k]] - 1)
        return axis, combos, first

    def kept(self, index):
        p = self.at
        linear = 0
        for axis in sorted(self.order):
            if axis != self.order[0]:
                linear = linear * p.size[axis] + index.get(axis, p.own[axis])
        return linear

    def now(self, number, index):
        p = self.at
        if number:
            return self.keep[self.kept(index)]
        where = {axis: index.get(axis, p.own[axis]) for axis in self.order}
        if "s" in where:
            where["y"], where["x"] = lax.div(where["s"], 2), lax.rem(where["s"], 2)
        where = [where[axis] for axis in "yxz"]
        lead = (slice(None),) * (len(self.get_core.shape) - 5)
        return self.view(*where, p.c)[...].astype(WIDE) + self.get_core[lead + tuple(where)].astype(WIDE)

    def copies(self, stage):
        p = self.at
        if stage == 0:
            source = self.far(pl.ds(0, 2), pl.ds(0, 2), pl.ds(0, p.depth), 1 - p.c)
            return [copy_to(source, self.get_core, self.sems, self.base, p.over_core())]
        axis, combos, first = self.plan(stage - 1)
        slot = 1 + sum(p.size[other] - 1 for other in self.order[: stage - 1])
        made = []
        for i, peer in enumerate(p.others(axis)):
            here = pl.ds(first + i * len(combos), len(combos))
            made.append(copy_to(self.give.at[here], self.get.at[here], self.sems, self.base + slot + i, peer))
        return made

    def step(self, stage):
        p = self.at
        last = len(self.order) + 1
        if stage:
            for made in self.copies(stage - 1):
                made.wait()
        if stage >= 2:
            axis, combos, first = self.plan(stage - 2)
            for k, index in enumerate(combos):
                total = self.keep[self.kept(index)]
                for i in range(p.size[axis] - 1):
                    total = total + self.get[first + i * len(combos) + k].astype(WIDE)
                if stage == last:
                    self.out(total)
                else:
                    self.keep[self.kept(index)] = total
        if 1 <= stage < last:
            axis, combos, first = self.plan(stage - 1)
            for i in range(p.size[axis] - 1):
                for k, index in enumerate(combos):
                    target = {**index, axis: p.step_of(axis, i + 1)}
                    self.give[first + i * len(combos) + k] = self.now(stage - 1, target).astype(LOW)
        if stage < last:
            for made in self.copies(stage):
                made.start()
        if stage == 1:
            axis, combos, first = self.plan(0)
            for index in combos:
                self.keep[self.kept(index)] = self.now(0, index)


def scatter_slots(depth):
    return depth + 3


def scatter_scratch(depth, order, shape):
    kept = {"z": 4, "s": depth}.get(order[0], 2 * depth)
    return [
        pltpu.VMEM(shape[:-2] + (2, 2, depth) + shape[-2:], LOW),
        pltpu.VMEM((4 * depth - 1,) + shape, LOW),
        pltpu.VMEM((4 * depth - 1,) + shape, LOW),
        pltpu.VMEM((kept,) + shape, WIDE),
    ]


class SumTile:
    def __init__(self, place, out, give, get, sems, base):
        self.at, self.out, self.give, self.get, self.sems, self.base = place, out, give, get, sems, base

    def copies(self, stage):
        p = self.at
        if stage == 0:
            moves = [(p.shard(turn), turn - 1, p.over_seq(turn)) for turn in (1, 2, 3)]
        else:
            moves = [(4, 2 + step, p.over_grp(step)) for step in range(1, 2 * p.depth)]
        return [
            copy_to(self.give.at[a], self.get.at[b], self.sems, self.base + b, peer) for a, b, peer in moves
        ]

    def step(self, stage):
        if stage:
            for made in self.copies(stage - 1):
                made.wait()
        if stage == 1:
            self.give[4] = (self.give[self.at.seq] + self.get[0]) + (self.get[1] + self.get[2])
        if stage == 2:
            total = self.give[4]
            for step in range(1, 2 * self.at.depth):
                total = total + self.get[2 + step]
            self.out[...] = total
            return
        for made in self.copies(stage):
            made.start()


def run(steps):
    for piece, stage in steps:
        piece.step(stage)


def skewed(pieces, stages):
    stages = list(stages)
    return [
        (piece, stages[slot - k])
        for slot in range(len(pieces) + len(stages) - 1)
        for k, piece in enumerate(pieces)
        if 0 <= slot - k < len(stages)
    ]


def unit_rows_of(values):
    centred = values - jnp.mean(values, axis=-1, keepdims=True)
    factor = lax.rsqrt(jnp.mean(centred * centred, axis=-1, keepdims=True) + NORM_EPSILON)
    return centred * factor, factor


def put_tiles(ref, here, value):
    for k in range(ref.shape[0]):
        ref[k, here, :] = value[:, 128 * k : 128 * (k + 1)]


def get_tiles(ref, here):
    return jnp.concatenate([ref[k, here, :] for k in range(ref.shape[0])], axis=1)


def hide_future(scores, first_slot, first_row):
    slot = lax.broadcasted_iota(jnp.int32, scores.shape, 0) + first_slot
    row = lax.broadcasted_iota(jnp.int32, scores.shape, 1) + first_row
    return jnp.where(3 * slot <= row, scores, MASKED_SCORE)


def span(number, size):
    return pl.ds(pl.multiple_of(number * size, size), size)


def front_kernel(depth, tok, wq, wm, wo, wu, wd, vec, *refs):
    early_out, late, down, vectors, edge, qh_out, kv_out, mixed_out, lse, attended = refs[:10]
    tiles, wide_a, low_a, qs, ms, kvt, own_late, own_down, tile, early, qh, kv, mixed = refs[10:23]
    gsend, grecv, xsend, xrecv, lsem, osem = refs[23:]
    p = Place(depth)
    own = (p.y, p.x, p.z, p.c)
    rows, width = tok.shape
    slots = rows // 3
    size = qh.shape[1]
    lanes = 2 * size
    shard_lanes = vec.shape[1]
    tile[...] = jnp.zeros_like(tile)
    tile[0 : vec.shape[0], 0:shard_lanes] = vec[...]
    tiles[own] = pltpu.roll(tile[...], p.grp * shard_lanes, 1).astype(LOW)
    early[(0,) + own] = wq[...].astype(LOW)
    for tap in range(3):
        for half in range(2):
            columns = []
            for head in range(4 * half, 4 * half + 4):
                columns.append(wm[tap, :, head * size : (head + 1) * size])
                columns.append(wm[tap, :, width + head * size : width + (head + 1) * size])
            early[(1 + 3 * half + tap,) + own] = jnp.concatenate(columns, axis=1).astype(LOW)
    own_late[0] = wo[...].astype(LOW)
    for part in range(4):
        own_late[1 + part] = wu[:, part * width : (part + 1) * width].astype(LOW)
    own_down[...] = wd[...].astype(LOW)
    p.greet()
    half_down = down.shape[4] // 2
    views = [
        (lambda *i: tiles.at[i], "zxy", None),
        (bind(early, 0, 1), "zxy", None),
        (bind(early, 1, 1), "zyx", None),
        (bind(early, 2, 1), "zxy", None),
        (bind(early, 3, 1), "yzx", None),
        (bind(early, 4, 1), "zyx", None),
        (bind(early, 5, 1), "xzy", None),
        (bind(early, 6, 1), "xyz", None),
        (bind(late, 0, 3), "xyz", own_late.at[pl.ds(0, 3)]),
        (bind(late, 3, 2), "yzx", own_late.at[pl.ds(3, 2)]),
        (bind_rows(down, 0, half_down), "xzy", own_down.at[pl.ds(0, half_down)]),
        (bind_rows(down, half_down, half_down), "yxz", own_down.at[pl.ds(half_down, half_down)]),
    ]
    step = gather_slots(depth)
    pieces = [
        Gather(p, view, (gsend, grecv), step * k, order, first) for k, (view, order, first) in enumerate(views)
    ]
    vector_piece, query_piece, soon, later = pieces[0], pieces[1], pieces[2:8], pieces[8:]
    for piece in pieces[:8]:
        piece.step(0)
    for k, piece in enumerate(later):
        piece.place_own(lsem.at[k]).start()
        piece.step(0)

    block = 128

    @pl.loop(0, rows // block)
    def _(number):
        at = pl.multiple_of(number * block, block)
        unit, _ = unit_rows_of(tok[pl.ds(at, block), :].astype(WIDE))
        put_tiles(wide_a, pl.ds(at + 8, block), unit)

    for stage in (1, 2):
        vector_piece.step(stage)
        query_piece.step(stage)
    for piece in soon[2:3] + soon[4:] + soon[:2] + soon[3:4]:
        piece.step(1)
    vector_piece.step(3)
    query_piece.step(3)
    vector_piece.step(4)
    tile_lanes = tiles.shape[-1]
    for y in range(2):
        for x in range(2):
            total = jnp.zeros(tiles.shape[-2:], WIDE)
            for z in range(depth):
                for c in range(2):
                    total += tiles[y, x, z, c].astype(WIDE)
            s = 2 * y + x
            vectors[:, s * tile_lanes : (s + 1) * tile_lanes] = total
    gain, shift = vectors[0:1, :], vectors[1:2, :]

    @pl.loop(0, rows // block)
    def _(number):
        at = pl.multiple_of(number * block, block)
        normed = (get_tiles(wide_a, pl.ds(at + 8, block)) * gain + shift).astype(LOW)
        low_a[pl.ds(at, block), :] = normed
        put_tiles(wide_a, pl.ds(at + 8, block), normed.astype(WIDE))

    def query_copy(half, turn):
        return copy_to(
            qs.at[half, p.shard(turn)],
            qh.at[half, :, span(p.seq, rows)],
            (xsend, xrecv),
            7 + 3 * half + turn - 1,
            p.over_seq(turn),
        )

    def send_queries(half):
        for turn in (1, 2, 3):
            query_copy(half, turn).start()
        qh[half, :, span(p.seq, rows)] = qs[half, p.seq]

    last = p.seq == 3

    def edge_copy():
        return copy_to(
            wide_a.at[:, pl.ds(rows, 8)], wide_a.at[:, pl.ds(0, 8)], (xsend, xrecv), 0, {"seq": lax.rem(p.seq + 1, 4)}
        )

    @pl.when(jnp.logical_not(last))
    def _():
        edge_copy().start()

    query_piece.step(4)
    turned = lax.dot_general(early[0].reshape(width, width).T, low_a[...], NT, preferred_element_type=WIDE)
    qs[...] = turned.astype(LOW).reshape(qs.shape)
    for piece in soon[5:] + soon[:2] + soon[3:4] + soon[2:3] + soon[4:5]:
        piece.step(2)
    send_queries(0)
    for k, piece in enumerate(later):
        piece.place_own(lsem.at[k]).wait()
        piece.step(1)
    for piece in soon:
        piece.step(3)
    for piece in later[:1] + later[3:]:
        piece.step(2)
    for piece in soon:
        piece.step(4)

    @pl.when(p.seq > 0)
    def _():
        edge_copy().wait_recv()

    @pl.when(jnp.logical_not(last))
    def _():
        edge_copy().wait_send()

    @pl.when(p.seq == 0)
    def _():
        wide_a[:, 0:8, :] = jnp.zeros((width // 128, 8, 128), WIDE)

    edge[...] = wide_a[:, 0:8, :]
    parts = rows // PART
    strips = qh.shape[2] // STRIP

    def early_leaves():
        return pltpu.make_async_copy(early, early_out, osem.at[0])

    def kv_leaves(half):
        return pltpu.make_async_copy(kv.at[half], kv_out.at[half], osem.at[1 + half])

    def qh_leaves(half):
        return pltpu.make_async_copy(qh.at[half], qh_out.at[half], osem.at[3 + half])

    def mixed_leaves(half, strip, index):
        here = span(strip, STRIP)
        return pltpu.make_async_copy(mixed.at[half, :, here], mixed_out.at[half, :, here], osem.at[index])

    def mixed_stays(half, part):
        return pltpu.make_async_copy(
            mixed.at[half, :, span(p.seq * parts + part, PART)],
            attended.at[half, p.seq, :, span(part, PART)],
            osem.at[5 + 2 * strips + half * parts + part],
        )

    early_leaves().start()

    def weight(j):
        return early[j].reshape(width, width)

    mine = span(p.seq, slots)

    def memory_copy(half, turn):
        return copy_to(
            ms.at[half, :, span(p.shard(turn), lanes)],
            kv.at[half, mine],
            (xsend, xrecv),
            1 + 3 * half + turn - 1,
            p.over_seq(turn),
        )

    def project(half):
        for tap in range(3):
            window = get_tiles(wide_a, pl.ds(6 + tap, slots, stride=3)).astype(LOW)
            part = dot(window, weight(1 + 3 * half + tap))
            total = part if tap == 0 else total + part
        ms[half] = total.astype(LOW)
        for turn in (3, 1, 2):
            memory_copy(half, turn).start()
        kv[half, mine, :] = ms[half, :, span(p.seq, lanes)]

    project(0)
    project(1)
    send_queries(1)
    for turn in (1, 2, 3):
        memory_copy(0, turn).wait()
    kvt[0] = kv[0].T
    kv_leaves(0).start()

    def mixed_copy(half, turn, part):
        shard = p.shard(turn)
        return copy_to(
            mixed.at[half, :, span(shard * parts + part, PART)],
            attended.at[half, p.seq, :, span(part, PART)],
            (xsend, xrecv),
            13 + (3 * half + turn - 1) * parts + part,
            p.over_seq(turn),
        )

    def attend(half, seen, strip):
        here = span(strip, STRIP)
        queries = qh[half, :, here] * jnp.bfloat16(size ** (-0.5))
        queries = jnp.concatenate([queries, jnp.zeros_like(queries)], axis=0)
        whole = seen - SLOTS
        scores = hide_future(dot(kv[half, whole:seen, :], queries), whole, strip * STRIP)
        if whole:
            scores = jnp.concatenate([dot(kv[half, 0:whole, :], queries), scores], axis=0)
        highest = jnp.max(scores, axis=0, keepdims=True)
        exponent = jnp.exp(scores - highest)
        summed = jnp.sum(exponent, axis=0, keepdims=True)
        out = dot(kvt[half, size:lanes, 0:seen], exponent.astype(LOW)) * (1.0 / summed)
        lse[half, strip] = highest + jnp.log(summed)
        mixed[half, :, here] = out.astype(LOW)

    def work(half):
        @pl.loop(0, strips)
        def _(it):
            for number, turn in ((1, 1), (3, 2), (4, 3)):

                @pl.when(it == number)
                def _():
                    query_copy(half, turn).wait()

            strip = p.strip(it)
            for group in range(strips):

                @pl.when(strip == group)
                def _():
                    attend(half, SLOTS * (group + 1), strip)

            mixed_leaves(half, strip, 5 + half * strips + it).start()
            for k in range(2):
                granule = 2 * strip + k
                shard, part = lax.div(granule, parts), lax.rem(granule, parts)
                turn = p.turn_to(shard)

                @pl.when(turn > 0)
                def _():
                    mixed_copy(half, turn, part).start()

                @pl.when(turn == 0)
                def _():
                    mixed_stays(half, part).start()

            @pl.when(it == (5, 3)[half])
            def _():
                for piece in later[1:3]:
                    piece.step(2 + half)

    work(0)
    for turn in (1, 2, 3):
        memory_copy(1, turn).wait()
    kvt[1] = kv[1].T
    kv_leaves(1).start()
    qh_leaves(0).start()
    work(1)
    qh_leaves(1).start()
    for piece in later[:1] + later[3:]:
        piece.step(3)
    for piece in later:
        piece.step(4)
    early_leaves().wait()
    for half in range(2):
        kv_leaves(half).wait()
        qh_leaves(half).wait()
        for it in range(strips):
            mixed_leaves(half, p.strip(it), 5 + half * strips + it).wait()
        for part in range(parts):
            mixed_stays(half, part).wait()
            for turn in (1, 2, 3):
                mixed_copy(half, turn, part).wait()


def front(tok, params):
    wq, wm, wo, wu, wd, vec = params
    groups = lax.axis_size("grp")
    depth = groups // 2
    rows, width = tok.shape
    own, slots, size = wq.shape[0], rows // 3, width // H
    lanes = 2 * size
    tile_lanes = vec.shape[1] * groups
    whole = (2, 2, depth, 2)
    sems = pltpu.SemaphoreType.DMA((12 * gather_slots(depth),))
    parts = rows // PART
    swaps = pltpu.SemaphoreType.DMA((13 + 6 * parts,))
    anywhere = pl.BlockSpec(memory_space=pl.ANY)
    vmem = pl.BlockSpec(memory_space=pltpu.VMEM)
    return pl.pallas_call(
        functools.partial(front_kernel, depth),
        out_shape=(
            shaped(EARLY, *whole, own, width),
            shaped(LATE, *whole, own, width),
            shaped(*whole, *wd.shape),
            shaped(ROWS, 4 * tile_lanes, kind=WIDE),
            shaped(width // 128, 8, 128, kind=WIDE),
            shaped(2, size, 4 * rows),
            shaped(2, 4 * slots, lanes),
            shaped(2, size, 4 * rows),
            shaped(2, 4 * rows // STRIP, 1, STRIP, kind=WIDE),
            shaped(2, 4, size, rows),
        ),
        in_specs=in_vmem(7),
        out_specs=[anywhere] * 3 + [vmem] * 2 + [anywhere] * 3 + [vmem, anywhere],
        scratch_shapes=[
            pltpu.VMEM((*whole, ROWS, tile_lanes), LOW),
            pltpu.VMEM((width // 128, rows + 8, 128), WIDE),
            pltpu.VMEM((rows, width), LOW),
            pltpu.VMEM((2, 4, size, rows), LOW),
            pltpu.VMEM((2, slots, width), LOW),
            pltpu.VMEM((2, lanes, 4 * slots), LOW),
            pltpu.VMEM((LATE, own, width), LOW),
            pltpu.VMEM(wd.shape, LOW),
            pltpu.VMEM((ROWS, tile_lanes), WIDE),
            pltpu.VMEM((EARLY, *whole, own, width), LOW),
            pltpu.VMEM((2, size, 4 * rows), LOW),
            pltpu.VMEM((2, 4 * slots, lanes), LOW),
            pltpu.VMEM((2, size, 4 * rows), LOW),
            sems,
            sems,
            swaps,
            swaps,
            pltpu.SemaphoreType.DMA((4,)),
            pltpu.SemaphoreType.DMA((5 + 2 * (4 * rows // STRIP) + 2 * parts,)),
        ],
        compiler_params=pltpu.CompilerParams(
            collective_id=0, has_side_effects=True, vmem_limit_bytes=58 * MEGA
        ),
    )(tok, wq, wm, wo, wu, wd, vec)


def middle_kernel(depth, tok_in, cot_in, att_in, late_in, down_in, vec, length, *refs):
    out_to, dres_to, doh, g_stack_to, g_down_to, g_vec = refs[:6]
    tok, cot, att, late, down, out, dres, g_stack, g_down = refs[6:15]
    zs, dus, cs, es, ys, dos, xsend, xrecv, isem, osem, gsem = refs[15:]
    p = Place(depth)
    arriving = [
        pltpu.make_async_copy(source, target, isem.at[k])
        for k, (source, target) in enumerate(
            ((att_in, att), (tok_in, tok), (late_in, late), (down_in, down), (cot_in, cot))
        )
    ]
    for made in arriving:
        made.start()
    p.greet(beyond=False)
    rows, width = tok.shape
    hidden = zs.shape[1]
    gain, shift, bias = vec[2:3, :], vec[3:4, :], vec[4:5, :]
    inner = 0.7978845608028654
    cubic = inner * 0.044715
    g_vec[...] = jnp.zeros_like(g_vec)

    parts = rows // PART

    def do_copy(number, turn):
        return copy_to(
            dos.at[:, p.shard(turn), :, span(number, PART)],
            doh.at[:, :, span(p.seq * parts + number, PART)],
            (xsend, xrecv),
            3 * number + turn - 1,
            p.over_seq(turn),
        )

    def leave(number):
        here = span(number, PART)
        pairs = (
            (out.at[here], out_to.at[here]),
            (dres.at[here], dres_to.at[here]),
            (dos.at[:, p.seq, :, here], doh.at[:, :, span(p.seq * parts + number, PART)]),
        )
        return [pltpu.make_async_copy(a, b, osem.at[3 * number + k]) for k, (a, b) in enumerate(pairs)]

    for made in arriving:
        made.wait()

    @pl.loop(0, parts)
    def _(number):
        at = pl.multiple_of(number * PART, PART)
        here = pl.ds(at, PART)
        attended = att[:, :, :, here].reshape(width, PART).T
        residual = tok[here, :].astype(WIDE) + dot(attended, late[0])
        unit, factor = unit_rows_of(residual)
        normed = (unit * gain + shift).astype(LOW)
        cs[here, :] = normed
        place = lax.broadcasted_iota(jnp.int32, (PART, 1), 0) + (p.seq * rows + at)
        live = (place < length[0, 0]).astype(WIDE)
        upstream = cot[here, :].astype(WIDE) * live
        upstream_low = upstream.astype(LOW)
        es[here, :] = upstream_low
        result = residual + bias
        back = jnp.zeros((PART, width), WIDE)
        for part in range(hidden // width):
            here_hidden = pl.ds(part * width, width)
            u = dot(normed, late[1 + part]) + vec[5 + part : 6 + part, :]
            square = u * u
            half = 0.5 + 0.5 * jnp.tanh(u * (inner + cubic * square))
            active = u * half
            slope = half + active * (1.0 - half) * (2.0 * inner + 6.0 * cubic * square)
            active_low = active.astype(LOW)
            zs[here, here_hidden] = active_low
            result += dot(active_low, down[here_hidden, :])
            pulled = lax.dot_general(upstream_low, down[here_hidden, :], NT, preferred_element_type=WIDE)
            grad = (pulled * slope).astype(LOW)
            dus[here, here_hidden] = grad
            g_vec[5 + part : 6 + part, :] += jnp.sum(grad.astype(WIDE), axis=0, keepdims=True)
            back += lax.dot_general(grad, late[1 + part], NT, preferred_element_type=WIDE)
        out[here, :] = result.astype(LOW)
        scaled = back * gain
        total = upstream + factor * (
            scaled
            - jnp.mean(scaled, axis=-1, keepdims=True)
            - unit * jnp.mean(scaled * unit, axis=-1, keepdims=True)
        )
        dres[here, :] = total
        branch = total.astype(LOW)
        ys[here, :] = branch
        turned = lax.dot_general(late[0], branch, NT, preferred_element_type=WIDE)
        dos[:, :, :, here] = turned.astype(LOW).reshape(dos.shape[:3] + (PART,))
        for turn in (3, 1, 2):
            do_copy(number, turn).start()
        for made in leave(number):
            made.start()
        g_vec[2:3, :] += jnp.sum(back * unit, axis=0, keepdims=True)
        g_vec[3:4, :] += jnp.sum(back, axis=0, keepdims=True)
        g_vec[4:5, :] += jnp.sum(upstream, axis=0, keepdims=True)

    def finished(ref, target, index):
        made = pltpu.make_async_copy(ref, target, gsem.at[index])
        made.start()
        return made

    left = []
    for part in range(hidden // width):
        piece = pl.ds(part * width, width)
        g_down[piece, :] = over_rows(zs[:, piece], es[...]).astype(LOW)
        left.append(finished(g_down.at[piece], g_down_to.at[piece], 5 + part))
    g_stack[0] = dot(att[...].reshape(width, rows), ys[...]).astype(LOW)
    left.append(finished(g_stack.at[0], g_stack_to.at[0], 0))
    for part in range(hidden // width):
        piece = pl.ds(part * width, width)
        g_stack[1 + part] = over_rows(cs[...], dus[:, piece]).astype(LOW)
        left.append(finished(g_stack.at[1 + part], g_stack_to.at[1 + part], 1 + part))
    for number in range(parts):
        for turn in (1, 2, 3):
            do_copy(number, turn).wait()
        for made in leave(number):
            made.wait()
    for made in left:
        made.wait()


def middle(tok, cot, att, late, down, vec, length):
    rows, width = tok.shape
    hidden = down.shape[0]
    sems = pltpu.SemaphoreType.DMA((3 * (rows // PART),))
    return pl.pallas_call(
        functools.partial(middle_kernel, lax.axis_size("grp") // 2),
        out_shape=(
            shaped(rows, width),
            shaped(rows, width, kind=WIDE),
            shaped(2, width // H, 4 * rows),
            shaped(LATE, width, width),
            shaped(hidden, width),
            shaped(*vec.shape, kind=WIDE),
        ),
        in_specs=[pl.BlockSpec(memory_space=pl.ANY)] * 5
        + [pl.BlockSpec(memory_space=pltpu.VMEM), pl.BlockSpec(memory_space=pltpu.SMEM)],
        out_specs=[pl.BlockSpec(memory_space=pl.ANY)] * 5 + [pl.BlockSpec(memory_space=pltpu.VMEM)],
        scratch_shapes=[pltpu.VMEM(x.shape, x.dtype) for x in (tok, cot, att, late, down)]
        + [
            pltpu.VMEM((rows, width), LOW),
            pltpu.VMEM((rows, width), WIDE),
            pltpu.VMEM((LATE, width, width), LOW),
            pltpu.VMEM((hidden, width), LOW),
            pltpu.VMEM((rows, hidden), LOW),
            pltpu.VMEM((rows, hidden), LOW),
            pltpu.VMEM((rows, width), LOW),
            pltpu.VMEM((rows, width), LOW),
            pltpu.VMEM((rows, width), LOW),
            pltpu.VMEM(att.shape, LOW),
            sems,
            sems,
            pltpu.SemaphoreType.DMA((5,)),
            sems,
            pltpu.SemaphoreType.DMA((LATE + hidden // width,)),
        ],
        compiler_params=pltpu.CompilerParams(
            collective_id=1, has_side_effects=True, vmem_limit_bytes=58 * MEGA
        ),
    )(tok, cot, att, late, down, vec, length)


def back_kernel(depth, *refs):
    far_inputs, (lse, vec, edge, g_vec) = refs[:9], refs[9:13]
    grad, out_early, out_late, out_down, out_vec = refs[13:18]
    scatter, refs = refs[18:54], refs[54:]
    near_inputs, refs = refs[:9], refs[9:]
    tok, kv, doh, qh, mixed, g_late, g_down, early, dres = near_inputs
    g_early, dkv, kvt, dqs, dq, dms, dm, wide_a, low_a, wide_da, da, after, give, get, out_sum = refs[:15]
    rsend, rrecv, xsend, xrecv, isem = refs[15:]
    p = Place(depth)
    arriving = [
        pltpu.make_async_copy(a, b, isem.at[k]) for k, (a, b) in enumerate(zip(far_inputs, near_inputs))
    ]
    for made in arriving:
        made.start()
    rows, width = tok.shape
    slots = rows // 3
    size = qh.shape[1]
    lanes = 2 * size
    scale = size ** (-0.5)
    parts = rows // PART
    strips = qh.shape[2] // STRIP
    step = scatter_slots(depth)
    p.greet()

    def out_to(ref, first, count):
        def put(value):
            ref[first : first + count] = value

        return put

    half_down = g_down.shape[4] // 2
    todo = [
        (bind(g_late, 0, 3), out_to(out_late, 0, 3), bind(far_inputs[5], 0, 3)),
        (bind(g_late, 3, 2), out_to(out_late, 3, 2), bind(far_inputs[5], 3, 2)),
        (bind_rows(g_down, 0, half_down), out_to(out_down, 0, half_down), bind_rows(far_inputs[6], 0, half_down)),
        (
            bind_rows(g_down, half_down, half_down),
            out_to(out_down, half_down, half_down),
            bind_rows(far_inputs[6], half_down, half_down),
        ),
        (bind(g_early, 0, 1), out_to(out_early, 0, 1), None),
        (bind(g_early, 1, 2), out_to(out_early, 1, 2), None),
        (bind(g_early, 3, 1), out_to(out_early, 3, 1), None),
        (bind(g_early, 4, 2), out_to(out_early, 4, 2), None),
        (bind(g_early, 6, 1), out_to(out_early, 6, 1), None),
    ]
    pieces = [
        Scatter(p, view, out, scatter[4 * k : 4 * k + 4], (rsend, rrecv), step * k, SCATTER_ORDERS[k], far)
        for k, (view, out, far) in enumerate(todo)
    ]
    soon, query, first, second = pieces[:4], pieces[4:5], pieces[5:7], pieces[7:]
    small = SumTile(p, out_vec, give, get, (rsend, rrecv), step * len(pieces))
    for piece in soon:
        piece.step(0)
    gain, shift = vec[0:1, :], vec[1:2, :]
    block = 128
    wide_a[:, 0:8, :] = edge[...]
    arriving[0].wait()

    @pl.loop(0, rows // block)
    def _(number):
        at = pl.multiple_of(number * block, block)
        unit, _ = unit_rows_of(tok[pl.ds(at, block), :].astype(WIDE))
        normed = (unit * gain + shift).astype(LOW)
        low_a[pl.ds(at, block), :] = normed
        put_tiles(wide_a, pl.ds(at + 8, block), normed.astype(WIDE))

    for made in arriving[1:5]:
        made.wait()
    for half in range(2):
        kvt[half] = kv[half].T
    dkv[...] = jnp.zeros_like(dkv)

    def dq_copy(half, turn, part):
        return copy_to(
            dqs.at[half, :, span(p.shard(turn) * parts + part, PART)],
            dq.at[half, p.seq, :, span(part, PART)],
            (xsend, xrecv),
            (3 * half + turn - 1) * parts + part,
            p.over_seq(turn),
        )

    def attend(half, seen, strip):
        here = span(strip, STRIP)
        queries = qh[half, :, here] * jnp.bfloat16(scale)
        incoming = doh[half, :, here]
        middle = jnp.sum(incoming.astype(WIDE) * mixed[half, :, here].astype(WIDE), axis=0, keepdims=True)
        blank = jnp.zeros_like(queries)
        queries = jnp.concatenate([queries, blank], axis=0)
        incoming = jnp.concatenate([blank, incoming], axis=0)
        total = lse[half, strip]
        turned = jnp.zeros((size, STRIP), WIDE)
        for start in range(0, seen, 2 * SLOTS):
            stop = min(start + 2 * SLOTS, seen)
            keys = kv[half, start:stop, :]
            scores = dot(keys, queries)
            if stop == seen:
                clear = stop - SLOTS - start
                masked = hide_future(scores[clear:], stop - SLOTS, strip * STRIP)
                scores = jnp.concatenate([scores[:clear], masked], axis=0) if clear else masked
            weights = jnp.exp(scores - total)
            slope = (weights * (dot(keys, incoming) - middle)).astype(LOW)
            dkv[half, start:stop, :] += lax.dot_general(
                slope, queries, NT, preferred_element_type=WIDE
            ) + lax.dot_general(weights.astype(LOW), incoming, NT, preferred_element_type=WIDE)
            turned += dot(kvt[half, 0:size, start:stop], slope)
        dqs[half, :, here] = (turned * scale).astype(LOW)

    def memory_copy(half, turn):
        return copy_to(
            dms.at[half, span(p.shard(turn), slots)],
            dm.at[half, :, span(p.seq, lanes)],
            (xsend, xrecv),
            6 * parts + 3 * half + turn - 1,
            p.over_seq(turn),
        )

    def send_memory(half):
        dms[half] = dkv[half].astype(LOW)
        for turn in (3, 1, 2):
            memory_copy(half, turn).start()
        dm[half, :, span(p.seq, lanes)] = dms[half, span(p.seq, slots), :]

    def put_early(j, value):
        g_early[j] = value.astype(LOW).reshape(g_early.shape[1:])

    def memory_gradient(half, tap):
        window = get_tiles(wide_a, pl.ds(6 + tap, slots, stride=3)).astype(LOW)
        put_early(1 + 3 * half + tap, over_rows(window, dm[half]))

    @pl.loop(0, 2 * strips)
    def _(turn_number):
        half, it = lax.div(turn_number, strips), lax.rem(turn_number, strips)

        @pl.when(turn_number == strips)
        def _():
            send_memory(0)

        @pl.when(turn_number == strips + 2)
        def _():
            for turn in (1, 2, 3):
                memory_copy(0, turn).wait()
            for tap in range(3):
                memory_gradient(0, tap)
            for piece in first:
                piece.step(0)

        strip = p.strip(strips - 1 - it)
        for group in range(strips):

            @pl.when(strip == group)
            def _():
                attend(half, SLOTS * (group + 1), strip)

        for k in range(2):
            granule = 2 * strip + k
            shard, part = lax.div(granule, parts), lax.rem(granule, parts)
            turn = p.turn_to(shard)

            @pl.when(turn > 0)
            def _():
                dq_copy(half, turn, part).start()

            @pl.when(turn == 0)
            def _():
                dq[half, p.seq, :, span(part, PART)] = dqs[half, :, span(granule, PART)]

        @pl.when(turn_number == 1)
        def _():
            for k in (5, 6):
                pltpu.make_async_copy(far_inputs[k], near_inputs[k], isem.at[k]).wait()

        for when, steps in (
            (1, [(piece, 1) for piece in soon]),
            (7, [(piece, 2) for piece in soon]),
            (9, [(piece, 1) for piece in first]),
            (10, [(piece, 3) for piece in soon]),
        ):

            @pl.when(turn_number == when)
            def _():
                run(steps)

    send_memory(1)
    for half in range(2):
        for turn in (1, 2, 3):
            for part in range(parts):
                dq_copy(half, turn, part).wait()
    for made in arriving[7:]:
        made.wait()
    turned = dq[...].reshape(width, rows)
    put_early(0, dot(turned, low_a[...]).T)
    query[0].step(0)
    da[...] = lax.dot_general(turned.T, early[0], NT, preferred_element_type=WIDE)
    query[0].step(1)
    run([(piece, 2) for piece in first])
    for turn in (1, 2, 3):
        memory_copy(1, turn).wait()
    for tap in range(3):
        memory_gradient(1, tap)
        if tap:
            second[tap - 1].step(0)
    wide_da[:, 0:8, :] = jnp.zeros((width // 128, 8, 128), WIDE)
    for tap in range(3):
        pulled = lax.dot_general(dm[0], early[1 + tap], NT, preferred_element_type=WIDE)
        pulled += lax.dot_general(dm[1], early[4 + tap], NT, preferred_element_type=WIDE)
        put_tiles(wide_da, pl.ds(6 + tap, slots, stride=3), pulled)

    def edge_copy():
        return copy_to(
            wide_da.at[:, pl.ds(0, 8)], after, (xsend, xrecv), 6 * parts + 6, {"seq": lax.rem(p.seq + 3, 4)}
        )

    @pl.when(p.seq > 0)
    def _():
        edge_copy().start()

    run([(piece, 1) for piece in second])
    run([(piece, 4) for piece in soon])
    run([(query[0], 2), (first[0], 3), (first[1], 3)])

    @pl.when(p.seq < 3)
    def _():
        edge_copy().wait_recv()

    @pl.when(p.seq > 0)
    def _():
        edge_copy().wait_send()

    @pl.when(p.seq == 3)
    def _():
        after[...] = jnp.zeros_like(after)

    wide_da[:, rows + 6 : rows + 8, :] = after[:, 6:8, :]
    out_sum[...] = g_vec[...]

    @pl.loop(0, rows // block)
    def _(number):
        at = pl.multiple_of(number * block, block)
        here = pl.ds(at, block)
        unit, factor = unit_rows_of(tok[here, :].astype(WIDE))
        upstream = da[here, :] + get_tiles(wide_da, pl.ds(at + 8, block))
        scaled = upstream * gain
        inward = factor * (
            scaled
            - jnp.mean(scaled, axis=-1, keepdims=True)
            - unit * jnp.mean(scaled * unit, axis=-1, keepdims=True)
        )
        grad[here, :] = (dres[here, :] + inward).astype(LOW)
        out_sum[0:1, :] += jnp.sum(upstream * unit, axis=0, keepdims=True)
        out_sum[1:2, :] += jnp.sum(upstream, axis=0, keepdims=True)

    tile_lanes = width // 4
    for shard in range(4):
        give[shard] = out_sum[:, shard * tile_lanes : (shard + 1) * tile_lanes]
    small.step(0)
    run([(piece, 2) for piece in second])
    small.step(1)
    run([(query[0], 3), (first[0], 4), (first[1], 4)])
    run([(piece, 3) for piece in second])
    small.step(2)


def back(saved, tok, dres, early, vec, edge, grads):
    qh, kv, mixed, lse, doh = saved
    g_late, g_down, g_vec = grads
    depth = lax.axis_size("grp") // 2
    rows, width = tok.shape
    size, slots = qh.shape[1], rows // 3
    lanes = 2 * size
    whole = (2, 2, depth, 2)
    own_down = g_down.shape[0] // (8 * depth)
    parts = rows // PART
    shapes = [(3, ROWS, width), (2, ROWS, width)] + [(own_down // 2, width)] * 2
    shapes += [(1, ROWS, width)] + [(2, ROWS, width), (1, ROWS, width)] * 2
    ring = pltpu.SemaphoreType.DMA((9 * scatter_slots(depth) + 2 * depth + 2,))
    swaps = pltpu.SemaphoreType.DMA((6 * parts + 7,))
    g_late = g_late.reshape(LATE, *whole, ROWS, width)
    g_down = g_down.reshape(*whole, own_down, width)
    inputs = (tok, kv, doh, qh, mixed, g_late, g_down, early, dres)
    return pl.pallas_call(
        functools.partial(back_kernel, depth),
        out_shape=(
            shaped(rows, width),
            shaped(EARLY, ROWS, width, kind=WIDE),
            shaped(LATE, ROWS, width, kind=WIDE),
            shaped(own_down, width, kind=WIDE),
            shaped(ROWS, width // 4, kind=WIDE),
        ),
        in_specs=[pl.BlockSpec(memory_space=pl.ANY)] * 9 + in_vmem(4),
        out_specs=in_vmem(5),
        scratch_shapes=[
            buf for order, shape in zip(SCATTER_ORDERS, shapes) for buf in scatter_scratch(depth, order, shape)
        ]
        + [pltpu.VMEM(x.shape, x.dtype) for x in inputs]
        + [
            pltpu.VMEM((EARLY, *whole, ROWS, width), LOW),
            pltpu.VMEM(kv.shape, WIDE),
            pltpu.VMEM((2, lanes, 4 * slots), LOW),
            pltpu.VMEM(qh.shape, LOW),
            pltpu.VMEM((2, 4, size, rows), LOW),
            pltpu.VMEM(kv.shape, LOW),
            pltpu.VMEM((2, slots, width), LOW),
            pltpu.VMEM((width // 128, rows + 8, 128), WIDE),
            pltpu.VMEM((rows, width), LOW),
            pltpu.VMEM((width // 128, rows + 8, 128), WIDE),
            pltpu.VMEM((rows, width), WIDE),
            pltpu.VMEM((width // 128, 8, 128), WIDE),
            pltpu.VMEM((5, ROWS, width // 4), WIDE),
            pltpu.VMEM((2 * depth + 2, ROWS, width // 4), WIDE),
            pltpu.VMEM(vec.shape, WIDE),
            ring,
            ring,
            swaps,
            swaps,
            pltpu.SemaphoreType.DMA((9,)),
        ],
        compiler_params=pltpu.CompilerParams(
            collective_id=2, has_side_effects=True, vmem_limit_bytes=62 * MEGA
        ),
    )(*inputs, lse, vec, edge, g_vec)


def update_kernel(*refs):
    weights, firsts, seconds = refs[0:6], refs[6:12], refs[12:18]
    early, late, down, vec = refs[18:22]
    held, outs, passed, kept, sems = refs[22:24], refs[24:48], refs[48:50], refs[50:52], refs[52]
    arriving = [pltpu.make_async_copy(held[k], kept[k], sems.at[k]) for k in range(2)]
    leaving = [pltpu.make_async_copy(kept[k], passed[k], sems.at[2 + k]) for k in range(2)]
    for made in arriving:
        made.start()
    width = early.shape[-1]

    def put(which, at, gradient):
        results = adamw(
            weights[which][at], gradient, firsts[which][at], seconds[which][at], LEARNING_RATES[which]
        )
        for group, value in enumerate(results):
            outs[6 * group + which][at] = value

    every = slice(None)
    put(0, (every, every), early[0])
    for k in range(2):
        arriving[k].wait()
        leaving[k].start()
    size = width // H
    for tap in range(3):
        for kind in range(2):
            columns = [
                early[1 + 3 * half + tap, :, (2 * s + kind) * size : (2 * s + kind + 1) * size]
                for half in range(2)
                for s in range(4)
            ]
            put(1, (tap, every, slice(kind * width, (kind + 1) * width)), jnp.concatenate(columns, axis=1))
    put(2, (every, every), late[0])
    for part in range(4):
        put(3, (every, slice(part * width, (part + 1) * width)), late[1 + part])
    put(4, (every, every), down[...])
    share = weights[5].shape[1]
    tile_lanes = vec.shape[1]
    tile = pltpu.roll(vec[...], lax.rem(tile_lanes - lax.axis_index("grp") * share, tile_lanes), 1)
    put(5, (every, every), tile[0 : weights[5].shape[0], 0:share])
    for made in leaving:
        made.wait()


def update(params, firsts, seconds, grads, held):
    outs = [jax.ShapeDtypeStruct(member.shape, WIDE) for member in params] * 3
    outs += [jax.ShapeDtypeStruct(member.shape, LOW) for member in params]
    return pl.pallas_call(
        update_kernel,
        out_shape=tuple(outs) + tuple(jax.ShapeDtypeStruct(x.shape, x.dtype) for x in held),
        in_specs=in_vmem(22) + [pl.BlockSpec(memory_space=pl.ANY)] * 2,
        out_specs=in_vmem(24) + [pl.BlockSpec(memory_space=pl.ANY)] * 2,
        scratch_shapes=[pltpu.VMEM(x.shape, x.dtype) for x in held] + [pltpu.SemaphoreType.DMA((4,))],
    )(*params, *firsts, *seconds, *grads, *held)


def fused(tokens, cotangent, lengths, *state):
    params, firsts, seconds = state[0:6], state[6:12], state[12:18]
    width = tokens.shape[2]
    tok, cot = tokens[0], cotangent[0]
    early, late, down, vec, edge, qh, kv, mixed, lse, attended = front(tok, params)
    early = early.reshape(EARLY, width, width)
    late = late.reshape(LATE, width, width)
    down = down.reshape(-1, width)
    out, dres, doh, g_late, g_down, g_vec = middle(
        tok, cot, attended, late, down, vec, lengths.reshape(1, 1)
    )
    grad, r_early, r_late, r_down, r_vec = back(
        (qh, kv, mixed, lse, doh), tok, dres, early, vec, edge, (g_late, g_down, g_vec)
    )
    *new, out, grad = update(params, firsts, seconds, (r_early, r_late, r_down, r_vec), (out, grad))
    return (out[None], grad[None], *new)


def body(*arguments):
    tokens, shard = arguments[0], arguments[3]
    whole_tiles = shard.shape[0] % ROWS == 0 and tokens.shape[1] % PART == 0
    four = lax.axis_size("seq") == 4 and lax.axis_size("grp") % 2 == 0
    return (fused if whole_tiles and four else plain)(*arguments)


def solution(mesh):
    in_specs = (
        P("grp", "seq", None),
        P("grp", "seq", None),
        P("grp"),
        P(("seq", "grp"), None),
        P(None, ("seq", "grp"), None),
        P(("seq", "grp"), None),
        P(("seq", "grp"), None),
        P(("seq", "grp"), None),
        P(None, ("seq", "grp")),
        P(("seq", "grp"), None),
        P(None, ("seq", "grp"), None),
        P(("seq", "grp"), None),
        P(("seq", "grp"), None),
        P(("seq", "grp"), None),
        P(None, ("seq", "grp")),
        P(("seq", "grp"), None),
        P(None, ("seq", "grp"), None),
        P(("seq", "grp"), None),
        P(("seq", "grp"), None),
        P(("seq", "grp"), None),
        P(None, ("seq", "grp")),
    )
    out_specs = (
        P("grp", "seq", None),
        P("grp", "seq", None),
        P(("seq", "grp"), None),
        P(None, ("seq", "grp"), None),
        P(("seq", "grp"), None),
        P(("seq", "grp"), None),
        P(("seq", "grp"), None),
        P(None, ("seq", "grp")),
        P(("seq", "grp"), None),
        P(None, ("seq", "grp"), None),
        P(("seq", "grp"), None),
        P(("seq", "grp"), None),
        P(("seq", "grp"), None),
        P(None, ("seq", "grp")),
        P(("seq", "grp"), None),
        P(None, ("seq", "grp"), None),
        P(("seq", "grp"), None),
        P(("seq", "grp"), None),
        P(("seq", "grp"), None),
        P(None, ("seq", "grp")),
        P(("seq", "grp"), None),
        P(None, ("seq", "grp"), None),
        P(("seq", "grp"), None),
        P(("seq", "grp"), None),
        P(("seq", "grp"), None),
        P(None, ("seq", "grp")),
    )
    return jax.shard_map(body, mesh=mesh, in_specs=in_specs, out_specs=out_specs, check_vma=False)
```

```python
import functools

import jax
import jax.numpy as jnp
from jax import lax
from jax.experimental import pallas as pl
from jax.experimental.pallas import tpu as pltpu
from jax.sharding import PartitionSpec as P

H = 8
STEP = 10


NORM_EPSILON = 1e-05
BETA_FIRST = 0.9
BETA_SECOND = 0.95
ADAM_EPSILON = 1e-08
WEIGHT_DECAY = 0.1
LEARNING_RATES = (0.05, 0.04, 0.3, 0.05, 0.03, 0.5)
MASKED_SCORE = -1e30
NT = (((1,), (1,)), ((), ()))


def from_behind(x, axis, by):
    peers = lax.axis_size(axis)
    pairs = [(i, i + by) for i in range(peers) if 0 <= i + by < peers]
    return lax.ppermute(x, axis, pairs)


def matmul(left, right):
    return jnp.dot(left, right, preferred_element_type=jnp.float32)


def over_rows(left, right):
    return lax.dot_general(
        left, right, (((0,), (0,)), ((), ())), preferred_element_type=jnp.float32
    )


def against(left, right):
    return lax.dot_general(
        left, right, (((1,), (1,)), ((), ())), preferred_element_type=jnp.float32
    )


def norm_forward(values, gain, shift):
    centred = values - jnp.mean(values, axis=-1, keepdims=True)
    factor = lax.rsqrt(jnp.mean(centred * centred, axis=-1, keepdims=True) + NORM_EPSILON)
    unit_rows = centred * factor
    return (unit_rows * gain + shift, unit_rows, factor)


def norm_backward(upstream, unit_rows, factor, gain):
    scaled = upstream * gain
    inward = factor * (
        scaled
        - jnp.mean(scaled, axis=-1, keepdims=True)
        - unit_rows * jnp.mean(scaled * unit_rows, axis=-1, keepdims=True)
    )
    return (inward, jnp.sum(upstream * unit_rows, axis=0), jnp.sum(upstream, axis=0))


def masked_scores(query_tile_rows, key_row_block, positions):
    slot_starts = 3 * jnp.arange(key_row_block.shape[0], dtype=jnp.int32)
    score_matrix = jnp.einsum(
        "azv,lzv->zal", query_tile_rows, key_row_block, preferred_element_type=jnp.float32
    ) * query_tile_rows.shape[2] ** (-0.5)
    visible = slot_starts[None, :] <= positions[:, None]
    return jnp.where(visible[None], score_matrix, MASKED_SCORE)


def attend_forward(queries, key_row_block, value_row_block, anchor, block_rows):
    block_count = queries.shape[0] // block_rows
    offsets = block_rows * jnp.arange(block_count, dtype=jnp.int32)

    def attend_block(inputs):
        query_tile_rows, offset_rows = inputs
        score_matrix = masked_scores(
            query_tile_rows,
            key_row_block,
            anchor + offset_rows + jnp.arange(block_rows, dtype=jnp.int32),
        )
        highest = jnp.max(score_matrix, axis=-1, keepdims=True)
        exponent = jnp.exp(score_matrix - highest)
        summed = jnp.sum(exponent, axis=-1, keepdims=True)
        reduced_weights = (exponent / summed).astype(jnp.bfloat16)
        mixed = jnp.einsum(
            "yup,pyb->uyb", reduced_weights, value_row_block, preferred_element_type=jnp.float32
        )
        return (mixed, (highest + jnp.log(summed))[..., 0])

    blocks_in = queries.reshape(block_count, block_rows, queries.shape[1], queries.shape[2])
    mixed, logsum = lax.map(attend_block, (blocks_in, offsets))
    return (mixed.reshape(queries.shape), logsum)


def attend_backward(queries, key_row_block, value_row_block, upstream, logsum, anchor, block_rows):
    block_count = queries.shape[0] // block_rows
    offsets = block_rows * jnp.arange(block_count, dtype=jnp.int32)
    scale_factor = queries.shape[2] ** (-0.5)

    def attend_back(carry, inputs):
        grad_keys, grad_values = carry
        query_tile_rows, incoming_gradient_rows, logsum_block, offset_rows = inputs
        score_matrix = masked_scores(
            query_tile_rows,
            key_row_block,
            anchor + offset_rows + jnp.arange(block_rows, dtype=jnp.int32),
        )
        weights_soft = jnp.exp(score_matrix - logsum_block[..., None])
        grad_weights = jnp.einsum(
            "azv,lzv->zal",
            incoming_gradient_rows,
            value_row_block,
            preferred_element_type=jnp.float32,
        )
        centre = jnp.sum(weights_soft * grad_weights, axis=-1, keepdims=True)
        score_gradient = (weights_soft * (grad_weights - centre)).astype(jnp.bfloat16)
        grad_query = (
            jnp.einsum(
                "yup,pyb->uyb", score_gradient, key_row_block, preferred_element_type=jnp.float32
            )
            * scale_factor
        )
        grad_keys = (
            grad_keys
            + jnp.einsum(
                "xof,oxa->fxa", score_gradient, query_tile_rows, preferred_element_type=jnp.float32
            )
            * scale_factor
        )
        grad_values = grad_values + jnp.einsum(
            "xof,oxa->fxa",
            weights_soft.astype(jnp.bfloat16),
            incoming_gradient_rows,
            preferred_element_type=jnp.float32,
        )
        return ((grad_keys, grad_values), grad_query)

    shape_blocks = (block_count, block_rows, queries.shape[1], queries.shape[2])
    zeros_init = jnp.zeros(key_row_block.shape, jnp.float32)
    (grad_keys, grad_values), grad_query = lax.scan(
        attend_back,
        (zeros_init, zeros_init),
        (queries.reshape(shape_blocks), upstream.reshape(shape_blocks), logsum, offsets),
    )
    return (grad_query.reshape(queries.shape), grad_keys, grad_values)


def adamw(weight, gradient, moment, square, step_rate):
    moment_new = BETA_FIRST * moment + (1.0 - BETA_FIRST) * gradient
    square_new = BETA_SECOND * square + (1.0 - BETA_SECOND) * gradient * gradient
    fixed_first = 1.0 - BETA_FIRST**STEP
    fixed_second = 1.0 - BETA_SECOND**STEP
    update = (
        moment_new / fixed_first / (jnp.sqrt(square_new / fixed_second) + ADAM_EPSILON)
        + WEIGHT_DECAY * weight
    )
    master = weight - step_rate * update
    return (moment_new, square_new, master, master.astype(jnp.bfloat16))


def plain(
    tokens,
    cotangent,
    lengths,
    weight_query,
    weight_memory,
    weight_out,
    weight_up,
    weight_down,
    vectors,
    first_query,
    first_memory,
    first_out,
    first_up,
    first_down,
    first_vectors,
    second_query,
    second_memory,
    second_out,
    second_up,
    second_down,
    second_vectors,
):
    gathered = (
        lax.all_gather(weight_query.astype(jnp.bfloat16), ("seq", "grp"), axis=0, tiled=True),
        lax.all_gather(weight_memory.astype(jnp.bfloat16), ("seq", "grp"), axis=1, tiled=True),
        lax.all_gather(weight_out.astype(jnp.bfloat16), ("seq", "grp"), axis=0, tiled=True),
        lax.all_gather(weight_up.astype(jnp.bfloat16), ("seq", "grp"), axis=0, tiled=True),
        lax.all_gather(weight_down.astype(jnp.bfloat16), ("seq", "grp"), axis=0, tiled=True),
        lax.all_gather(vectors.astype(jnp.bfloat16), ("seq", "grp"), axis=1, tiled=True),
    )
    query_w, memory_w, out_w, up_w, down_w, vector_low = gathered
    vector_rows = vector_low.astype(jnp.float32)
    model_width = query_w.shape[0]
    hidden_units = up_w.shape[1]
    head_size = model_width // H
    seq_count = lax.axis_size("seq")
    seq_index = lax.axis_index("seq")
    local_rows = tokens.shape[1]
    local_slots = local_rows // 3
    inputs = tokens[0].astype(jnp.float32)
    normed, unit_one, factor_one = norm_forward(inputs, vector_rows[0], vector_rows[1])
    normed_low = normed.astype(jnp.bfloat16)
    queries = matmul(normed_low, query_w).astype(jnp.bfloat16)
    borrowed = from_behind(normed_low[local_rows - 2 :], "seq", 1)
    extended = jnp.concatenate([borrowed, normed_low], axis=0)
    windows = extended[:local_rows].reshape(local_slots, 3 * model_width)
    memory_flat = memory_w.reshape(3 * model_width, 2 * model_width)
    memory = matmul(windows, memory_flat).astype(jnp.bfloat16)
    share_width = model_width // seq_count
    local_heads = H // seq_count
    head_queries, head_memory = (
        lax.all_to_all(
            queries.reshape(local_rows, 1, seq_count, share_width),
            "seq",
            split_axis=2,
            concat_axis=0,
            tiled=True,
        ),
        lax.all_to_all(
            memory.reshape(local_slots, 2, seq_count, share_width),
            "seq",
            split_axis=2,
            concat_axis=0,
            tiled=True,
        ),
    )
    total_rows = head_queries.shape[0]
    total_slots = head_memory.shape[0]
    query_heads = head_queries.reshape(total_rows, local_heads, head_size)
    key_heads = head_memory[:, 0].reshape(total_slots, local_heads, head_size)
    value_heads = head_memory[:, 1].reshape(total_slots, local_heads, head_size)
    block_rows = min(512, total_rows)
    mixed, logsum = attend_forward(query_heads, key_heads, value_heads, 0, block_rows)
    mixed_low = mixed.astype(jnp.bfloat16).reshape(total_rows, 1, share_width)
    attended = lax.all_to_all(mixed_low, "seq", split_axis=0, concat_axis=1, tiled=True).reshape(
        local_rows, model_width
    )
    residual = inputs + matmul(attended, out_w)
    normed_two, unit_two, factor_two = norm_forward(residual, vector_rows[2], vector_rows[3])
    normed_two_low = normed_two.astype(jnp.bfloat16)
    pre_act = matmul(normed_two_low, up_w) + vector_rows[5:].reshape(hidden_units)
    activated, gelu_pull = jax.vjp(jax.nn.gelu, pre_act)
    activated_low = activated.astype(jnp.bfloat16)
    result = residual + matmul(activated_low, down_w) + vector_rows[4]
    positions = seq_index * local_rows + jnp.arange(local_rows, dtype=jnp.int32)
    live_mask = (positions < lengths[0]).astype(jnp.float32)
    grad_out = cotangent[0].astype(jnp.float32) * live_mask[:, None]
    grad_out_low = grad_out.astype(jnp.bfloat16)
    grad_down = over_rows(activated_low, grad_out_low)
    grad_activated = against(grad_out_low, down_w)
    grad_pre_low = gelu_pull(grad_activated)[0].astype(jnp.bfloat16)
    grad_up = over_rows(normed_two_low, grad_pre_low)
    grad_up_bias = jnp.sum(grad_pre_low.astype(jnp.float32), axis=0)
    grad_normed_two = against(grad_pre_low, up_w)
    grad_norm_two, grad_gain_two, grad_shift_two = norm_backward(
        grad_normed_two, unit_two, factor_two, vector_rows[2]
    )
    grad_residual = grad_out + grad_norm_two
    grad_branch_low = grad_residual.astype(jnp.bfloat16)
    grad_outw = over_rows(attended, grad_branch_low)
    grad_attended_low = against(grad_branch_low, out_w).astype(jnp.bfloat16)
    grad_heads = lax.all_to_all(
        grad_attended_low.reshape(local_rows, 1, seq_count, share_width),
        "seq",
        split_axis=2,
        concat_axis=0,
        tiled=True,
    ).reshape(total_rows, local_heads, head_size)
    grad_q, grad_k, grad_v = attend_backward(
        query_heads, key_heads, value_heads, grad_heads, logsum, 0, block_rows
    )
    packed = (
        jnp.stack([grad_k, grad_v], axis=1)
        .astype(jnp.bfloat16)
        .reshape(total_slots, 2, 1, share_width)
    )
    token_queries, token_memory = (
        lax.all_to_all(
            grad_q.astype(jnp.bfloat16).reshape(total_rows, 1, 1, share_width),
            "seq",
            split_axis=0,
            concat_axis=2,
            tiled=True,
        ),
        lax.all_to_all(packed, "seq", split_axis=0, concat_axis=2, tiled=True),
    )
    grad_queries_low = token_queries.reshape(local_rows, model_width)
    grad_memory_low = token_memory.reshape(local_slots, 2 * model_width)
    grad_queryw = over_rows(normed_low, grad_queries_low)
    grad_normed = against(grad_queries_low, query_w)
    grad_memoryw = over_rows(windows, grad_memory_low).reshape(3, model_width, 2 * model_width)
    grad_windows = against(grad_memory_low, memory_flat).reshape(local_rows, model_width)
    returned = from_behind(grad_windows[:2], "seq", -1)
    grad_normed = grad_normed + jnp.concatenate([grad_windows[2:], returned], axis=0)
    grad_norm_one, grad_gain_one, grad_shift_one = norm_backward(
        grad_normed, unit_one, factor_one, vector_rows[0]
    )
    grad_inputs = (grad_residual + grad_norm_one).astype(jnp.bfloat16)
    grad_vector_rows = jnp.concatenate(
        [
            jnp.stack(
                [
                    grad_gain_one,
                    grad_shift_one,
                    grad_gain_two,
                    grad_shift_two,
                    jnp.sum(grad_out, axis=0),
                ]
            ),
            grad_up_bias.reshape(4, model_width),
        ],
        axis=0,
    )
    reduced = (
        lax.psum_scatter(grad_queryw, ("seq", "grp"), scatter_dimension=0, tiled=True),
        lax.psum_scatter(grad_memoryw, ("seq", "grp"), scatter_dimension=1, tiled=True),
        lax.psum_scatter(grad_outw, ("seq", "grp"), scatter_dimension=0, tiled=True),
        lax.psum_scatter(grad_up, ("seq", "grp"), scatter_dimension=0, tiled=True),
        lax.psum_scatter(grad_down, ("seq", "grp"), scatter_dimension=0, tiled=True),
        lax.psum_scatter(grad_vector_rows, ("seq", "grp"), scatter_dimension=1, tiled=True),
    )
    new_query = adamw(weight_query, reduced[0], first_query, second_query, LEARNING_RATES[0])
    new_memory = adamw(weight_memory, reduced[1], first_memory, second_memory, LEARNING_RATES[1])
    new_out = adamw(weight_out, reduced[2], first_out, second_out, LEARNING_RATES[2])
    new_up = adamw(weight_up, reduced[3], first_up, second_up, LEARNING_RATES[3])
    new_down = adamw(weight_down, reduced[4], first_down, second_down, LEARNING_RATES[4])
    new_vectors = adamw(vectors, reduced[5], first_vectors, second_vectors, LEARNING_RATES[5])
    return (
        result.astype(jnp.bfloat16)[None],
        grad_inputs[None],
        new_query[0],
        new_memory[0],
        new_out[0],
        new_up[0],
        new_down[0],
        new_vectors[0],
        new_query[1],
        new_memory[1],
        new_out[1],
        new_up[1],
        new_down[1],
        new_vectors[1],
        new_query[2],
        new_memory[2],
        new_out[2],
        new_up[2],
        new_down[2],
        new_vectors[2],
        new_query[3],
        new_memory[3],
        new_out[3],
        new_up[3],
        new_down[3],
        new_vectors[3],
    )


MESH = pl.DeviceIdType.MESH
LOW, WIDE = jnp.bfloat16, jnp.float32
ROWS = 16
PART = 384
STRIP = 2 * PART
SLOTS = STRIP // 3
EARLY = 7
LATE = 5
MEGA = 1024 * 1024
SCATTER_ORDERS = ("yzx", "xyz", "zxy", "xyz", "sz", "xyz", "yzx", "sz", "sz")


def in_vmem(count):
    return [pl.BlockSpec(memory_space=pltpu.VMEM)] * count


def shaped(*shape, kind=jnp.bfloat16):
    return jax.ShapeDtypeStruct(shape, kind)


def dot(left, right):
    return jnp.dot(left, right, preferred_element_type=jnp.float32)


def differ(bit, other):
    return bit + other - 2 * bit * other


class Place:
    def __init__(self, depth):
        self.seq, self.grp = lax.axis_index("seq"), lax.axis_index("grp")
        self.depth = depth
        self.y, self.x = lax.div(self.seq, 2), lax.rem(self.seq, 2)
        self.z, self.c = lax.div(self.grp, 2), lax.rem(self.grp, 2)
        self.own = {"y": self.y, "x": self.x, "z": self.z, "s": self.seq}
        self.size = {"y": 2, "x": 2, "z": depth, "s": 4}

    def turn_to(self, shard):
        return 2 * differ(self.y, lax.div(shard, 2)) + differ(self.x, lax.rem(shard, 2))

    def strip(self, it):
        half, pos = differ(lax.div(it, 3), self.y), lax.rem(it, 3)
        return 3 * half + pos + self.x * (2 - 2 * pos)

    def shard(self, turn):
        return 2 * differ(self.y, lax.div(turn, 2)) + differ(self.x, lax.rem(turn, 2))

    def over_seq(self, turn):
        return {"seq": self.shard(turn)}

    def over_core(self):
        return {"grp": 2 * self.z + 1 - self.c}

    def z_of(self, step):
        return lax.rem(self.z + step, self.depth)

    def over_grp(self, step):
        return {"grp": lax.rem(self.grp + step, 2 * self.depth)}

    def over_z(self, step):
        return {"grp": 2 * self.z_of(step) + self.c}

    def step_of(self, axis, step):
        if axis == "s":
            return self.shard(step)
        return self.z_of(step) if axis == "z" else 1 - self.own[axis]

    def others(self, axis):
        if axis == "z":
            return [self.over_z(step) for step in range(1, self.depth)]
        if axis == "s":
            return [self.over_seq(turn) for turn in (1, 2, 3)]
        return [self.over_seq({"x": 1, "y": 2}[axis])]

    def greet(self, beyond=True):
        peers = [self.over_seq(turn) for turn in (1, 2, 3)]
        if beyond:
            peers += [self.over_grp(step) for step in range(1, 2 * self.depth)]
        barrier = pltpu.get_barrier_semaphore()
        for peer in peers:
            pl.semaphore_signal(barrier, inc=1, device_id=peer, device_id_type=MESH)
        pl.semaphore_wait(barrier, len(peers))


def copy_to(source, target, sems, index, peer):
    send, recv = sems
    return pltpu.make_async_remote_copy(
        src_ref=source,
        dst_ref=target,
        send_sem=send.at[index],
        recv_sem=recv.at[index],
        device_id=peer,
        device_id_type=MESH,
    )


class Gather:
    def __init__(self, place, view, sems, base, order, own=None):
        self.at, self.view, self.sems, self.base, self.order = place, view, sems, base, order
        self.own = own

    def moves(self, stage):
        p = self.at
        done = self.order[:stage]
        where = [pl.ds(0, p.size[axis]) if axis in done else p.own[axis] for axis in "yxz"]
        region = self.view(*where, p.c)
        if stage == 3:
            return [(region, p.depth + 1, p.over_core())]
        base = sum(p.size[axis] - 1 for axis in done)
        return [(region, base + i, peer) for i, peer in enumerate(p.others(self.order[stage]))]

    def copies(self, stage):
        source = self.own if stage == 0 else None
        return [
            copy_to(r if source is None else source, r, self.sems, self.base + slot, peer)
            for r, slot, peer in self.moves(stage)
        ]

    def place_own(self, sem):
        p = self.at
        return pltpu.make_async_copy(self.own, self.view(p.y, p.x, p.z, p.c), sem)

    def step(self, stage):
        if stage:
            for made in self.copies(stage - 1):
                made.wait()
        if stage < 4:
            for made in self.copies(stage):
                made.start()


def gather_slots(depth):
    return depth + 2


def bind(ref, first, count):
    return lambda *i: ref.at[(pl.ds(first, count),) + i]


def bind_rows(ref, first, count):
    return lambda *i: ref.at[i + (pl.ds(first, count),)]


class Scatter:
    def __init__(self, place, view, out, bufs, sems, base, order, far=None):
        self.far = far or view
        self.at, self.view, self.out, self.sems, self.base, self.order = place, view, out, sems, base, order
        self.get_core, self.give, self.get, self.keep = bufs

    def plan(self, number):
        p = self.at
        axis = self.order[number]
        rest = [other for other in sorted(self.order) if other not in self.order[: number + 1]]
        combos = [{}]
        for other in rest:
            combos = [{**c, other: i} for c in combos for i in range(p.size[other])]
        first = 0
        for k in range(number):
            left = 1
            for other in self.order[k + 1 :]:
                left *= p.size[other]
            first += left * (p.size[self.order[k]] - 1)
        return axis, combos, first

    def kept(self, index):
        p = self.at
        linear = 0
        for axis in sorted(self.order):
            if axis != self.order[0]:
                linear = linear * p.size[axis] + index.get(axis, p.own[axis])
        return linear

    def now(self, number, index):
        p = self.at
        if number:
            return self.keep[self.kept(index)]
        where = {axis: index.get(axis, p.own[axis]) for axis in self.order}
        if "s" in where:
            where["y"], where["x"] = lax.div(where["s"], 2), lax.rem(where["s"], 2)
        where = [where[axis] for axis in "yxz"]
        lead = (slice(None),) * (len(self.get_core.shape) - 5)
        return self.view(*where, p.c)[...].astype(WIDE) + self.get_core[lead + tuple(where)].astype(WIDE)

    def copies(self, stage):
        p = self.at
        if stage == 0:
            source = self.far(pl.ds(0, 2), pl.ds(0, 2), pl.ds(0, p.depth), 1 - p.c)
            return [copy_to(source, self.get_core, self.sems, self.base, p.over_core())]
        axis, combos, first = self.plan(stage - 1)
        slot = 1 + sum(p.size[other] - 1 for other in self.order[: stage - 1])
        made = []
        for i, peer in enumerate(p.others(axis)):
            here = pl.ds(first + i * len(combos), len(combos))
            made.append(copy_to(self.give.at[here], self.get.at[here], self.sems, self.base + slot + i, peer))
        return made

    def step(self, stage):
        p = self.at
        last = len(self.order) + 1
        if stage:
            for made in self.copies(stage - 1):
                made.wait()
        if stage >= 2:
            axis, combos, first = self.plan(stage - 2)
            for k, index in enumerate(combos):
                total = self.keep[self.kept(index)]
                for i in range(p.size[axis] - 1):
                    total = total + self.get[first + i * len(combos) + k].astype(WIDE)
                if stage == last:
                    self.out(total)
                else:
                    self.keep[self.kept(index)] = total
        if 1 <= stage < last:
            axis, combos, first = self.plan(stage - 1)
            for i in range(p.size[axis] - 1):
                for k, index in enumerate(combos):
                    target = {**index, axis: p.step_of(axis, i + 1)}
                    self.give[first + i * len(combos) + k] = self.now(stage - 1, target).astype(LOW)
        if stage < last:
            for made in self.copies(stage):
                made.start()
        if stage == 1:
            axis, combos, first = self.plan(0)
            for index in combos:
                self.keep[self.kept(index)] = self.now(0, index)


def scatter_slots(depth):
    return depth + 3


def scatter_scratch(depth, order, shape):
    kept = {"z": 4, "s": depth}.get(order[0], 2 * depth)
    return [
        pltpu.VMEM(shape[:-2] + (2, 2, depth) + shape[-2:], LOW),
        pltpu.VMEM((4 * depth - 1,) + shape, LOW),
        pltpu.VMEM((4 * depth - 1,) + shape, LOW),
        pltpu.VMEM((kept,) + shape, WIDE),
    ]


class SumTile:
    def __init__(self, place, out, give, get, sems, base):
        self.at, self.out, self.give, self.get, self.sems, self.base = place, out, give, get, sems, base

    def copies(self, stage):
        p = self.at
        if stage == 0:
            moves = [(p.shard(turn), turn - 1, p.over_seq(turn)) for turn in (1, 2, 3)]
        else:
            moves = [(4, 2 + step, p.over_grp(step)) for step in range(1, 2 * p.depth)]
        return [
            copy_to(self.give.at[a], self.get.at[b], self.sems, self.base + b, peer) for a, b, peer in moves
        ]

    def step(self, stage):
        if stage:
            for made in self.copies(stage - 1):
                made.wait()
        if stage == 1:
            self.give[4] = (self.give[self.at.seq] + self.get[0]) + (self.get[1] + self.get[2])
        if stage == 2:
            total = self.give[4]
            for step in range(1, 2 * self.at.depth):
                total = total + self.get[2 + step]
            self.out[...] = total
            return
        for made in self.copies(stage):
            made.start()


def run(steps):
    for piece, stage in steps:
        piece.step(stage)


def skewed(pieces, stages):
    stages = list(stages)
    return [
        (piece, stages[slot - k])
        for slot in range(len(pieces) + len(stages) - 1)
        for k, piece in enumerate(pieces)
        if 0 <= slot - k < len(stages)
    ]


def unit_rows_of(values):
    centred = values - jnp.mean(values, axis=-1, keepdims=True)
    factor = lax.rsqrt(jnp.mean(centred * centred, axis=-1, keepdims=True) + NORM_EPSILON)
    return centred * factor, factor


def put_tiles(ref, here, value):
    for k in range(ref.shape[0]):
        ref[k, here, :] = value[:, 128 * k : 128 * (k + 1)]


def get_tiles(ref, here):
    return jnp.concatenate([ref[k, here, :] for k in range(ref.shape[0])], axis=1)


def hide_future(scores, first_slot, first_row):
    slot = lax.broadcasted_iota(jnp.int32, scores.shape, 0) + first_slot
    row = lax.broadcasted_iota(jnp.int32, scores.shape, 1) + first_row
    return jnp.where(3 * slot <= row, scores, MASKED_SCORE)


def span(number, size):
    return pl.ds(pl.multiple_of(number * size, size), size)


def front_kernel(depth, tok, wq, wm, wo, wu, wd, vec, *refs):
    early_out, late, down, vectors, edge, qh_out, kv_out, mixed_out, lse, attended = refs[:10]
    tiles, wide_a, low_a, qs, ms, kvt, own_late, own_down, tile, early, qh, kv, mixed = refs[10:23]
    gsend, grecv, xsend, xrecv, lsem, osem = refs[23:]
    p = Place(depth)
    own = (p.y, p.x, p.z, p.c)
    rows, width = tok.shape
    slots = rows // 3
    size = qh.shape[1]
    lanes = 2 * size
    shard_lanes = vec.shape[1]
    tile[...] = jnp.zeros_like(tile)
    tile[0 : vec.shape[0], 0:shard_lanes] = vec[...]
    tiles[own] = pltpu.roll(tile[...], p.grp * shard_lanes, 1).astype(LOW)
    early[(0,) + own] = wq[...].astype(LOW)
    for tap in range(3):
        for half in range(2):
            columns = []
            for head in range(4 * half, 4 * half + 4):
                columns.append(wm[tap, :, head * size : (head + 1) * size])
                columns.append(wm[tap, :, width + head * size : width + (head + 1) * size])
            early[(1 + 3 * half + tap,) + own] = jnp.concatenate(columns, axis=1).astype(LOW)
    own_late[0] = wo[...].astype(LOW)
    for part in range(4):
        own_late[1 + part] = wu[:, part * width : (part + 1) * width].astype(LOW)
    own_down[...] = wd[...].astype(LOW)
    p.greet()
    half_down = down.shape[4] // 2
    views = [
        (lambda *i: tiles.at[i], "zxy", None),
        (bind(early, 0, 1), "zxy", None),
        (bind(early, 1, 1), "zyx", None),
        (bind(early, 2, 1), "zxy", None),
        (bind(early, 3, 1), "yzx", None),
        (bind(early, 4, 1), "zyx", None),
        (bind(early, 5, 1), "xzy", None),
        (bind(early, 6, 1), "xyz", None),
        (bind(late, 0, 3), "xyz", own_late.at[pl.ds(0, 3)]),
        (bind(late, 3, 2), "yzx", own_late.at[pl.ds(3, 2)]),
        (bind_rows(down, 0, half_down), "xzy", own_down.at[pl.ds(0, half_down)]),
        (bind_rows(down, half_down, half_down), "yxz", own_down.at[pl.ds(half_down, half_down)]),
    ]
    step = gather_slots(depth)
    pieces = [
        Gather(p, view, (gsend, grecv), step * k, order, first) for k, (view, order, first) in enumerate(views)
    ]
    vector_piece, query_piece, soon, later = pieces[0], pieces[1], pieces[2:8], pieces[8:]
    for piece in pieces[:8]:
        piece.step(0)
    for k, piece in enumerate(later):
        piece.place_own(lsem.at[k]).start()
        piece.step(0)

    block = 128

    @pl.loop(0, rows // block)
    def _(number):
        at = pl.multiple_of(number * block, block)
        unit, _ = unit_rows_of(tok[pl.ds(at, block), :].astype(WIDE))
        put_tiles(wide_a, pl.ds(at + 8, block), unit)

    for stage in (1, 2):
        vector_piece.step(stage)
        query_piece.step(stage)
    for piece in soon[2:3] + soon[4:] + soon[:2] + soon[3:4]:
        piece.step(1)
    vector_piece.step(3)
    query_piece.step(3)
    vector_piece.step(4)
    tile_lanes = tiles.shape[-1]
    for y in range(2):
        for x in range(2):
            total = jnp.zeros(tiles.shape[-2:], WIDE)
            for z in range(depth):
                for c in range(2):
                    total += tiles[y, x, z, c].astype(WIDE)
            s = 2 * y + x
            vectors[:, s * tile_lanes : (s + 1) * tile_lanes] = total
    gain, shift = vectors[0:1, :], vectors[1:2, :]

    @pl.loop(0, rows // block)
    def _(number):
        at = pl.multiple_of(number * block, block)
        normed = (get_tiles(wide_a, pl.ds(at + 8, block)) * gain + shift).astype(LOW)
        low_a[pl.ds(at, block), :] = normed
        put_tiles(wide_a, pl.ds(at + 8, block), normed.astype(WIDE))

    def query_copy(half, turn):
        return copy_to(
            qs.at[half, p.shard(turn)],
            qh.at[half, :, span(p.seq, rows)],
            (xsend, xrecv),
            7 + 3 * half + turn - 1,
            p.over_seq(turn),
        )

    def send_queries(half):
        for turn in (1, 2, 3):
            query_copy(half, turn).start()
        qh[half, :, span(p.seq, rows)] = qs[half, p.seq]

    last = p.seq == 3

    def edge_copy():
        return copy_to(
            wide_a.at[:, pl.ds(rows, 8)], wide_a.at[:, pl.ds(0, 8)], (xsend, xrecv), 0, {"seq": lax.rem(p.seq + 1, 4)}
        )

    @pl.when(jnp.logical_not(last))
    def _():
        edge_copy().start()

    query_piece.step(4)
    turned = lax.dot_general(early[0].reshape(width, width).T, low_a[...], NT, preferred_element_type=WIDE)
    qs[...] = turned.astype(LOW).reshape(qs.shape)
    for piece in soon[5:] + soon[:2] + soon[3:4] + soon[2:3] + soon[4:5]:
        piece.step(2)
    send_queries(0)
    for k, piece in enumerate(later):
        piece.place_own(lsem.at[k]).wait()
        piece.step(1)
    for piece in soon:
        piece.step(3)
    for piece in later[:1] + later[3:]:
        piece.step(2)
    for piece in soon:
        piece.step(4)

    @pl.when(p.seq > 0)
    def _():
        edge_copy().wait_recv()

    @pl.when(jnp.logical_not(last))
    def _():
        edge_copy().wait_send()

    @pl.when(p.seq == 0)
    def _():
        wide_a[:, 0:8, :] = jnp.zeros((width // 128, 8, 128), WIDE)

    edge[...] = wide_a[:, 0:8, :]
    parts = rows // PART
    strips = qh.shape[2] // STRIP

    def early_leaves():
        return pltpu.make_async_copy(early, early_out, osem.at[0])

    def kv_leaves(half):
        return pltpu.make_async_copy(kv.at[half], kv_out.at[half], osem.at[1 + half])

    def qh_leaves(half):
        return pltpu.make_async_copy(qh.at[half], qh_out.at[half], osem.at[3 + half])

    def mixed_leaves(half, strip, index):
        here = span(strip, STRIP)
        return pltpu.make_async_copy(mixed.at[half, :, here], mixed_out.at[half, :, here], osem.at[index])

    def mixed_stays(half, part):
        return pltpu.make_async_copy(
            mixed.at[half, :, span(p.seq * parts + part, PART)],
            attended.at[half, p.seq, :, span(part, PART)],
            osem.at[5 + 2 * strips + half * parts + part],
        )

    early_leaves().start()

    def weight(j):
        return early[j].reshape(width, width)

    mine = span(p.seq, slots)

    def memory_copy(half, turn):
        return copy_to(
            ms.at[half, :, span(p.shard(turn), lanes)],
            kv.at[half, mine],
            (xsend, xrecv),
            1 + 3 * half + turn - 1,
            p.over_seq(turn),
        )

    def project(half):
        for tap in range(3):
            window = get_tiles(wide_a, pl.ds(6 + tap, slots, stride=3)).astype(LOW)
            part = dot(window, weight(1 + 3 * half + tap))
            total = part if tap == 0 else total + part
        ms[half] = total.astype(LOW)
        for turn in (3, 1, 2):
            memory_copy(half, turn).start()
        kv[half, mine, :] = ms[half, :, span(p.seq, lanes)]

    project(0)
    project(1)
    send_queries(1)
    for turn in (1, 2, 3):
        memory_copy(0, turn).wait()
    kvt[0] = kv[0].T
    kv_leaves(0).start()

    def mixed_copy(half, turn, part):
        shard = p.shard(turn)
        return copy_to(
            mixed.at[half, :, span(shard * parts + part, PART)],
            attended.at[half, p.seq, :, span(part, PART)],
            (xsend, xrecv),
            13 + (3 * half + turn - 1) * parts + part,
            p.over_seq(turn),
        )

    def attend(half, seen, strip):
        here = span(strip, STRIP)
        queries = qh[half, :, here] * jnp.bfloat16(size ** (-0.5))
        queries = jnp.concatenate([queries, jnp.zeros_like(queries)], axis=0)
        whole = seen - SLOTS
        scores = hide_future(dot(kv[half, whole:seen, :], queries), whole, strip * STRIP)
        if whole:
            scores = jnp.concatenate([dot(kv[half, 0:whole, :], queries), scores], axis=0)
        highest = jnp.max(scores, axis=0, keepdims=True)
        exponent = jnp.exp(scores - highest)
        summed = jnp.sum(exponent, axis=0, keepdims=True)
        out = dot(kvt[half, size:lanes, 0:seen], exponent.astype(LOW)) * (1.0 / summed)
        lse[half, strip] = highest + jnp.log(summed)
        mixed[half, :, here] = out.astype(LOW)

    def work(half):
        @pl.loop(0, strips)
        def _(it):
            for number, turn in ((1, 1), (3, 2), (4, 3)):

                @pl.when(it == number)
                def _():
                    query_copy(half, turn).wait()

            strip = p.strip(it)
            for group in range(strips):

                @pl.when(strip == group)
                def _():
                    attend(half, SLOTS * (group + 1), strip)

            mixed_leaves(half, strip, 5 + half * strips + it).start()
            for k in range(2):
                granule = 2 * strip + k
                shard, part = lax.div(granule, parts), lax.rem(granule, parts)
                turn = p.turn_to(shard)

                @pl.when(turn > 0)
                def _():
                    mixed_copy(half, turn, part).start()

                @pl.when(turn == 0)
                def _():
                    mixed_stays(half, part).start()

            @pl.when(it == (5, 3)[half])
            def _():
                for piece in later[1:3]:
                    piece.step(2 + half)

    work(0)
    for turn in (1, 2, 3):
        memory_copy(1, turn).wait()
    kvt[1] = kv[1].T
    kv_leaves(1).start()
    qh_leaves(0).start()
    work(1)
    qh_leaves(1).start()
    for piece in later[:1] + later[3:]:
        piece.step(3)
    for piece in later:
        piece.step(4)
    early_leaves().wait()
    for half in range(2):
        kv_leaves(half).wait()
        qh_leaves(half).wait()
        for it in range(strips):
            mixed_leaves(half, p.strip(it), 5 + half * strips + it).wait()
        for part in range(parts):
            mixed_stays(half, part).wait()
            for turn in (1, 2, 3):
                mixed_copy(half, turn, part).wait()


def front(tok, params):
    wq, wm, wo, wu, wd, vec = params
    groups = lax.axis_size("grp")
    depth = groups // 2
    rows, width = tok.shape
    own, slots, size = wq.shape[0], rows // 3, width // H
    lanes = 2 * size
    tile_lanes = vec.shape[1] * groups
    whole = (2, 2, depth, 2)
    sems = pltpu.SemaphoreType.DMA((12 * gather_slots(depth),))
    parts = rows // PART
    swaps = pltpu.SemaphoreType.DMA((13 + 6 * parts,))
    anywhere = pl.BlockSpec(memory_space=pl.ANY)
    vmem = pl.BlockSpec(memory_space=pltpu.VMEM)
    return pl.pallas_call(
        functools.partial(front_kernel, depth),
        out_shape=(
            shaped(EARLY, *whole, own, width),
            shaped(LATE, *whole, own, width),
            shaped(*whole, *wd.shape),
            shaped(ROWS, 4 * tile_lanes, kind=WIDE),
            shaped(width // 128, 8, 128, kind=WIDE),
            shaped(2, size, 4 * rows),
            shaped(2, 4 * slots, lanes),
            shaped(2, size, 4 * rows),
            shaped(2, 4 * rows // STRIP, 1, STRIP, kind=WIDE),
            shaped(2, 4, size, rows),
        ),
        in_specs=in_vmem(7),
        out_specs=[anywhere] * 3 + [vmem] * 2 + [anywhere] * 3 + [vmem, anywhere],
        scratch_shapes=[
            pltpu.VMEM((*whole, ROWS, tile_lanes), LOW),
            pltpu.VMEM((width // 128, rows + 8, 128), WIDE),
            pltpu.VMEM((rows, width), LOW),
            pltpu.VMEM((2, 4, size, rows), LOW),
            pltpu.VMEM((2, slots, width), LOW),
            pltpu.VMEM((2, lanes, 4 * slots), LOW),
            pltpu.VMEM((LATE, own, width), LOW),
            pltpu.VMEM(wd.shape, LOW),
            pltpu.VMEM((ROWS, tile_lanes), WIDE),
            pltpu.VMEM((EARLY, *whole, own, width), LOW),
            pltpu.VMEM((2, size, 4 * rows), LOW),
            pltpu.VMEM((2, 4 * slots, lanes), LOW),
            pltpu.VMEM((2, size, 4 * rows), LOW),
            sems,
            sems,
            swaps,
            swaps,
            pltpu.SemaphoreType.DMA((4,)),
            pltpu.SemaphoreType.DMA((5 + 2 * (4 * rows // STRIP) + 2 * parts,)),
        ],
        compiler_params=pltpu.CompilerParams(
            collective_id=0, has_side_effects=True, vmem_limit_bytes=58 * MEGA
        ),
    )(tok, wq, wm, wo, wu, wd, vec)


def middle_kernel(depth, tok_in, cot_in, att_in, late_in, down_in, vec, length, *refs):
    out_to, dres_to, doh, g_stack_to, g_down_to, g_vec = refs[:6]
    tok, cot, att, late, down, out, dres, g_stack, g_down = refs[6:15]
    zs, dus, cs, es, ys, dos, xsend, xrecv, isem, osem, gsem = refs[15:]
    p = Place(depth)
    arriving = [
        pltpu.make_async_copy(source, target, isem.at[k])
        for k, (source, target) in enumerate(
            ((att_in, att), (tok_in, tok), (late_in, late), (down_in, down), (cot_in, cot))
        )
    ]
    for made in arriving:
        made.start()
    p.greet(beyond=False)
    rows, width = tok.shape
    hidden = zs.shape[1]
    gain, shift, bias = vec[2:3, :], vec[3:4, :], vec[4:5, :]
    inner = 0.7978845608028654
    cubic = inner * 0.044715
    g_vec[...] = jnp.zeros_like(g_vec)

    parts = rows // PART

    def do_copy(number, turn):
        return copy_to(
            dos.at[:, p.shard(turn), :, span(number, PART)],
            doh.at[:, :, span(p.seq * parts + number, PART)],
            (xsend, xrecv),
            3 * number + turn - 1,
            p.over_seq(turn),
        )

    def leave(number):
        here = span(number, PART)
        pairs = (
            (out.at[here], out_to.at[here]),
            (dres.at[here], dres_to.at[here]),
            (dos.at[:, p.seq, :, here], doh.at[:, :, span(p.seq * parts + number, PART)]),
        )
        return [pltpu.make_async_copy(a, b, osem.at[3 * number + k]) for k, (a, b) in enumerate(pairs)]

    for made in arriving:
        made.wait()

    @pl.loop(0, parts)
    def _(number):
        at = pl.multiple_of(number * PART, PART)
        here = pl.ds(at, PART)
        attended = att[:, :, :, here].reshape(width, PART).T
        residual = tok[here, :].astype(WIDE) + dot(attended, late[0])
        unit, factor = unit_rows_of(residual)
        normed = (unit * gain + shift).astype(LOW)
        cs[here, :] = normed
        place = lax.broadcasted_iota(jnp.int32, (PART, 1), 0) + (p.seq * rows + at)
        live = (place < length[0, 0]).astype(WIDE)
        upstream = cot[here, :].astype(WIDE) * live
        upstream_low = upstream.astype(LOW)
        es[here, :] = upstream_low
        result = residual + bias
        back = jnp.zeros((PART, width), WIDE)
        for part in range(hidden // width):
            here_hidden = pl.ds(part * width, width)
            u = dot(normed, late[1 + part]) + vec[5 + part : 6 + part, :]
            square = u * u
            half = 0.5 + 0.5 * jnp.tanh(u * (inner + cubic * square))
            active = u * half
            slope = half + active * (1.0 - half) * (2.0 * inner + 6.0 * cubic * square)
            active_low = active.astype(LOW)
            zs[here, here_hidden] = active_low
            result += dot(active_low, down[here_hidden, :])
            pulled = lax.dot_general(upstream_low, down[here_hidden, :], NT, preferred_element_type=WIDE)
            grad = (pulled * slope).astype(LOW)
            dus[here, here_hidden] = grad
            g_vec[5 + part : 6 + part, :] += jnp.sum(grad.astype(WIDE), axis=0, keepdims=True)
            back += lax.dot_general(grad, late[1 + part], NT, preferred_element_type=WIDE)
        out[here, :] = result.astype(LOW)
        scaled = back * gain
        total = upstream + factor * (
            scaled
            - jnp.mean(scaled, axis=-1, keepdims=True)
            - unit * jnp.mean(scaled * unit, axis=-1, keepdims=True)
        )
        dres[here, :] = total
        branch = total.astype(LOW)
        ys[here, :] = branch
        turned = lax.dot_general(late[0], branch, NT, preferred_element_type=WIDE)
        dos[:, :, :, here] = turned.astype(LOW).reshape(dos.shape[:3] + (PART,))
        for turn in (3, 1, 2):
            do_copy(number, turn).start()
        for made in leave(number):
            made.start()
        g_vec[2:3, :] += jnp.sum(back * unit, axis=0, keepdims=True)
        g_vec[3:4, :] += jnp.sum(back, axis=0, keepdims=True)
        g_vec[4:5, :] += jnp.sum(upstream, axis=0, keepdims=True)

    def finished(ref, target, index):
        made = pltpu.make_async_copy(ref, target, gsem.at[index])
        made.start()
        return made

    left = []
    for part in range(hidden // width):
        piece = pl.ds(part * width, width)
        g_down[piece, :] = over_rows(zs[:, piece], es[...]).astype(LOW)
        left.append(finished(g_down.at[piece], g_down_to.at[piece], 5 + part))
    g_stack[0] = dot(att[...].reshape(width, rows), ys[...]).astype(LOW)
    left.append(finished(g_stack.at[0], g_stack_to.at[0], 0))
    for part in range(hidden // width):
        piece = pl.ds(part * width, width)
        g_stack[1 + part] = over_rows(cs[...], dus[:, piece]).astype(LOW)
        left.append(finished(g_stack.at[1 + part], g_stack_to.at[1 + part], 1 + part))
    for number in range(parts):
        for turn in (1, 2, 3):
            do_copy(number, turn).wait()
        for made in leave(number):
            made.wait()
    for made in left:
        made.wait()


def middle(tok, cot, att, late, down, vec, length):
    rows, width = tok.shape
    hidden = down.shape[0]
    sems = pltpu.SemaphoreType.DMA((3 * (rows // PART),))
    return pl.pallas_call(
        functools.partial(middle_kernel, lax.axis_size("grp") // 2),
        out_shape=(
            shaped(rows, width),
            shaped(rows, width, kind=WIDE),
            shaped(2, width // H, 4 * rows),
            shaped(LATE, width, width),
            shaped(hidden, width),
            shaped(*vec.shape, kind=WIDE),
        ),
        in_specs=[pl.BlockSpec(memory_space=pl.ANY)] * 5
        + [pl.BlockSpec(memory_space=pltpu.VMEM), pl.BlockSpec(memory_space=pltpu.SMEM)],
        out_specs=[pl.BlockSpec(memory_space=pl.ANY)] * 5 + [pl.BlockSpec(memory_space=pltpu.VMEM)],
        scratch_shapes=[pltpu.VMEM(x.shape, x.dtype) for x in (tok, cot, att, late, down)]
        + [
            pltpu.VMEM((rows, width), LOW),
            pltpu.VMEM((rows, width), WIDE),
            pltpu.VMEM((LATE, width, width), LOW),
            pltpu.VMEM((hidden, width), LOW),
            pltpu.VMEM((rows, hidden), LOW),
            pltpu.VMEM((rows, hidden), LOW),
            pltpu.VMEM((rows, width), LOW),
            pltpu.VMEM((rows, width), LOW),
            pltpu.VMEM((rows, width), LOW),
            pltpu.VMEM(att.shape, LOW),
            sems,
            sems,
            pltpu.SemaphoreType.DMA((5,)),
            sems,
            pltpu.SemaphoreType.DMA((LATE + hidden // width,)),
        ],
        compiler_params=pltpu.CompilerParams(
            collective_id=1, has_side_effects=True, vmem_limit_bytes=58 * MEGA
        ),
    )(tok, cot, att, late, down, vec, length)


def back_kernel(depth, *refs):
    far_inputs, (lse, vec, edge, g_vec) = refs[:9], refs[9:13]
    grad, out_early, out_late, out_down, out_vec = refs[13:18]
    scatter, refs = refs[18:54], refs[54:]
    near_inputs, refs = refs[:9], refs[9:]
    tok, kv, doh, qh, mixed, g_late, g_down, early, dres = near_inputs
    g_early, dkv, kvt, dqs, dq, dms, dm, wide_a, low_a, wide_da, da, after, give, get, out_sum = refs[:15]
    rsend, rrecv, xsend, xrecv, isem = refs[15:]
    p = Place(depth)
    arriving = [
        pltpu.make_async_copy(a, b, isem.at[k]) for k, (a, b) in enumerate(zip(far_inputs, near_inputs))
    ]
    for made in arriving:
        made.start()
    rows, width = tok.shape
    slots = rows // 3
    size = qh.shape[1]
    lanes = 2 * size
    scale = size ** (-0.5)
    parts = rows // PART
    strips = qh.shape[2] // STRIP
    step = scatter_slots(depth)
    p.greet()

    def out_to(ref, first, count):
        def put(value):
            ref[first : first + count] = value

        return put

    half_down = g_down.shape[4] // 2
    todo = [
        (bind(g_late, 0, 3), out_to(out_late, 0, 3), bind(far_inputs[5], 0, 3)),
        (bind(g_late, 3, 2), out_to(out_late, 3, 2), bind(far_inputs[5], 3, 2)),
        (bind_rows(g_down, 0, half_down), out_to(out_down, 0, half_down), bind_rows(far_inputs[6], 0, half_down)),
        (
            bind_rows(g_down, half_down, half_down),
            out_to(out_down, half_down, half_down),
            bind_rows(far_inputs[6], half_down, half_down),
        ),
        (bind(g_early, 0, 1), out_to(out_early, 0, 1), None),
        (bind(g_early, 1, 2), out_to(out_early, 1, 2), None),
        (bind(g_early, 3, 1), out_to(out_early, 3, 1), None),
        (bind(g_early, 4, 2), out_to(out_early, 4, 2), None),
        (bind(g_early, 6, 1), out_to(out_early, 6, 1), None),
    ]
    pieces = [
        Scatter(p, view, out, scatter[4 * k : 4 * k + 4], (rsend, rrecv), step * k, SCATTER_ORDERS[k], far)
        for k, (view, out, far) in enumerate(todo)
    ]
    soon, query, first, second = pieces[:4], pieces[4:5], pieces[5:7], pieces[7:]
    small = SumTile(p, out_vec, give, get, (rsend, rrecv), step * len(pieces))
    for piece in soon:
        piece.step(0)
    gain, shift = vec[0:1, :], vec[1:2, :]
    block = 128
    wide_a[:, 0:8, :] = edge[...]
    arriving[0].wait()

    @pl.loop(0, rows // block)
    def _(number):
        at = pl.multiple_of(number * block, block)
        unit, _ = unit_rows_of(tok[pl.ds(at, block), :].astype(WIDE))
        normed = (unit * gain + shift).astype(LOW)
        low_a[pl.ds(at, block), :] = normed
        put_tiles(wide_a, pl.ds(at + 8, block), normed.astype(WIDE))

    for made in arriving[1:5]:
        made.wait()
    for half in range(2):
        kvt[half] = kv[half].T
    dkv[...] = jnp.zeros_like(dkv)

    def dq_copy(half, turn, part):
        return copy_to(
            dqs.at[half, :, span(p.shard(turn) * parts + part, PART)],
            dq.at[half, p.seq, :, span(part, PART)],
            (xsend, xrecv),
            (3 * half + turn - 1) * parts + part,
            p.over_seq(turn),
        )

    def attend(half, seen, strip):
        here = span(strip, STRIP)
        queries = qh[half, :, here] * jnp.bfloat16(scale)
        incoming = doh[half, :, here]
        middle = jnp.sum(incoming.astype(WIDE) * mixed[half, :, here].astype(WIDE), axis=0, keepdims=True)
        blank = jnp.zeros_like(queries)
        queries = jnp.concatenate([queries, blank], axis=0)
        incoming = jnp.concatenate([blank, incoming], axis=0)
        total = lse[half, strip]
        turned = jnp.zeros((size, STRIP), WIDE)
        for start in range(0, seen, 2 * SLOTS):
            stop = min(start + 2 * SLOTS, seen)
            keys = kv[half, start:stop, :]
            scores = dot(keys, queries)
            if stop == seen:
                clear = stop - SLOTS - start
                masked = hide_future(scores[clear:], stop - SLOTS, strip * STRIP)
                scores = jnp.concatenate([scores[:clear], masked], axis=0) if clear else masked
            weights = jnp.exp(scores - total)
            slope = (weights * (dot(keys, incoming) - middle)).astype(LOW)
            dkv[half, start:stop, :] += lax.dot_general(
                slope, queries, NT, preferred_element_type=WIDE
            ) + lax.dot_general(weights.astype(LOW), incoming, NT, preferred_element_type=WIDE)
            turned += dot(kvt[half, 0:size, start:stop], slope)
        dqs[half, :, here] = (turned * scale).astype(LOW)

    def memory_copy(half, turn):
        return copy_to(
            dms.at[half, span(p.shard(turn), slots)],
            dm.at[half, :, span(p.seq, lanes)],
            (xsend, xrecv),
            6 * parts + 3 * half + turn - 1,
            p.over_seq(turn),
        )

    def send_memory(half):
        dms[half] = dkv[half].astype(LOW)
        for turn in (3, 1, 2):
            memory_copy(half, turn).start()
        dm[half, :, span(p.seq, lanes)] = dms[half, span(p.seq, slots), :]

    def put_early(j, value):
        g_early[j] = value.astype(LOW).reshape(g_early.shape[1:])

    def memory_gradient(half, tap):
        window = get_tiles(wide_a, pl.ds(6 + tap, slots, stride=3)).astype(LOW)
        put_early(1 + 3 * half + tap, over_rows(window, dm[half]))

    @pl.loop(0, 2 * strips)
    def _(turn_number):
        half, it = lax.div(turn_number, strips), lax.rem(turn_number, strips)

        @pl.when(turn_number == strips)
        def _():
            send_memory(0)

        @pl.when(turn_number == strips + 2)
        def _():
            for turn in (1, 2, 3):
                memory_copy(0, turn).wait()
            for tap in range(3):
                memory_gradient(0, tap)
            for piece in first:
                piece.step(0)

        strip = p.strip(strips - 1 - it)
        for group in range(strips):

            @pl.when(strip == group)
            def _():
                attend(half, SLOTS * (group + 1), strip)

        for k in range(2):
            granule = 2 * strip + k
            shard, part = lax.div(granule, parts), lax.rem(granule, parts)
            turn = p.turn_to(shard)

            @pl.when(turn > 0)
            def _():
                dq_copy(half, turn, part).start()

            @pl.when(turn == 0)
            def _():
                dq[half, p.seq, :, span(part, PART)] = dqs[half, :, span(granule, PART)]

        @pl.when(turn_number == 1)
        def _():
            for k in (5, 6):
                pltpu.make_async_copy(far_inputs[k], near_inputs[k], isem.at[k]).wait()

        for when, steps in (
            (1, [(piece, 1) for piece in soon]),
            (7, [(piece, 2) for piece in soon]),
            (9, [(piece, 1) for piece in first]),
            (10, [(piece, 3) for piece in soon]),
        ):

            @pl.when(turn_number == when)
            def _():
                run(steps)

    send_memory(1)
    for half in range(2):
        for turn in (1, 2, 3):
            for part in range(parts):
                dq_copy(half, turn, part).wait()
    for made in arriving[7:]:
        made.wait()
    turned = dq[...].reshape(width, rows)
    put_early(0, dot(turned, low_a[...]).T)
    query[0].step(0)
    da[...] = lax.dot_general(turned.T, early[0], NT, preferred_element_type=WIDE)
    for turn in (1, 2, 3):
        memory_copy(1, turn).wait()
    run([(piece, 2) for piece in first])
    query[0].step(1)
    for tap in range(3):
        memory_gradient(1, tap)
        if tap:
            second[tap - 1].step(0)
    wide_da[:, 0:8, :] = jnp.zeros((width // 128, 8, 128), WIDE)
    for tap in range(3):
        pulled = lax.dot_general(dm[0], early[1 + tap], NT, preferred_element_type=WIDE)
        pulled += lax.dot_general(dm[1], early[4 + tap], NT, preferred_element_type=WIDE)
        put_tiles(wide_da, pl.ds(6 + tap, slots, stride=3), pulled)

    def edge_copy():
        return copy_to(
            wide_da.at[:, pl.ds(0, 8)], after, (xsend, xrecv), 6 * parts + 6, {"seq": lax.rem(p.seq + 3, 4)}
        )

    @pl.when(p.seq > 0)
    def _():
        edge_copy().start()

    run([(piece, 1) for piece in second])
    run([(query[0], 2), (first[0], 3), (first[1], 3)])

    @pl.when(p.seq < 3)
    def _():
        edge_copy().wait_recv()

    @pl.when(p.seq > 0)
    def _():
        edge_copy().wait_send()

    @pl.when(p.seq == 3)
    def _():
        after[...] = jnp.zeros_like(after)

    wide_da[:, rows + 6 : rows + 8, :] = after[:, 6:8, :]
    out_sum[...] = g_vec[...]

    @pl.loop(0, rows // block)
    def _(number):
        at = pl.multiple_of(number * block, block)
        here = pl.ds(at, block)
        unit, factor = unit_rows_of(tok[here, :].astype(WIDE))
        upstream = da[here, :] + get_tiles(wide_da, pl.ds(at + 8, block))
        scaled = upstream * gain
        inward = factor * (
            scaled
            - jnp.mean(scaled, axis=-1, keepdims=True)
            - unit * jnp.mean(scaled * unit, axis=-1, keepdims=True)
        )
        grad[here, :] = (dres[here, :] + inward).astype(LOW)
        out_sum[0:1, :] += jnp.sum(upstream * unit, axis=0, keepdims=True)
        out_sum[1:2, :] += jnp.sum(upstream, axis=0, keepdims=True)

    tile_lanes = width // 4
    for shard in range(4):
        give[shard] = out_sum[:, shard * tile_lanes : (shard + 1) * tile_lanes]
    small.step(0)
    run([(piece, 2) for piece in second])
    run([(piece, 4) for piece in soon])
    small.step(1)
    run([(query[0], 3), (first[0], 4), (first[1], 4)])
    run([(piece, 3) for piece in second])
    small.step(2)


def back(saved, tok, dres, early, vec, edge, grads):
    qh, kv, mixed, lse, doh = saved
    g_late, g_down, g_vec = grads
    depth = lax.axis_size("grp") // 2
    rows, width = tok.shape
    size, slots = qh.shape[1], rows // 3
    lanes = 2 * size
    whole = (2, 2, depth, 2)
    own_down = g_down.shape[0] // (8 * depth)
    parts = rows // PART
    shapes = [(3, ROWS, width), (2, ROWS, width)] + [(own_down // 2, width)] * 2
    shapes += [(1, ROWS, width)] + [(2, ROWS, width), (1, ROWS, width)] * 2
    ring = pltpu.SemaphoreType.DMA((9 * scatter_slots(depth) + 2 * depth + 2,))
    swaps = pltpu.SemaphoreType.DMA((6 * parts + 7,))
    g_late = g_late.reshape(LATE, *whole, ROWS, width)
    g_down = g_down.reshape(*whole, own_down, width)
    inputs = (tok, kv, doh, qh, mixed, g_late, g_down, early, dres)
    return pl.pallas_call(
        functools.partial(back_kernel, depth),
        out_shape=(
            shaped(rows, width),
            shaped(EARLY, ROWS, width, kind=WIDE),
            shaped(LATE, ROWS, width, kind=WIDE),
            shaped(own_down, width, kind=WIDE),
            shaped(ROWS, width // 4, kind=WIDE),
        ),
        in_specs=[pl.BlockSpec(memory_space=pl.ANY)] * 9 + in_vmem(4),
        out_specs=in_vmem(5),
        scratch_shapes=[
            buf for order, shape in zip(SCATTER_ORDERS, shapes) for buf in scatter_scratch(depth, order, shape)
        ]
        + [pltpu.VMEM(x.shape, x.dtype) for x in inputs]
        + [
            pltpu.VMEM((EARLY, *whole, ROWS, width), LOW),
            pltpu.VMEM(kv.shape, WIDE),
            pltpu.VMEM((2, lanes, 4 * slots), LOW),
            pltpu.VMEM(qh.shape, LOW),
            pltpu.VMEM((2, 4, size, rows), LOW),
            pltpu.VMEM(kv.shape, LOW),
            pltpu.VMEM((2, slots, width), LOW),
            pltpu.VMEM((width // 128, rows + 8, 128), WIDE),
            pltpu.VMEM((rows, width), LOW),
            pltpu.VMEM((width // 128, rows + 8, 128), WIDE),
            pltpu.VMEM((rows, width), WIDE),
            pltpu.VMEM((width // 128, 8, 128), WIDE),
            pltpu.VMEM((5, ROWS, width // 4), WIDE),
            pltpu.VMEM((2 * depth + 2, ROWS, width // 4), WIDE),
            pltpu.VMEM(vec.shape, WIDE),
            ring,
            ring,
            swaps,
            swaps,
            pltpu.SemaphoreType.DMA((9,)),
        ],
        compiler_params=pltpu.CompilerParams(
            collective_id=2, has_side_effects=True, vmem_limit_bytes=62 * MEGA
        ),
    )(*inputs, lse, vec, edge, g_vec)


def update_kernel(*refs):
    weights, firsts, seconds = refs[0:6], refs[6:12], refs[12:18]
    early, late, down, vec = refs[18:22]
    held, outs, passed = refs[22:24], refs[24:48], refs[48:50]
    for source, target in zip(held, passed):
        target[...] = source[...]
    width = early.shape[-1]

    def put(which, at, gradient):
        results = adamw(
            weights[which][at], gradient, firsts[which][at], seconds[which][at], LEARNING_RATES[which]
        )
        for group, value in enumerate(results):
            outs[6 * group + which][at] = value

    every = slice(None)
    put(0, (every, every), early[0])
    size = width // H
    for tap in range(3):
        for kind in range(2):
            columns = [
                early[1 + 3 * half + tap, :, (2 * s + kind) * size : (2 * s + kind + 1) * size]
                for half in range(2)
                for s in range(4)
            ]
            put(1, (tap, every, slice(kind * width, (kind + 1) * width)), jnp.concatenate(columns, axis=1))
    put(2, (every, every), late[0])
    for part in range(4):
        put(3, (every, slice(part * width, (part + 1) * width)), late[1 + part])
    put(4, (every, every), down[...])
    share = weights[5].shape[1]
    tile_lanes = vec.shape[1]
    tile = pltpu.roll(vec[...], lax.rem(tile_lanes - lax.axis_index("grp") * share, tile_lanes), 1)
    put(5, (every, every), tile[0 : weights[5].shape[0], 0:share])


def update(params, firsts, seconds, grads, held):
    outs = [jax.ShapeDtypeStruct(member.shape, WIDE) for member in params] * 3
    outs += [jax.ShapeDtypeStruct(member.shape, LOW) for member in params]
    return pl.pallas_call(
        update_kernel,
        out_shape=tuple(outs) + tuple(jax.ShapeDtypeStruct(x.shape, x.dtype) for x in held),
        in_specs=in_vmem(24),
        out_specs=in_vmem(26),
    )(*params, *firsts, *seconds, *grads, *held)


def fused(tokens, cotangent, lengths, *state):
    params, firsts, seconds = state[0:6], state[6:12], state[12:18]
    width = tokens.shape[2]
    tok, cot = tokens[0], cotangent[0]
    early, late, down, vec, edge, qh, kv, mixed, lse, attended = front(tok, params)
    early = early.reshape(EARLY, width, width)
    late = late.reshape(LATE, width, width)
    down = down.reshape(-1, width)
    out, dres, doh, g_late, g_down, g_vec = middle(
        tok, cot, attended, late, down, vec, lengths.reshape(1, 1)
    )
    grad, r_early, r_late, r_down, r_vec = back(
        (qh, kv, mixed, lse, doh), tok, dres, early, vec, edge, (g_late, g_down, g_vec)
    )
    *new, out, grad = update(params, firsts, seconds, (r_early, r_late, r_down, r_vec), (out, grad))
    return (out[None], grad[None], *new)


def body(*arguments):
    tokens, shard = arguments[0], arguments[3]
    whole_tiles = shard.shape[0] % ROWS == 0 and tokens.shape[1] % PART == 0
    four = lax.axis_size("seq") == 4 and lax.axis_size("grp") % 2 == 0
    return (fused if whole_tiles and four else plain)(*arguments)


def solution(mesh):
    in_specs = (
        P("grp", "seq", None),
        P("grp", "seq", None),
        P("grp"),
        P(("seq", "grp"), None),
        P(None, ("seq", "grp"), None),
        P(("seq", "grp"), None),
        P(("seq", "grp"), None),
        P(("seq", "grp"), None),
        P(None, ("seq", "grp")),
        P(("seq", "grp"), None),
        P(None, ("seq", "grp"), None),
        P(("seq", "grp"), None),
        P(("seq", "grp"), None),
        P(("seq", "grp"), None),
        P(None, ("seq", "grp")),
        P(("seq", "grp"), None),
        P(None, ("seq", "grp"), None),
        P(("seq", "grp"), None),
        P(("seq", "grp"), None),
        P(("seq", "grp"), None),
        P(None, ("seq", "grp")),
    )
    out_specs = (
        P("grp", "seq", None),
        P("grp", "seq", None),
        P(("seq", "grp"), None),
        P(None, ("seq", "grp"), None),
        P(("seq", "grp"), None),
        P(("seq", "grp"), None),
        P(("seq", "grp"), None),
        P(None, ("seq", "grp")),
        P(("seq", "grp"), None),
        P(None, ("seq", "grp"), None),
        P(("seq", "grp"), None),
        P(("seq", "grp"), None),
        P(("seq", "grp"), None),
        P(None, ("seq", "grp")),
        P(("seq", "grp"), None),
        P(None, ("seq", "grp"), None),
        P(("seq", "grp"), None),
        P(("seq", "grp"), None),
        P(("seq", "grp"), None),
        P(None, ("seq", "grp")),
        P(("seq", "grp"), None),
        P(None, ("seq", "grp"), None),
        P(("seq", "grp"), None),
        P(("seq", "grp"), None),
        P(("seq", "grp"), None),
        P(None, ("seq", "grp")),
    )
    return jax.shard_map(body, mesh=mesh, in_specs=in_specs, out_specs=out_specs, check_vma=False)
```

```python
import functools

import jax
import jax.numpy as jnp
from jax import lax
from jax.experimental import pallas as pl
from jax.experimental.pallas import tpu as pltpu
from jax.sharding import PartitionSpec as P

H = 8
STEP = 10


NORM_EPSILON = 1e-05
BETA_FIRST = 0.9
BETA_SECOND = 0.95
ADAM_EPSILON = 1e-08
WEIGHT_DECAY = 0.1
LEARNING_RATES = (0.05, 0.04, 0.3, 0.05, 0.03, 0.5)
MASKED_SCORE = -1e30
NT = (((1,), (1,)), ((), ()))


def from_behind(x, axis, by):
    peers = lax.axis_size(axis)
    pairs = [(i, i + by) for i in range(peers) if 0 <= i + by < peers]
    return lax.ppermute(x, axis, pairs)


def matmul(left, right):
    return jnp.dot(left, right, preferred_element_type=jnp.float32)


def over_rows(left, right):
    return lax.dot_general(
        left, right, (((0,), (0,)), ((), ())), preferred_element_type=jnp.float32
    )


def against(left, right):
    return lax.dot_general(
        left, right, (((1,), (1,)), ((), ())), preferred_element_type=jnp.float32
    )


def norm_forward(values, gain, shift):
    centred = values - jnp.mean(values, axis=-1, keepdims=True)
    factor = lax.rsqrt(jnp.mean(centred * centred, axis=-1, keepdims=True) + NORM_EPSILON)
    unit_rows = centred * factor
    return (unit_rows * gain + shift, unit_rows, factor)


def norm_backward(upstream, unit_rows, factor, gain):
    scaled = upstream * gain
    inward = factor * (
        scaled
        - jnp.mean(scaled, axis=-1, keepdims=True)
        - unit_rows * jnp.mean(scaled * unit_rows, axis=-1, keepdims=True)
    )
    return (inward, jnp.sum(upstream * unit_rows, axis=0), jnp.sum(upstream, axis=0))


def masked_scores(query_tile_rows, key_row_block, positions):
    slot_starts = 3 * jnp.arange(key_row_block.shape[0], dtype=jnp.int32)
    score_matrix = jnp.einsum(
        "azv,lzv->zal", query_tile_rows, key_row_block, preferred_element_type=jnp.float32
    ) * query_tile_rows.shape[2] ** (-0.5)
    visible = slot_starts[None, :] <= positions[:, None]
    return jnp.where(visible[None], score_matrix, MASKED_SCORE)


def attend_forward(queries, key_row_block, value_row_block, anchor, block_rows):
    block_count = queries.shape[0] // block_rows
    offsets = block_rows * jnp.arange(block_count, dtype=jnp.int32)

    def attend_block(inputs):
        query_tile_rows, offset_rows = inputs
        score_matrix = masked_scores(
            query_tile_rows,
            key_row_block,
            anchor + offset_rows + jnp.arange(block_rows, dtype=jnp.int32),
        )
        highest = jnp.max(score_matrix, axis=-1, keepdims=True)
        exponent = jnp.exp(score_matrix - highest)
        summed = jnp.sum(exponent, axis=-1, keepdims=True)
        reduced_weights = (exponent / summed).astype(jnp.bfloat16)
        mixed = jnp.einsum(
            "yup,pyb->uyb", reduced_weights, value_row_block, preferred_element_type=jnp.float32
        )
        return (mixed, (highest + jnp.log(summed))[..., 0])

    blocks_in = queries.reshape(block_count, block_rows, queries.shape[1], queries.shape[2])
    mixed, logsum = lax.map(attend_block, (blocks_in, offsets))
    return (mixed.reshape(queries.shape), logsum)


def attend_backward(queries, key_row_block, value_row_block, upstream, logsum, anchor, block_rows):
    block_count = queries.shape[0] // block_rows
    offsets = block_rows * jnp.arange(block_count, dtype=jnp.int32)
    scale_factor = queries.shape[2] ** (-0.5)

    def attend_back(carry, inputs):
        grad_keys, grad_values = carry
        query_tile_rows, incoming_gradient_rows, logsum_block, offset_rows = inputs
        score_matrix = masked_scores(
            query_tile_rows,
            key_row_block,
            anchor + offset_rows + jnp.arange(block_rows, dtype=jnp.int32),
        )
        weights_soft = jnp.exp(score_matrix - logsum_block[..., None])
        grad_weights = jnp.einsum(
            "azv,lzv->zal",
            incoming_gradient_rows,
            value_row_block,
            preferred_element_type=jnp.float32,
        )
        centre = jnp.sum(weights_soft * grad_weights, axis=-1, keepdims=True)
        score_gradient = (weights_soft * (grad_weights - centre)).astype(jnp.bfloat16)
        grad_query = (
            jnp.einsum(
                "yup,pyb->uyb", score_gradient, key_row_block, preferred_element_type=jnp.float32
            )
            * scale_factor
        )
        grad_keys = (
            grad_keys
            + jnp.einsum(
                "xof,oxa->fxa", score_gradient, query_tile_rows, preferred_element_type=jnp.float32
            )
            * scale_factor
        )
        grad_values = grad_values + jnp.einsum(
            "xof,oxa->fxa",
            weights_soft.astype(jnp.bfloat16),
            incoming_gradient_rows,
            preferred_element_type=jnp.float32,
        )
        return ((grad_keys, grad_values), grad_query)

    shape_blocks = (block_count, block_rows, queries.shape[1], queries.shape[2])
    zeros_init = jnp.zeros(key_row_block.shape, jnp.float32)
    (grad_keys, grad_values), grad_query = lax.scan(
        attend_back,
        (zeros_init, zeros_init),
        (queries.reshape(shape_blocks), upstream.reshape(shape_blocks), logsum, offsets),
    )
    return (grad_query.reshape(queries.shape), grad_keys, grad_values)


def adamw(weight, gradient, moment, square, step_rate):
    moment_new = BETA_FIRST * moment + (1.0 - BETA_FIRST) * gradient
    square_new = BETA_SECOND * square + (1.0 - BETA_SECOND) * gradient * gradient
    fixed_first = 1.0 - BETA_FIRST**STEP
    fixed_second = 1.0 - BETA_SECOND**STEP
    update = (
        moment_new / fixed_first / (jnp.sqrt(square_new / fixed_second) + ADAM_EPSILON)
        + WEIGHT_DECAY * weight
    )
    master = weight - step_rate * update
    return (moment_new, square_new, master, master.astype(jnp.bfloat16))


def plain(
    tokens,
    cotangent,
    lengths,
    weight_query,
    weight_memory,
    weight_out,
    weight_up,
    weight_down,
    vectors,
    first_query,
    first_memory,
    first_out,
    first_up,
    first_down,
    first_vectors,
    second_query,
    second_memory,
    second_out,
    second_up,
    second_down,
    second_vectors,
):
    gathered = (
        lax.all_gather(weight_query.astype(jnp.bfloat16), ("seq", "grp"), axis=0, tiled=True),
        lax.all_gather(weight_memory.astype(jnp.bfloat16), ("seq", "grp"), axis=1, tiled=True),
        lax.all_gather(weight_out.astype(jnp.bfloat16), ("seq", "grp"), axis=0, tiled=True),
        lax.all_gather(weight_up.astype(jnp.bfloat16), ("seq", "grp"), axis=0, tiled=True),
        lax.all_gather(weight_down.astype(jnp.bfloat16), ("seq", "grp"), axis=0, tiled=True),
        lax.all_gather(vectors.astype(jnp.bfloat16), ("seq", "grp"), axis=1, tiled=True),
    )
    query_w, memory_w, out_w, up_w, down_w, vector_low = gathered
    vector_rows = vector_low.astype(jnp.float32)
    model_width = query_w.shape[0]
    hidden_units = up_w.shape[1]
    head_size = model_width // H
    seq_count = lax.axis_size("seq")
    seq_index = lax.axis_index("seq")
    local_rows = tokens.shape[1]
    local_slots = local_rows // 3
    inputs = tokens[0].astype(jnp.float32)
    normed, unit_one, factor_one = norm_forward(inputs, vector_rows[0], vector_rows[1])
    normed_low = normed.astype(jnp.bfloat16)
    queries = matmul(normed_low, query_w).astype(jnp.bfloat16)
    borrowed = from_behind(normed_low[local_rows - 2 :], "seq", 1)
    extended = jnp.concatenate([borrowed, normed_low], axis=0)
    windows = extended[:local_rows].reshape(local_slots, 3 * model_width)
    memory_flat = memory_w.reshape(3 * model_width, 2 * model_width)
    memory = matmul(windows, memory_flat).astype(jnp.bfloat16)
    share_width = model_width // seq_count
    local_heads = H // seq_count
    head_queries, head_memory = (
        lax.all_to_all(
            queries.reshape(local_rows, 1, seq_count, share_width),
            "seq",
            split_axis=2,
            concat_axis=0,
            tiled=True,
        ),
        lax.all_to_all(
            memory.reshape(local_slots, 2, seq_count, share_width),
            "seq",
            split_axis=2,
            concat_axis=0,
            tiled=True,
        ),
    )
    total_rows = head_queries.shape[0]
    total_slots = head_memory.shape[0]
    query_heads = head_queries.reshape(total_rows, local_heads, head_size)
    key_heads = head_memory[:, 0].reshape(total_slots, local_heads, head_size)
    value_heads = head_memory[:, 1].reshape(total_slots, local_heads, head_size)
    block_rows = min(512, total_rows)
    mixed, logsum = attend_forward(query_heads, key_heads, value_heads, 0, block_rows)
    mixed_low = mixed.astype(jnp.bfloat16).reshape(total_rows, 1, share_width)
    attended = lax.all_to_all(mixed_low, "seq", split_axis=0, concat_axis=1, tiled=True).reshape(
        local_rows, model_width
    )
    residual = inputs + matmul(attended, out_w)
    normed_two, unit_two, factor_two = norm_forward(residual, vector_rows[2], vector_rows[3])
    normed_two_low = normed_two.astype(jnp.bfloat16)
    pre_act = matmul(normed_two_low, up_w) + vector_rows[5:].reshape(hidden_units)
    activated, gelu_pull = jax.vjp(jax.nn.gelu, pre_act)
    activated_low = activated.astype(jnp.bfloat16)
    result = residual + matmul(activated_low, down_w) + vector_rows[4]
    positions = seq_index * local_rows + jnp.arange(local_rows, dtype=jnp.int32)
    live_mask = (positions < lengths[0]).astype(jnp.float32)
    grad_out = cotangent[0].astype(jnp.float32) * live_mask[:, None]
    grad_out_low = grad_out.astype(jnp.bfloat16)
    grad_down = over_rows(activated_low, grad_out_low)
    grad_activated = against(grad_out_low, down_w)
    grad_pre_low = gelu_pull(grad_activated)[0].astype(jnp.bfloat16)
    grad_up = over_rows(normed_two_low, grad_pre_low)
    grad_up_bias = jnp.sum(grad_pre_low.astype(jnp.float32), axis=0)
    grad_normed_two = against(grad_pre_low, up_w)
    grad_norm_two, grad_gain_two, grad_shift_two = norm_backward(
        grad_normed_two, unit_two, factor_two, vector_rows[2]
    )
    grad_residual = grad_out + grad_norm_two
    grad_branch_low = grad_residual.astype(jnp.bfloat16)
    grad_outw = over_rows(attended, grad_branch_low)
    grad_attended_low = against(grad_branch_low, out_w).astype(jnp.bfloat16)
    grad_heads = lax.all_to_all(
        grad_attended_low.reshape(local_rows, 1, seq_count, share_width),
        "seq",
        split_axis=2,
        concat_axis=0,
        tiled=True,
    ).reshape(total_rows, local_heads, head_size)
    grad_q, grad_k, grad_v = attend_backward(
        query_heads, key_heads, value_heads, grad_heads, logsum, 0, block_rows
    )
    packed = (
        jnp.stack([grad_k, grad_v], axis=1)
        .astype(jnp.bfloat16)
        .reshape(total_slots, 2, 1, share_width)
    )
    token_queries, token_memory = (
        lax.all_to_all(
            grad_q.astype(jnp.bfloat16).reshape(total_rows, 1, 1, share_width),
            "seq",
            split_axis=0,
            concat_axis=2,
            tiled=True,
        ),
        lax.all_to_all(packed, "seq", split_axis=0, concat_axis=2, tiled=True),
    )
    grad_queries_low = token_queries.reshape(local_rows, model_width)
    grad_memory_low = token_memory.reshape(local_slots, 2 * model_width)
    grad_queryw = over_rows(normed_low, grad_queries_low)
    grad_normed = against(grad_queries_low, query_w)
    grad_memoryw = over_rows(windows, grad_memory_low).reshape(3, model_width, 2 * model_width)
    grad_windows = against(grad_memory_low, memory_flat).reshape(local_rows, model_width)
    returned = from_behind(grad_windows[:2], "seq", -1)
    grad_normed = grad_normed + jnp.concatenate([grad_windows[2:], returned], axis=0)
    grad_norm_one, grad_gain_one, grad_shift_one = norm_backward(
        grad_normed, unit_one, factor_one, vector_rows[0]
    )
    grad_inputs = (grad_residual + grad_norm_one).astype(jnp.bfloat16)
    grad_vector_rows = jnp.concatenate(
        [
            jnp.stack(
                [
                    grad_gain_one,
                    grad_shift_one,
                    grad_gain_two,
                    grad_shift_two,
                    jnp.sum(grad_out, axis=0),
                ]
            ),
            grad_up_bias.reshape(4, model_width),
        ],
        axis=0,
    )
    reduced = (
        lax.psum_scatter(grad_queryw, ("seq", "grp"), scatter_dimension=0, tiled=True),
        lax.psum_scatter(grad_memoryw, ("seq", "grp"), scatter_dimension=1, tiled=True),
        lax.psum_scatter(grad_outw, ("seq", "grp"), scatter_dimension=0, tiled=True),
        lax.psum_scatter(grad_up, ("seq", "grp"), scatter_dimension=0, tiled=True),
        lax.psum_scatter(grad_down, ("seq", "grp"), scatter_dimension=0, tiled=True),
        lax.psum_scatter(grad_vector_rows, ("seq", "grp"), scatter_dimension=1, tiled=True),
    )
    new_query = adamw(weight_query, reduced[0], first_query, second_query, LEARNING_RATES[0])
    new_memory = adamw(weight_memory, reduced[1], first_memory, second_memory, LEARNING_RATES[1])
    new_out = adamw(weight_out, reduced[2], first_out, second_out, LEARNING_RATES[2])
    new_up = adamw(weight_up, reduced[3], first_up, second_up, LEARNING_RATES[3])
    new_down = adamw(weight_down, reduced[4], first_down, second_down, LEARNING_RATES[4])
    new_vectors = adamw(vectors, reduced[5], first_vectors, second_vectors, LEARNING_RATES[5])
    return (
        result.astype(jnp.bfloat16)[None],
        grad_inputs[None],
        new_query[0],
        new_memory[0],
        new_out[0],
        new_up[0],
        new_down[0],
        new_vectors[0],
        new_query[1],
        new_memory[1],
        new_out[1],
        new_up[1],
        new_down[1],
        new_vectors[1],
        new_query[2],
        new_memory[2],
        new_out[2],
        new_up[2],
        new_down[2],
        new_vectors[2],
        new_query[3],
        new_memory[3],
        new_out[3],
        new_up[3],
        new_down[3],
        new_vectors[3],
    )


MESH = pl.DeviceIdType.MESH
LOW, WIDE = jnp.bfloat16, jnp.float32
ROWS = 16
PART = 384
STRIP = 2 * PART
SLOTS = STRIP // 3
EARLY = 7
LATE = 5
MEGA = 1024 * 1024
SCATTER_ORDERS = ("yzx", "xyz", "zxy", "xyz", "sz", "xyz", "yzx", "sz", "sz")


def in_vmem(count):
    return [pl.BlockSpec(memory_space=pltpu.VMEM)] * count


def shaped(*shape, kind=jnp.bfloat16):
    return jax.ShapeDtypeStruct(shape, kind)


def dot(left, right):
    return jnp.dot(left, right, preferred_element_type=jnp.float32)


def differ(bit, other):
    return bit + other - 2 * bit * other


class Place:
    def __init__(self, depth):
        self.seq, self.grp = lax.axis_index("seq"), lax.axis_index("grp")
        self.depth = depth
        self.y, self.x = lax.div(self.seq, 2), lax.rem(self.seq, 2)
        self.z, self.c = lax.div(self.grp, 2), lax.rem(self.grp, 2)
        self.own = {"y": self.y, "x": self.x, "z": self.z, "s": self.seq}
        self.size = {"y": 2, "x": 2, "z": depth, "s": 4}

    def turn_to(self, shard):
        return 2 * differ(self.y, lax.div(shard, 2)) + differ(self.x, lax.rem(shard, 2))

    def strip(self, it):
        half, pos = differ(lax.div(it, 3), self.y), lax.rem(it, 3)
        return 3 * half + pos + self.x * (2 - 2 * pos)

    def shard(self, turn):
        return 2 * differ(self.y, lax.div(turn, 2)) + differ(self.x, lax.rem(turn, 2))

    def over_seq(self, turn):
        return {"seq": self.shard(turn)}

    def over_core(self):
        return {"grp": 2 * self.z + 1 - self.c}

    def z_of(self, step):
        return lax.rem(self.z + step, self.depth)

    def over_grp(self, step):
        return {"grp": lax.rem(self.grp + step, 2 * self.depth)}

    def over_z(self, step):
        return {"grp": 2 * self.z_of(step) + self.c}

    def step_of(self, axis, step):
        if axis == "s":
            return self.shard(step)
        return self.z_of(step) if axis == "z" else 1 - self.own[axis]

    def others(self, axis):
        if axis == "z":
            return [self.over_z(step) for step in range(1, self.depth)]
        if axis == "s":
            return [self.over_seq(turn) for turn in (1, 2, 3)]
        return [self.over_seq({"x": 1, "y": 2}[axis])]

    def greet(self, beyond=True):
        peers = [self.over_seq(turn) for turn in (1, 2, 3)]
        if beyond:
            peers += [self.over_grp(step) for step in range(1, 2 * self.depth)]
        barrier = pltpu.get_barrier_semaphore()
        for peer in peers:
            pl.semaphore_signal(barrier, inc=1, device_id=peer, device_id_type=MESH)
        pl.semaphore_wait(barrier, len(peers))


def copy_to(source, target, sems, index, peer):
    send, recv = sems
    return pltpu.make_async_remote_copy(
        src_ref=source,
        dst_ref=target,
        send_sem=send.at[index],
        recv_sem=recv.at[index],
        device_id=peer,
        device_id_type=MESH,
    )


class Gather:
    def __init__(self, place, view, sems, base, order, own=None):
        self.at, self.view, self.sems, self.base, self.order = place, view, sems, base, order
        self.own = own

    def moves(self, stage):
        p = self.at
        done = self.order[:stage]
        where = [pl.ds(0, p.size[axis]) if axis in done else p.own[axis] for axis in "yxz"]
        region = self.view(*where, p.c)
        if stage == 3:
            return [(region, p.depth + 1, p.over_core())]
        base = sum(p.size[axis] - 1 for axis in done)
        return [(region, base + i, peer) for i, peer in enumerate(p.others(self.order[stage]))]

    def copies(self, stage):
        source = self.own if stage == 0 else None
        return [
            copy_to(r if source is None else source, r, self.sems, self.base + slot, peer)
            for r, slot, peer in self.moves(stage)
        ]

    def place_own(self, sem):
        p = self.at
        return pltpu.make_async_copy(self.own, self.view(p.y, p.x, p.z, p.c), sem)

    def step(self, stage):
        if stage:
            for made in self.copies(stage - 1):
                made.wait()
        if stage < 4:
            for made in self.copies(stage):
                made.start()


def gather_slots(depth):
    return depth + 2


def bind(ref, first, count):
    return lambda *i: ref.at[(pl.ds(first, count),) + i]


def bind_rows(ref, first, count):
    return lambda *i: ref.at[i + (pl.ds(first, count),)]


class Scatter:
    def __init__(self, place, view, out, bufs, sems, base, order, far=None):
        self.far = far or view
        self.at, self.view, self.out, self.sems, self.base, self.order = place, view, out, sems, base, order
        self.get_core, self.give, self.get, self.keep = bufs

    def plan(self, number):
        p = self.at
        axis = self.order[number]
        rest = [other for other in sorted(self.order) if other not in self.order[: number + 1]]
        combos = [{}]
        for other in rest:
            combos = [{**c, other: i} for c in combos for i in range(p.size[other])]
        first = 0
        for k in range(number):
            left = 1
            for other in self.order[k + 1 :]:
                left *= p.size[other]
            first += left * (p.size[self.order[k]] - 1)
        return axis, combos, first

    def kept(self, index):
        p = self.at
        linear = 0
        for axis in sorted(self.order):
            if axis != self.order[0]:
                linear = linear * p.size[axis] + index.get(axis, p.own[axis])
        return linear

    def now(self, number, index):
        p = self.at
        if number:
            return self.keep[self.kept(index)]
        where = {axis: index.get(axis, p.own[axis]) for axis in self.order}
        if "s" in where:
            where["y"], where["x"] = lax.div(where["s"], 2), lax.rem(where["s"], 2)
        where = [where[axis] for axis in "yxz"]
        lead = (slice(None),) * (len(self.get_core.shape) - 5)
        return self.view(*where, p.c)[...].astype(WIDE) + self.get_core[lead + tuple(where)].astype(WIDE)

    def copies(self, stage):
        p = self.at
        if stage == 0:
            source = self.far(pl.ds(0, 2), pl.ds(0, 2), pl.ds(0, p.depth), 1 - p.c)
            return [copy_to(source, self.get_core, self.sems, self.base, p.over_core())]
        axis, combos, first = self.plan(stage - 1)
        slot = 1 + sum(p.size[other] - 1 for other in self.order[: stage - 1])
        made = []
        for i, peer in enumerate(p.others(axis)):
            here = pl.ds(first + i * len(combos), len(combos))
            made.append(copy_to(self.give.at[here], self.get.at[here], self.sems, self.base + slot + i, peer))
        return made

    def step(self, stage):
        p = self.at
        last = len(self.order) + 1
        if stage:
            for made in self.copies(stage - 1):
                made.wait()
        if stage >= 2:
            axis, combos, first = self.plan(stage - 2)
            for k, index in enumerate(combos):
                total = self.keep[self.kept(index)]
                for i in range(p.size[axis] - 1):
                    total = total + self.get[first + i * len(combos) + k].astype(WIDE)
                if stage == last:
                    self.out(total)
                else:
                    self.keep[self.kept(index)] = total
        if 1 <= stage < last:
            axis, combos, first = self.plan(stage - 1)
            for i in range(p.size[axis] - 1):
                for k, index in enumerate(combos):
                    target = {**index, axis: p.step_of(axis, i + 1)}
                    self.give[first + i * len(combos) + k] = self.now(stage - 1, target).astype(LOW)
        if stage < last:
            for made in self.copies(stage):
                made.start()
        if stage == 1:
            axis, combos, first = self.plan(0)
            for index in combos:
                self.keep[self.kept(index)] = self.now(0, index)


def scatter_slots(depth):
    return depth + 3


def scatter_scratch(depth, order, shape):
    kept = {"z": 4, "s": depth}.get(order[0], 2 * depth)
    return [
        pltpu.VMEM(shape[:-2] + (2, 2, depth) + shape[-2:], LOW),
        pltpu.VMEM((4 * depth - 1,) + shape, LOW),
        pltpu.VMEM((4 * depth - 1,) + shape, LOW),
        pltpu.VMEM((kept,) + shape, WIDE),
    ]


class SumTile:
    def __init__(self, place, out, give, get, sems, base):
        self.at, self.out, self.give, self.get, self.sems, self.base = place, out, give, get, sems, base

    def copies(self, stage):
        p = self.at
        if stage == 0:
            moves = [(p.shard(turn), turn - 1, p.over_seq(turn)) for turn in (1, 2, 3)]
        else:
            moves = [(4, 2 + step, p.over_grp(step)) for step in range(1, 2 * p.depth)]
        return [
            copy_to(self.give.at[a], self.get.at[b], self.sems, self.base + b, peer) for a, b, peer in moves
        ]

    def step(self, stage):
        if stage:
            for made in self.copies(stage - 1):
                made.wait()
        if stage == 1:
            self.give[4] = (self.give[self.at.seq] + self.get[0]) + (self.get[1] + self.get[2])
        if stage == 2:
            total = self.give[4]
            for step in range(1, 2 * self.at.depth):
                total = total + self.get[2 + step]
            self.out[...] = total
            return
        for made in self.copies(stage):
            made.start()


def run(steps):
    for piece, stage in steps:
        piece.step(stage)


def skewed(pieces, stages):
    stages = list(stages)
    return [
        (piece, stages[slot - k])
        for slot in range(len(pieces) + len(stages) - 1)
        for k, piece in enumerate(pieces)
        if 0 <= slot - k < len(stages)
    ]


def unit_rows_of(values):
    centred = values - jnp.mean(values, axis=-1, keepdims=True)
    factor = lax.rsqrt(jnp.mean(centred * centred, axis=-1, keepdims=True) + NORM_EPSILON)
    return centred * factor, factor


def put_tiles(ref, here, value):
    for k in range(ref.shape[0]):
        ref[k, here, :] = value[:, 128 * k : 128 * (k + 1)]


def get_tiles(ref, here):
    return jnp.concatenate([ref[k, here, :] for k in range(ref.shape[0])], axis=1)


def hide_future(scores, first_slot, first_row):
    slot = lax.broadcasted_iota(jnp.int32, scores.shape, 0) + first_slot
    row = lax.broadcasted_iota(jnp.int32, scores.shape, 1) + first_row
    return jnp.where(3 * slot <= row, scores, MASKED_SCORE)


def span(number, size):
    return pl.ds(pl.multiple_of(number * size, size), size)


def front_kernel(depth, tok, wq, wm, wo, wu, wd, vec, *refs):
    early_out, late, down, vectors, edge, qh_out, kv_out, mixed_out, lse, attended = refs[:10]
    tiles, wide_a, low_a, qs, ms, kvt, own_late, own_down, tile, early, qh, kv, mixed = refs[10:23]
    gsend, grecv, xsend, xrecv, lsem, osem = refs[23:]
    p = Place(depth)
    own = (p.y, p.x, p.z, p.c)
    rows, width = tok.shape
    slots = rows // 3
    size = qh.shape[1]
    lanes = 2 * size
    shard_lanes = vec.shape[1]
    tile[...] = jnp.zeros_like(tile)
    tile[0 : vec.shape[0], 0:shard_lanes] = vec[...]
    tiles[own] = pltpu.roll(tile[...], p.grp * shard_lanes, 1).astype(LOW)
    early[(0,) + own] = wq[...].astype(LOW)
    for tap in range(3):
        for half in range(2):
            columns = []
            for head in range(4 * half, 4 * half + 4):
                columns.append(wm[tap, :, head * size : (head + 1) * size])
                columns.append(wm[tap, :, width + head * size : width + (head + 1) * size])
            early[(1 + 3 * half + tap,) + own] = jnp.concatenate(columns, axis=1).astype(LOW)
    own_late[0] = wo[...].astype(LOW)
    for part in range(4):
        own_late[1 + part] = wu[:, part * width : (part + 1) * width].astype(LOW)
    own_down[...] = wd[...].astype(LOW)
    p.greet()
    half_down = down.shape[4] // 2
    views = [
        (lambda *i: tiles.at[i], "zxy", None),
        (bind(early, 0, 1), "zxy", None),
        (bind(early, 1, 1), "zyx", None),
        (bind(early, 2, 1), "zxy", None),
        (bind(early, 3, 1), "yzx", None),
        (bind(early, 4, 1), "zyx", None),
        (bind(early, 5, 1), "xzy", None),
        (bind(early, 6, 1), "xyz", None),
        (bind(late, 0, 3), "xyz", own_late.at[pl.ds(0, 3)]),
        (bind(late, 3, 2), "yzx", own_late.at[pl.ds(3, 2)]),
        (bind_rows(down, 0, half_down), "xzy", own_down.at[pl.ds(0, half_down)]),
        (bind_rows(down, half_down, half_down), "yxz", own_down.at[pl.ds(half_down, half_down)]),
    ]
    step = gather_slots(depth)
    pieces = [
        Gather(p, view, (gsend, grecv), step * k, order, first) for k, (view, order, first) in enumerate(views)
    ]
    vector_piece, query_piece, soon, later = pieces[0], pieces[1], pieces[2:8], pieces[8:]
    for piece in pieces[:8]:
        piece.step(0)
    for k, piece in enumerate(later):
        piece.place_own(lsem.at[k]).start()
        piece.step(0)

    block = 128

    @pl.loop(0, rows // block)
    def _(number):
        at = pl.multiple_of(number * block, block)
        unit, _ = unit_rows_of(tok[pl.ds(at, block), :].astype(WIDE))
        put_tiles(wide_a, pl.ds(at + 8, block), unit)

    for stage in (1, 2):
        vector_piece.step(stage)
        query_piece.step(stage)
    for piece in soon[2:3] + soon[4:] + soon[:2] + soon[3:4]:
        piece.step(1)
    vector_piece.step(3)
    query_piece.step(3)
    vector_piece.step(4)
    tile_lanes = tiles.shape[-1]
    for y in range(2):
        for x in range(2):
            total = jnp.zeros(tiles.shape[-2:], WIDE)
            for z in range(depth):
                for c in range(2):
                    total += tiles[y, x, z, c].astype(WIDE)
            s = 2 * y + x
            vectors[:, s * tile_lanes : (s + 1) * tile_lanes] = total
    gain, shift = vectors[0:1, :], vectors[1:2, :]

    @pl.loop(0, rows // block)
    def _(number):
        at = pl.multiple_of(number * block, block)
        normed = (get_tiles(wide_a, pl.ds(at + 8, block)) * gain + shift).astype(LOW)
        low_a[pl.ds(at, block), :] = normed
        put_tiles(wide_a, pl.ds(at + 8, block), normed.astype(WIDE))

    def query_copy(half, turn):
        return copy_to(
            qs.at[half, p.shard(turn)],
            qh.at[half, :, span(p.seq, rows)],
            (xsend, xrecv),
            7 + 3 * half + turn - 1,
            p.over_seq(turn),
        )

    def send_queries(half):
        for turn in (1, 2, 3):
            query_copy(half, turn).start()
        qh[half, :, span(p.seq, rows)] = qs[half, p.seq]

    last = p.seq == 3

    def edge_copy():
        return copy_to(
            wide_a.at[:, pl.ds(rows, 8)], wide_a.at[:, pl.ds(0, 8)], (xsend, xrecv), 0, {"seq": lax.rem(p.seq + 1, 4)}
        )

    @pl.when(jnp.logical_not(last))
    def _():
        edge_copy().start()

    query_piece.step(4)
    turned = lax.dot_general(early[0].reshape(width, width).T, low_a[...], NT, preferred_element_type=WIDE)
    qs[...] = turned.astype(LOW).reshape(qs.shape)
    for piece in soon[5:] + soon[:2] + soon[3:4] + soon[2:3] + soon[4:5]:
        piece.step(2)
    send_queries(0)
    for k, piece in enumerate(later):
        piece.place_own(lsem.at[k]).wait()
        piece.step(1)
    for piece in soon:
        piece.step(3)
    for piece in soon:
        piece.step(4)
    for piece in later[:1] + later[3:]:
        piece.step(2)

    @pl.when(p.seq > 0)
    def _():
        edge_copy().wait_recv()

    @pl.when(jnp.logical_not(last))
    def _():
        edge_copy().wait_send()

    @pl.when(p.seq == 0)
    def _():
        wide_a[:, 0:8, :] = jnp.zeros((width // 128, 8, 128), WIDE)

    edge[...] = wide_a[:, 0:8, :]
    parts = rows // PART
    strips = qh.shape[2] // STRIP

    def early_leaves():
        return pltpu.make_async_copy(early, early_out, osem.at[0])

    def kv_leaves(half):
        return pltpu.make_async_copy(kv.at[half], kv_out.at[half], osem.at[1 + half])

    def qh_leaves(half):
        return pltpu.make_async_copy(qh.at[half], qh_out.at[half], osem.at[3 + half])

    def mixed_leaves(half, strip, index):
        here = span(strip, STRIP)
        return pltpu.make_async_copy(mixed.at[half, :, here], mixed_out.at[half, :, here], osem.at[index])

    def mixed_stays(half, part):
        return pltpu.make_async_copy(
            mixed.at[half, :, span(p.seq * parts + part, PART)],
            attended.at[half, p.seq, :, span(part, PART)],
            osem.at[5 + 2 * strips + half * parts + part],
        )

    early_leaves().start()

    def weight(j):
        return early[j].reshape(width, width)

    mine = span(p.seq, slots)

    def memory_copy(half, turn):
        return copy_to(
            ms.at[half, :, span(p.shard(turn), lanes)],
            kv.at[half, mine],
            (xsend, xrecv),
            1 + 3 * half + turn - 1,
            p.over_seq(turn),
        )

    def project(half):
        for tap in range(3):
            window = get_tiles(wide_a, pl.ds(6 + tap, slots, stride=3)).astype(LOW)
            part = dot(window, weight(1 + 3 * half + tap))
            total = part if tap == 0 else total + part
        ms[half] = total.astype(LOW)
        for turn in (3, 1, 2):
            memory_copy(half, turn).start()
        kv[half, mine, :] = ms[half, :, span(p.seq, lanes)]

    project(0)
    project(1)
    send_queries(1)
    for turn in (1, 2, 3):
        memory_copy(0, turn).wait()
    kvt[0] = kv[0].T
    kv_leaves(0).start()

    def mixed_copy(half, turn, part):
        shard = p.shard(turn)
        return copy_to(
            mixed.at[half, :, span(shard * parts + part, PART)],
            attended.at[half, p.seq, :, span(part, PART)],
            (xsend, xrecv),
            13 + (3 * half + turn - 1) * parts + part,
            p.over_seq(turn),
        )

    def attend(half, seen, strip):
        here = span(strip, STRIP)
        queries = qh[half, :, here] * jnp.bfloat16(size ** (-0.5))
        queries = jnp.concatenate([queries, jnp.zeros_like(queries)], axis=0)
        whole = seen - SLOTS
        scores = hide_future(dot(kv[half, whole:seen, :], queries), whole, strip * STRIP)
        if whole:
            scores = jnp.concatenate([dot(kv[half, 0:whole, :], queries), scores], axis=0)
        highest = jnp.max(scores, axis=0, keepdims=True)
        exponent = jnp.exp(scores - highest)
        summed = jnp.sum(exponent, axis=0, keepdims=True)
        out = dot(kvt[half, size:lanes, 0:seen], exponent.astype(LOW)) * (1.0 / summed)
        lse[half, strip] = highest + jnp.log(summed)
        mixed[half, :, here] = out.astype(LOW)

    def work(half):
        @pl.loop(0, strips)
        def _(it):
            for number, turn in ((1, 1), (3, 2), (4, 3)):

                @pl.when(it == number)
                def _():
                    query_copy(half, turn).wait()

            strip = p.strip(it)
            for group in range(strips):

                @pl.when(strip == group)
                def _():
                    attend(half, SLOTS * (group + 1), strip)

            mixed_leaves(half, strip, 5 + half * strips + it).start()
            for k in range(2):
                granule = 2 * strip + k
                shard, part = lax.div(granule, parts), lax.rem(granule, parts)
                turn = p.turn_to(shard)

                @pl.when(turn > 0)
                def _():
                    mixed_copy(half, turn, part).start()

                @pl.when(turn == 0)
                def _():
                    mixed_stays(half, part).start()

            @pl.when(it == (5, 3)[half])
            def _():
                for piece in later[1:3]:
                    piece.step(2 + half)

    work(0)
    for turn in (1, 2, 3):
        memory_copy(1, turn).wait()
    kvt[1] = kv[1].T
    kv_leaves(1).start()
    qh_leaves(0).start()
    work(1)
    qh_leaves(1).start()
    for piece in later[:1] + later[3:]:
        piece.step(3)
    for piece in later:
        piece.step(4)
    early_leaves().wait()
    for half in range(2):
        kv_leaves(half).wait()
        qh_leaves(half).wait()
        for it in range(strips):
            mixed_leaves(half, p.strip(it), 5 + half * strips + it).wait()
        for part in range(parts):
            mixed_stays(half, part).wait()
            for turn in (1, 2, 3):
                mixed_copy(half, turn, part).wait()


def front(tok, params):
    wq, wm, wo, wu, wd, vec = params
    groups = lax.axis_size("grp")
    depth = groups // 2
    rows, width = tok.shape
    own, slots, size = wq.shape[0], rows // 3, width // H
    lanes = 2 * size
    tile_lanes = vec.shape[1] * groups
    whole = (2, 2, depth, 2)
    sems = pltpu.SemaphoreType.DMA((12 * gather_slots(depth),))
    parts = rows // PART
    swaps = pltpu.SemaphoreType.DMA((13 + 6 * parts,))
    anywhere = pl.BlockSpec(memory_space=pl.ANY)
    vmem = pl.BlockSpec(memory_space=pltpu.VMEM)
    return pl.pallas_call(
        functools.partial(front_kernel, depth),
        out_shape=(
            shaped(EARLY, *whole, own, width),
            shaped(LATE, *whole, own, width),
            shaped(*whole, *wd.shape),
            shaped(ROWS, 4 * tile_lanes, kind=WIDE),
            shaped(width // 128, 8, 128, kind=WIDE),
            shaped(2, size, 4 * rows),
            shaped(2, 4 * slots, lanes),
            shaped(2, size, 4 * rows),
            shaped(2, 4 * rows // STRIP, 1, STRIP, kind=WIDE),
            shaped(2, 4, size, rows),
        ),
        in_specs=in_vmem(7),
        out_specs=[anywhere] * 3 + [vmem] * 2 + [anywhere] * 3 + [vmem, anywhere],
        scratch_shapes=[
            pltpu.VMEM((*whole, ROWS, tile_lanes), LOW),
            pltpu.VMEM((width // 128, rows + 8, 128), WIDE),
            pltpu.VMEM((rows, width), LOW),
            pltpu.VMEM((2, 4, size, rows), LOW),
            pltpu.VMEM((2, slots, width), LOW),
            pltpu.VMEM((2, lanes, 4 * slots), LOW),
            pltpu.VMEM((LATE, own, width), LOW),
            pltpu.VMEM(wd.shape, LOW),
            pltpu.VMEM((ROWS, tile_lanes), WIDE),
            pltpu.VMEM((EARLY, *whole, own, width), LOW),
            pltpu.VMEM((2, size, 4 * rows), LOW),
            pltpu.VMEM((2, 4 * slots, lanes), LOW),
            pltpu.VMEM((2, size, 4 * rows), LOW),
            sems,
            sems,
            swaps,
            swaps,
            pltpu.SemaphoreType.DMA((4,)),
            pltpu.SemaphoreType.DMA((5 + 2 * (4 * rows // STRIP) + 2 * parts,)),
        ],
        compiler_params=pltpu.CompilerParams(
            collective_id=0, has_side_effects=True, vmem_limit_bytes=58 * MEGA
        ),
    )(tok, wq, wm, wo, wu, wd, vec)


def middle_kernel(depth, tok_in, cot_in, att_in, late_in, down_in, vec, length, *refs):
    out_to, dres_to, doh, g_stack_to, g_down_to, g_vec = refs[:6]
    tok, cot, att, late, down, out, dres, g_stack, g_down = refs[6:15]
    zs, dus, cs, es, ys, dos, xsend, xrecv, isem, osem, gsem = refs[15:]
    p = Place(depth)
    arriving = [
        pltpu.make_async_copy(source, target, isem.at[k])
        for k, (source, target) in enumerate(
            ((att_in, att), (tok_in, tok), (late_in, late), (down_in, down), (cot_in, cot))
        )
    ]
    for made in arriving:
        made.start()
    p.greet(beyond=False)
    rows, width = tok.shape
    hidden = zs.shape[1]
    gain, shift, bias = vec[2:3, :], vec[3:4, :], vec[4:5, :]
    inner = 0.7978845608028654
    cubic = inner * 0.044715
    g_vec[...] = jnp.zeros_like(g_vec)

    parts = rows // PART

    def do_copy(number, turn):
        return copy_to(
            dos.at[:, p.shard(turn), :, span(number, PART)],
            doh.at[:, :, span(p.seq * parts + number, PART)],
            (xsend, xrecv),
            3 * number + turn - 1,
            p.over_seq(turn),
        )

    def leave(number):
        here = span(number, PART)
        pairs = (
            (out.at[here], out_to.at[here]),
            (dres.at[here], dres_to.at[here]),
            (dos.at[:, p.seq, :, here], doh.at[:, :, span(p.seq * parts + number, PART)]),
        )
        return [pltpu.make_async_copy(a, b, osem.at[3 * number + k]) for k, (a, b) in enumerate(pairs)]

    for made in arriving[:3]:
        made.wait()

    @pl.loop(0, parts)
    def _(number):
        at = pl.multiple_of(number * PART, PART)
        here = pl.ds(at, PART)
        attended = att[:, :, :, here].reshape(width, PART).T
        residual = tok[here, :].astype(WIDE) + dot(attended, late[0])
        unit, factor = unit_rows_of(residual)
        normed = (unit * gain + shift).astype(LOW)
        cs[here, :] = normed
        @pl.when(number == 0)
        def _():
            for k, (source, target) in ((3, (down_in, down)), (4, (cot_in, cot))):
                pltpu.make_async_copy(source, target, isem.at[k]).wait()

        place = lax.broadcasted_iota(jnp.int32, (PART, 1), 0) + (p.seq * rows + at)
        live = (place < length[0, 0]).astype(WIDE)
        upstream = cot[here, :].astype(WIDE) * live
        upstream_low = upstream.astype(LOW)
        es[here, :] = upstream_low
        result = residual + bias
        back = jnp.zeros((PART, width), WIDE)
        for part in range(hidden // width):
            here_hidden = pl.ds(part * width, width)
            u = dot(normed, late[1 + part]) + vec[5 + part : 6 + part, :]
            square = u * u
            half = 0.5 + 0.5 * jnp.tanh(u * (inner + cubic * square))
            active = u * half
            slope = half + active * (1.0 - half) * (2.0 * inner + 6.0 * cubic * square)
            active_low = active.astype(LOW)
            zs[here, here_hidden] = active_low
            result += dot(active_low, down[here_hidden, :])
            pulled = lax.dot_general(upstream_low, down[here_hidden, :], NT, preferred_element_type=WIDE)
            grad = (pulled * slope).astype(LOW)
            dus[here, here_hidden] = grad
            g_vec[5 + part : 6 + part, :] += jnp.sum(grad.astype(WIDE), axis=0, keepdims=True)
            back += lax.dot_general(grad, late[1 + part], NT, preferred_element_type=WIDE)
        out[here, :] = result.astype(LOW)
        scaled = back * gain
        total = upstream + factor * (
            scaled
            - jnp.mean(scaled, axis=-1, keepdims=True)
            - unit * jnp.mean(scaled * unit, axis=-1, keepdims=True)
        )
        dres[here, :] = total
        branch = total.astype(LOW)
        ys[here, :] = branch
        turned = lax.dot_general(late[0], branch, NT, preferred_element_type=WIDE)
        dos[:, :, :, here] = turned.astype(LOW).reshape(dos.shape[:3] + (PART,))
        for turn in (3, 1, 2):
            do_copy(number, turn).start()
        for made in leave(number):
            made.start()
        g_vec[2:3, :] += jnp.sum(back * unit, axis=0, keepdims=True)
        g_vec[3:4, :] += jnp.sum(back, axis=0, keepdims=True)
        g_vec[4:5, :] += jnp.sum(upstream, axis=0, keepdims=True)

    def finished(ref, target, index):
        made = pltpu.make_async_copy(ref, target, gsem.at[index])
        made.start()
        return made

    left = []
    for part in range(hidden // width):
        piece = pl.ds(part * width, width)
        g_down[piece, :] = over_rows(zs[:, piece], es[...]).astype(LOW)
        left.append(finished(g_down.at[piece], g_down_to.at[piece], 5 + part))
    g_stack[0] = dot(att[...].reshape(width, rows), ys[...]).astype(LOW)
    left.append(finished(g_stack.at[0], g_stack_to.at[0], 0))
    for part in range(hidden // width):
        piece = pl.ds(part * width, width)
        g_stack[1 + part] = over_rows(cs[...], dus[:, piece]).astype(LOW)
        left.append(finished(g_stack.at[1 + part], g_stack_to.at[1 + part], 1 + part))
    for number in range(parts):
        for turn in (1, 2, 3):
            do_copy(number, turn).wait()
        for made in leave(number):
            made.wait()
    for made in left:
        made.wait()


def middle(tok, cot, att, late, down, vec, length):
    rows, width = tok.shape
    hidden = down.shape[0]
    sems = pltpu.SemaphoreType.DMA((3 * (rows // PART),))
    return pl.pallas_call(
        functools.partial(middle_kernel, lax.axis_size("grp") // 2),
        out_shape=(
            shaped(rows, width),
            shaped(rows, width, kind=WIDE),
            shaped(2, width // H, 4 * rows),
            shaped(LATE, width, width),
            shaped(hidden, width),
            shaped(*vec.shape, kind=WIDE),
        ),
        in_specs=[pl.BlockSpec(memory_space=pl.ANY)] * 5
        + [pl.BlockSpec(memory_space=pltpu.VMEM), pl.BlockSpec(memory_space=pltpu.SMEM)],
        out_specs=[pl.BlockSpec(memory_space=pl.ANY)] * 5 + [pl.BlockSpec(memory_space=pltpu.VMEM)],
        scratch_shapes=[pltpu.VMEM(x.shape, x.dtype) for x in (tok, cot, att, late, down)]
        + [
            pltpu.VMEM((rows, width), LOW),
            pltpu.VMEM((rows, width), WIDE),
            pltpu.VMEM((LATE, width, width), LOW),
            pltpu.VMEM((hidden, width), LOW),
            pltpu.VMEM((rows, hidden), LOW),
            pltpu.VMEM((rows, hidden), LOW),
            pltpu.VMEM((rows, width), LOW),
            pltpu.VMEM((rows, width), LOW),
            pltpu.VMEM((rows, width), LOW),
            pltpu.VMEM(att.shape, LOW),
            sems,
            sems,
            pltpu.SemaphoreType.DMA((5,)),
            sems,
            pltpu.SemaphoreType.DMA((LATE + hidden // width,)),
        ],
        compiler_params=pltpu.CompilerParams(
            collective_id=1, has_side_effects=True, vmem_limit_bytes=58 * MEGA
        ),
    )(tok, cot, att, late, down, vec, length)


def back_kernel(depth, *refs):
    far_inputs, (lse, vec, edge, g_vec) = refs[:9], refs[9:13]
    grad, out_early, out_late, out_down, out_vec = refs[13:18]
    scatter, refs = refs[18:54], refs[54:]
    near_inputs, refs = refs[:9], refs[9:]
    tok, kv, doh, qh, mixed, g_late, g_down, early, dres = near_inputs
    g_early, dkv, kvt, dqs, dq, dms, dm, wide_a, low_a, wide_da, da, after, give, get, out_sum = refs[:15]
    rsend, rrecv, xsend, xrecv, isem = refs[15:]
    p = Place(depth)
    arriving = [
        pltpu.make_async_copy(a, b, isem.at[k]) for k, (a, b) in enumerate(zip(far_inputs, near_inputs))
    ]
    for made in arriving:
        made.start()
    rows, width = tok.shape
    slots = rows // 3
    size = qh.shape[1]
    lanes = 2 * size
    scale = size ** (-0.5)
    parts = rows // PART
    strips = qh.shape[2] // STRIP
    step = scatter_slots(depth)
    p.greet()

    def out_to(ref, first, count):
        def put(value):
            ref[first : first + count] = value

        return put

    half_down = g_down.shape[4] // 2
    todo = [
        (bind(g_late, 0, 3), out_to(out_late, 0, 3), bind(far_inputs[5], 0, 3)),
        (bind(g_late, 3, 2), out_to(out_late, 3, 2), bind(far_inputs[5], 3, 2)),
        (bind_rows(g_down, 0, half_down), out_to(out_down, 0, half_down), bind_rows(far_inputs[6], 0, half_down)),
        (
            bind_rows(g_down, half_down, half_down),
            out_to(out_down, half_down, half_down),
            bind_rows(far_inputs[6], half_down, half_down),
        ),
        (bind(g_early, 0, 1), out_to(out_early, 0, 1), None),
        (bind(g_early, 1, 2), out_to(out_early, 1, 2), None),
        (bind(g_early, 3, 1), out_to(out_early, 3, 1), None),
        (bind(g_early, 4, 2), out_to(out_early, 4, 2), None),
        (bind(g_early, 6, 1), out_to(out_early, 6, 1), None),
    ]
    pieces = [
        Scatter(p, view, out, scatter[4 * k : 4 * k + 4], (rsend, rrecv), step * k, SCATTER_ORDERS[k], far)
        for k, (view, out, far) in enumerate(todo)
    ]
    soon, query, first, second = pieces[:4], pieces[4:5], pieces[5:7], pieces[7:]
    small = SumTile(p, out_vec, give, get, (rsend, rrecv), step * len(pieces))
    for piece in soon:
        piece.step(0)
    gain, shift = vec[0:1, :], vec[1:2, :]
    block = 128
    wide_a[:, 0:8, :] = edge[...]
    arriving[0].wait()

    @pl.loop(0, rows // block)
    def _(number):
        at = pl.multiple_of(number * block, block)
        unit, _ = unit_rows_of(tok[pl.ds(at, block), :].astype(WIDE))
        normed = (unit * gain + shift).astype(LOW)
        low_a[pl.ds(at, block), :] = normed
        put_tiles(wide_a, pl.ds(at + 8, block), normed.astype(WIDE))

    for made in arriving[1:5]:
        made.wait()
    for half in range(2):
        kvt[half] = kv[half].T
    dkv[...] = jnp.zeros_like(dkv)

    def dq_copy(half, turn, part):
        return copy_to(
            dqs.at[half, :, span(p.shard(turn) * parts + part, PART)],
            dq.at[half, p.seq, :, span(part, PART)],
            (xsend, xrecv),
            (3 * half + turn - 1) * parts + part,
            p.over_seq(turn),
        )

    def attend(half, seen, strip):
        here = span(strip, STRIP)
        queries = qh[half, :, here] * jnp.bfloat16(scale)
        incoming = doh[half, :, here]
        middle = jnp.sum(incoming.astype(WIDE) * mixed[half, :, here].astype(WIDE), axis=0, keepdims=True)
        blank = jnp.zeros_like(queries)
        queries = jnp.concatenate([queries, blank], axis=0)
        incoming = jnp.concatenate([blank, incoming], axis=0)
        total = lse[half, strip]
        turned = jnp.zeros((size, STRIP), WIDE)
        for start in range(0, seen, 2 * SLOTS):
            stop = min(start + 2 * SLOTS, seen)
            keys = kv[half, start:stop, :]
            scores = dot(keys, queries)
            if stop == seen:
                clear = stop - SLOTS - start
                masked = hide_future(scores[clear:], stop - SLOTS, strip * STRIP)
                scores = jnp.concatenate([scores[:clear], masked], axis=0) if clear else masked
            weights = jnp.exp(scores - total)
            slope = (weights * (dot(keys, incoming) - middle)).astype(LOW)
            dkv[half, start:stop, :] += lax.dot_general(
                slope, queries, NT, preferred_element_type=WIDE
            ) + lax.dot_general(weights.astype(LOW), incoming, NT, preferred_element_type=WIDE)
            turned += dot(kvt[half, 0:size, start:stop], slope)
        dqs[half, :, here] = (turned * scale).astype(LOW)

    def memory_copy(half, turn):
        return copy_to(
            dms.at[half, span(p.shard(turn), slots)],
            dm.at[half, :, span(p.seq, lanes)],
            (xsend, xrecv),
            6 * parts + 3 * half + turn - 1,
            p.over_seq(turn),
        )

    def send_memory(half):
        dms[half] = dkv[half].astype(LOW)
        for turn in (3, 1, 2):
            memory_copy(half, turn).start()
        dm[half, :, span(p.seq, lanes)] = dms[half, span(p.seq, slots), :]

    def put_early(j, value):
        g_early[j] = value.astype(LOW).reshape(g_early.shape[1:])

    def memory_gradient(half, tap):
        window = get_tiles(wide_a, pl.ds(6 + tap, slots, stride=3)).astype(LOW)
        put_early(1 + 3 * half + tap, over_rows(window, dm[half]))

    @pl.loop(0, 2 * strips)
    def _(turn_number):
        half, it = lax.div(turn_number, strips), lax.rem(turn_number, strips)

        @pl.when(turn_number == strips)
        def _():
            send_memory(0)

        @pl.when(turn_number == strips + 3)
        def _():
            for turn in (1, 2, 3):
                memory_copy(0, turn).wait()
            for tap in range(3):
                memory_gradient(0, tap)
            for piece in first:
                piece.step(0)

        strip = p.strip(strips - 1 - it)
        for group in range(strips):

            @pl.when(strip == group)
            def _():
                attend(half, SLOTS * (group + 1), strip)

        for k in range(2):
            granule = 2 * strip + k
            shard, part = lax.div(granule, parts), lax.rem(granule, parts)
            turn = p.turn_to(shard)

            @pl.when(turn > 0)
            def _():
                dq_copy(half, turn, part).start()

            @pl.when(turn == 0)
            def _():
                dq[half, p.seq, :, span(part, PART)] = dqs[half, :, span(granule, PART)]

        @pl.when(turn_number == 1)
        def _():
            for k in (5, 6):
                pltpu.make_async_copy(far_inputs[k], near_inputs[k], isem.at[k]).wait()

        for when, steps in (
            (1, [(piece, 1) for piece in soon]),
            (7, [(piece, 2) for piece in soon]),
            (10, [(piece, 1) for piece in first]),
            (10, [(piece, 3) for piece in soon]),
        ):

            @pl.when(turn_number == when)
            def _():
                run(steps)

    send_memory(1)
    for half in range(2):
        for turn in (1, 2, 3):
            for part in range(parts):
                dq_copy(half, turn, part).wait()
    for made in arriving[7:]:
        made.wait()
    turned = dq[...].reshape(width, rows)
    put_early(0, dot(turned, low_a[...]).T)
    query[0].step(0)
    da[...] = lax.dot_general(turned.T, early[0], NT, preferred_element_type=WIDE)
    for turn in (1, 2, 3):
        memory_copy(1, turn).wait()
    run([(piece, 2) for piece in first])
    query[0].step(1)
    for tap in range(3):
        memory_gradient(1, tap)
        if tap:
            second[tap - 1].step(0)
    wide_da[:, 0:8, :] = jnp.zeros((width // 128, 8, 128), WIDE)
    for tap in range(3):
        pulled = lax.dot_general(dm[0], early[1 + tap], NT, preferred_element_type=WIDE)
        pulled += lax.dot_general(dm[1], early[4 + tap], NT, preferred_element_type=WIDE)
        put_tiles(wide_da, pl.ds(6 + tap, slots, stride=3), pulled)

    def edge_copy():
        return copy_to(
            wide_da.at[:, pl.ds(0, 8)], after, (xsend, xrecv), 6 * parts + 6, {"seq": lax.rem(p.seq + 3, 4)}
        )

    @pl.when(p.seq > 0)
    def _():
        edge_copy().start()

    run([(piece, 1) for piece in second])
    run([(query[0], 2), (first[0], 3), (first[1], 3)])

    @pl.when(p.seq < 3)
    def _():
        edge_copy().wait_recv()

    @pl.when(p.seq > 0)
    def _():
        edge_copy().wait_send()

    @pl.when(p.seq == 3)
    def _():
        after[...] = jnp.zeros_like(after)

    wide_da[:, rows + 6 : rows + 8, :] = after[:, 6:8, :]
    out_sum[...] = g_vec[...]

    @pl.loop(0, rows // block)
    def _(number):
        at = pl.multiple_of(number * block, block)
        here = pl.ds(at, block)
        unit, factor = unit_rows_of(tok[here, :].astype(WIDE))
        upstream = da[here, :] + get_tiles(wide_da, pl.ds(at + 8, block))
        scaled = upstream * gain
        inward = factor * (
            scaled
            - jnp.mean(scaled, axis=-1, keepdims=True)
            - unit * jnp.mean(scaled * unit, axis=-1, keepdims=True)
        )
        grad[here, :] = (dres[here, :] + inward).astype(LOW)
        out_sum[0:1, :] += jnp.sum(upstream * unit, axis=0, keepdims=True)
        out_sum[1:2, :] += jnp.sum(upstream, axis=0, keepdims=True)

    tile_lanes = width // 4
    for shard in range(4):
        give[shard] = out_sum[:, shard * tile_lanes : (shard + 1) * tile_lanes]
    small.step(0)
    run([(piece, 2) for piece in second])
    run([(piece, 4) for piece in soon])
    small.step(1)
    run([(query[0], 3), (first[0], 4), (first[1], 4)])
    run([(piece, 3) for piece in second])
    small.step(2)


def back(saved, tok, dres, early, vec, edge, grads):
    qh, kv, mixed, lse, doh = saved
    g_late, g_down, g_vec = grads
    depth = lax.axis_size("grp") // 2
    rows, width = tok.shape
    size, slots = qh.shape[1], rows // 3
    lanes = 2 * size
    whole = (2, 2, depth, 2)
    own_down = g_down.shape[0] // (8 * depth)
    parts = rows // PART
    shapes = [(3, ROWS, width), (2, ROWS, width)] + [(own_down // 2, width)] * 2
    shapes += [(1, ROWS, width)] + [(2, ROWS, width), (1, ROWS, width)] * 2
    ring = pltpu.SemaphoreType.DMA((9 * scatter_slots(depth) + 2 * depth + 2,))
    swaps = pltpu.SemaphoreType.DMA((6 * parts + 7,))
    g_late = g_late.reshape(LATE, *whole, ROWS, width)
    g_down = g_down.reshape(*whole, own_down, width)
    inputs = (tok, kv, doh, qh, mixed, g_late, g_down, early, dres)
    return pl.pallas_call(
        functools.partial(back_kernel, depth),
        out_shape=(
            shaped(rows, width),
            shaped(EARLY, ROWS, width, kind=WIDE),
            shaped(LATE, ROWS, width, kind=WIDE),
            shaped(own_down, width, kind=WIDE),
            shaped(ROWS, width // 4, kind=WIDE),
        ),
        in_specs=[pl.BlockSpec(memory_space=pl.ANY)] * 9 + in_vmem(4),
        out_specs=in_vmem(5),
        scratch_shapes=[
            buf for order, shape in zip(SCATTER_ORDERS, shapes) for buf in scatter_scratch(depth, order, shape)
        ]
        + [pltpu.VMEM(x.shape, x.dtype) for x in inputs]
        + [
            pltpu.VMEM((EARLY, *whole, ROWS, width), LOW),
            pltpu.VMEM(kv.shape, WIDE),
            pltpu.VMEM((2, lanes, 4 * slots), LOW),
            pltpu.VMEM(qh.shape, LOW),
            pltpu.VMEM((2, 4, size, rows), LOW),
            pltpu.VMEM(kv.shape, LOW),
            pltpu.VMEM((2, slots, width), LOW),
            pltpu.VMEM((width // 128, rows + 8, 128), WIDE),
            pltpu.VMEM((rows, width), LOW),
            pltpu.VMEM((width // 128, rows + 8, 128), WIDE),
            pltpu.VMEM((rows, width), WIDE),
            pltpu.VMEM((width // 128, 8, 128), WIDE),
            pltpu.VMEM((5, ROWS, width // 4), WIDE),
            pltpu.VMEM((2 * depth + 2, ROWS, width // 4), WIDE),
            pltpu.VMEM(vec.shape, WIDE),
            ring,
            ring,
            swaps,
            swaps,
            pltpu.SemaphoreType.DMA((9,)),
        ],
        compiler_params=pltpu.CompilerParams(
            collective_id=2, has_side_effects=True, vmem_limit_bytes=62 * MEGA
        ),
    )(*inputs, lse, vec, edge, g_vec)


def update_kernel(*refs):
    weights, firsts, seconds = refs[0:6], refs[6:12], refs[12:18]
    early, late, down, vec = refs[18:22]
    held, outs, passed = refs[22:24], refs[24:48], refs[48:50]
    for source, target in zip(held, passed):
        target[...] = source[...]
    width = early.shape[-1]

    def put(which, at, gradient):
        results = adamw(
            weights[which][at], gradient, firsts[which][at], seconds[which][at], LEARNING_RATES[which]
        )
        for group, value in enumerate(results):
            outs[6 * group + which][at] = value

    every = slice(None)
    put(0, (every, every), early[0])
    size = width // H
    for tap in range(3):
        for kind in range(2):
            columns = [
                early[1 + 3 * half + tap, :, (2 * s + kind) * size : (2 * s + kind + 1) * size]
                for half in range(2)
                for s in range(4)
            ]
            put(1, (tap, every, slice(kind * width, (kind + 1) * width)), jnp.concatenate(columns, axis=1))
    put(2, (every, every), late[0])
    for part in range(4):
        put(3, (every, slice(part * width, (part + 1) * width)), late[1 + part])
    put(4, (every, every), down[...])
    share = weights[5].shape[1]
    tile_lanes = vec.shape[1]
    tile = pltpu.roll(vec[...], lax.rem(tile_lanes - lax.axis_index("grp") * share, tile_lanes), 1)
    put(5, (every, every), tile[0 : weights[5].shape[0], 0:share])


def update(params, firsts, seconds, grads, held):
    outs = [jax.ShapeDtypeStruct(member.shape, WIDE) for member in params] * 3
    outs += [jax.ShapeDtypeStruct(member.shape, LOW) for member in params]
    return pl.pallas_call(
        update_kernel,
        out_shape=tuple(outs) + tuple(jax.ShapeDtypeStruct(x.shape, x.dtype) for x in held),
        in_specs=in_vmem(24),
        out_specs=in_vmem(26),
    )(*params, *firsts, *seconds, *grads, *held)


def fused(tokens, cotangent, lengths, *state):
    params, firsts, seconds = state[0:6], state[6:12], state[12:18]
    width = tokens.shape[2]
    tok, cot = tokens[0], cotangent[0]
    early, late, down, vec, edge, qh, kv, mixed, lse, attended = front(tok, params)
    early = early.reshape(EARLY, width, width)
    late = late.reshape(LATE, width, width)
    down = down.reshape(-1, width)
    out, dres, doh, g_late, g_down, g_vec = middle(
        tok, cot, attended, late, down, vec, lengths.reshape(1, 1)
    )
    grad, r_early, r_late, r_down, r_vec = back(
        (qh, kv, mixed, lse, doh), tok, dres, early, vec, edge, (g_late, g_down, g_vec)
    )
    *new, out, grad = update(params, firsts, seconds, (r_early, r_late, r_down, r_vec), (out, grad))
    return (out[None], grad[None], *new)


def body(*arguments):
    tokens, shard = arguments[0], arguments[3]
    whole_tiles = shard.shape[0] % ROWS == 0 and tokens.shape[1] % PART == 0
    four = lax.axis_size("seq") == 4 and lax.axis_size("grp") % 2 == 0
    return (fused if whole_tiles and four else plain)(*arguments)


def solution(mesh):
    in_specs = (
        P("grp", "seq", None),
        P("grp", "seq", None),
        P("grp"),
        P(("seq", "grp"), None),
        P(None, ("seq", "grp"), None),
        P(("seq", "grp"), None),
        P(("seq", "grp"), None),
        P(("seq", "grp"), None),
        P(None, ("seq", "grp")),
        P(("seq", "grp"), None),
        P(None, ("seq", "grp"), None),
        P(("seq", "grp"), None),
        P(("seq", "grp"), None),
        P(("seq", "grp"), None),
        P(None, ("seq", "grp")),
        P(("seq", "grp"), None),
        P(None, ("seq", "grp"), None),
        P(("seq", "grp"), None),
        P(("seq", "grp"), None),
        P(("seq", "grp"), None),
        P(None, ("seq", "grp")),
    )
    out_specs = (
        P("grp", "seq", None),
        P("grp", "seq", None),
        P(("seq", "grp"), None),
        P(None, ("seq", "grp"), None),
        P(("seq", "grp"), None),
        P(("seq", "grp"), None),
        P(("seq", "grp"), None),
        P(None, ("seq", "grp")),
        P(("seq", "grp"), None),
        P(None, ("seq", "grp"), None),
        P(("seq", "grp"), None),
        P(("seq", "grp"), None),
        P(("seq", "grp"), None),
        P(None, ("seq", "grp")),
        P(("seq", "grp"), None),
        P(None, ("seq", "grp"), None),
        P(("seq", "grp"), None),
        P(("seq", "grp"), None),
        P(("seq", "grp"), None),
        P(None, ("seq", "grp")),
        P(("seq", "grp"), None),
        P(None, ("seq", "grp"), None),
        P(("seq", "grp"), None),
        P(("seq", "grp"), None),
        P(("seq", "grp"), None),
        P(None, ("seq", "grp")),
    )
    return jax.shard_map(body, mesh=mesh, in_specs=in_specs, out_specs=out_specs, check_vma=False)
```
